32 devices in a mesh: dp: 8 (over z, x), fsdp: 4 (over y, core).
Axes of the slice: x: 2, y: 2, z: 4, core: 2. Of those that a mesh axis runs over, the one named last changes fastest.
Arguments:
- byte_states: bfloat16 [8192, 1024], P(('dp', 'fsdp')), may hold values from -6 to 6
- doc_lengths: int32 [8, 2], P('dp'), may hold values from 0 to 128, as said below
- out_grad: bfloat16 [8192, 1024], P(('dp', 'fsdp')), may hold values from -6 to 6
- patch_proj: bfloat16 [8192, 1024], P(('dp', 'fsdp')), may hold values from -0.0625 to 0.0625
- global_gain: bfloat16 [1024], P(('dp', 'fsdp')), may hold values from 0.099609375 to 1.8984375
- in_proj: bfloat16 [1024, 4384], P(('dp', 'fsdp')), may hold values from -0.1875 to 0.1875
- conv_weight: bfloat16 [2304, 4], P(('dp', 'fsdp')), may hold values from -3 to 3
- conv_bias: bfloat16 [2304], P(('dp', 'fsdp')), may hold values from -3 to 3
- dt_bias: float32 [32], replicated, may hold values from -4 to -1
- a_log: float32 [32], replicated, may hold values from -4 to 1
- skip_weight: float32 [32], replicated, may hold values from 0.5 to 1.5
- mixer_gain: bfloat16 [2048], P(('dp', 'fsdp')), may hold values from 0.099609375 to 1.8984375
- out_proj: bfloat16 [2048, 1024], P(('dp', 'fsdp')), may hold values from -0.125 to 0.125
- attn_gain: bfloat16 [1024], P(('dp', 'fsdp')), may hold values from 0.099609375 to 1.8984375
- qkv_proj: bfloat16 [1024, 3072], P(('dp', 'fsdp')), may hold values from -0.1875 to 0.1875
- attn_out: bfloat16 [1024, 1024], P(('dp', 'fsdp')), may hold values from -0.375 to 0.375
- ffn_gain: bfloat16 [1024], P(('dp', 'fsdp')), may hold values from 0.099609375 to 1.8984375
- gate_proj: bfloat16 [1024, 4096], P(('dp', 'fsdp')), may hold values from -0.1875 to 0.1875
- up_proj: bfloat16 [1024, 4096], P(('dp', 'fsdp')), may hold values from -0.1875 to 0.1875
- down_proj: bfloat16 [4096, 1024], P(('dp', 'fsdp')), may hold values from -0.09375 to 0.09375
Outputs:
- block_out: bfloat16 [8192, 1024], P(('dp', 'fsdp'))
- grad_states: float32 [8192, 1024], P(('dp', 'fsdp'))
- grad_patch_proj: float32 [8192, 1024], P(('dp', 'fsdp'))
- grad_global_gain: float32 [1024], P(('dp', 'fsdp'))
- grad_in_proj: float32 [1024, 4384], P(('dp', 'fsdp'))
- grad_conv_weight: float32 [2304, 4], P(('dp', 'fsdp'))
- grad_conv_bias: float32 [2304], P(('dp', 'fsdp'))
- grad_dt_bias: float32 [32], replicated
- grad_a_log: float32 [32], replicated
- grad_skip_weight: float32 [32], replicated
- grad_mixer_gain: float32 [2048], P(('dp', 'fsdp'))
- grad_out_proj: float32 [2048, 1024], P(('dp', 'fsdp'))
- grad_attn_gain: float32 [1024], P(('dp', 'fsdp'))
- grad_qkv_proj: float32 [1024, 3072], P(('dp', 'fsdp'))
- grad_attn_out: float32 [1024, 1024], P(('dp', 'fsdp'))
- grad_ffn_gain: float32 [1024], P(('dp', 'fsdp'))
- grad_gate_proj: float32 [1024, 4096], P(('dp', 'fsdp'))
- grad_up_proj: float32 [1024, 4096], P(('dp', 'fsdp'))
- grad_down_proj: float32 [4096, 1024], P(('dp', 'fsdp'))
The draws below stay inside these ranges and needn't reach their ends.
Inputs may be any that keep to these rules, and one draw needn't show every extreme that they name: `doc_lengths`: each row gives, in patches, the lengths of the two documents packed from the start of one slot of 128 patches; the rest of the slot is padding and the two lengths sum to at most 128.
All inputs are finite; a program needn't handle non-finite values.
Results may differ from the reference program's by a relative error of at most 0.017.
Values may be sent and summed in bfloat16 or wider, within the bound.
A program may use at most 448 MiB of HBM per device.

```python
import jax
import jax.numpy as jnp
from jax import lax

D = 1024
FF = 4096
HEADS = 16
HEAD = 64
HEAD_M = 64
STATE = 128
CONV = 4
PATCH = 8
DI = 2048
MHEADS = 32
CONV_CH = 2304
IN_COLS = 4384
PATCH_DEV = 32
GROUP_P = 128
GROUP = 1024
GROUPS = 8
BYTES = 8192


def draw_doc_lengths(key, part):
    keys = jax.random.split(jax.random.fold_in(key, 7), 6)
    coin = jax.random.randint(keys[0], (GROUPS,), 0, 2)
    long_first = jax.random.randint(keys[1], (GROUPS,), GROUP_P - PATCH_DEV + 1, GROUP_P + 1)
    tail_second = jax.random.randint(keys[2], (GROUPS,), 0, GROUP_P - long_first + 1)
    short_first = jax.random.randint(keys[3], (GROUPS,), 1, PATCH_DEV)
    long_second = jax.random.randint(keys[4], (GROUPS,), GROUP_P - PATCH_DEV + 1 - short_first, GROUP_P - short_first + 1)
    first = jnp.where(coin == 1, long_first, short_first)
    second = jnp.where(coin == 1, tail_second, long_second)
    full_row = jax.random.randint(keys[5], (), 0, GROUPS)
    rows = jnp.arange(GROUPS)
    first = jnp.where(rows == full_row, GROUP_P, first)
    second = jnp.where(rows == full_row, 0, second)
    return jnp.stack([first, second], axis=1).astype(jnp.int32)


def shard_levels(stream_key, extent, cuts, least, largest):
    level, own = 1.0, jax.random.fold_in(stream_key, 6)
    for dim, shards_of in cuts:
        steps = jnp.exp(jax.random.uniform(jax.random.fold_in(own, dim), (shards_of,), jnp.float32, least / len(cuts), largest / len(cuts)))
        level = level * jnp.repeat(steps, extent[dim] // shards_of).reshape([-1 if axis == dim else 1 for axis in range(len(extent))])
    return level


def noise(key, dims, scale, most, shards=(), kind=jnp.bfloat16):
    factor_of = shard_levels(key, dims, shards, -0.22, 0.18) if shards else 1.0
    array = jax.random.normal(key, dims, jnp.float32) * scale * factor_of
    return jnp.minimum(jnp.maximum(array, -most), most).astype(kind)


def setup_inputs(seed: int = 0) -> dict:
    streams_of = jax.random.split(jax.random.key(seed), 21)
    byte_states = noise(streams_of[0], (BYTES, D), 1.0, 6.0, ((0, 32),))
    doc_lengths = draw_doc_lengths(jax.random.fold_in(streams_of[20], 71), 0)
    out_grad = noise(streams_of[2], (BYTES, D), 1.0, 6.0, ((0, 32),))
    patch_proj = noise(streams_of[3], (PATCH * D, D), (PATCH * D) ** -0.5, 0.0625, ((0, 32),))
    global_gain = jnp.clip(1.0 + 0.18 * jax.random.normal(streams_of[4], (D,), jnp.float32), 0.099609375, 1.8984375).astype(jnp.bfloat16)
    in_proj = noise(streams_of[5], (D, IN_COLS), D ** -0.5, 0.1875, ((0, 32),))
    conv_weight = noise(streams_of[6], (CONV_CH, CONV), CONV ** -0.5, 3.0, ((0, 32),))
    conv_bias = noise(streams_of[7], (CONV_CH,), 0.5, 3.0, ((0, 32),))
    dt_bias = jnp.clip(jax.random.uniform(streams_of[8], (MHEADS,), jnp.float32, -4.0, -1.0), -4.0, -1.0)
    a_log = jnp.clip(jax.random.uniform(streams_of[9], (MHEADS,), jnp.float32, -4.0, 1.0), -4.0, 1.0)
    skip_weight = jnp.clip(jax.random.uniform(streams_of[10], (MHEADS,), jnp.float32, 0.5, 1.5), 0.5, 1.5)
    mixer_gain = jnp.clip(1.0 + 0.18 * jax.random.normal(streams_of[11], (DI,), jnp.float32), 0.099609375, 1.8984375).astype(jnp.bfloat16)
    out_proj = noise(streams_of[12], (DI, D), DI ** -0.5, 0.125, ((0, 32),))
    attn_gain = jnp.clip(1.0 + 0.18 * jax.random.normal(streams_of[13], (D,), jnp.float32), 0.099609375, 1.8984375).astype(jnp.bfloat16)
    qkv_proj = noise(streams_of[14], (D, 3 * D), D ** -0.5, 0.1875, ((0, 32),))
    attn_out = noise(streams_of[15], (D, D), (D // 4) ** -0.5, 0.375, ((0, 32),))
    ffn_gain = jnp.clip(1.0 + 0.18 * jax.random.normal(streams_of[16], (D,), jnp.float32), 0.099609375, 1.8984375).astype(jnp.bfloat16)
    gate_proj = noise(streams_of[17], (D, FF), D ** -0.5, 0.1875, ((0, 32),))
    up_proj = noise(streams_of[18], (D, FF), D ** -0.5, 0.1875, ((0, 32),))
    down_proj = noise(streams_of[19], (FF, D), FF ** -0.5, 0.09375, ((0, 32),))
    return dict(byte_states=byte_states, doc_lengths=doc_lengths, out_grad=out_grad, patch_proj=patch_proj, global_gain=global_gain, in_proj=in_proj, conv_weight=conv_weight, conv_bias=conv_bias, dt_bias=dt_bias, a_log=a_log, skip_weight=skip_weight, mixer_gain=mixer_gain, out_proj=out_proj, attn_gain=attn_gain, qkv_proj=qkv_proj, attn_out=attn_out, ffn_gain=ffn_gain, gate_proj=gate_proj, up_proj=up_proj, down_proj=down_proj)


EPSILON = 1e-05
HIGHEST = lax.Precision.HIGHEST

@jax.custom_vjp
def low(v):
    return lax.optimization_barrier(v.astype(jnp.bfloat16)).astype(jnp.float32)

@jax.custom_vjp
def low_back(v):
    return v

def low_keep(v):
    return (low(v), None)

def low_pass(kept, grad):
    return (grad,)

def back_keep(v):
    return (v, None)

def back_low(kept, grad):
    return (low(grad),)
low.defvjp(low_keep, low_pass)
low_back.defvjp(back_keep, back_low)

def matmul_high(left, right):
    return jnp.dot(left, right, precision=HIGHEST, preferred_element_type=jnp.float32)

def rms_scale(value, gain):
    return value * lax.rsqrt(lax.optimization_barrier(jnp.mean(value * value, axis=-1, keepdims=True)) + EPSILON) * gain

def doc_numbers(length_row):
    places = jnp.arange(GROUP_P, dtype=jnp.int32)
    first_end = length_row[0]
    second_end = first_end + length_row[1]
    return (places >= first_end).astype(jnp.int32) + (places >= second_end).astype(jnp.int32)

def causal_conv(channels, conv_weight, conv_bias, docs):
    count = channels.shape[0]
    padded = jnp.concatenate([jnp.zeros((CONV - 1, channels.shape[1]), jnp.float32), channels], axis=0)
    padded_docs = jnp.concatenate([jnp.full((CONV - 1,), -1, jnp.int32), docs])
    total = conv_bias[None, :]
    for shift_k in range(CONV):
        same_doc = (padded_docs[shift_k:shift_k + count] == docs).astype(jnp.float32)
        total = total + padded[shift_k:shift_k + count] * conv_weight[:, shift_k][None, :] * same_doc[:, None]
    return total

def state_space(inputs, step_size, rate, in_map, out_map, docs):
    count = inputs.shape[0]
    places = jnp.arange(count, dtype=jnp.int32)
    cumulative = jnp.cumsum(step_size * rate[None, :], axis=0)
    keep = ((places[:, None] >= places[None, :]) & (docs[:, None] == docs[None, :]))[:, :, None]
    spread = cumulative[:, None, :] - cumulative[None, :, :]
    decay_table = jnp.where(keep, jnp.exp(jnp.where(keep, spread, 0.0)), 0.0)
    inner = matmul_high(out_map, in_map.T)
    mixing = decay_table * inner[:, :, None] * step_size[None, :, :]
    return jnp.einsum('tsh,shp->thp', mixing, inputs, precision=HIGHEST)

def slot_forward(states, docs, weights):
    patch_proj, global_gain, in_proj, conv_weight, conv_bias, dt_bias, a_log, skip_weight, mixer_gain, out_proj, attn_gain, qkv_proj, attn_out, ffn_gain, gate_proj, up_proj, down_proj = weights
    patch_rows = states.reshape(GROUP_P, PATCH * D)
    patch_sum = low_back(matmul_high(patch_rows, patch_proj))
    global_norm = rms_scale(patch_sum, global_gain)
    projected = low_back(matmul_high(low(global_norm), in_proj))
    gate_raw = projected[:, :DI]
    channels = projected[:, DI:DI + CONV_CH]
    step_raw = projected[:, DI + CONV_CH:]
    activated = jax.nn.silu(causal_conv(channels, conv_weight, conv_bias, docs))
    inputs = activated[:, :DI].reshape(GROUP_P, MHEADS, HEAD_M)
    in_map = activated[:, DI:DI + STATE]
    out_map = activated[:, DI + STATE:]
    step_size = jax.nn.softplus(step_raw + dt_bias[None, :])
    rate = -jnp.exp(a_log)
    core = state_space(inputs, step_size, rate, in_map, out_map, docs) + skip_weight[None, :, None] * inputs
    mixer_norm = rms_scale(core.reshape(GROUP_P, DI) * jax.nn.silu(gate_raw), mixer_gain)
    mixer_value = low_back(matmul_high(low(mixer_norm), out_proj))
    mixed_patch = patch_sum + mixer_value
    streams = states + jnp.repeat(mixed_patch, PATCH, axis=0)
    attn_norm = rms_scale(streams, attn_gain)
    qkv = low(low_back(matmul_high(low(attn_norm), qkv_proj)))
    heads = qkv.reshape(GROUP_P, PATCH, 3, HEADS, HEAD)
    queries = heads[:, :, 0]
    key_rows = heads[:, :, 1]
    value_rows = heads[:, :, 2]
    scores = low_back(jnp.einsum('pihd,pjhd->phij', queries, key_rows, precision=HIGHEST) * HEAD ** (-0.5))
    places = jnp.arange(PATCH)
    causal = places[:, None] >= places[None, :]
    scores = jnp.where(causal, scores, -1e+30)
    attn_low = low(jax.nn.softmax(scores, axis=-1))
    mixed_heads = low(low_back(jnp.einsum('phij,pjhd->pihd', attn_low, value_rows, precision=HIGHEST)))
    attended = streams + low_back(matmul_high(mixed_heads.reshape(GROUP, D), attn_out))
    ffn_norm = low(rms_scale(attended, ffn_gain))
    gate = low_back(matmul_high(ffn_norm, gate_proj))
    upward = low_back(matmul_high(ffn_norm, up_proj))
    hidden = low(jax.nn.silu(gate) * upward)
    ffn_value = low_back(matmul_high(hidden, down_proj))
    live = jnp.repeat((docs < 2).astype(jnp.float32), PATCH)
    return live[:, None] * (attended + ffn_value)

def reference(byte_states, doc_lengths, out_grad, patch_proj, global_gain, in_proj, conv_weight, conv_bias, dt_bias, a_log, skip_weight, mixer_gain, out_proj, attn_gain, qkv_proj, attn_out, ffn_gain, gate_proj, up_proj, down_proj):
    weights = tuple((item.astype(jnp.float32) for item in (patch_proj, global_gain, in_proj, conv_weight, conv_bias, dt_bias, a_log, skip_weight, mixer_gain, out_proj, attn_gain, qkv_proj, attn_out, ffn_gain, gate_proj, up_proj, down_proj)))
    states = byte_states.astype(jnp.float32)
    docs_all = jax.vmap(doc_numbers)(doc_lengths)

    def forward(state_rows, weight_set):

        def one_slot(item):
            return slot_forward(item[0], item[1], weight_set)
        slots = state_rows.reshape(GROUPS, GROUP, D)
        return lax.map(jax.checkpoint(one_slot), (slots, docs_all)).reshape(BYTES, D)
    block, pullback = jax.vjp(forward, states, weights)
    grad_rows, grads = pullback(out_grad.astype(jnp.float32))
    return (block.astype(jnp.bfloat16), grad_rows, grads[0], grads[1], grads[2], grads[3], grads[4], grads[5], grads[6], grads[7], grads[8], grads[9], grads[10], grads[11], grads[12], grads[13], grads[14], grads[15], grads[16])
```

```python
from functools import partial

import jax
import jax.numpy as jnp
from jax import lax
from jax.sharding import PartitionSpec as P

D = 1024
HEAD = 64
HEAD_M = 64
STATE = 128
CONV = 4
PATCH = 8
DI = 2048
MHEADS = 32
CONV_CH = 2304


EPSILON = 1e-05
HIGHEST = lax.Precision.HIGHEST


def shifted(block, axis, distance):
    devices = range(lax.axis_size(axis))
    route = [(i - distance, i) for i in devices if i - distance in devices]
    return lax.ppermute(block, axis, route)


def prefix(value, axis, combine, identity):
    devices, place = (lax.axis_size(axis), lax.axis_index(axis))
    everything = jax.tree.map(
        lambda part, kind: lax.all_gather(part.astype(kind), axis),
        value,
        (jnp.bfloat16, jnp.bfloat16),
    )
    start = jax.tree.map(
        lambda part, zero: jnp.broadcast_to(jnp.asarray(zero, part.dtype), part.shape),
        value,
        identity,
    )

    def prefix_step(k, before):
        reached = k < place
        new = combine(
            before, jax.tree.map(lambda part, own: part[k].astype(own.dtype), everything, value)
        )
        return jax.tree.map(lambda a, b: jnp.where(reached, a, b), new, before)

    return lax.fori_loop(0, devices, prefix_step, start)


def carried_in(value, axis, combine, identity):
    devices, place = (lax.axis_size(axis), lax.axis_index(axis))
    everything = jax.tree.map(
        lambda part, kind: lax.all_gather(part.astype(kind), axis),
        value,
        jax.tree.map(lambda a: jnp.bfloat16 if a.dtype == jnp.float32 else a.dtype, value),
    )
    start = jax.tree.map(
        lambda part, zero: jnp.broadcast_to(jnp.asarray(zero, part.dtype), part.shape),
        value,
        identity,
    )

    def carried_step(k, before):
        at = devices - 1 - k
        reached = at > place
        new = combine(
            before, jax.tree.map(lambda part, own: part[at].astype(own.dtype), everything, value)
        )
        return jax.tree.map(lambda a, b: jnp.where(reached, a, b), new, before)

    return lax.fori_loop(0, devices, carried_step, start)


def product(left, right):
    return jnp.dot(left, right, preferred_element_type=jnp.float32)


def weight_grad(left, right):
    return lax.dot_general(
        left, right, (((0,), (0,)), ((), ())), preferred_element_type=jnp.float32
    )


def input_grad(grad_rows, weight):
    return lax.dot_general(
        grad_rows, weight, (((1,), (1,)), ((), ())), preferred_element_type=jnp.float32
    )


def rms_scale(value, gain):
    return value * lax.rsqrt(jnp.mean(value * value, axis=-1, keepdims=True) + EPSILON) * gain


def gated_norm(core_out, gate_raw, gain):
    count = core_out.shape[0]
    return rms_scale(core_out.reshape(count, DI) * jax.nn.silu(gate_raw), gain)


def patch_docs(doc_lengths, start, count):
    places = start + jnp.arange(count, dtype=jnp.int32)
    first_end = doc_lengths[0, 0]
    second_end = first_end + doc_lengths[0, 1]
    numbers = (places >= first_end).astype(jnp.int32) + (places >= second_end).astype(jnp.int32)
    return jnp.where(places >= 0, numbers, -1)


def chain(earlier, later):
    return (earlier[0] * later[0], later[1] + later[0][:, None, None] * earlier[1])


def mixer_core(
    channels,
    rim,
    step_raw,
    state_in,
    conv_weight,
    conv_bias,
    dt_bias,
    a_log,
    skip_weight,
    docs,
    rim_docs,
    prev_doc,
):
    count = channels.shape[0]
    padded = jnp.concatenate([rim, channels], axis=0)
    padded_docs = jnp.concatenate([rim_docs, docs])
    total = conv_bias[None, :]
    for shift_k in range(CONV):
        same_doc = (padded_docs[shift_k : shift_k + count] == docs).astype(jnp.float32)
        total = (
            total
            + padded[shift_k : shift_k + count]
            * conv_weight[:, shift_k][None, :]
            * same_doc[:, None]
        )
    activated = jax.nn.silu(total)
    inputs = activated[:, :DI].reshape(count, MHEADS, HEAD_M)
    in_map = activated[:, DI : DI + STATE]
    out_map = activated[:, DI + STATE :]
    step_size = jax.nn.softplus(step_raw + dt_bias[None, :])
    rate = -jnp.exp(a_log)
    lower = jnp.tril(jnp.ones((count, count), jnp.float32))
    cumulative = jnp.dot(lower, step_size * rate[None, :], precision=HIGHEST)
    places = jnp.arange(count, dtype=jnp.int32)
    keep = ((places[:, None] >= places[None, :]) & (docs[:, None] == docs[None, :]))[:, :, None]
    spread = cumulative[:, None, :] - cumulative[None, :, :]
    decay_table = jnp.where(keep, jnp.exp(jnp.where(keep, spread, 0.0)), 0.0)
    inner = jnp.dot(out_map, in_map.T, precision=HIGHEST, preferred_element_type=jnp.float32)
    mixing = decay_table * inner[:, :, None] * step_size[None, :, :]
    outputs = jnp.einsum("tsh,shp->thp", mixing, inputs, precision=HIGHEST)
    carry_in = jnp.where((docs == prev_doc)[:, None], jnp.exp(cumulative), 0.0)
    outputs = outputs + carry_in[:, :, None] * jnp.einsum(
        "tn,hpn->thp", out_map, state_in, precision=HIGHEST
    )
    outputs = outputs + skip_weight[None, :, None] * inputs
    last_doc = docs[count - 1]
    tail_keep = (docs == last_doc)[:, None]
    tail_gap = cumulative[count - 1][None, :] - cumulative
    tail_weight = (
        jnp.where(tail_keep, jnp.exp(jnp.where(tail_keep, tail_gap, 0.0)), 0.0) * step_size
    )
    decay_total = jnp.where(prev_doc == last_doc, jnp.exp(cumulative[count - 1]), 0.0)
    state_out = jnp.einsum("sh,shp,sn->hpn", tail_weight, inputs, in_map, precision=HIGHEST)
    state_out = state_out + decay_total[:, None, None] * state_in
    return ((outputs, state_out), (decay_total, carry_in, out_map))


def attend(qkv_low, patches):
    heads = qkv_low.reshape(patches, PATCH, 3, -1, HEAD)
    queries = heads[:, :, 0]
    key_rows = heads[:, :, 1]
    value_rows = heads[:, :, 2]
    scores = jnp.einsum(
        "pihd,pjhd->phij", queries, key_rows, preferred_element_type=jnp.float32
    ) * HEAD ** (-0.5)
    places = jnp.arange(PATCH)
    causal = places[:, None] >= places[None, :]
    scores = jnp.where(causal, scores, -1e30)
    attn_weights = jax.nn.softmax(scores, axis=-1)
    attn_low = attn_weights.astype(jnp.bfloat16)
    mixed = jnp.einsum("phij,pjhd->pihd", attn_low, value_rows, preferred_element_type=jnp.float32)
    mixed = mixed.astype(jnp.bfloat16).reshape(patches * PATCH, -1)
    return ((queries, key_rows, value_rows, attn_weights, attn_low), mixed)


def attend_back(grad_mixed_low, pieces):
    queries, key_rows, value_rows, attn_weights, attn_low = pieces
    patches = queries.shape[0]
    grad_mixed = grad_mixed_low.reshape(patches, PATCH, -1, HEAD)
    grad_values = jnp.einsum(
        "phij,pihd->pjhd", attn_low, grad_mixed, preferred_element_type=jnp.float32
    )
    grad_weights = jnp.einsum(
        "pihd,pjhd->phij", grad_mixed, value_rows, preferred_element_type=jnp.float32
    )
    grad_scores = attn_weights * (
        grad_weights - jnp.sum(attn_weights * grad_weights, axis=-1, keepdims=True)
    )
    scores_low = grad_scores.astype(jnp.bfloat16)
    scale = HEAD ** (-0.5)
    grad_queries = (
        jnp.einsum("phij,pjhd->pihd", scores_low, key_rows, preferred_element_type=jnp.float32)
        * scale
    )
    grad_keys = (
        jnp.einsum("phij,pihd->pjhd", scores_low, queries, preferred_element_type=jnp.float32)
        * scale
    )
    stacked = jnp.stack([grad_queries, grad_keys, grad_values], axis=2).reshape(patches * PATCH, -1)
    return stacked.astype(jnp.bfloat16)


def local_forward(byte_states, mixed_patch, local_set, live):
    attn_gain, qkv_proj, attn_out, ffn_gain, gate_proj, up_proj, down_proj = local_set
    rows = byte_states.shape[0]
    streams = byte_states.astype(jnp.float32) + jnp.repeat(mixed_patch, PATCH, axis=0)
    normed_low = rms_scale(streams, attn_gain.astype(jnp.float32)).astype(jnp.bfloat16)
    qkv_low = product(normed_low, qkv_proj).astype(jnp.bfloat16)
    pieces, mixed_heads = attend(qkv_low, rows // PATCH)
    attended = streams + product(mixed_heads, attn_out)
    ffn_low = rms_scale(attended, ffn_gain.astype(jnp.float32)).astype(jnp.bfloat16)
    gate = product(ffn_low, gate_proj)
    upward = product(ffn_low, up_proj)
    hidden_low = (jax.nn.silu(gate) * upward).astype(jnp.bfloat16)
    block = live * (attended + product(hidden_low, down_proj))
    cache = (streams, normed_low, pieces, mixed_heads, attended, ffn_low, gate, upward, hidden_low)
    return (block, cache)


def local_backward(grad_block, cache, local_set):
    attn_gain, qkv_proj, attn_out, ffn_gain, gate_proj, up_proj, down_proj = local_set
    streams, normed_low, pieces, mixed_heads, attended, ffn_low, gate, upward, hidden_low = cache
    down_low = grad_block.astype(jnp.bfloat16)
    grad_down = weight_grad(hidden_low, down_low)
    grad_hidden = input_grad(down_low, down_proj)
    sigma = jax.nn.sigmoid(gate)
    grad_gate_low = (grad_hidden * upward * sigma * (1.0 + gate * (1.0 - sigma))).astype(
        jnp.bfloat16
    )
    grad_up_low = (grad_hidden * gate * sigma).astype(jnp.bfloat16)
    grad_gate = weight_grad(ffn_low, grad_gate_low)
    grad_up = weight_grad(ffn_low, grad_up_low)
    grad_ffn_in = input_grad(grad_gate_low, gate_proj) + input_grad(grad_up_low, up_proj)
    _, norm_back = jax.vjp(rms_scale, attended, ffn_gain.astype(jnp.float32))
    grad_attended_norm, grad_ffn_gain = norm_back(grad_ffn_in)
    grad_attended = grad_block + grad_attended_norm
    attn_grad_low = grad_attended.astype(jnp.bfloat16)
    grad_attn_out = weight_grad(mixed_heads, attn_grad_low)
    grad_mixed_low = input_grad(attn_grad_low, attn_out).astype(jnp.bfloat16)
    grad_qkv_low = attend_back(grad_mixed_low, pieces)
    grad_qkv = weight_grad(normed_low, grad_qkv_low)
    grad_normed = input_grad(grad_qkv_low, qkv_proj)
    _, norm_back = jax.vjp(rms_scale, streams, attn_gain.astype(jnp.float32))
    grad_streams_norm, grad_attn_gain = norm_back(grad_normed)
    grad_streams = grad_attended + grad_streams_norm
    return (
        grad_streams,
        (grad_qkv, grad_attn_out, grad_gate, grad_up, grad_down, grad_attn_gain, grad_ffn_gain),
    )


def body(
    byte_states,
    doc_lengths,
    out_grad,
    patch_proj,
    global_gain,
    in_proj,
    conv_weight,
    conv_bias,
    dt_bias,
    a_log,
    skip_weight,
    mixer_gain,
    out_proj,
    attn_gain,
    qkv_proj,
    attn_out,
    ffn_gain,
    gate_proj,
    up_proj,
    down_proj,
):
    rows = byte_states.shape[0]
    patches = rows // PATCH
    share = lax.axis_index("fsdp")
    start = share * patches
    docs = patch_docs(doc_lengths, start, patches)
    rim_docs = patch_docs(doc_lengths, start - (CONV - 1), CONV - 1)
    prev_doc = patch_docs(doc_lengths, start - 1, 1)[0]
    live = jnp.repeat((docs < 2).astype(jnp.float32), PATCH)[:, None]
    all_set = (
        lax.all_gather(patch_proj, ("dp", "fsdp"), axis=0, tiled=True),
        lax.all_gather(global_gain, ("dp", "fsdp"), axis=0, tiled=True),
        lax.all_gather(in_proj, ("dp", "fsdp"), axis=0, tiled=True),
        lax.all_gather(conv_weight, ("dp", "fsdp"), axis=0, tiled=True),
        lax.all_gather(conv_bias, ("dp", "fsdp"), axis=0, tiled=True),
        lax.all_gather(mixer_gain, ("dp", "fsdp"), axis=0, tiled=True),
        lax.all_gather(out_proj, ("dp", "fsdp"), axis=0, tiled=True),
        lax.all_gather(attn_gain, ("dp", "fsdp"), axis=0, tiled=True),
        lax.all_gather(qkv_proj, ("dp", "fsdp"), axis=0, tiled=True),
        lax.all_gather(attn_out, ("dp", "fsdp"), axis=0, tiled=True),
        lax.all_gather(ffn_gain, ("dp", "fsdp"), axis=0, tiled=True),
        lax.all_gather(gate_proj, ("dp", "fsdp"), axis=0, tiled=True),
        lax.all_gather(up_proj, ("dp", "fsdp"), axis=0, tiled=True),
        lax.all_gather(down_proj, ("dp", "fsdp"), axis=0, tiled=True),
    )
    global_set = all_set[:7]
    local_set = all_set[7:]
    patch_full, gain_g_full, in_full, conv_w_full, conv_b_full, gain_m_full, out_full = global_set
    patch_rows = byte_states.reshape(patches, PATCH * D)
    patch_sum = product(patch_rows, patch_full)
    gain_g = gain_g_full.astype(jnp.float32)
    global_low = rms_scale(patch_sum, gain_g).astype(jnp.bfloat16)
    projected = product(global_low, in_full)
    gate_raw = projected[:, :DI]
    channels = projected[:, DI : DI + CONV_CH]
    step_raw = projected[:, DI + CONV_CH :]
    rim = shifted(channels[patches - (CONV - 1) :], "fsdp", 1)
    core = partial(mixer_core, docs=docs, rim_docs=rim_docs, prev_doc=prev_doc)
    conv_w = conv_w_full.astype(jnp.float32)
    conv_b = conv_b_full.astype(jnp.float32)
    empty_state = jnp.zeros((MHEADS, HEAD_M, STATE), jnp.float32)
    (partial_out, local_state), aux = core(
        channels, rim, step_raw, empty_state, conv_w, conv_b, dt_bias, a_log, skip_weight
    )
    decay_total, carry_in, out_map = aux
    identity = (jnp.ones((MHEADS,), jnp.float32), jnp.zeros((MHEADS, HEAD_M, STATE), jnp.float32))
    arrived = prefix((decay_total, local_state), "fsdp", chain, identity)
    state_in = arrived[1]
    mixer_out = partial_out + carry_in[:, :, None] * jnp.einsum(
        "tn,hpn->thp", out_map, state_in, precision=HIGHEST
    )
    gain_m = gain_m_full.astype(jnp.float32)
    mixer_low = gated_norm(mixer_out, gate_raw, gain_m).astype(jnp.bfloat16)
    mixed_patch = patch_sum + product(mixer_low, out_full)
    block, cache = local_forward(byte_states, mixed_patch, local_set, live)
    block_out = block.astype(jnp.bfloat16)
    back_set = (
        lax.all_gather(patch_proj, ("dp", "fsdp"), axis=0, tiled=True),
        lax.all_gather(global_gain, ("dp", "fsdp"), axis=0, tiled=True),
        lax.all_gather(in_proj, ("dp", "fsdp"), axis=0, tiled=True),
        lax.all_gather(conv_weight, ("dp", "fsdp"), axis=0, tiled=True),
        lax.all_gather(conv_bias, ("dp", "fsdp"), axis=0, tiled=True),
        lax.all_gather(mixer_gain, ("dp", "fsdp"), axis=0, tiled=True),
        lax.all_gather(out_proj, ("dp", "fsdp"), axis=0, tiled=True),
        lax.all_gather(attn_gain, ("dp", "fsdp"), axis=0, tiled=True),
        lax.all_gather(qkv_proj, ("dp", "fsdp"), axis=0, tiled=True),
        lax.all_gather(attn_out, ("dp", "fsdp"), axis=0, tiled=True),
        lax.all_gather(ffn_gain, ("dp", "fsdp"), axis=0, tiled=True),
        lax.all_gather(gate_proj, ("dp", "fsdp"), axis=0, tiled=True),
        lax.all_gather(up_proj, ("dp", "fsdp"), axis=0, tiled=True),
        lax.all_gather(down_proj, ("dp", "fsdp"), axis=0, tiled=True),
    )
    global_back = back_set[:7]
    local_back = back_set[7:]
    _, cache = local_forward(byte_states, mixed_patch, local_back, live)
    patch_back, _, in_back, conv_w_back, conv_b_back, _, out_back = global_back
    grad_block = live * out_grad.astype(jnp.float32)
    grad_streams, local_grads = local_backward(grad_block, cache, local_back)
    reduced_local = (
        lax.psum_scatter(local_grads[0], ("dp", "fsdp"), scatter_dimension=0, tiled=True),
        lax.psum_scatter(local_grads[1], ("dp", "fsdp"), scatter_dimension=0, tiled=True),
        lax.psum_scatter(local_grads[2], ("dp", "fsdp"), scatter_dimension=0, tiled=True),
        lax.psum_scatter(local_grads[3], ("dp", "fsdp"), scatter_dimension=0, tiled=True),
        lax.psum_scatter(local_grads[4], ("dp", "fsdp"), scatter_dimension=0, tiled=True),
        lax.psum_scatter(local_grads[5], ("dp", "fsdp"), scatter_dimension=0, tiled=True),
        lax.psum_scatter(local_grads[6], ("dp", "fsdp"), scatter_dimension=0, tiled=True),
    )
    grad_patch_mix = grad_streams.reshape(patches, PATCH, D).sum(axis=1)
    mix_low = grad_patch_mix.astype(jnp.bfloat16)
    grad_out_proj = weight_grad(mixer_low, mix_low)
    grad_mixer_low = input_grad(mix_low, out_back)
    _, norm_back = jax.vjp(gated_norm, mixer_out, gate_raw, gain_m)
    grad_core, grad_gate_raw, grad_mixer_gain = norm_back(grad_mixer_low)
    state_part = jnp.einsum("th,thp,tn->hpn", carry_in, grad_core, out_map, precision=HIGHEST)
    returned = carried_in((decay_total, state_part), "fsdp", chain, identity)
    _, core_back, _ = jax.vjp(
        core,
        channels,
        rim,
        step_raw,
        state_in,
        conv_w_back.astype(jnp.float32),
        conv_b_back.astype(jnp.float32),
        dt_bias,
        a_log,
        skip_weight,
        has_aux=True,
    )
    core_grads = core_back((grad_core, returned[1]))
    (
        grad_channels,
        grad_rim,
        grad_step,
        _,
        grad_conv_w,
        grad_conv_b,
        grad_dt_bias,
        grad_a_log,
        grad_skip,
    ) = core_grads
    rim_grad = shifted(grad_rim, "fsdp", -1)
    cut = patches - (CONV - 1)
    grad_channels = jnp.concatenate([grad_channels[:cut], grad_channels[cut:] + rim_grad], axis=0)
    proj_low = jnp.concatenate([grad_gate_raw, grad_channels, grad_step], axis=1).astype(
        jnp.bfloat16
    )
    grad_in_proj = weight_grad(global_low, proj_low)
    grad_global_norm = input_grad(proj_low, in_back)
    _, norm_back = jax.vjp(rms_scale, patch_sum, gain_g)
    grad_sum_norm, grad_global_gain = norm_back(grad_global_norm)
    sum_low = (grad_patch_mix + grad_sum_norm).astype(jnp.bfloat16)
    grad_patch_proj = weight_grad(patch_rows, sum_low)
    grad_states = grad_streams + input_grad(sum_low, patch_back).reshape(rows, D)
    reduced_global = (
        lax.psum_scatter(grad_patch_proj, ("dp", "fsdp"), scatter_dimension=0, tiled=True),
        lax.psum_scatter(grad_global_gain, ("dp", "fsdp"), scatter_dimension=0, tiled=True),
        lax.psum_scatter(grad_in_proj, ("dp", "fsdp"), scatter_dimension=0, tiled=True),
        lax.psum_scatter(grad_conv_w, ("dp", "fsdp"), scatter_dimension=0, tiled=True),
        lax.psum_scatter(grad_conv_b, ("dp", "fsdp"), scatter_dimension=0, tiled=True),
        lax.psum_scatter(grad_mixer_gain, ("dp", "fsdp"), scatter_dimension=0, tiled=True),
        lax.psum_scatter(grad_out_proj, ("dp", "fsdp"), scatter_dimension=0, tiled=True),
    )
    head_sums = lax.psum((grad_dt_bias, grad_a_log, grad_skip), ("dp", "fsdp"))
    return (
        block_out,
        grad_states,
        reduced_global[0],
        reduced_global[1],
        reduced_global[2],
        reduced_global[3],
        reduced_global[4],
        head_sums[0],
        head_sums[1],
        head_sums[2],
        reduced_global[5],
        reduced_global[6],
        reduced_local[5],
        reduced_local[0],
        reduced_local[1],
        reduced_local[6],
        reduced_local[2],
        reduced_local[3],
        reduced_local[4],
    )


AX = ("dp", "fsdp")
BC = 2 * STATE
OWN = 2 * HEAD_M + 1


class Grid:
    def __init__(self, dp, fsdp):
        self.depth, self.count = dp // 2, dp * fsdp
        dp_at, fs_at = lax.axis_index("dp"), lax.axis_index("fsdp")
        self.z, self.x, self.y, self.c = dp_at // 2, dp_at % 2, fs_at // 2, fs_at % 2
        self.at = {"z": self.z, "x": self.x, "y": self.y, "c": self.c}

    def route(self, dim, step=1):
        pairs = []
        for i in range(self.count):
            z, x, y, c = i // 8, i // 4 % 2, i // 2 % 2, i % 2
            if dim == "z":
                z = (z + step) % self.depth
            elif dim == "x":
                x = 1 - x
            elif dim == "y":
                y = 1 - y
            else:
                c = 1 - c
            pairs.append((i, z * 8 + x * 4 + y * 2 + c))
        return pairs

    def send(self, block, dim, step=1):
        return lax.ppermute(block, AX, self.route(dim, step))


def put(whole, part, place):
    return lax.dynamic_update_slice(whole, part, [jnp.asarray(p, jnp.int32) for p in place])


def gather_stream(grid, own, order):
    rows, n = own.shape
    pieces = [(own[None], {})]
    zs = 1
    for dim in order:
        if dim == "z":
            stacked = jnp.stack([p for p, _ in pieces], axis=0)
            blocks = [stacked]
            for _ in range(grid.depth - 1):
                blocks.append(grid.send(blocks[-1], "z"))
            whole = jnp.zeros((len(pieces), grid.depth, rows, n), own.dtype)
            for k, block in enumerate(blocks):
                whole = put(whole, block, (0, (grid.z - k) % grid.depth, 0, 0))
            pieces = [(whole[i], at) for i, (_, at) in enumerate(pieces)]
        else:
            pieces = pieces + [(grid.send(p, dim), {**at, dim: True}) for p, at in pieces]
    out = jnp.zeros((grid.depth, 2, 2, 2, rows, n), own.dtype)
    for piece, at in pieces:
        place = [1 - grid.at[d] if d in at else grid.at[d] for d in "xyc"]
        out = put(out, piece[:, None, None, None], (0, *place, 0, 0))
    return out.reshape(grid.count, rows, n)


def pick(part, where, axis):
    return lax.dynamic_index_in_dim(part, where, axis, keepdims=False)


def scatter_stream(grid, part, order):
    low = jnp.bfloat16
    dims = ["z", "x", "y"]
    for dim in order:
        axis = dims.index(dim)
        here = grid.at[dim]
        if dim == "z":
            total = None
            for k in range(1, grid.depth + 1):
                mine = pick(part, (here - k) % grid.depth, axis).astype(jnp.float32)
                total = mine if total is None else mine + total.astype(jnp.float32)
                if k < grid.depth:
                    total = grid.send(total.astype(low), "z")
            part = total
        else:
            arrived = grid.send(pick(part, 1 - here, axis).astype(low), dim)
            part = pick(part, here, axis).astype(jnp.float32) + arrived.astype(jnp.float32)
        dims.pop(axis)
    return part


def gather_small(grid, own):
    rows, n = own.shape
    column = jnp.zeros((grid.depth, rows, n), own.dtype)
    for k in range(grid.depth):
        block = own if k == 0 else grid.send(own, "z", k)
        column = put(column, block[None], ((grid.z - k) % grid.depth, 0, 0))
    half = n // 2
    plane = jnp.zeros((grid.depth, 2, 2, rows, n), own.dtype)
    for first, second, at in (("x", "y", 0), ("y", "x", half)):
        mine = column[:, :, at : at + half]
        both = jnp.stack([mine, grid.send(mine, first)])
        far = grid.send(both, second)
        for i in range(2):
            for j, block in enumerate((both[i], far[i])):
                place = {first: grid.at[first] ^ i, second: grid.at[second] ^ j}
                plane = put(plane, block[:, None, None], (0, place["x"], place["y"], 0, at))
    other = grid.send(plane, "c")
    pair = jnp.where(grid.c == 0, jnp.stack([plane, other], 3), jnp.stack([other, plane], 3))
    return pair.reshape(grid.count * rows, n)


def scatter_small(grid, part):
    low = jnp.bfloat16
    n = part.shape[1]
    part = part.reshape(grid.depth, 2, 2, 2, -1, n)
    arrived = grid.send(pick(part, 1 - grid.c, 3).astype(low), "c")
    part = pick(part, grid.c, 3) + arrived.astype(jnp.float32)
    half = n // 2
    sums = []
    for order, at in (("yx", 0), ("xy", half)):
        piece = part[..., at : at + half]
        dims = ["z", "x", "y"]
        for dim in order:
            axis = dims.index(dim)
            arrived = grid.send(pick(piece, 1 - grid.at[dim], axis).astype(low), dim)
            piece = pick(piece, grid.at[dim], axis) + arrived.astype(jnp.float32)
            dims.pop(axis)
        sums.append(piece)
    column = jnp.concatenate(sums, axis=-1)
    total = pick(column, grid.z, 0)
    for k in range(1, grid.depth):
        block = pick(column, (grid.z + k) % grid.depth, 0).astype(low)
        total = total + grid.send(block, "z", k).astype(jnp.float32)
    return total


def exchange(blocks):
    return lax.all_to_all(blocks, AX, 0, 0, tiled=False)


def causal_taps(channels, weight, bias, docs):
    slots, count = docs.shape
    padded = jnp.pad(channels, ((0, 0), (CONV - 1, 0), (0, 0)))
    padded_docs = jnp.pad(docs, ((0, 0), (CONV - 1, 0)), constant_values=-1)
    total = bias[None, None, :]
    for k in range(CONV):
        same = (padded_docs[:, k : k + count] == docs).astype(jnp.float32)
        total = total + padded[:, k : k + count] * weight[:, k][None, None, :] * same[:, :, None]
    return total


def head_core(channels, maps, step_raw, conv_w, conv_b, maps_w, maps_b, dt_bias, a_log, skip, docs):
    count = docs.shape[1]
    inputs = jax.nn.silu(causal_taps(channels, conv_w, conv_b, docs))
    both = jax.nn.silu(causal_taps(maps, maps_w, maps_b, docs))
    in_map, out_map = both[..., :STATE], both[..., STATE:]
    step_size = jax.nn.softplus(step_raw + dt_bias)
    lower = jnp.tril(jnp.ones((count, count), jnp.float32))
    cumulative = jnp.dot(step_size * -jnp.exp(a_log), lower.T, precision=HIGHEST)
    keep = (lower > 0)[None] & (docs[:, :, None] == docs[:, None, :])
    spread = cumulative[:, :, None] - cumulative[:, None, :]
    decay = jnp.where(keep, jnp.exp(jnp.where(keep, spread, 0.0)), 0.0)
    inner = jnp.einsum("gtn,gsn->gts", out_map, in_map, precision=HIGHEST)
    mixing = decay * inner * step_size[:, None, :]
    return jnp.einsum("gts,gsp->gtp", mixing, inputs, precision=HIGHEST) + skip * inputs


def split_heads(rows_by_cols):
    rows = rows_by_cols.shape[0]
    return rows_by_cols.reshape(rows // 128, 128, -1, HEAD).transpose(2, 0, 1, 3)


def join_heads(heads):
    return heads.transpose(1, 2, 0, 3).reshape(heads.shape[1] * heads.shape[2], -1)


def patch_mask():
    places = jnp.arange(128)
    return (places[:, None] >= places[None, :]) & (places[:, None] // PATCH == places[None, :] // PATCH)


def dot_f32(spec, a, b):
    return jnp.einsum(spec, a, b, preferred_element_type=jnp.float32)


def fast_body(
    depth_fsdp,
    byte_states,
    doc_lengths,
    out_grad,
    patch_proj,
    global_gain,
    in_proj,
    conv_weight,
    conv_bias,
    dt_bias,
    a_log,
    skip_weight,
    mixer_gain,
    out_proj,
    attn_gain,
    qkv_proj,
    attn_out,
    ffn_gain,
    gate_proj,
    up_proj,
    down_proj,
):
    f32, low = jnp.float32, jnp.bfloat16
    grid = Grid(*depth_fsdp)
    n_dev = grid.count
    me = lax.axis_index("dp") * depth_fsdp[1] + lax.axis_index("fsdp")
    rows = byte_states.shape[0]
    patches = rows // PATCH
    slots = depth_fsdp[0]
    slot_patches = patches * depth_fsdp[1]

    vector = jnp.concatenate(
        [
            global_gain,
            mixer_gain,
            attn_gain,
            ffn_gain,
            conv_weight.reshape(-1),
            conv_bias,
            doc_lengths.reshape(-1).astype(low),
        ]
    )
    shard_rows = in_proj.shape[0]
    tail = -(-vector.shape[0] // BC)
    vector = jnp.pad(vector, (0, tail * BC - vector.shape[0])).reshape(tail, BC)
    small = jnp.concatenate([in_proj[:, 2 * DI : 2 * DI + BC], vector], axis=0)
    small = gather_small(grid, small).reshape(n_dev, shard_rows + tail, BC)
    maps_proj = small[:, :shard_rows].reshape(D, BC)
    flat = small[:, shard_rows:].reshape(n_dev, -1)
    cuts, at = [], 0
    for width in (D, DI, D, D, CONV_CH * CONV, CONV_CH, n_dev * 2):
        width //= n_dev
        cuts.append(flat[:, at : at + width])
        at += width
    gain_g, gain_m, gain_a, gain_f = (cut.reshape(-1).astype(f32) for cut in cuts[:4])
    conv_w = cuts[4].reshape(CONV_CH, CONV).astype(f32)
    conv_b = cuts[5].reshape(CONV_CH).astype(f32)
    lengths = cuts[6].reshape(slots, depth_fsdp[1], 2)[:, 0].astype(jnp.int32)
    places = jnp.arange(slot_patches, dtype=jnp.int32)[None, :]
    first_end = lengths[:, :1]
    docs = (places >= first_end).astype(jnp.int32) + (places >= first_end + lengths[:, 1:]).astype(jnp.int32)
    my_docs = lax.dynamic_slice(docs.reshape(-1), (me * patches,), (patches,))
    live = jnp.repeat((my_docs < 2).astype(f32), PATCH)[:, None]

    def gathered(shard, order):
        return gather_stream(grid, shard, order).reshape(-1, shard.shape[1])

    patch_bytes = byte_states.reshape(patches, n_dev, -1).transpose(1, 0, 2)
    all_bytes = exchange(patch_bytes).reshape(n_dev * patches, -1)
    heads_of = lambda cols: cols.reshape(shard_rows, MHEADS, -1)
    own_cols = jnp.concatenate(
        [heads_of(in_proj[:, :DI]), heads_of(in_proj[:, DI : 2 * DI]), heads_of(in_proj[:, 2 * DI + BC :])],
        axis=2,
    ).transpose(1, 0, 2)
    own_proj = exchange(own_cols).reshape(D, OWN)

    qk = gathered(qkv_proj[:, : 2 * D], "zxyc")
    vals = gathered(qkv_proj[:, 2 * D :], "zyxc")
    attn_o = gathered(attn_out, "zyxc")
    gate_w = gathered(gate_proj, "zxyc")
    up_w = gathered(up_proj, "zyxc")
    down_a = gathered(down_proj[:, : D // 2], "xyzc")
    down_b = gathered(down_proj[:, D // 2 :], "yxzc")

    patch_sum = scatter_small(grid, product(all_bytes, patch_proj))
    global_low = rms_scale(patch_sum, gain_g).astype(low)
    global_all = gather_small(grid, global_low)
    own = product(global_all, own_proj)
    maps = product(global_all, maps_proj)
    by_slot = lambda cols: cols.reshape(slots, slot_patches, -1)
    gate_raw = own[:, :HEAD_M]
    mine = lambda vec, width: lax.dynamic_slice_in_dim(vec, me * width, width, 0)
    core_args = (
        by_slot(own[:, HEAD_M : 2 * HEAD_M]),
        by_slot(maps),
        by_slot(own[:, 2 * HEAD_M :])[..., 0],
        mine(conv_w, HEAD_M),
        mine(conv_b, HEAD_M),
        conv_w[DI:],
        conv_b[DI:],
        mine(dt_bias, 1),
        mine(a_log, 1),
        mine(skip_weight, 1),
    )
    core, core_back = jax.vjp(partial(head_core, docs=docs), *core_args)
    core = core.reshape(-1, HEAD_M)
    sig_m = jax.nn.sigmoid(gate_raw)
    gated = core * gate_raw * sig_m
    my_gain = mine(gain_m, HEAD_M)[None]
    mixer_part = product((gated * my_gain).astype(low), out_proj)
    squares = jnp.sum(gated * gated, axis=1, keepdims=True)
    mixed = scatter_small(grid, jnp.concatenate([mixer_part, jnp.pad(squares, ((0, 0), (0, 127)))], axis=1))
    raw_mixed = mixed[:, :D]
    mixer_r = lax.rsqrt(mixed[:, D : D + 1] / DI + EPSILON)
    mixed_patch = patch_sum + raw_mixed * mixer_r

    streams = byte_states.astype(f32) + jnp.repeat(mixed_patch, PATCH, axis=0)
    normed = rms_scale(streams, gain_a).astype(low)
    queries, key_rows = jnp.split(product(normed, qk).astype(low), 2, axis=1)
    queries, key_rows = split_heads(queries), split_heads(key_rows)
    value_rows = split_heads(product(normed, vals).astype(low))
    scale = HEAD ** (-0.5)
    scores = dot_f32("hbid,hbjd->hbij", queries, key_rows) * scale
    attn_weights = jax.nn.softmax(jnp.where(patch_mask(), scores, -1e30), axis=-1)
    attn_low = attn_weights.astype(low)
    mixed_heads = join_heads(dot_f32("hbij,hbjd->hbid", attn_low, value_rows).astype(low))
    attended = streams + product(mixed_heads, attn_o)
    ffn_low = rms_scale(attended, gain_f).astype(low)
    gate = product(ffn_low, gate_w)
    upward = product(ffn_low, up_w)
    sigma = jax.nn.sigmoid(gate)
    hidden = (gate * sigma * upward).astype(low)
    ffn_out = jnp.concatenate([product(hidden, down_a), product(hidden, down_b)], axis=1)
    block_out = (live * (attended + ffn_out)).astype(low)

    def plane_of(act, which):
        cols = act.reshape(rows, n_dev // 2, 2, -1)
        return pick(cols, which, 2).reshape(rows, -1)

    def scattered(act, grad, order):
        there = weight_grad(plane_of(act, 1 - grid.c), grad).astype(low)
        arrived = grid.send(there, "c")
        part = (weight_grad(plane_of(act, grid.c), grad) + arrived.astype(f32)).astype(low)
        part = part.reshape(grid.depth, 2, 2, -1, grad.shape[1])
        return scatter_stream(grid, part, order)

    grad_block = live * out_grad.astype(f32)
    down_low = grad_block.astype(low)
    grad_down = jnp.concatenate(
        [scattered(hidden, down_low[:, : D // 2], "zyx"), scattered(hidden, down_low[:, D // 2 :], "zxy")],
        axis=1,
    )
    grad_hidden = input_grad(down_low[:, : D // 2], down_a) + input_grad(down_low[:, D // 2 :], down_b)
    grad_gate_low = (grad_hidden * upward * sigma * (1.0 + gate * (1.0 - sigma))).astype(low)
    grad_up_low = (grad_hidden * gate * sigma).astype(low)
    grad_gate = scattered(ffn_low, grad_gate_low, "yxz")
    grad_up = scattered(ffn_low, grad_up_low, "xyz")
    grad_ffn_in = input_grad(grad_gate_low, gate_w) + input_grad(grad_up_low, up_w)
    _, norm_back = jax.vjp(rms_scale, attended, gain_f)
    grad_attended_norm, grad_gain_f = norm_back(grad_ffn_in)
    grad_attended = grad_block + grad_attended_norm
    attn_grad_low = grad_attended.astype(low)
    grad_attn_out = scattered(mixed_heads, attn_grad_low, "xyz")
    grad_mixed = split_heads(input_grad(attn_grad_low, attn_o).astype(low))
    grad_values = dot_f32("hbij,hbid->hbjd", attn_low, grad_mixed)
    grad_weights = dot_f32("hbid,hbjd->hbij", grad_mixed, value_rows)
    grad_scores = attn_weights * (
        grad_weights - jnp.sum(attn_weights * grad_weights, axis=-1, keepdims=True)
    )
    scores_low = grad_scores.astype(low)
    grad_queries = dot_f32("hbij,hbjd->hbid", scores_low, key_rows) * scale
    grad_keys = dot_f32("hbij,hbid->hbjd", scores_low, queries) * scale
    grad_qk = jnp.concatenate([join_heads(grad_queries.astype(low)), join_heads(grad_keys.astype(low))], axis=1)
    grad_v = join_heads(grad_values.astype(low))
    grad_qkv = jnp.concatenate(
        [scattered(normed, grad_qk, "yxz"), scattered(normed, grad_v, "xyz")], axis=1
    )
    grad_normed = input_grad(grad_qk, qk) + input_grad(grad_v, vals)
    _, norm_back = jax.vjp(rms_scale, streams, gain_a)
    grad_streams_norm, grad_gain_a = norm_back(grad_normed)
    grad_streams = grad_attended + grad_streams_norm

    grad_patch_mix = grad_streams.reshape(patches, PATCH, D).sum(axis=1)
    mix_low = grad_patch_mix.astype(low)
    along = jnp.sum(mix_low.astype(f32) * raw_mixed, axis=1, keepdims=True)
    pair = jnp.concatenate([mixer_r, along], axis=1)
    pair_high = pair.astype(low)
    pair_rest = (pair - pair_high.astype(f32)).astype(low)
    extra = jnp.pad(jnp.concatenate([pair_high, pair_rest], axis=1), ((0, 0), (0, 124)))
    mix_all = gather_small(grid, jnp.concatenate([mix_low, extra], axis=1))
    extra = mix_all[:, D : D + 4].astype(f32)
    r_all, along_all = extra[:, 0:1] + extra[:, 2:3], extra[:, 1:2] + extra[:, 3:4]
    mix_all = mix_all[:, :D]
    grad_out_proj = weight_grad((gated * r_all * my_gain).astype(low), mix_all)
    back_m = input_grad(mix_all, out_proj)
    grad_gain_m = jnp.sum(back_m * gated * r_all, axis=0)
    grad_gated = r_all * my_gain * back_m - gated * (r_all * r_all * r_all * along_all / DI)
    grad_core = grad_gated * gate_raw * sig_m
    grad_gate_raw = grad_gated * core * sig_m * (1.0 + gate_raw * (1.0 - sig_m))
    (d_chan, d_maps, d_step, d_cw, d_cb, d_mw, d_mb, d_dt, d_alog, d_skip) = core_back(by_slot(grad_core))
    d_own = jnp.concatenate(
        [grad_gate_raw, d_chan.reshape(-1, HEAD_M), d_step.reshape(-1, 1)], axis=1
    ).astype(low)
    d_maps = d_maps.reshape(-1, BC).astype(low)
    grad_norm = scatter_small(grid, input_grad(d_own, own_proj) + input_grad(d_maps, maps_proj))
    grad_own_cols = weight_grad(global_all, d_own)
    grad_maps_cols = weight_grad(global_all, d_maps)
    _, norm_back = jax.vjp(rms_scale, patch_sum, gain_g)
    grad_sum_norm, grad_gain_g = norm_back(grad_norm)
    sum_low = (grad_patch_mix + grad_sum_norm).astype(low)
    sum_all = gather_small(grid, sum_low)
    grad_patch_proj = weight_grad(all_bytes, sum_all)
    back_bytes = input_grad(sum_all, patch_proj).astype(low).reshape(n_dev, patches, -1)
    back_bytes = exchange(back_bytes).transpose(1, 0, 2).reshape(rows, D)
    grad_states = grad_streams + back_bytes.astype(f32)

    taps = jnp.zeros((CONV_CH, CONV + 1), f32)
    taps = put(taps, jnp.concatenate([d_cw, d_cb[:, None]], axis=1), (me * HEAD_M, 0))
    taps = put(taps, jnp.concatenate([d_mw, d_mb[:, None]], axis=1), (DI, 0))
    sums = [taps.reshape(n_dev, -1)]
    sums += [g.reshape(n_dev, -1) for g in (grad_gain_g, grad_gain_a, grad_gain_f)]
    heads = jnp.zeros((3, MHEADS), f32)
    heads = put(heads, jnp.stack([d_dt, d_alog, d_skip]), (0, me)).reshape(1, -1)
    sums += [jnp.broadcast_to(heads, (n_dev, 3 * MHEADS))]
    sums = jnp.concatenate(sums, axis=1)
    width = sums.shape[1]
    extra_cols = -(-width // shard_rows)
    sums = jnp.pad(sums, ((0, 0), (0, extra_cols * shard_rows - width))).reshape(n_dev, shard_rows, extra_cols)
    parcel = jnp.concatenate(
        [
            grad_own_cols.reshape(n_dev, shard_rows, OWN),
            grad_maps_cols.reshape(n_dev, shard_rows, BC),
            sums,
        ],
        axis=2,
    ).astype(low)
    parcel = exchange(parcel).astype(f32)
    side = lambda a, b: parcel[:, :, a:b].transpose(1, 0, 2).reshape(shard_rows, -1)
    summed = jnp.sum(parcel[:, :, OWN:], axis=0)
    grad_in_proj = jnp.concatenate(
        [side(0, HEAD_M), side(HEAD_M, 2 * HEAD_M), summed[:, :BC], side(2 * HEAD_M, OWN)], axis=1
    )
    flat = summed[:, BC:].reshape(-1)
    taps = flat[: CONV_CH * (CONV + 1) // n_dev].reshape(-1, CONV + 1)
    at = CONV_CH * (CONV + 1) // n_dev
    grad_gain_g, grad_gain_a, grad_gain_f = (flat[at + i * D // n_dev : at + (i + 1) * D // n_dev] for i in range(3))
    at += 3 * D // n_dev
    heads = flat[at : at + 3 * MHEADS].reshape(3, MHEADS)
    return (
        block_out,
        grad_states,
        grad_patch_proj,
        grad_gain_g,
        grad_in_proj,
        taps[:, :CONV],
        taps[:, CONV],
        heads[0],
        heads[1],
        heads[2],
        grad_gain_m,
        grad_out_proj,
        grad_gain_a,
        grad_qkv,
        grad_attn_out,
        grad_gain_f,
        grad_gate,
        grad_up,
        grad_down,
    )


def solution(mesh):
    in_specs = (
        P(("dp", "fsdp"), None),
        P("dp", None),
        P(("dp", "fsdp"), None),
        P(("dp", "fsdp"), None),
        P(("dp", "fsdp")),
        P(("dp", "fsdp"), None),
        P(("dp", "fsdp"), None),
        P(("dp", "fsdp")),
        P(),
        P(),
        P(),
        P(("dp", "fsdp")),
        P(("dp", "fsdp"), None),
        P(("dp", "fsdp")),
        P(("dp", "fsdp"), None),
        P(("dp", "fsdp"), None),
        P(("dp", "fsdp")),
        P(("dp", "fsdp"), None),
        P(("dp", "fsdp"), None),
        P(("dp", "fsdp"), None),
    )
    out_specs = (
        P(("dp", "fsdp"), None),
        P(("dp", "fsdp"), None),
        P(("dp", "fsdp"), None),
        P(("dp", "fsdp")),
        P(("dp", "fsdp"), None),
        P(("dp", "fsdp"), None),
        P(("dp", "fsdp")),
        P(),
        P(),
        P(),
        P(("dp", "fsdp")),
        P(("dp", "fsdp"), None),
        P(("dp", "fsdp")),
        P(("dp", "fsdp"), None),
        P(("dp", "fsdp"), None),
        P(("dp", "fsdp")),
        P(("dp", "fsdp"), None),
        P(("dp", "fsdp"), None),
        P(("dp", "fsdp"), None),
    )
    dp, fsdp = mesh.shape["dp"], mesh.shape["fsdp"]
    fast = dp * fsdp == MHEADS and fsdp == 4
    chosen = partial(fast_body, (dp, fsdp)) if fast else body
    return jax.shard_map(chosen, mesh=mesh, in_specs=in_specs, out_specs=out_specs, check_vma=False)
```

```python
from functools import partial

import jax
import jax.numpy as jnp
from jax import lax
from jax.experimental import pallas as pl
from jax.experimental.pallas import tpu as pltpu
from jax.sharding import PartitionSpec as P

D = 1024
HEAD = 64
HEAD_M = 64
STATE = 128
CONV = 4
PATCH = 8
DI = 2048
MHEADS = 32
CONV_CH = 2304


EPSILON = 1e-05
HIGHEST = lax.Precision.HIGHEST


def shifted(block, axis, distance):
    devices = range(lax.axis_size(axis))
    route = [(i - distance, i) for i in devices if i - distance in devices]
    return lax.ppermute(block, axis, route)


def prefix(value, axis, combine, identity):
    devices, place = (lax.axis_size(axis), lax.axis_index(axis))
    everything = jax.tree.map(
        lambda part, kind: lax.all_gather(part.astype(kind), axis),
        value,
        (jnp.bfloat16, jnp.bfloat16),
    )
    start = jax.tree.map(
        lambda part, zero: jnp.broadcast_to(jnp.asarray(zero, part.dtype), part.shape),
        value,
        identity,
    )

    def prefix_step(k, before):
        reached = k < place
        new = combine(
            before, jax.tree.map(lambda part, own: part[k].astype(own.dtype), everything, value)
        )
        return jax.tree.map(lambda a, b: jnp.where(reached, a, b), new, before)

    return lax.fori_loop(0, devices, prefix_step, start)


def carried_in(value, axis, combine, identity):
    devices, place = (lax.axis_size(axis), lax.axis_index(axis))
    everything = jax.tree.map(
        lambda part, kind: lax.all_gather(part.astype(kind), axis),
        value,
        jax.tree.map(lambda a: jnp.bfloat16 if a.dtype == jnp.float32 else a.dtype, value),
    )
    start = jax.tree.map(
        lambda part, zero: jnp.broadcast_to(jnp.asarray(zero, part.dtype), part.shape),
        value,
        identity,
    )

    def carried_step(k, before):
        at = devices - 1 - k
        reached = at > place
        new = combine(
            before, jax.tree.map(lambda part, own: part[at].astype(own.dtype), everything, value)
        )
        return jax.tree.map(lambda a, b: jnp.where(reached, a, b), new, before)

    return lax.fori_loop(0, devices, carried_step, start)


def product(left, right):
    return jnp.dot(left, right, preferred_element_type=jnp.float32)


def weight_grad(left, right):
    return lax.dot_general(
        left, right, (((0,), (0,)), ((), ())), preferred_element_type=jnp.float32
    )


def input_grad(grad_rows, weight):
    return lax.dot_general(
        grad_rows, weight, (((1,), (1,)), ((), ())), preferred_element_type=jnp.float32
    )


def rms_scale(value, gain):
    return value * lax.rsqrt(jnp.mean(value * value, axis=-1, keepdims=True) + EPSILON) * gain


def gated_norm(core_out, gate_raw, gain):
    count = core_out.shape[0]
    return rms_scale(core_out.reshape(count, DI) * jax.nn.silu(gate_raw), gain)


def patch_docs(doc_lengths, start, count):
    places = start + jnp.arange(count, dtype=jnp.int32)
    first_end = doc_lengths[0, 0]
    second_end = first_end + doc_lengths[0, 1]
    numbers = (places >= first_end).astype(jnp.int32) + (places >= second_end).astype(jnp.int32)
    return jnp.where(places >= 0, numbers, -1)


def chain(earlier, later):
    return (earlier[0] * later[0], later[1] + later[0][:, None, None] * earlier[1])


def mixer_core(
    channels,
    rim,
    step_raw,
    state_in,
    conv_weight,
    conv_bias,
    dt_bias,
    a_log,
    skip_weight,
    docs,
    rim_docs,
    prev_doc,
):
    count = channels.shape[0]
    padded = jnp.concatenate([rim, channels], axis=0)
    padded_docs = jnp.concatenate([rim_docs, docs])
    total = conv_bias[None, :]
    for shift_k in range(CONV):
        same_doc = (padded_docs[shift_k : shift_k + count] == docs).astype(jnp.float32)
        total = (
            total
            + padded[shift_k : shift_k + count]
            * conv_weight[:, shift_k][None, :]
            * same_doc[:, None]
        )
    activated = jax.nn.silu(total)
    inputs = activated[:, :DI].reshape(count, MHEADS, HEAD_M)
    in_map = activated[:, DI : DI + STATE]
    out_map = activated[:, DI + STATE :]
    step_size = jax.nn.softplus(step_raw + dt_bias[None, :])
    rate = -jnp.exp(a_log)
    lower = jnp.tril(jnp.ones((count, count), jnp.float32))
    cumulative = jnp.dot(lower, step_size * rate[None, :], precision=HIGHEST)
    places = jnp.arange(count, dtype=jnp.int32)
    keep = ((places[:, None] >= places[None, :]) & (docs[:, None] == docs[None, :]))[:, :, None]
    spread = cumulative[:, None, :] - cumulative[None, :, :]
    decay_table = jnp.where(keep, jnp.exp(jnp.where(keep, spread, 0.0)), 0.0)
    inner = jnp.dot(out_map, in_map.T, precision=HIGHEST, preferred_element_type=jnp.float32)
    mixing = decay_table * inner[:, :, None] * step_size[None, :, :]
    outputs = jnp.einsum("tsh,shp->thp", mixing, inputs, precision=HIGHEST)
    carry_in = jnp.where((docs == prev_doc)[:, None], jnp.exp(cumulative), 0.0)
    outputs = outputs + carry_in[:, :, None] * jnp.einsum(
        "tn,hpn->thp", out_map, state_in, precision=HIGHEST
    )
    outputs = outputs + skip_weight[None, :, None] * inputs
    last_doc = docs[count - 1]
    tail_keep = (docs == last_doc)[:, None]
    tail_gap = cumulative[count - 1][None, :] - cumulative
    tail_weight = (
        jnp.where(tail_keep, jnp.exp(jnp.where(tail_keep, tail_gap, 0.0)), 0.0) * step_size
    )
    decay_total = jnp.where(prev_doc == last_doc, jnp.exp(cumulative[count - 1]), 0.0)
    state_out = jnp.einsum("sh,shp,sn->hpn", tail_weight, inputs, in_map, precision=HIGHEST)
    state_out = state_out + decay_total[:, None, None] * state_in
    return ((outputs, state_out), (decay_total, carry_in, out_map))


def attend(qkv_low, patches):
    heads = qkv_low.reshape(patches, PATCH, 3, -1, HEAD)
    queries = heads[:, :, 0]
    key_rows = heads[:, :, 1]
    value_rows = heads[:, :, 2]
    scores = jnp.einsum(
        "pihd,pjhd->phij", queries, key_rows, preferred_element_type=jnp.float32
    ) * HEAD ** (-0.5)
    places = jnp.arange(PATCH)
    causal = places[:, None] >= places[None, :]
    scores = jnp.where(causal, scores, -1e30)
    attn_weights = jax.nn.softmax(scores, axis=-1)
    attn_low = attn_weights.astype(jnp.bfloat16)
    mixed = jnp.einsum("phij,pjhd->pihd", attn_low, value_rows, preferred_element_type=jnp.float32)
    mixed = mixed.astype(jnp.bfloat16).reshape(patches * PATCH, -1)
    return ((queries, key_rows, value_rows, attn_weights, attn_low), mixed)


def attend_back(grad_mixed_low, pieces):
    queries, key_rows, value_rows, attn_weights, attn_low = pieces
    patches = queries.shape[0]
    grad_mixed = grad_mixed_low.reshape(patches, PATCH, -1, HEAD)
    grad_values = jnp.einsum(
        "phij,pihd->pjhd", attn_low, grad_mixed, preferred_element_type=jnp.float32
    )
    grad_weights = jnp.einsum(
        "pihd,pjhd->phij", grad_mixed, value_rows, preferred_element_type=jnp.float32
    )
    grad_scores = attn_weights * (
        grad_weights - jnp.sum(attn_weights * grad_weights, axis=-1, keepdims=True)
    )
    scores_low = grad_scores.astype(jnp.bfloat16)
    scale = HEAD ** (-0.5)
    grad_queries = (
        jnp.einsum("phij,pjhd->pihd", scores_low, key_rows, preferred_element_type=jnp.float32)
        * scale
    )
    grad_keys = (
        jnp.einsum("phij,pihd->pjhd", scores_low, queries, preferred_element_type=jnp.float32)
        * scale
    )
    stacked = jnp.stack([grad_queries, grad_keys, grad_values], axis=2).reshape(patches * PATCH, -1)
    return stacked.astype(jnp.bfloat16)


def local_forward(byte_states, mixed_patch, local_set, live):
    attn_gain, qkv_proj, attn_out, ffn_gain, gate_proj, up_proj, down_proj = local_set
    rows = byte_states.shape[0]
    streams = byte_states.astype(jnp.float32) + jnp.repeat(mixed_patch, PATCH, axis=0)
    normed_low = rms_scale(streams, attn_gain.astype(jnp.float32)).astype(jnp.bfloat16)
    qkv_low = product(normed_low, qkv_proj).astype(jnp.bfloat16)
    pieces, mixed_heads = attend(qkv_low, rows // PATCH)
    attended = streams + product(mixed_heads, attn_out)
    ffn_low = rms_scale(attended, ffn_gain.astype(jnp.float32)).astype(jnp.bfloat16)
    gate = product(ffn_low, gate_proj)
    upward = product(ffn_low, up_proj)
    hidden_low = (jax.nn.silu(gate) * upward).astype(jnp.bfloat16)
    block = live * (attended + product(hidden_low, down_proj))
    cache = (streams, normed_low, pieces, mixed_heads, attended, ffn_low, gate, upward, hidden_low)
    return (block, cache)


def local_backward(grad_block, cache, local_set):
    attn_gain, qkv_proj, attn_out, ffn_gain, gate_proj, up_proj, down_proj = local_set
    streams, normed_low, pieces, mixed_heads, attended, ffn_low, gate, upward, hidden_low = cache
    down_low = grad_block.astype(jnp.bfloat16)
    grad_down = weight_grad(hidden_low, down_low)
    grad_hidden = input_grad(down_low, down_proj)
    sigma = jax.nn.sigmoid(gate)
    grad_gate_low = (grad_hidden * upward * sigma * (1.0 + gate * (1.0 - sigma))).astype(
        jnp.bfloat16
    )
    grad_up_low = (grad_hidden * gate * sigma).astype(jnp.bfloat16)
    grad_gate = weight_grad(ffn_low, grad_gate_low)
    grad_up = weight_grad(ffn_low, grad_up_low)
    grad_ffn_in = input_grad(grad_gate_low, gate_proj) + input_grad(grad_up_low, up_proj)
    _, norm_back = jax.vjp(rms_scale, attended, ffn_gain.astype(jnp.float32))
    grad_attended_norm, grad_ffn_gain = norm_back(grad_ffn_in)
    grad_attended = grad_block + grad_attended_norm
    attn_grad_low = grad_attended.astype(jnp.bfloat16)
    grad_attn_out = weight_grad(mixed_heads, attn_grad_low)
    grad_mixed_low = input_grad(attn_grad_low, attn_out).astype(jnp.bfloat16)
    grad_qkv_low = attend_back(grad_mixed_low, pieces)
    grad_qkv = weight_grad(normed_low, grad_qkv_low)
    grad_normed = input_grad(grad_qkv_low, qkv_proj)
    _, norm_back = jax.vjp(rms_scale, streams, attn_gain.astype(jnp.float32))
    grad_streams_norm, grad_attn_gain = norm_back(grad_normed)
    grad_streams = grad_attended + grad_streams_norm
    return (
        grad_streams,
        (grad_qkv, grad_attn_out, grad_gate, grad_up, grad_down, grad_attn_gain, grad_ffn_gain),
    )


def body(
    byte_states,
    doc_lengths,
    out_grad,
    patch_proj,
    global_gain,
    in_proj,
    conv_weight,
    conv_bias,
    dt_bias,
    a_log,
    skip_weight,
    mixer_gain,
    out_proj,
    attn_gain,
    qkv_proj,
    attn_out,
    ffn_gain,
    gate_proj,
    up_proj,
    down_proj,
):
    rows = byte_states.shape[0]
    patches = rows // PATCH
    share = lax.axis_index("fsdp")
    start = share * patches
    docs = patch_docs(doc_lengths, start, patches)
    rim_docs = patch_docs(doc_lengths, start - (CONV - 1), CONV - 1)
    prev_doc = patch_docs(doc_lengths, start - 1, 1)[0]
    live = jnp.repeat((docs < 2).astype(jnp.float32), PATCH)[:, None]
    all_set = (
        lax.all_gather(patch_proj, ("dp", "fsdp"), axis=0, tiled=True),
        lax.all_gather(global_gain, ("dp", "fsdp"), axis=0, tiled=True),
        lax.all_gather(in_proj, ("dp", "fsdp"), axis=0, tiled=True),
        lax.all_gather(conv_weight, ("dp", "fsdp"), axis=0, tiled=True),
        lax.all_gather(conv_bias, ("dp", "fsdp"), axis=0, tiled=True),
        lax.all_gather(mixer_gain, ("dp", "fsdp"), axis=0, tiled=True),
        lax.all_gather(out_proj, ("dp", "fsdp"), axis=0, tiled=True),
        lax.all_gather(attn_gain, ("dp", "fsdp"), axis=0, tiled=True),
        lax.all_gather(qkv_proj, ("dp", "fsdp"), axis=0, tiled=True),
        lax.all_gather(attn_out, ("dp", "fsdp"), axis=0, tiled=True),
        lax.all_gather(ffn_gain, ("dp", "fsdp"), axis=0, tiled=True),
        lax.all_gather(gate_proj, ("dp", "fsdp"), axis=0, tiled=True),
        lax.all_gather(up_proj, ("dp", "fsdp"), axis=0, tiled=True),
        lax.all_gather(down_proj, ("dp", "fsdp"), axis=0, tiled=True),
    )
    global_set = all_set[:7]
    local_set = all_set[7:]
    patch_full, gain_g_full, in_full, conv_w_full, conv_b_full, gain_m_full, out_full = global_set
    patch_rows = byte_states.reshape(patches, PATCH * D)
    patch_sum = product(patch_rows, patch_full)
    gain_g = gain_g_full.astype(jnp.float32)
    global_low = rms_scale(patch_sum, gain_g).astype(jnp.bfloat16)
    projected = product(global_low, in_full)
    gate_raw = projected[:, :DI]
    channels = projected[:, DI : DI + CONV_CH]
    step_raw = projected[:, DI + CONV_CH :]
    rim = shifted(channels[patches - (CONV - 1) :], "fsdp", 1)
    core = partial(mixer_core, docs=docs, rim_docs=rim_docs, prev_doc=prev_doc)
    conv_w = conv_w_full.astype(jnp.float32)
    conv_b = conv_b_full.astype(jnp.float32)
    empty_state = jnp.zeros((MHEADS, HEAD_M, STATE), jnp.float32)
    (partial_out, local_state), aux = core(
        channels, rim, step_raw, empty_state, conv_w, conv_b, dt_bias, a_log, skip_weight
    )
    decay_total, carry_in, out_map = aux
    identity = (jnp.ones((MHEADS,), jnp.float32), jnp.zeros((MHEADS, HEAD_M, STATE), jnp.float32))
    arrived = prefix((decay_total, local_state), "fsdp", chain, identity)
    state_in = arrived[1]
    mixer_out = partial_out + carry_in[:, :, None] * jnp.einsum(
        "tn,hpn->thp", out_map, state_in, precision=HIGHEST
    )
    gain_m = gain_m_full.astype(jnp.float32)
    mixer_low = gated_norm(mixer_out, gate_raw, gain_m).astype(jnp.bfloat16)
    mixed_patch = patch_sum + product(mixer_low, out_full)
    block, cache = local_forward(byte_states, mixed_patch, local_set, live)
    block_out = block.astype(jnp.bfloat16)
    back_set = (
        lax.all_gather(patch_proj, ("dp", "fsdp"), axis=0, tiled=True),
        lax.all_gather(global_gain, ("dp", "fsdp"), axis=0, tiled=True),
        lax.all_gather(in_proj, ("dp", "fsdp"), axis=0, tiled=True),
        lax.all_gather(conv_weight, ("dp", "fsdp"), axis=0, tiled=True),
        lax.all_gather(conv_bias, ("dp", "fsdp"), axis=0, tiled=True),
        lax.all_gather(mixer_gain, ("dp", "fsdp"), axis=0, tiled=True),
        lax.all_gather(out_proj, ("dp", "fsdp"), axis=0, tiled=True),
        lax.all_gather(attn_gain, ("dp", "fsdp"), axis=0, tiled=True),
        lax.all_gather(qkv_proj, ("dp", "fsdp"), axis=0, tiled=True),
        lax.all_gather(attn_out, ("dp", "fsdp"), axis=0, tiled=True),
        lax.all_gather(ffn_gain, ("dp", "fsdp"), axis=0, tiled=True),
        lax.all_gather(gate_proj, ("dp", "fsdp"), axis=0, tiled=True),
        lax.all_gather(up_proj, ("dp", "fsdp"), axis=0, tiled=True),
        lax.all_gather(down_proj, ("dp", "fsdp"), axis=0, tiled=True),
    )
    global_back = back_set[:7]
    local_back = back_set[7:]
    _, cache = local_forward(byte_states, mixed_patch, local_back, live)
    patch_back, _, in_back, conv_w_back, conv_b_back, _, out_back = global_back
    grad_block = live * out_grad.astype(jnp.float32)
    grad_streams, local_grads = local_backward(grad_block, cache, local_back)
    reduced_local = (
        lax.psum_scatter(local_grads[0], ("dp", "fsdp"), scatter_dimension=0, tiled=True),
        lax.psum_scatter(local_grads[1], ("dp", "fsdp"), scatter_dimension=0, tiled=True),
        lax.psum_scatter(local_grads[2], ("dp", "fsdp"), scatter_dimension=0, tiled=True),
        lax.psum_scatter(local_grads[3], ("dp", "fsdp"), scatter_dimension=0, tiled=True),
        lax.psum_scatter(local_grads[4], ("dp", "fsdp"), scatter_dimension=0, tiled=True),
        lax.psum_scatter(local_grads[5], ("dp", "fsdp"), scatter_dimension=0, tiled=True),
        lax.psum_scatter(local_grads[6], ("dp", "fsdp"), scatter_dimension=0, tiled=True),
    )
    grad_patch_mix = grad_streams.reshape(patches, PATCH, D).sum(axis=1)
    mix_low = grad_patch_mix.astype(jnp.bfloat16)
    grad_out_proj = weight_grad(mixer_low, mix_low)
    grad_mixer_low = input_grad(mix_low, out_back)
    _, norm_back = jax.vjp(gated_norm, mixer_out, gate_raw, gain_m)
    grad_core, grad_gate_raw, grad_mixer_gain = norm_back(grad_mixer_low)
    state_part = jnp.einsum("th,thp,tn->hpn", carry_in, grad_core, out_map, precision=HIGHEST)
    returned = carried_in((decay_total, state_part), "fsdp", chain, identity)
    _, core_back, _ = jax.vjp(
        core,
        channels,
        rim,
        step_raw,
        state_in,
        conv_w_back.astype(jnp.float32),
        conv_b_back.astype(jnp.float32),
        dt_bias,
        a_log,
        skip_weight,
        has_aux=True,
    )
    core_grads = core_back((grad_core, returned[1]))
    (
        grad_channels,
        grad_rim,
        grad_step,
        _,
        grad_conv_w,
        grad_conv_b,
        grad_dt_bias,
        grad_a_log,
        grad_skip,
    ) = core_grads
    rim_grad = shifted(grad_rim, "fsdp", -1)
    cut = patches - (CONV - 1)
    grad_channels = jnp.concatenate([grad_channels[:cut], grad_channels[cut:] + rim_grad], axis=0)
    proj_low = jnp.concatenate([grad_gate_raw, grad_channels, grad_step], axis=1).astype(
        jnp.bfloat16
    )
    grad_in_proj = weight_grad(global_low, proj_low)
    grad_global_norm = input_grad(proj_low, in_back)
    _, norm_back = jax.vjp(rms_scale, patch_sum, gain_g)
    grad_sum_norm, grad_global_gain = norm_back(grad_global_norm)
    sum_low = (grad_patch_mix + grad_sum_norm).astype(jnp.bfloat16)
    grad_patch_proj = weight_grad(patch_rows, sum_low)
    grad_states = grad_streams + input_grad(sum_low, patch_back).reshape(rows, D)
    reduced_global = (
        lax.psum_scatter(grad_patch_proj, ("dp", "fsdp"), scatter_dimension=0, tiled=True),
        lax.psum_scatter(grad_global_gain, ("dp", "fsdp"), scatter_dimension=0, tiled=True),
        lax.psum_scatter(grad_in_proj, ("dp", "fsdp"), scatter_dimension=0, tiled=True),
        lax.psum_scatter(grad_conv_w, ("dp", "fsdp"), scatter_dimension=0, tiled=True),
        lax.psum_scatter(grad_conv_b, ("dp", "fsdp"), scatter_dimension=0, tiled=True),
        lax.psum_scatter(grad_mixer_gain, ("dp", "fsdp"), scatter_dimension=0, tiled=True),
        lax.psum_scatter(grad_out_proj, ("dp", "fsdp"), scatter_dimension=0, tiled=True),
    )
    head_sums = lax.psum((grad_dt_bias, grad_a_log, grad_skip), ("dp", "fsdp"))
    return (
        block_out,
        grad_states,
        reduced_global[0],
        reduced_global[1],
        reduced_global[2],
        reduced_global[3],
        reduced_global[4],
        head_sums[0],
        head_sums[1],
        head_sums[2],
        reduced_global[5],
        reduced_global[6],
        reduced_local[5],
        reduced_local[0],
        reduced_local[1],
        reduced_local[6],
        reduced_local[2],
        reduced_local[3],
        reduced_local[4],
    )


MESH = pl.DeviceIdType.MESH
WIDE = 12288
TILE = 32
SMALL_ROWS, SMALL_COLS = 48, 384
EXT = D + 128


def device(z, x, y, c):
    return (z * 2 + x, y * 2 + c)


class Spot:
    def __init__(self, depth):
        dp, fs = lax.axis_index("dp"), lax.axis_index("fsdp")
        self.depth, self.count = depth, depth * 8
        self.me = dp * 4 + fs
        self.z, self.x, self.y, self.c = dp // 2, dp % 2, fs // 2, fs % 2
        self.q = self.x * 4 + self.y * 2 + self.c
        self.plane = self.x * 2 + self.y
        self.column = [(self.z + depth - j) % depth for j in range(depth)]

    def flip(self, way):
        x = 1 - self.x if way & 2 else self.x
        y = 1 - self.y if way & 1 else self.y
        return device(self.z, x, y, self.c), x * 2 + y

    def sibling(self):
        return device(self.z, self.x, self.y, 1 - self.c)

    def above(self, k):
        return device((self.z + k) % self.depth, self.x, self.y, self.c)


def greet(spot):
    barrier = pltpu.get_barrier_semaphore()

    def one(i, carry):
        to = (spot.me + i) % spot.count
        pl.semaphore_signal(barrier, inc=1, device_id=(to // 4, to % 4), device_id_type=MESH)
        return carry

    lax.fori_loop(1, spot.count, one, 0)
    pl.semaphore_wait(barrier, spot.count - 1)


class Wires:
    def __init__(self, send, recv):
        self.send, self.recv, self.used, self.open = send, recv, 0, []

    def copy(self, src, dst, to):
        i = self.used
        self.used += 1
        copy = pltpu.make_async_remote_copy(
            src_ref=src,
            dst_ref=dst,
            send_sem=self.send.at[i],
            recv_sem=self.recv.at[i],
            device_id=to,
            device_id_type=MESH,
        )
        copy.start()
        self.open.append(copy)
        return copy

    def drain(self):
        for copy in self.open:
            copy.wait_send()


def got(copies):
    for copy in copies:
        copy.wait_recv()


class Swap:
    def __init__(self, spot, send, recv, src_at, dst_at):
        self.spot, self.send, self.recv, self.src_at, self.dst_at = spot, send, recv, src_at, dst_at

    def copy(self, i):
        to = (self.spot.me + i) % self.spot.count
        return pltpu.make_async_remote_copy(
            src_ref=self.src_at(to),
            dst_ref=self.dst_at(self.spot.me),
            send_sem=self.send.at[i],
            recv_sem=self.recv.at[i],
            device_id=(to // 4, to % 4),
            device_id_type=MESH,
        )

    def each(self, act):
        def one(i, carry):
            act(self.copy(i))
            return carry

        lax.fori_loop(1, self.spot.count, one, 0)

    def start(self):
        self.each(lambda copy: copy.start())

    def arrive(self):
        self.each(lambda copy: copy.wait_recv())

    def leave(self):
        self.each(lambda copy: copy.wait_send())


def block_row(t, plane, c):
    return (t * 4 + plane) * 2 + c


def spread_all(wires, spot, buf, own=None):
    at = lambda t, plane, c: buf.at[block_row(t, plane, c)]
    mine = at(spot.z, spot.plane, spot.c)
    src = mine if own is None else own
    ring, flat, core = [], [], []
    for k in range(1, spot.depth):
        ring.append(wires.copy(src, mine, spot.above(k)))
    flat.append([wires.copy(src, mine, spot.flip(way)[0]) for way in (1, 2, 3)])
    core.append(wires.copy(src, mine, spot.sibling()))
    yield
    for j in range(1, spot.depth):
        got([ring[j - 1]])
        block = at(spot.column[j], spot.plane, spot.c)
        flat.append([wires.copy(block, block, spot.flip(way)[0]) for way in (1, 2, 3)])
        core.append(wires.copy(block, block, spot.sibling()))
    yield
    for j in range(spot.depth):
        for way in (1, 2, 3):
            got([flat[j][way - 1]])
            block = at(spot.column[j], spot.flip(way)[1], spot.c)
            core.append(wires.copy(block, block, spot.sibling()))
    yield
    got(core)


def spread_plane(wires, spot, buf):
    at = lambda plane: buf.at[plane * 2 + spot.c]
    mine = at(spot.plane)
    flat = [wires.copy(mine, mine, spot.flip(way)[0]) for way in (1, 2, 3)]
    core = [wires.copy(mine, mine, spot.sibling())]
    yield
    for way in (1, 2, 3):
        got([flat[way - 1]])
        block = at(spot.flip(way)[1])
        core.append(wires.copy(block, block, spot.sibling()))
    yield
    got(core)


def sum_plane(wires, spot, parts, pair, near):
    first = wires.copy(parts.at[:, 1 - spot.c], pair, spot.sibling())
    yield None
    got([first])
    f32 = jnp.float32
    pair[...] = (parts[:, spot.c].astype(f32) + pair[...].astype(f32)).astype(jnp.bfloat16)
    flat = [
        wires.copy(pair.at[spot.flip(way)[1]], near.at[way - 1], spot.flip(way)[0]) for way in (1, 2, 3)
    ]
    yield None
    got(flat)
    total = pair[spot.plane].astype(f32)
    for way in range(3):
        total = total + near[way].astype(f32)
    yield total


def sum_all(wires, spot, parts, pair, near, column, far, out):
    f32, low = jnp.float32, jnp.bfloat16
    half = parts.shape[-1] // 2
    cut = [pl.ds(h * half, half) for h in range(2)]
    first = [
        wires.copy(parts.at[:, 1 - spot.c, :, cut[h]], pair.at[:, :, cut[h]], spot.sibling()) for h in range(2)
    ]
    yield
    flat, ring = [], []
    rows = pair.shape[1]
    for h in range(2):
        got([first[h]])
        for b in range(4 * spot.depth):
            pair[b, :, cut[h]] = (
                parts[b, spot.c, :, cut[h]].astype(f32) + pair[b, :, cut[h]].astype(f32)
            ).astype(low)
        step = []
        for way in (1, 2, 3):
            to, plane = spot.flip(way)
            for t in range(spot.depth):
                step.append(
                    wires.copy(pair.at[t * 4 + plane, :, cut[h]], near.at[way - 1, t, :, cut[h]], to)
                )
        flat.append(step)
    yield
    for h in range(2):
        got(flat[h])
        for t in range(spot.depth):
            total = pair[t * 4 + spot.plane, :, cut[h]].astype(f32)
            for way in range(3):
                total = total + near[way, t, :, cut[h]].astype(f32)
            column[t, :, cut[h]] = total.astype(low)
        ring.append(
            [
                wires.copy(
                    column.at[(spot.z + k) % spot.depth, :, cut[h]], far.at[k - 1, :, cut[h]], spot.above(k)
                )
                for k in range(1, spot.depth)
            ]
        )
    yield
    for h in range(2):
        got(ring[h])
        total = column[spot.z, :, cut[h]].astype(f32)
        for k in range(1, spot.depth):
            total = total + far[k - 1, :, cut[h]].astype(f32)
        out[:, cut[h]] = total
    yield


def big_gather(wires, spot, ow, od, shards):
    half, down = WIDE // 2, od.shape[0] // spot.count
    xn, yn, cn, zn = spot.flip(2)[0], spot.flip(1)[0], spot.sibling(), spot.above(1)
    here, xp, yp, xy = spot.plane, spot.flip(2)[1], spot.flip(1)[1], spot.flip(3)[1]

    def refs(t, plane, part):
        r = block_row(t, plane, spot.c)
        wide, deep = pl.multiple_of(r * TILE, TILE), pl.multiple_of(r * down, down)
        if part == "A":
            return [ow.at[pl.ds(wide, TILE), pl.ds(0, half)], od.at[pl.ds(deep, down // 2)]]
        if part == "B":
            return [
                ow.at[pl.ds(wide, TILE), pl.ds(half, half)],
                od.at[pl.ds(pl.multiple_of(deep + down // 2, down // 2), down // 2)],
            ]
        return [ow.at[pl.ds(wide, TILE)], od.at[pl.ds(deep, down)]]

    def go(t, plane, part, to):
        return [wires.copy(r, r, to) for r in refs(t, plane, part)]

    qkv, attn, gate, up, deep = shards
    cols, at = [], 0
    mine = pl.multiple_of(spot.me * TILE, TILE)
    for ref, a, b in ((qkv, 0, 3072), (attn, 0, 1024), (gate, 0, 2048), (gate, 2048, 2048), (up, 0, 4096)):
        cols.append((ref.at[:, pl.ds(a, b)], ow.at[pl.ds(mine, TILE), pl.ds(at, b)]))
        at += b
    row = pl.multiple_of(spot.me * down, down)
    deeps = [
        (deep.at[pl.ds(h * down // 2, down // 2)], od.at[pl.ds(pl.multiple_of(row + h * (down // 2), down // 2), down // 2)])
        for h in range(2)
    ]

    def own(part, to):
        pairs = {"A": cols[:3] + deeps[:1], "B": cols[3:] + deeps[1:], "AB": cols + deeps}[part]
        return [wires.copy(a, b, to) for a, b in pairs]

    T = spot.column
    core, ring, fx, fy, sx, sy = [], {}, {}, {}, {}, {}

    def first(j):
        send = own if j == 0 else (lambda part, to: go(T[j], here, part, to))
        if j < spot.depth - 1:
            ring[j] = send("AB", zn)
        fx[j], fy[j] = send("A", xn), send("B", yn)
        core.append(send("AB", cn))

    def second(j):
        got(fx[j])
        sy[j] = (own("A", yn) if j == 0 else go(T[j], here, "A", yn)) + go(T[j], xp, "A", yn)
        got(fy[j])
        sx[j] = (own("B", xn) if j == 0 else go(T[j], here, "B", xn)) + go(T[j], yp, "B", xn)
        core.append(go(T[j], xp, "A", cn) + go(T[j], yp, "B", cn))

    def third(j):
        got(sy[j])
        core.append(go(T[j], yp, "A", cn) + go(T[j], xy, "A", cn))
        got(sx[j])
        core.append(go(T[j], xp, "B", cn) + go(T[j], xy, "B", cn))

    first(0)
    yield
    for j in range(1, spot.depth):
        second(j - 1)
        yield
        got(ring[j - 1])
        first(j)
        yield
        if j >= 2:
            third(j - 2)
            yield
    second(spot.depth - 1)
    yield
    third(spot.depth - 2)
    third(spot.depth - 1)
    yield
    for copies in core:
        got(copies)
    yield


def run(steps):
    for _ in steps:
        pass


def sigmoid(v):
    return 1.0 / (1.0 + jnp.exp(-v))


def lanes(shape, axis):
    return lax.broadcasted_iota(jnp.int32, shape, axis)


def flat_dot(a, b, dims=((1,), (0,))):
    return lax.dot_general(a, b, (dims, ((), ())), preferred_element_type=jnp.float32)


def exact_dot(a, b):
    return jnp.dot(a, b, precision=HIGHEST, preferred_element_type=jnp.float32)


def gain_row(values):
    n_dev, width = values.shape[0], D // values.shape[0]
    spread = (lanes((128, D), 0) == lanes((128, D), 1) & (width - 1)).astype(jnp.bfloat16)
    rows = flat_dot(values, spread)
    return jnp.sum(jnp.where(lanes((n_dev, D), 0) == lanes((n_dev, D), 1) >> (width.bit_length() - 1), rows, 0.0), axis=0, keepdims=True)


def tap_rows(spot, small):
    n_dev = spot.count
    share = CONV_CH // n_dev
    col = lanes((1, 512), 1)
    channel = jnp.where(col < 256, (spot.q + 8 * (col >> 6)) * HEAD_M + (col & 63), DI + col - 256)
    dev = lanes((n_dev, 512), 0)
    picks = (channel >= dev * share) & (channel < dev * share + share)
    owner = jnp.sum(jnp.where(picks, dev, 0), axis=0, keepdims=True)
    within = lanes((128, 512), 0) == channel - owner * share
    rows = []
    for k in range(CONV + 1):
        values = small[:, TILE + k, 0:128]
        spread = flat_dot(values, picks.astype(jnp.bfloat16), ((0,), (0,)))
        rows.append(jnp.sum(jnp.where(within, spread, 0.0), axis=0, keepdims=True))
    return rows


def entry(block, row, lane):
    at = (lanes(block.shape, 0) == row) & (lanes(block.shape, 1) == lane)
    return jnp.sum(jnp.where(at, block.astype(jnp.float32), 0.0), keepdims=True).reshape(1, 1)


class Slot:
    def __init__(self, spot, small, x, count):
        block = small[(spot.z * 2 + x) * 4, TILE : TILE + 16, 0:128].astype(jnp.float32)
        first = entry(block, 9, 0)
        second = first + entry(block, 9, 1)
        number = lambda p: (p >= first).astype(jnp.float32) + (p >= second).astype(jnp.float32)
        col = lanes((count, 1), 0).astype(jnp.float32)
        row = lanes((1, count), 1).astype(jnp.float32)
        docs = number(col)
        self.keep = (col >= row) & (docs == number(row))
        self.same = [((col >= s) & (number(col - s) == docs)).astype(jnp.float32) for s in range(CONV)]


def shift(block, by):
    return block if by == 0 else pltpu.roll(block, by % block.shape[0], 0)


class Mixed:
    def __init__(self, spot, slot, own, maps, step_raw, taps, dt_row, rate_row):
        count = own.shape[0]
        self.spot, self.slot, self.count = spot, slot, count
        self.channels = jnp.concatenate([own[:, 256:], maps], axis=1)
        conv = taps[CONV] + sum(
            taps[CONV - 1 - s] * (shift(self.channels, s) * slot.same[s]) for s in range(CONV)
        )
        self.conv, self.sig = conv, sigmoid(conv)
        act = conv * self.sig
        self.inputs = act[:, :256]
        self.in_map, self.out_map = act[:, 256:384].astype(jnp.bfloat16), act[:, 384:].astype(jnp.bfloat16)
        self.raw = step_raw + dt_row
        self.step = jnp.where(self.raw > 20.0, self.raw, jnp.log(1.0 + jnp.exp(jnp.minimum(self.raw, 20.0))))
        lower = lanes((count, count), 0) >= lanes((count, count), 1)
        self.upper = (lanes((count, count), 0) <= lanes((count, count), 1)).astype(jnp.float32)
        self.cum = exact_dot(lower.astype(jnp.float32), self.step * rate_row)
        self.cum_t, self.step_t = self.cum.T, self.step.T
        self.inner = flat_dot(self.out_map, self.in_map, ((1,), (1,)))

    def head(self, i):
        return self.spot.q + 8 * i

    def col(self, by_head, i):
        return jnp.sum(jnp.where(lanes((1, 128), 1) == self.head(i), by_head, 0.0), axis=1, keepdims=True)

    def row(self, by_head_t, i):
        return jnp.sum(jnp.where(lanes((128, 1), 0) == self.head(i), by_head_t, 0.0), axis=0, keepdims=True)

    def decay(self, i):
        gap = jnp.where(self.slot.keep, self.col(self.cum, i) - self.row(self.cum_t, i), 0.0)
        return jnp.where(self.slot.keep, jnp.exp(gap), 0.0)


def pick_lane(row, lane):
    return jnp.sum(jnp.where(lanes(row.shape, 1) == lane, row, 0.0), axis=1, keepdims=True)


N_WIRES = 256


def forward_kernel(
    depth,
    rows_ref,
    patch_ref,
    cols_ref,
    vec_ref,
    out_ref,
    heads_ref,
    qkv,
    attn,
    gate,
    up,
    down,
    ow,
    od,
    sum_ref,
    mixed_ref,
    small_ref,
    bytes_ref,
    norm_ref,
    proj_ref,
    head_w_ref,
    own_ref,
    maps_ref,
    step_ref,
    core_ref,
    parts,
    pair,
    near,
    column,
    far,
    parts8,
    pair8,
    near8,
    send,
    recv,
    swap_send,
    swap_recv,
    local,
):
    f32, low = jnp.float32, jnp.bfloat16
    spot = Spot(depth)
    count = 128
    wires = Wires(send, recv)
    mine = pl.multiple_of(spot.me * TILE, TILE)
    bytes_ref[pl.ds(mine, TILE)] = rows_ref[:, pl.ds(pl.multiple_of(spot.me * 256, 256), 256)]
    small_ref[spot.me] = vec_ref[...]
    proj_ref[pl.ds(mine, TILE)] = cols_ref[spot.q]
    head_w_ref[spot.z] = out_ref[...]
    greet(spot)

    def lanes_of(to):
        return rows_ref.at[:, pl.ds(pl.multiple_of(to * 256, 256), 256)]

    swap_bytes = Swap(
        spot,
        swap_send.at[0],
        swap_recv.at[0],
        lanes_of,
        lambda me: bytes_ref.at[pl.ds(pl.multiple_of(me * TILE, TILE), TILE)],
    )
    swap_bytes.start()
    big = big_gather(wires, spot, ow, od, (qkv, attn, gate, up, down))
    swap_proj = Swap(
        spot,
        swap_send.at[1],
        swap_recv.at[1],
        lambda to: cols_ref.at[to % 8],
        lambda me: proj_ref.at[pl.ds(pl.multiple_of(me * TILE, TILE), TILE)],
    )
    swap_proj.start()
    small = spread_all(wires, spot, small_ref)
    next(small)
    head_w = [wires.copy(out_ref, head_w_ref.at[spot.z], spot.above(k)) for k in range(1, depth)]
    next(big)
    own_rows = []
    at = 0
    for i, ref in enumerate((qkv, attn, gate, up)):
        width = ref.shape[1]
        own_rows.append(pltpu.make_async_copy(ref, ow.at[pl.ds(mine, TILE), pl.ds(at, width)], local.at[i]))
        at += width
    deep = down.shape[0]
    own_rows.append(
        pltpu.make_async_copy(down, od.at[pl.ds(pl.multiple_of(spot.me * deep, deep), deep)], local.at[4])
    )
    for copy in own_rows:
        copy.start()
    swap_bytes.arrive()

    for b in range(4):
        block = flat_dot(bytes_ref[pl.ds(b * 256, 256)], patch_ref[...]).astype(low)
        parts[pl.ds(b * 4, 4)] = block.reshape(4, 2, TILE, D)
    total = sum_all(wires, spot, parts, pair, near, column, far, sum_ref)
    next(total)
    next(small)
    next(total)
    next(big)
    next(total)
    next(small)
    next(total)
    run(small)
    patch_sum = sum_ref[...]
    scale = lax.rsqrt(jnp.mean(patch_sum * patch_sum, axis=1, keepdims=True) + EPSILON)
    gain = gain_row(small_ref[:, TILE + 5, 0:128])
    norm_ref[spot.q] = (patch_sum * scale * gain).astype(low)
    plane = spread_plane(wires, spot, norm_ref)
    next(plane)
    next(plane)
    swap_proj.arrive()
    taps = tap_rows(spot, small_ref)
    run(plane)
    next(big)

    norm = norm_ref[...].reshape(2 * count, D)
    own_ref[...] = flat_dot(norm, proj_ref[...])
    maps_ref[...] = flat_dot(norm, small_ref[:, :TILE, 0:256].reshape(D, 256))
    step_ref[...] = flat_dot(norm, small_ref[:, :TILE, 256:384].reshape(D, 128))
    dt_row, rate_row, skip_row = heads_ref[0:1], heads_ref[1:2], heads_ref[2:3]
    got(head_w)
    gains = jnp.concatenate(
        [small_ref[spot.q + 8 * i, TILE : TILE + 16, 0:HEAD_M][6:7].astype(f32) for i in range(4)], axis=1
    )
    for x in range(2):
        at = pl.ds(x * count, count)
        slot = Slot(spot, small_ref, x, count)
        own, maps = own_ref[at], maps_ref[at]
        mix = Mixed(spot, slot, own, maps, step_ref[at], taps, dt_row, rate_row)
        outs = []
        for i in range(4):
            inputs = mix.inputs[:, i * HEAD_M : (i + 1) * HEAD_M]
            mixing = (mix.decay(i) * mix.inner * mix.row(mix.step_t, i)).astype(low)
            skip = pick_lane(skip_row, mix.head(i))
            outs.append(flat_dot(mixing, inputs.astype(low)) + skip * inputs)
        core = jnp.concatenate(outs, axis=1)
        core_ref[at] = core
        raw = own[:, :256]
        gated = core * raw * sigmoid(raw)
        part = flat_dot((gated * gains).astype(low), head_w_ref[...].reshape(256, D))
        squares = jnp.sum(gated * gated, axis=1, keepdims=True)
        parts8[pl.ds(x * 2, 2), :, :, pl.ds(0, D)] = part.astype(low).reshape(2, 2, TILE, D)
        parts8[pl.ds(x * 2, 2), :, :, pl.ds(D, 128)] = (
            jnp.broadcast_to(squares, (count, 128)).astype(low).reshape(2, 2, TILE, 128)
        )
    for total in sum_plane(wires, spot, parts8, pair8, near8):
        pass
    mixed_ref[...] = total
    for copy in own_rows:
        copy.wait()
    run(big)
    wires.drain()
    swap_bytes.leave()
    swap_proj.leave()


def forward_call(depth, n_dev, rows2, patch_proj, cols, vectors, out_proj, heads, qkv, attn, gate, up, down):
    f32, low = jnp.float32, jnp.bfloat16
    vmem = pl.BlockSpec(memory_space=pltpu.VMEM)
    anywhere = pl.BlockSpec(memory_space=pl.ANY)
    shape = jax.ShapeDtypeStruct
    plane_patches = 8 * TILE
    outs = [
        shape((D, WIDE), low),
        shape((down.shape[0] * n_dev, D), low),
        shape((TILE, D), f32),
        shape((TILE, EXT), f32),
        shape((n_dev, SMALL_ROWS, SMALL_COLS), low),
        shape((n_dev * TILE, 256), low),
        shape((8, TILE, D), low),
        shape((n_dev * TILE, 512), low),
        shape((depth, HEAD_M, D), low),
        shape((plane_patches, 512), f32),
        shape((plane_patches, 256), f32),
        shape((plane_patches, 128), f32),
        shape((plane_patches, 256), f32),
    ]
    scratch = [
        pltpu.VMEM((16, 2, TILE, D), low),
        pltpu.VMEM((16, TILE, D), low),
        pltpu.VMEM((3, depth, TILE, D), low),
        pltpu.VMEM((depth, TILE, D), low),
        pltpu.VMEM((depth - 1, TILE, D), low),
        pltpu.VMEM((4, 2, TILE, EXT), low),
        pltpu.VMEM((4, TILE, EXT), low),
        pltpu.VMEM((3, TILE, EXT), low),
        pltpu.SemaphoreType.DMA((N_WIRES,)),
        pltpu.SemaphoreType.DMA((N_WIRES,)),
        pltpu.SemaphoreType.DMA((2, n_dev)),
        pltpu.SemaphoreType.DMA((2, n_dev)),
        pltpu.SemaphoreType.DMA((5,)),
    ]
    return pl.pallas_call(
        partial(forward_kernel, depth),
        out_shape=outs,
        in_specs=[vmem] * 6 + [anywhere] * 5,
        out_specs=[anywhere] * 2 + [vmem] * 11,
        scratch_shapes=scratch,
        compiler_params=pltpu.CompilerParams(
            collective_id=0, has_side_effects=True, vmem_limit_bytes=56 * 2**20
        ),
        name="global_forward",
    )(rows2, patch_proj, cols, vectors, out_proj, heads, qkv, attn, gate, up, down)


AX = ("dp", "fsdp")
BC = 2 * STATE
OWN = 2 * HEAD_M + 1


class Grid:
    def __init__(self, dp, fsdp):
        self.depth, self.count = dp // 2, dp * fsdp
        dp_at, fs_at = lax.axis_index("dp"), lax.axis_index("fsdp")
        self.z, self.x, self.y, self.c = dp_at // 2, dp_at % 2, fs_at // 2, fs_at % 2
        self.at = {"z": self.z, "x": self.x, "y": self.y, "c": self.c}

    def route(self, dim, step=1):
        pairs = []
        for i in range(self.count):
            z, x, y, c = i // 8, i // 4 % 2, i // 2 % 2, i % 2
            if dim == "z":
                z = (z + step) % self.depth
            elif dim == "x":
                x = 1 - x
            elif dim == "y":
                y = 1 - y
            else:
                c = 1 - c
            pairs.append((i, z * 8 + x * 4 + y * 2 + c))
        return pairs

    def send(self, block, dim, step=1):
        return lax.ppermute(block, AX, self.route(dim, step))


def put(whole, part, place):
    return lax.dynamic_update_slice(whole, part, [jnp.asarray(p, jnp.int32) for p in place])


def gather_stream(grid, own, order):
    rows, n = own.shape
    pieces = [(own[None], {})]
    zs = 1
    for dim in order:
        if dim == "z":
            stacked = jnp.stack([p for p, _ in pieces], axis=0)
            blocks = [stacked]
            for _ in range(grid.depth - 1):
                blocks.append(grid.send(blocks[-1], "z"))
            whole = jnp.zeros((len(pieces), grid.depth, rows, n), own.dtype)
            for k, block in enumerate(blocks):
                whole = put(whole, block, (0, (grid.z - k) % grid.depth, 0, 0))
            pieces = [(whole[i], at) for i, (_, at) in enumerate(pieces)]
        else:
            pieces = pieces + [(grid.send(p, dim), {**at, dim: True}) for p, at in pieces]
    out = jnp.zeros((grid.depth, 2, 2, 2, rows, n), own.dtype)
    for piece, at in pieces:
        place = [1 - grid.at[d] if d in at else grid.at[d] for d in "xyc"]
        out = put(out, piece[:, None, None, None], (0, *place, 0, 0))
    return out.reshape(grid.count, rows, n)


def pick(part, where, axis):
    return lax.dynamic_index_in_dim(part, where, axis, keepdims=False)


def scatter_stream(grid, part, order):
    low = jnp.bfloat16
    dims = ["z", "x", "y"]
    for dim in order:
        axis = dims.index(dim)
        here = grid.at[dim]
        if dim == "z":
            total = None
            for k in range(1, grid.depth + 1):
                mine = pick(part, (here - k) % grid.depth, axis).astype(jnp.float32)
                total = mine if total is None else mine + total.astype(jnp.float32)
                if k < grid.depth:
                    total = grid.send(total.astype(low), "z")
            part = total
        else:
            arrived = grid.send(pick(part, 1 - here, axis).astype(low), dim)
            part = pick(part, here, axis).astype(jnp.float32) + arrived.astype(jnp.float32)
        dims.pop(axis)
    return part


def gather_small(grid, own):
    rows, n = own.shape
    column = jnp.zeros((grid.depth, rows, n), own.dtype)
    for k in range(grid.depth):
        block = own if k == 0 else grid.send(own, "z", k)
        column = put(column, block[None], ((grid.z - k) % grid.depth, 0, 0))
    half = n // 2
    plane = jnp.zeros((grid.depth, 2, 2, rows, n), own.dtype)
    for first, second, at in (("x", "y", 0), ("y", "x", half)):
        mine = column[:, :, at : at + half]
        both = jnp.stack([mine, grid.send(mine, first)])
        far = grid.send(both, second)
        for i in range(2):
            for j, block in enumerate((both[i], far[i])):
                place = {first: grid.at[first] ^ i, second: grid.at[second] ^ j}
                plane = put(plane, block[:, None, None], (0, place["x"], place["y"], 0, at))
    other = grid.send(plane, "c")
    pair = jnp.where(grid.c == 0, jnp.stack([plane, other], 3), jnp.stack([other, plane], 3))
    return pair.reshape(grid.count * rows, n)


def scatter_small(grid, part):
    low = jnp.bfloat16
    n = part.shape[1]
    part = part.reshape(grid.depth, 2, 2, 2, -1, n)
    arrived = grid.send(pick(part, 1 - grid.c, 3).astype(low), "c")
    part = pick(part, grid.c, 3) + arrived.astype(jnp.float32)
    half = n // 2
    sums = []
    for order, at in (("yx", 0), ("xy", half)):
        piece = part[..., at : at + half]
        dims = ["z", "x", "y"]
        for dim in order:
            axis = dims.index(dim)
            arrived = grid.send(pick(piece, 1 - grid.at[dim], axis).astype(low), dim)
            piece = pick(piece, grid.at[dim], axis) + arrived.astype(jnp.float32)
            dims.pop(axis)
        sums.append(piece)
    column = jnp.concatenate(sums, axis=-1)
    total = pick(column, grid.z, 0)
    for k in range(1, grid.depth):
        block = pick(column, (grid.z + k) % grid.depth, 0).astype(low)
        total = total + grid.send(block, "z", k).astype(jnp.float32)
    return total


def exchange(blocks):
    return lax.all_to_all(blocks, AX, 0, 0, tiled=False)


def causal_taps(channels, weight, bias, docs):
    slots, count = docs.shape
    padded = jnp.pad(channels, ((0, 0), (CONV - 1, 0), (0, 0)))
    padded_docs = jnp.pad(docs, ((0, 0), (CONV - 1, 0)), constant_values=-1)
    total = bias[None, None, :]
    for k in range(CONV):
        same = (padded_docs[:, k : k + count] == docs).astype(jnp.float32)
        total = total + padded[:, k : k + count] * weight[:, k][None, None, :] * same[:, :, None]
    return total


def head_core(channels, maps, step_raw, conv_w, conv_b, maps_w, maps_b, dt_bias, a_log, skip, docs):
    count = docs.shape[1]
    inputs = jax.nn.silu(causal_taps(channels, conv_w, conv_b, docs))
    both = jax.nn.silu(causal_taps(maps, maps_w, maps_b, docs))
    in_map, out_map = both[..., :STATE], both[..., STATE:]
    step_size = jax.nn.softplus(step_raw + dt_bias)
    lower = jnp.tril(jnp.ones((count, count), jnp.float32))
    cumulative = jnp.dot(step_size * -jnp.exp(a_log), lower.T, precision=HIGHEST)
    keep = (lower > 0)[None] & (docs[:, :, None] == docs[:, None, :])
    spread = cumulative[:, :, None] - cumulative[:, None, :]
    decay = jnp.where(keep, jnp.exp(jnp.where(keep, spread, 0.0)), 0.0)
    inner = jnp.einsum("gtn,gsn->gts", out_map, in_map, precision=HIGHEST)
    mixing = decay * inner * step_size[:, None, :]
    return jnp.einsum("gts,gsp->gtp", mixing, inputs, precision=HIGHEST) + skip * inputs


def split_heads(rows_by_cols):
    rows = rows_by_cols.shape[0]
    return rows_by_cols.reshape(rows // 128, 128, -1, HEAD).transpose(2, 0, 1, 3)


def join_heads(heads):
    return heads.transpose(1, 2, 0, 3).reshape(heads.shape[1] * heads.shape[2], -1)


def patch_mask():
    places = jnp.arange(128)
    return (places[:, None] >= places[None, :]) & (places[:, None] // PATCH == places[None, :] // PATCH)


def dot_f32(spec, a, b):
    return jnp.einsum(spec, a, b, preferred_element_type=jnp.float32)


def fast_body(
    depth_fsdp,
    byte_states,
    doc_lengths,
    out_grad,
    patch_proj,
    global_gain,
    in_proj,
    conv_weight,
    conv_bias,
    dt_bias,
    a_log,
    skip_weight,
    mixer_gain,
    out_proj,
    attn_gain,
    qkv_proj,
    attn_out,
    ffn_gain,
    gate_proj,
    up_proj,
    down_proj,
):
    f32, low = jnp.float32, jnp.bfloat16
    grid = Grid(*depth_fsdp)
    n_dev = grid.count
    me = lax.axis_index("dp") * depth_fsdp[1] + lax.axis_index("fsdp")
    rows = byte_states.shape[0]
    patches = rows // PATCH
    slots = depth_fsdp[0]
    slot_patches = patches * depth_fsdp[1]

    shard_rows = in_proj.shape[0]
    maps_and_steps = jnp.pad(in_proj[:, 2 * DI :], ((0, 0), (0, SMALL_COLS - BC - MHEADS)))
    lines = [conv_weight[:, k] for k in range(CONV)]
    lines += [conv_bias, global_gain, mixer_gain, attn_gain, ffn_gain, doc_lengths.reshape(-1).astype(low)]
    lines = jnp.stack([jnp.pad(line, (0, SMALL_COLS - line.shape[0])) for line in lines])
    vectors = jnp.concatenate(
        [maps_and_steps, lines, jnp.zeros((SMALL_ROWS - shard_rows - lines.shape[0], SMALL_COLS), low)]
    )
    by_place = lambda cols: cols.reshape(shard_rows, 4, 8, HEAD_M).transpose(2, 0, 1, 3).reshape(8, shard_rows, 256)
    cols = jnp.concatenate([by_place(in_proj[:, :DI]), by_place(in_proj[:, DI : 2 * DI])], axis=2)
    heads_in = jnp.pad(jnp.stack([dt_bias, -jnp.exp(a_log), skip_weight]), ((0, 5), (0, 128 - MHEADS)))
    rows2 = byte_states.reshape(patches, PATCH * D)
    (wide, deep, patch_sum, mixed, small, all_bytes, norm8, proj8, head_w, own8, maps8, step8, core8) = forward_call(
        grid.depth, n_dev, rows2, patch_proj, cols, vectors, out_proj, heads_in, qkv_proj, attn_out, gate_proj, up_proj, down_proj
    )
    lines = small[:, shard_rows : shard_rows + 10]
    gain_g, gain_a, gain_f = (lines[:, k, : D // n_dev].reshape(-1).astype(f32) for k in (5, 7, 8))
    gain_m = lines[:, 6, : DI // n_dev].reshape(-1).astype(f32)
    my_places = share_at = lax.axis_index("fsdp") * patches + jnp.arange(patches, dtype=jnp.int32)
    live = jnp.repeat((my_places < doc_lengths[0, 0] + doc_lengths[0, 1]).astype(f32), PATCH)[:, None]
    qk, vals, attn_o = wide[:, : 2 * D], wide[:, 2 * D : 3 * D], wide[:, 3 * D : 4 * D]
    gate_w, up_w = wide[:, 4 * D : 8 * D], wide[:, 8 * D :]
    down_a, down_b = deep[:, : D // 2], deep[:, D // 2 :]
    raw_mixed = mixed[:, :D]
    mixer_r = lax.rsqrt(mixed[:, D : D + 1] / DI + EPSILON)
    mixed_patch = patch_sum + raw_mixed * mixer_r

    conv_w = lines[:, :CONV, : CONV_CH // n_dev].transpose(0, 2, 1).reshape(CONV_CH, CONV).astype(f32)
    conv_b = lines[:, CONV, : CONV_CH // n_dev].reshape(-1).astype(f32)
    lengths = lines[:, 9, :2].reshape(slots, depth_fsdp[1], 2)[:, 0].astype(jnp.int32)
    places = jnp.arange(slot_patches, dtype=jnp.int32)[None, :]
    first_end = lengths[:, :1]
    docs = (places >= first_end).astype(jnp.int32) + (places >= first_end + lengths[:, 1:]).astype(jnp.int32)
    heads_of = lambda cols: cols.reshape(shard_rows, MHEADS, -1)
    own_cols = jnp.concatenate(
        [heads_of(in_proj[:, :DI]), heads_of(in_proj[:, DI : 2 * DI]), heads_of(in_proj[:, 2 * DI + BC :])],
        axis=2,
    ).transpose(1, 0, 2)
    own_proj = exchange(own_cols).reshape(D, OWN)
    maps_proj = small[:, :shard_rows, :BC].reshape(D, BC)
    global_low = rms_scale(patch_sum, gain_g).astype(low)
    global_all = gather_small(grid, global_low)
    own = product(global_all, own_proj)
    maps = product(global_all, maps_proj)
    by_slot = lambda cols: cols.reshape(slots, slot_patches, -1)
    gate_raw = own[:, :HEAD_M]
    mine = lambda vec, width: lax.dynamic_slice_in_dim(vec, me * width, width, 0)
    core_args = (
        by_slot(own[:, HEAD_M : 2 * HEAD_M]),
        by_slot(maps),
        by_slot(own[:, 2 * HEAD_M :])[..., 0],
        mine(conv_w, HEAD_M),
        mine(conv_b, HEAD_M),
        conv_w[DI:],
        conv_b[DI:],
        mine(dt_bias, 1),
        mine(a_log, 1),
        mine(skip_weight, 1),
    )
    core, core_back = jax.vjp(partial(head_core, docs=docs), *core_args)
    core = core.reshape(-1, HEAD_M)
    sig_m = jax.nn.sigmoid(gate_raw)
    gated = core * gate_raw * sig_m
    my_gain = mine(gain_m, HEAD_M)[None]

    streams = byte_states.astype(f32) + jnp.repeat(mixed_patch, PATCH, axis=0)
    normed = rms_scale(streams, gain_a).astype(low)
    queries, key_rows = jnp.split(product(normed, qk).astype(low), 2, axis=1)
    queries, key_rows = split_heads(queries), split_heads(key_rows)
    value_rows = split_heads(product(normed, vals).astype(low))
    scale = HEAD ** (-0.5)
    scores = dot_f32("hbid,hbjd->hbij", queries, key_rows) * scale
    attn_weights = jax.nn.softmax(jnp.where(patch_mask(), scores, -1e30), axis=-1)
    attn_low = attn_weights.astype(low)
    mixed_heads = join_heads(dot_f32("hbij,hbjd->hbid", attn_low, value_rows).astype(low))
    attended = streams + product(mixed_heads, attn_o)
    ffn_low = rms_scale(attended, gain_f).astype(low)
    gate = product(ffn_low, gate_w)
    upward = product(ffn_low, up_w)
    sigma = jax.nn.sigmoid(gate)
    hidden = (gate * sigma * upward).astype(low)
    ffn_out = jnp.concatenate([product(hidden, down_a), product(hidden, down_b)], axis=1)
    block_out = (live * (attended + ffn_out)).astype(low)

    def plane_of(act, which):
        cols = act.reshape(rows, n_dev // 2, 2, -1)
        return pick(cols, which, 2).reshape(rows, -1)

    def scattered(act, grad, order):
        there = weight_grad(plane_of(act, 1 - grid.c), grad).astype(low)
        arrived = grid.send(there, "c")
        part = (weight_grad(plane_of(act, grid.c), grad) + arrived.astype(f32)).astype(low)
        part = part.reshape(grid.depth, 2, 2, -1, grad.shape[1])
        return scatter_stream(grid, part, order)

    grad_block = live * out_grad.astype(f32)
    down_low = grad_block.astype(low)
    grad_down = jnp.concatenate(
        [scattered(hidden, down_low[:, : D // 2], "zyx"), scattered(hidden, down_low[:, D // 2 :], "zxy")],
        axis=1,
    )
    grad_hidden = input_grad(down_low[:, : D // 2], down_a) + input_grad(down_low[:, D // 2 :], down_b)
    grad_gate_low = (grad_hidden * upward * sigma * (1.0 + gate * (1.0 - sigma))).astype(low)
    grad_up_low = (grad_hidden * gate * sigma).astype(low)
    grad_gate = scattered(ffn_low, grad_gate_low, "yxz")
    grad_up = scattered(ffn_low, grad_up_low, "xyz")
    grad_ffn_in = input_grad(grad_gate_low, gate_w) + input_grad(grad_up_low, up_w)
    _, norm_back = jax.vjp(rms_scale, attended, gain_f)
    grad_attended_norm, grad_gain_f = norm_back(grad_ffn_in)
    grad_attended = grad_block + grad_attended_norm
    attn_grad_low = grad_attended.astype(low)
    grad_attn_out = scattered(mixed_heads, attn_grad_low, "xyz")
    grad_mixed = split_heads(input_grad(attn_grad_low, attn_o).astype(low))
    grad_values = dot_f32("hbij,hbid->hbjd", attn_low, grad_mixed)
    grad_weights = dot_f32("hbid,hbjd->hbij", grad_mixed, value_rows)
    grad_scores = attn_weights * (
        grad_weights - jnp.sum(attn_weights * grad_weights, axis=-1, keepdims=True)
    )
    scores_low = grad_scores.astype(low)
    grad_queries = dot_f32("hbij,hbjd->hbid", scores_low, key_rows) * scale
    grad_keys = dot_f32("hbij,hbid->hbjd", scores_low, queries) * scale
    grad_qk = jnp.concatenate([join_heads(grad_queries.astype(low)), join_heads(grad_keys.astype(low))], axis=1)
    grad_v = join_heads(grad_values.astype(low))
    grad_qkv = jnp.concatenate(
        [scattered(normed, grad_qk, "yxz"), scattered(normed, grad_v, "xyz")], axis=1
    )
    grad_normed = input_grad(grad_qk, qk) + input_grad(grad_v, vals)
    _, norm_back = jax.vjp(rms_scale, streams, gain_a)
    grad_streams_norm, grad_gain_a = norm_back(grad_normed)
    grad_streams = grad_attended + grad_streams_norm

    grad_patch_mix = grad_streams.reshape(patches, PATCH, D).sum(axis=1)
    mix_low = grad_patch_mix.astype(low)
    along = jnp.sum(mix_low.astype(f32) * raw_mixed, axis=1, keepdims=True)
    pair = jnp.concatenate([mixer_r, along], axis=1)
    pair_high = pair.astype(low)
    pair_rest = (pair - pair_high.astype(f32)).astype(low)
    extra = jnp.pad(jnp.concatenate([pair_high, pair_rest], axis=1), ((0, 0), (0, 124)))
    mix_all = gather_small(grid, jnp.concatenate([mix_low, extra], axis=1))
    extra = mix_all[:, D : D + 4].astype(f32)
    r_all, along_all = extra[:, 0:1] + extra[:, 2:3], extra[:, 1:2] + extra[:, 3:4]
    mix_all = mix_all[:, :D]
    grad_out_proj = weight_grad((gated * r_all * my_gain).astype(low), mix_all)
    back_m = input_grad(mix_all, out_proj)
    grad_gain_m = jnp.sum(back_m * gated * r_all, axis=0)
    grad_gated = r_all * my_gain * back_m - gated * (r_all * r_all * r_all * along_all / DI)
    grad_core = grad_gated * gate_raw * sig_m
    grad_gate_raw = grad_gated * core * sig_m * (1.0 + gate_raw * (1.0 - sig_m))
    (d_chan, d_maps, d_step, d_cw, d_cb, d_mw, d_mb, d_dt, d_alog, d_skip) = core_back(by_slot(grad_core))
    d_own = jnp.concatenate(
        [grad_gate_raw, d_chan.reshape(-1, HEAD_M), d_step.reshape(-1, 1)], axis=1
    ).astype(low)
    d_maps = d_maps.reshape(-1, BC).astype(low)
    grad_norm = scatter_small(grid, input_grad(d_own, own_proj) + input_grad(d_maps, maps_proj))
    grad_own_cols = weight_grad(global_all, d_own)
    grad_maps_cols = weight_grad(global_all, d_maps)
    _, norm_back = jax.vjp(rms_scale, patch_sum, gain_g)
    grad_sum_norm, grad_gain_g = norm_back(grad_norm)
    sum_low = (grad_patch_mix + grad_sum_norm).astype(low)
    sum_all = gather_small(grid, sum_low)
    grad_patch_proj = weight_grad(all_bytes, sum_all)
    back_bytes = input_grad(sum_all, patch_proj).astype(low).reshape(n_dev, patches, -1)
    back_bytes = exchange(back_bytes).transpose(1, 0, 2).reshape(rows, D)
    grad_states = grad_streams + back_bytes.astype(f32)

    taps = jnp.zeros((CONV_CH, CONV + 1), f32)
    taps = put(taps, jnp.concatenate([d_cw, d_cb[:, None]], axis=1), (me * HEAD_M, 0))
    taps = put(taps, jnp.concatenate([d_mw, d_mb[:, None]], axis=1), (DI, 0))
    sums = [taps.reshape(n_dev, -1)]
    sums += [g.reshape(n_dev, -1) for g in (grad_gain_g, grad_gain_a, grad_gain_f)]
    heads = jnp.zeros((3, MHEADS), f32)
    heads = put(heads, jnp.stack([d_dt, d_alog, d_skip]), (0, me)).reshape(1, -1)
    sums += [jnp.broadcast_to(heads, (n_dev, 3 * MHEADS))]
    sums = jnp.concatenate(sums, axis=1)
    width = sums.shape[1]
    extra_cols = -(-width // shard_rows)
    sums = jnp.pad(sums, ((0, 0), (0, extra_cols * shard_rows - width))).reshape(n_dev, shard_rows, extra_cols)
    parcel = jnp.concatenate(
        [
            grad_own_cols.reshape(n_dev, shard_rows, OWN),
            grad_maps_cols.reshape(n_dev, shard_rows, BC),
            sums,
        ],
        axis=2,
    ).astype(low)
    parcel = exchange(parcel).astype(f32)
    side = lambda a, b: parcel[:, :, a:b].transpose(1, 0, 2).reshape(shard_rows, -1)
    summed = jnp.sum(parcel[:, :, OWN:], axis=0)
    grad_in_proj = jnp.concatenate(
        [side(0, HEAD_M), side(HEAD_M, 2 * HEAD_M), summed[:, :BC], side(2 * HEAD_M, OWN)], axis=1
    )
    flat = summed[:, BC:].reshape(-1)
    taps = flat[: CONV_CH * (CONV + 1) // n_dev].reshape(-1, CONV + 1)
    at = CONV_CH * (CONV + 1) // n_dev
    grad_gain_g, grad_gain_a, grad_gain_f = (flat[at + i * D // n_dev : at + (i + 1) * D // n_dev] for i in range(3))
    at += 3 * D // n_dev
    heads = flat[at : at + 3 * MHEADS].reshape(3, MHEADS)
    return (
        block_out,
        grad_states,
        grad_patch_proj,
        grad_gain_g,
        grad_in_proj,
        taps[:, :CONV],
        taps[:, CONV],
        heads[0],
        heads[1],
        heads[2],
        grad_gain_m,
        grad_out_proj,
        grad_gain_a,
        grad_qkv,
        grad_attn_out,
        grad_gain_f,
        grad_gate,
        grad_up,
        grad_down,
    )


def solution(mesh):
    in_specs = (
        P(("dp", "fsdp"), None),
        P("dp", None),
        P(("dp", "fsdp"), None),
        P(("dp", "fsdp"), None),
        P(("dp", "fsdp")),
        P(("dp", "fsdp"), None),
        P(("dp", "fsdp"), None),
        P(("dp", "fsdp")),
        P(),
        P(),
        P(),
        P(("dp", "fsdp")),
        P(("dp", "fsdp"), None),
        P(("dp", "fsdp")),
        P(("dp", "fsdp"), None),
        P(("dp", "fsdp"), None),
        P(("dp", "fsdp")),
        P(("dp", "fsdp"), None),
        P(("dp", "fsdp"), None),
        P(("dp", "fsdp"), None),
    )
    out_specs = (
        P(("dp", "fsdp"), None),
        P(("dp", "fsdp"), None),
        P(("dp", "fsdp"), None),
        P(("dp", "fsdp")),
        P(("dp", "fsdp"), None),
        P(("dp", "fsdp"), None),
        P(("dp", "fsdp")),
        P(),
        P(),
        P(),
        P(("dp", "fsdp")),
        P(("dp", "fsdp"), None),
        P(("dp", "fsdp")),
        P(("dp", "fsdp"), None),
        P(("dp", "fsdp"), None),
        P(("dp", "fsdp")),
        P(("dp", "fsdp"), None),
        P(("dp", "fsdp"), None),
        P(("dp", "fsdp"), None),
    )
    dp, fsdp = mesh.shape["dp"], mesh.shape["fsdp"]
    fast = dp * fsdp == MHEADS and fsdp == 4
    chosen = partial(fast_body, (dp, fsdp)) if fast else body
    return jax.shard_map(chosen, mesh=mesh, in_specs=in_specs, out_specs=out_specs, check_vma=False)
```

```python
from functools import partial

import jax
import jax.numpy as jnp
from jax import lax
from jax.experimental import pallas as pl
from jax.experimental.pallas import tpu as pltpu
from jax.sharding import PartitionSpec as P

D = 1024
HEAD = 64
HEAD_M = 64
STATE = 128
CONV = 4
PATCH = 8
DI = 2048
MHEADS = 32
CONV_CH = 2304


EPSILON = 1e-05
HIGHEST = lax.Precision.HIGHEST


def shifted(block, axis, distance):
    devices = range(lax.axis_size(axis))
    route = [(i - distance, i) for i in devices if i - distance in devices]
    return lax.ppermute(block, axis, route)


def prefix(value, axis, combine, identity):
    devices, place = (lax.axis_size(axis), lax.axis_index(axis))
    everything = jax.tree.map(
        lambda part, kind: lax.all_gather(part.astype(kind), axis),
        value,
        (jnp.bfloat16, jnp.bfloat16),
    )
    start = jax.tree.map(
        lambda part, zero: jnp.broadcast_to(jnp.asarray(zero, part.dtype), part.shape),
        value,
        identity,
    )

    def prefix_step(k, before):
        reached = k < place
        new = combine(
            before, jax.tree.map(lambda part, own: part[k].astype(own.dtype), everything, value)
        )
        return jax.tree.map(lambda a, b: jnp.where(reached, a, b), new, before)

    return lax.fori_loop(0, devices, prefix_step, start)


def carried_in(value, axis, combine, identity):
    devices, place = (lax.axis_size(axis), lax.axis_index(axis))
    everything = jax.tree.map(
        lambda part, kind: lax.all_gather(part.astype(kind), axis),
        value,
        jax.tree.map(lambda a: jnp.bfloat16 if a.dtype == jnp.float32 else a.dtype, value),
    )
    start = jax.tree.map(
        lambda part, zero: jnp.broadcast_to(jnp.asarray(zero, part.dtype), part.shape),
        value,
        identity,
    )

    def carried_step(k, before):
        at = devices - 1 - k
        reached = at > place
        new = combine(
            before, jax.tree.map(lambda part, own: part[at].astype(own.dtype), everything, value)
        )
        return jax.tree.map(lambda a, b: jnp.where(reached, a, b), new, before)

    return lax.fori_loop(0, devices, carried_step, start)


def product(left, right):
    return jnp.dot(left, right, preferred_element_type=jnp.float32)


def weight_grad(left, right):
    return lax.dot_general(
        left, right, (((0,), (0,)), ((), ())), preferred_element_type=jnp.float32
    )


def input_grad(grad_rows, weight):
    return lax.dot_general(
        grad_rows, weight, (((1,), (1,)), ((), ())), preferred_element_type=jnp.float32
    )


def rms_scale(value, gain):
    return value * lax.rsqrt(jnp.mean(value * value, axis=-1, keepdims=True) + EPSILON) * gain


def gated_norm(core_out, gate_raw, gain):
    count = core_out.shape[0]
    return rms_scale(core_out.reshape(count, DI) * jax.nn.silu(gate_raw), gain)


def patch_docs(doc_lengths, start, count):
    places = start + jnp.arange(count, dtype=jnp.int32)
    first_end = doc_lengths[0, 0]
    second_end = first_end + doc_lengths[0, 1]
    numbers = (places >= first_end).astype(jnp.int32) + (places >= second_end).astype(jnp.int32)
    return jnp.where(places >= 0, numbers, -1)


def chain(earlier, later):
    return (earlier[0] * later[0], later[1] + later[0][:, None, None] * earlier[1])


def mixer_core(
    channels,
    rim,
    step_raw,
    state_in,
    conv_weight,
    conv_bias,
    dt_bias,
    a_log,
    skip_weight,
    docs,
    rim_docs,
    prev_doc,
):
    count = channels.shape[0]
    padded = jnp.concatenate([rim, channels], axis=0)
    padded_docs = jnp.concatenate([rim_docs, docs])
    total = conv_bias[None, :]
    for shift_k in range(CONV):
        same_doc = (padded_docs[shift_k : shift_k + count] == docs).astype(jnp.float32)
        total = (
            total
            + padded[shift_k : shift_k + count]
            * conv_weight[:, shift_k][None, :]
            * same_doc[:, None]
        )
    activated = jax.nn.silu(total)
    inputs = activated[:, :DI].reshape(count, MHEADS, HEAD_M)
    in_map = activated[:, DI : DI + STATE]
    out_map = activated[:, DI + STATE :]
    step_size = jax.nn.softplus(step_raw + dt_bias[None, :])
    rate = -jnp.exp(a_log)
    lower = jnp.tril(jnp.ones((count, count), jnp.float32))
    cumulative = jnp.dot(lower, step_size * rate[None, :], precision=HIGHEST)
    places = jnp.arange(count, dtype=jnp.int32)
    keep = ((places[:, None] >= places[None, :]) & (docs[:, None] == docs[None, :]))[:, :, None]
    spread = cumulative[:, None, :] - cumulative[None, :, :]
    decay_table = jnp.where(keep, jnp.exp(jnp.where(keep, spread, 0.0)), 0.0)
    inner = jnp.dot(out_map, in_map.T, precision=HIGHEST, preferred_element_type=jnp.float32)
    mixing = decay_table * inner[:, :, None] * step_size[None, :, :]
    outputs = jnp.einsum("tsh,shp->thp", mixing, inputs, precision=HIGHEST)
    carry_in = jnp.where((docs == prev_doc)[:, None], jnp.exp(cumulative), 0.0)
    outputs = outputs + carry_in[:, :, None] * jnp.einsum(
        "tn,hpn->thp", out_map, state_in, precision=HIGHEST
    )
    outputs = outputs + skip_weight[None, :, None] * inputs
    last_doc = docs[count - 1]
    tail_keep = (docs == last_doc)[:, None]
    tail_gap = cumulative[count - 1][None, :] - cumulative
    tail_weight = (
        jnp.where(tail_keep, jnp.exp(jnp.where(tail_keep, tail_gap, 0.0)), 0.0) * step_size
    )
    decay_total = jnp.where(prev_doc == last_doc, jnp.exp(cumulative[count - 1]), 0.0)
    state_out = jnp.einsum("sh,shp,sn->hpn", tail_weight, inputs, in_map, precision=HIGHEST)
    state_out = state_out + decay_total[:, None, None] * state_in
    return ((outputs, state_out), (decay_total, carry_in, out_map))


def attend(qkv_low, patches):
    heads = qkv_low.reshape(patches, PATCH, 3, -1, HEAD)
    queries = heads[:, :, 0]
    key_rows = heads[:, :, 1]
    value_rows = heads[:, :, 2]
    scores = jnp.einsum(
        "pihd,pjhd->phij", queries, key_rows, preferred_element_type=jnp.float32
    ) * HEAD ** (-0.5)
    places = jnp.arange(PATCH)
    causal = places[:, None] >= places[None, :]
    scores = jnp.where(causal, scores, -1e30)
    attn_weights = jax.nn.softmax(scores, axis=-1)
    attn_low = attn_weights.astype(jnp.bfloat16)
    mixed = jnp.einsum("phij,pjhd->pihd", attn_low, value_rows, preferred_element_type=jnp.float32)
    mixed = mixed.astype(jnp.bfloat16).reshape(patches * PATCH, -1)
    return ((queries, key_rows, value_rows, attn_weights, attn_low), mixed)


def attend_back(grad_mixed_low, pieces):
    queries, key_rows, value_rows, attn_weights, attn_low = pieces
    patches = queries.shape[0]
    grad_mixed = grad_mixed_low.reshape(patches, PATCH, -1, HEAD)
    grad_values = jnp.einsum(
        "phij,pihd->pjhd", attn_low, grad_mixed, preferred_element_type=jnp.float32
    )
    grad_weights = jnp.einsum(
        "pihd,pjhd->phij", grad_mixed, value_rows, preferred_element_type=jnp.float32
    )
    grad_scores = attn_weights * (
        grad_weights - jnp.sum(attn_weights * grad_weights, axis=-1, keepdims=True)
    )
    scores_low = grad_scores.astype(jnp.bfloat16)
    scale = HEAD ** (-0.5)
    grad_queries = (
        jnp.einsum("phij,pjhd->pihd", scores_low, key_rows, preferred_element_type=jnp.float32)
        * scale
    )
    grad_keys = (
        jnp.einsum("phij,pihd->pjhd", scores_low, queries, preferred_element_type=jnp.float32)
        * scale
    )
    stacked = jnp.stack([grad_queries, grad_keys, grad_values], axis=2).reshape(patches * PATCH, -1)
    return stacked.astype(jnp.bfloat16)


def local_forward(byte_states, mixed_patch, local_set, live):
    attn_gain, qkv_proj, attn_out, ffn_gain, gate_proj, up_proj, down_proj = local_set
    rows = byte_states.shape[0]
    streams = byte_states.astype(jnp.float32) + jnp.repeat(mixed_patch, PATCH, axis=0)
    normed_low = rms_scale(streams, attn_gain.astype(jnp.float32)).astype(jnp.bfloat16)
    qkv_low = product(normed_low, qkv_proj).astype(jnp.bfloat16)
    pieces, mixed_heads = attend(qkv_low, rows // PATCH)
    attended = streams + product(mixed_heads, attn_out)
    ffn_low = rms_scale(attended, ffn_gain.astype(jnp.float32)).astype(jnp.bfloat16)
    gate = product(ffn_low, gate_proj)
    upward = product(ffn_low, up_proj)
    hidden_low = (jax.nn.silu(gate) * upward).astype(jnp.bfloat16)
    block = live * (attended + product(hidden_low, down_proj))
    cache = (streams, normed_low, pieces, mixed_heads, attended, ffn_low, gate, upward, hidden_low)
    return (block, cache)


def local_backward(grad_block, cache, local_set):
    attn_gain, qkv_proj, attn_out, ffn_gain, gate_proj, up_proj, down_proj = local_set
    streams, normed_low, pieces, mixed_heads, attended, ffn_low, gate, upward, hidden_low = cache
    down_low = grad_block.astype(jnp.bfloat16)
    grad_down = weight_grad(hidden_low, down_low)
    grad_hidden = input_grad(down_low, down_proj)
    sigma = jax.nn.sigmoid(gate)
    grad_gate_low = (grad_hidden * upward * sigma * (1.0 + gate * (1.0 - sigma))).astype(
        jnp.bfloat16
    )
    grad_up_low = (grad_hidden * gate * sigma).astype(jnp.bfloat16)
    grad_gate = weight_grad(ffn_low, grad_gate_low)
    grad_up = weight_grad(ffn_low, grad_up_low)
    grad_ffn_in = input_grad(grad_gate_low, gate_proj) + input_grad(grad_up_low, up_proj)
    _, norm_back = jax.vjp(rms_scale, attended, ffn_gain.astype(jnp.float32))
    grad_attended_norm, grad_ffn_gain = norm_back(grad_ffn_in)
    grad_attended = grad_block + grad_attended_norm
    attn_grad_low = grad_attended.astype(jnp.bfloat16)
    grad_attn_out = weight_grad(mixed_heads, attn_grad_low)
    grad_mixed_low = input_grad(attn_grad_low, attn_out).astype(jnp.bfloat16)
    grad_qkv_low = attend_back(grad_mixed_low, pieces)
    grad_qkv = weight_grad(normed_low, grad_qkv_low)
    grad_normed = input_grad(grad_qkv_low, qkv_proj)
    _, norm_back = jax.vjp(rms_scale, streams, attn_gain.astype(jnp.float32))
    grad_streams_norm, grad_attn_gain = norm_back(grad_normed)
    grad_streams = grad_attended + grad_streams_norm
    return (
        grad_streams,
        (grad_qkv, grad_attn_out, grad_gate, grad_up, grad_down, grad_attn_gain, grad_ffn_gain),
    )


def body(
    byte_states,
    doc_lengths,
    out_grad,
    patch_proj,
    global_gain,
    in_proj,
    conv_weight,
    conv_bias,
    dt_bias,
    a_log,
    skip_weight,
    mixer_gain,
    out_proj,
    attn_gain,
    qkv_proj,
    attn_out,
    ffn_gain,
    gate_proj,
    up_proj,
    down_proj,
):
    rows = byte_states.shape[0]
    patches = rows // PATCH
    share = lax.axis_index("fsdp")
    start = share * patches
    docs = patch_docs(doc_lengths, start, patches)
    rim_docs = patch_docs(doc_lengths, start - (CONV - 1), CONV - 1)
    prev_doc = patch_docs(doc_lengths, start - 1, 1)[0]
    live = jnp.repeat((docs < 2).astype(jnp.float32), PATCH)[:, None]
    all_set = (
        lax.all_gather(patch_proj, ("dp", "fsdp"), axis=0, tiled=True),
        lax.all_gather(global_gain, ("dp", "fsdp"), axis=0, tiled=True),
        lax.all_gather(in_proj, ("dp", "fsdp"), axis=0, tiled=True),
        lax.all_gather(conv_weight, ("dp", "fsdp"), axis=0, tiled=True),
        lax.all_gather(conv_bias, ("dp", "fsdp"), axis=0, tiled=True),
        lax.all_gather(mixer_gain, ("dp", "fsdp"), axis=0, tiled=True),
        lax.all_gather(out_proj, ("dp", "fsdp"), axis=0, tiled=True),
        lax.all_gather(attn_gain, ("dp", "fsdp"), axis=0, tiled=True),
        lax.all_gather(qkv_proj, ("dp", "fsdp"), axis=0, tiled=True),
        lax.all_gather(attn_out, ("dp", "fsdp"), axis=0, tiled=True),
        lax.all_gather(ffn_gain, ("dp", "fsdp"), axis=0, tiled=True),
        lax.all_gather(gate_proj, ("dp", "fsdp"), axis=0, tiled=True),
        lax.all_gather(up_proj, ("dp", "fsdp"), axis=0, tiled=True),
        lax.all_gather(down_proj, ("dp", "fsdp"), axis=0, tiled=True),
    )
    global_set = all_set[:7]
    local_set = all_set[7:]
    patch_full, gain_g_full, in_full, conv_w_full, conv_b_full, gain_m_full, out_full = global_set
    patch_rows = byte_states.reshape(patches, PATCH * D)
    patch_sum = product(patch_rows, patch_full)
    gain_g = gain_g_full.astype(jnp.float32)
    global_low = rms_scale(patch_sum, gain_g).astype(jnp.bfloat16)
    projected = product(global_low, in_full)
    gate_raw = projected[:, :DI]
    channels = projected[:, DI : DI + CONV_CH]
    step_raw = projected[:, DI + CONV_CH :]
    rim = shifted(channels[patches - (CONV - 1) :], "fsdp", 1)
    core = partial(mixer_core, docs=docs, rim_docs=rim_docs, prev_doc=prev_doc)
    conv_w = conv_w_full.astype(jnp.float32)
    conv_b = conv_b_full.astype(jnp.float32)
    empty_state = jnp.zeros((MHEADS, HEAD_M, STATE), jnp.float32)
    (partial_out, local_state), aux = core(
        channels, rim, step_raw, empty_state, conv_w, conv_b, dt_bias, a_log, skip_weight
    )
    decay_total, carry_in, out_map = aux
    identity = (jnp.ones((MHEADS,), jnp.float32), jnp.zeros((MHEADS, HEAD_M, STATE), jnp.float32))
    arrived = prefix((decay_total, local_state), "fsdp", chain, identity)
    state_in = arrived[1]
    mixer_out = partial_out + carry_in[:, :, None] * jnp.einsum(
        "tn,hpn->thp", out_map, state_in, precision=HIGHEST
    )
    gain_m = gain_m_full.astype(jnp.float32)
    mixer_low = gated_norm(mixer_out, gate_raw, gain_m).astype(jnp.bfloat16)
    mixed_patch = patch_sum + product(mixer_low, out_full)
    block, cache = local_forward(byte_states, mixed_patch, local_set, live)
    block_out = block.astype(jnp.bfloat16)
    back_set = (
        lax.all_gather(patch_proj, ("dp", "fsdp"), axis=0, tiled=True),
        lax.all_gather(global_gain, ("dp", "fsdp"), axis=0, tiled=True),
        lax.all_gather(in_proj, ("dp", "fsdp"), axis=0, tiled=True),
        lax.all_gather(conv_weight, ("dp", "fsdp"), axis=0, tiled=True),
        lax.all_gather(conv_bias, ("dp", "fsdp"), axis=0, tiled=True),
        lax.all_gather(mixer_gain, ("dp", "fsdp"), axis=0, tiled=True),
        lax.all_gather(out_proj, ("dp", "fsdp"), axis=0, tiled=True),
        lax.all_gather(attn_gain, ("dp", "fsdp"), axis=0, tiled=True),
        lax.all_gather(qkv_proj, ("dp", "fsdp"), axis=0, tiled=True),
        lax.all_gather(attn_out, ("dp", "fsdp"), axis=0, tiled=True),
        lax.all_gather(ffn_gain, ("dp", "fsdp"), axis=0, tiled=True),
        lax.all_gather(gate_proj, ("dp", "fsdp"), axis=0, tiled=True),
        lax.all_gather(up_proj, ("dp", "fsdp"), axis=0, tiled=True),
        lax.all_gather(down_proj, ("dp", "fsdp"), axis=0, tiled=True),
    )
    global_back = back_set[:7]
    local_back = back_set[7:]
    _, cache = local_forward(byte_states, mixed_patch, local_back, live)
    patch_back, _, in_back, conv_w_back, conv_b_back, _, out_back = global_back
    grad_block = live * out_grad.astype(jnp.float32)
    grad_streams, local_grads = local_backward(grad_block, cache, local_back)
    reduced_local = (
        lax.psum_scatter(local_grads[0], ("dp", "fsdp"), scatter_dimension=0, tiled=True),
        lax.psum_scatter(local_grads[1], ("dp", "fsdp"), scatter_dimension=0, tiled=True),
        lax.psum_scatter(local_grads[2], ("dp", "fsdp"), scatter_dimension=0, tiled=True),
        lax.psum_scatter(local_grads[3], ("dp", "fsdp"), scatter_dimension=0, tiled=True),
        lax.psum_scatter(local_grads[4], ("dp", "fsdp"), scatter_dimension=0, tiled=True),
        lax.psum_scatter(local_grads[5], ("dp", "fsdp"), scatter_dimension=0, tiled=True),
        lax.psum_scatter(local_grads[6], ("dp", "fsdp"), scatter_dimension=0, tiled=True),
    )
    grad_patch_mix = grad_streams.reshape(patches, PATCH, D).sum(axis=1)
    mix_low = grad_patch_mix.astype(jnp.bfloat16)
    grad_out_proj = weight_grad(mixer_low, mix_low)
    grad_mixer_low = input_grad(mix_low, out_back)
    _, norm_back = jax.vjp(gated_norm, mixer_out, gate_raw, gain_m)
    grad_core, grad_gate_raw, grad_mixer_gain = norm_back(grad_mixer_low)
    state_part = jnp.einsum("th,thp,tn->hpn", carry_in, grad_core, out_map, precision=HIGHEST)
    returned = carried_in((decay_total, state_part), "fsdp", chain, identity)
    _, core_back, _ = jax.vjp(
        core,
        channels,
        rim,
        step_raw,
        state_in,
        conv_w_back.astype(jnp.float32),
        conv_b_back.astype(jnp.float32),
        dt_bias,
        a_log,
        skip_weight,
        has_aux=True,
    )
    core_grads = core_back((grad_core, returned[1]))
    (
        grad_channels,
        grad_rim,
        grad_step,
        _,
        grad_conv_w,
        grad_conv_b,
        grad_dt_bias,
        grad_a_log,
        grad_skip,
    ) = core_grads
    rim_grad = shifted(grad_rim, "fsdp", -1)
    cut = patches - (CONV - 1)
    grad_channels = jnp.concatenate([grad_channels[:cut], grad_channels[cut:] + rim_grad], axis=0)
    proj_low = jnp.concatenate([grad_gate_raw, grad_channels, grad_step], axis=1).astype(
        jnp.bfloat16
    )
    grad_in_proj = weight_grad(global_low, proj_low)
    grad_global_norm = input_grad(proj_low, in_back)
    _, norm_back = jax.vjp(rms_scale, patch_sum, gain_g)
    grad_sum_norm, grad_global_gain = norm_back(grad_global_norm)
    sum_low = (grad_patch_mix + grad_sum_norm).astype(jnp.bfloat16)
    grad_patch_proj = weight_grad(patch_rows, sum_low)
    grad_states = grad_streams + input_grad(sum_low, patch_back).reshape(rows, D)
    reduced_global = (
        lax.psum_scatter(grad_patch_proj, ("dp", "fsdp"), scatter_dimension=0, tiled=True),
        lax.psum_scatter(grad_global_gain, ("dp", "fsdp"), scatter_dimension=0, tiled=True),
        lax.psum_scatter(grad_in_proj, ("dp", "fsdp"), scatter_dimension=0, tiled=True),
        lax.psum_scatter(grad_conv_w, ("dp", "fsdp"), scatter_dimension=0, tiled=True),
        lax.psum_scatter(grad_conv_b, ("dp", "fsdp"), scatter_dimension=0, tiled=True),
        lax.psum_scatter(grad_mixer_gain, ("dp", "fsdp"), scatter_dimension=0, tiled=True),
        lax.psum_scatter(grad_out_proj, ("dp", "fsdp"), scatter_dimension=0, tiled=True),
    )
    head_sums = lax.psum((grad_dt_bias, grad_a_log, grad_skip), ("dp", "fsdp"))
    return (
        block_out,
        grad_states,
        reduced_global[0],
        reduced_global[1],
        reduced_global[2],
        reduced_global[3],
        reduced_global[4],
        head_sums[0],
        head_sums[1],
        head_sums[2],
        reduced_global[5],
        reduced_global[6],
        reduced_local[5],
        reduced_local[0],
        reduced_local[1],
        reduced_local[6],
        reduced_local[2],
        reduced_local[3],
        reduced_local[4],
    )


MESH = pl.DeviceIdType.MESH
WIDE = 12288
TILE = 32
SMALL_ROWS, SMALL_COLS = 48, 384
EXT = D + 128


def device(z, x, y, c):
    return (z * 2 + x, y * 2 + c)


class Spot:
    def __init__(self, depth):
        dp, fs = lax.axis_index("dp"), lax.axis_index("fsdp")
        self.depth, self.count = depth, depth * 8
        self.me = dp * 4 + fs
        self.z, self.x, self.y, self.c = dp // 2, dp % 2, fs // 2, fs % 2
        self.q = self.x * 4 + self.y * 2 + self.c
        self.plane = self.x * 2 + self.y
        self.column = [(self.z + depth - j) % depth for j in range(depth)]

    def flip(self, way):
        x = 1 - self.x if way & 2 else self.x
        y = 1 - self.y if way & 1 else self.y
        return device(self.z, x, y, self.c), x * 2 + y

    def sibling(self):
        return device(self.z, self.x, self.y, 1 - self.c)

    def above(self, k):
        return device((self.z + k) % self.depth, self.x, self.y, self.c)


def greet(spot):
    barrier = pltpu.get_barrier_semaphore()

    def one(i, carry):
        to = (spot.me + i) % spot.count
        pl.semaphore_signal(barrier, inc=1, device_id=(to // 4, to % 4), device_id_type=MESH)
        return carry

    lax.fori_loop(1, spot.count, one, 0)
    pl.semaphore_wait(barrier, spot.count - 1)


class Wires:
    def __init__(self, send, recv):
        self.send, self.recv, self.used, self.open = send, recv, 0, []

    def copy(self, src, dst, to):
        i = self.used
        self.used += 1
        copy = pltpu.make_async_remote_copy(
            src_ref=src,
            dst_ref=dst,
            send_sem=self.send.at[i],
            recv_sem=self.recv.at[i],
            device_id=to,
            device_id_type=MESH,
        )
        copy.start()
        self.open.append(copy)
        return copy

    def drain(self):
        for copy in self.open:
            copy.wait_send()


def got(copies):
    for copy in copies:
        copy.wait_recv()


class Swap:
    def __init__(self, spot, send, recv, src_at, dst_at):
        self.spot, self.send, self.recv, self.src_at, self.dst_at = spot, send, recv, src_at, dst_at

    def copy(self, i):
        to = (self.spot.me + i) % self.spot.count
        return pltpu.make_async_remote_copy(
            src_ref=self.src_at(to),
            dst_ref=self.dst_at(self.spot.me),
            send_sem=self.send.at[i],
            recv_sem=self.recv.at[i],
            device_id=(to // 4, to % 4),
            device_id_type=MESH,
        )

    def each(self, act):
        def one(i, carry):
            act(self.copy(i))
            return carry

        lax.fori_loop(1, self.spot.count, one, 0)

    def start(self):
        self.each(lambda copy: copy.start())

    def arrive(self):
        self.each(lambda copy: copy.wait_recv())

    def leave(self):
        self.each(lambda copy: copy.wait_send())


def block_row(t, plane, c):
    return (t * 4 + plane) * 2 + c


def spread_all(wires, spot, buf, own=None):
    at = lambda t, plane, c: buf.at[block_row(t, plane, c)]
    mine = at(spot.z, spot.plane, spot.c)
    src = mine if own is None else own
    ring, flat, core = [], [], []
    for k in range(1, spot.depth):
        ring.append(wires.copy(src, mine, spot.above(k)))
    flat.append([wires.copy(src, mine, spot.flip(way)[0]) for way in (1, 2, 3)])
    core.append(wires.copy(src, mine, spot.sibling()))
    yield
    for j in range(1, spot.depth):
        got([ring[j - 1]])
        block = at(spot.column[j], spot.plane, spot.c)
        flat.append([wires.copy(block, block, spot.flip(way)[0]) for way in (1, 2, 3)])
        core.append(wires.copy(block, block, spot.sibling()))
    yield
    for j in range(spot.depth):
        for way in (1, 2, 3):
            got([flat[j][way - 1]])
            block = at(spot.column[j], spot.flip(way)[1], spot.c)
            core.append(wires.copy(block, block, spot.sibling()))
    yield
    got(core)


def spread_plane(wires, spot, buf):
    at = lambda plane: buf.at[plane * 2 + spot.c]
    mine = at(spot.plane)
    flat = [wires.copy(mine, mine, spot.flip(way)[0]) for way in (1, 2, 3)]
    core = [wires.copy(mine, mine, spot.sibling())]
    yield
    for way in (1, 2, 3):
        got([flat[way - 1]])
        block = at(spot.flip(way)[1])
        core.append(wires.copy(block, block, spot.sibling()))
    yield
    got(core)


def sum_plane(wires, spot, parts, pair, near):
    first = wires.copy(parts.at[:, 1 - spot.c], pair, spot.sibling())
    yield None
    got([first])
    f32 = jnp.float32
    pair[...] = (parts[:, spot.c].astype(f32) + pair[...].astype(f32)).astype(jnp.bfloat16)
    flat = [
        wires.copy(pair.at[spot.flip(way)[1]], near.at[way - 1], spot.flip(way)[0]) for way in (1, 2, 3)
    ]
    yield None
    got(flat)
    total = pair[spot.plane].astype(f32)
    for way in range(3):
        total = total + near[way].astype(f32)
    yield total


def sum_all(wires, spot, parts, pair, near, column, far, out):
    f32, low = jnp.float32, jnp.bfloat16
    half = parts.shape[-1] // 2
    cut = [pl.ds(h * half, half) for h in range(2)]
    first = [
        wires.copy(parts.at[:, 1 - spot.c, :, cut[h]], pair.at[:, :, cut[h]], spot.sibling()) for h in range(2)
    ]
    yield
    flat, ring = [], []
    rows = pair.shape[1]
    for h in range(2):
        got([first[h]])
        for b in range(4 * spot.depth):
            pair[b, :, cut[h]] = (
                parts[b, spot.c, :, cut[h]].astype(f32) + pair[b, :, cut[h]].astype(f32)
            ).astype(low)
        step = []
        for way in (1, 2, 3):
            to, plane = spot.flip(way)
            for t in range(spot.depth):
                step.append(
                    wires.copy(pair.at[t * 4 + plane, :, cut[h]], near.at[way - 1, t, :, cut[h]], to)
                )
        flat.append(step)
    yield
    for h in range(2):
        got(flat[h])
        for t in range(spot.depth):
            total = pair[t * 4 + spot.plane, :, cut[h]].astype(f32)
            for way in range(3):
                total = total + near[way, t, :, cut[h]].astype(f32)
            column[t, :, cut[h]] = total.astype(low)
        ring.append(
            [
                wires.copy(
                    column.at[(spot.z + k) % spot.depth, :, cut[h]], far.at[k - 1, :, cut[h]], spot.above(k)
                )
                for k in range(1, spot.depth)
            ]
        )
    yield
    for h in range(2):
        got(ring[h])
        total = column[spot.z, :, cut[h]].astype(f32)
        for k in range(1, spot.depth):
            total = total + far[k - 1, :, cut[h]].astype(f32)
        out[:, cut[h]] = total
    yield


def big_gather(wires, spot, ow, od, shards):
    half, down = WIDE // 2, od.shape[0] // spot.count
    xn, yn, cn, zn = spot.flip(2)[0], spot.flip(1)[0], spot.sibling(), spot.above(1)
    here, xp, yp, xy = spot.plane, spot.flip(2)[1], spot.flip(1)[1], spot.flip(3)[1]

    def refs(t, plane, part):
        r = block_row(t, plane, spot.c)
        wide, deep = pl.multiple_of(r * TILE, TILE), pl.multiple_of(r * down, down)
        if part == "A":
            return [ow.at[pl.ds(wide, TILE), pl.ds(0, half)], od.at[pl.ds(deep, down // 2)]]
        if part == "B":
            return [
                ow.at[pl.ds(wide, TILE), pl.ds(half, half)],
                od.at[pl.ds(pl.multiple_of(deep + down // 2, down // 2), down // 2)],
            ]
        return [ow.at[pl.ds(wide, TILE)], od.at[pl.ds(deep, down)]]

    def go(t, plane, part, to):
        return [wires.copy(r, r, to) for r in refs(t, plane, part)]

    qkv, attn, gate, up, deep = shards
    cols, at = [], 0
    mine = pl.multiple_of(spot.me * TILE, TILE)
    for ref, a, b in ((qkv, 0, 3072), (attn, 0, 1024), (gate, 0, 2048), (gate, 2048, 2048), (up, 0, 4096)):
        cols.append((ref.at[:, pl.ds(a, b)], ow.at[pl.ds(mine, TILE), pl.ds(at, b)]))
        at += b
    row = pl.multiple_of(spot.me * down, down)
    deeps = [
        (deep.at[pl.ds(h * down // 2, down // 2)], od.at[pl.ds(pl.multiple_of(row + h * (down // 2), down // 2), down // 2)])
        for h in range(2)
    ]

    def own(part, to):
        pairs = {"A": cols[:3] + deeps[:1], "B": cols[3:] + deeps[1:], "AB": cols + deeps}[part]
        return [wires.copy(a, b, to) for a, b in pairs]

    T = spot.column
    core, ring, fx, fy, sx, sy = [], {}, {}, {}, {}, {}

    def first(j):
        send = own if j == 0 else (lambda part, to: go(T[j], here, part, to))
        if j < spot.depth - 1:
            ring[j] = send("AB", zn)
        fx[j], fy[j] = send("A", xn), send("B", yn)
        core.append(send("AB", cn))

    def second(j):
        got(fx[j])
        sy[j] = (own("A", yn) if j == 0 else go(T[j], here, "A", yn)) + go(T[j], xp, "A", yn)
        got(fy[j])
        sx[j] = (own("B", xn) if j == 0 else go(T[j], here, "B", xn)) + go(T[j], yp, "B", xn)
        core.append(go(T[j], xp, "A", cn) + go(T[j], yp, "B", cn))

    def third(j):
        got(sy[j])
        core.append(go(T[j], yp, "A", cn) + go(T[j], xy, "A", cn))
        got(sx[j])
        core.append(go(T[j], xp, "B", cn) + go(T[j], xy, "B", cn))

    first(0)
    yield
    for j in range(1, spot.depth):
        second(j - 1)
        yield
        got(ring[j - 1])
        first(j)
        yield
        if j >= 2:
            third(j - 2)
            yield
    second(spot.depth - 1)
    yield
    third(spot.depth - 2)
    third(spot.depth - 1)
    yield
    for copies in core:
        got(copies)
    yield


def run(steps):
    for _ in steps:
        pass


def sigmoid(v):
    return 1.0 / (1.0 + jnp.exp(-v))


def lanes(shape, axis):
    return lax.broadcasted_iota(jnp.int32, shape, axis)


def flat_dot(a, b, dims=((1,), (0,))):
    return lax.dot_general(a, b, (dims, ((), ())), preferred_element_type=jnp.float32)


def exact_dot(a, b):
    return jnp.dot(a, b, precision=HIGHEST, preferred_element_type=jnp.float32)


def gain_row(values):
    n_dev, width = values.shape[0], D // values.shape[0]
    spread = (lanes((128, D), 0) == lanes((128, D), 1) & (width - 1)).astype(jnp.bfloat16)
    rows = flat_dot(values, spread)
    return jnp.sum(jnp.where(lanes((n_dev, D), 0) == lanes((n_dev, D), 1) >> (width.bit_length() - 1), rows, 0.0), axis=0, keepdims=True)


def tap_rows(spot, small):
    n_dev = spot.count
    share = CONV_CH // n_dev
    col = lanes((1, 512), 1)
    channel = jnp.where(col < 256, (spot.q + 8 * (col >> 6)) * HEAD_M + (col & 63), DI + col - 256)
    dev = lanes((n_dev, 512), 0)
    picks = (channel >= dev * share) & (channel < dev * share + share)
    owner = jnp.sum(jnp.where(picks, dev, 0), axis=0, keepdims=True)
    within = lanes((128, 512), 0) == channel - owner * share
    rows = []
    for k in range(CONV + 1):
        values = small[:, TILE + k, 0:128]
        spread = flat_dot(values, picks.astype(jnp.bfloat16), ((0,), (0,)))
        rows.append(jnp.sum(jnp.where(within, spread, 0.0), axis=0, keepdims=True))
    return rows


def entry(block, row, lane):
    at = (lanes(block.shape, 0) == row) & (lanes(block.shape, 1) == lane)
    return jnp.sum(jnp.where(at, block.astype(jnp.float32), 0.0), keepdims=True).reshape(1, 1)


class Slot:
    def __init__(self, spot, small, x, count):
        block = small[(spot.z * 2 + x) * 4, TILE : TILE + 16, 0:128].astype(jnp.float32)
        first = entry(block, 9, 0)
        second = first + entry(block, 9, 1)
        number = lambda p: (p >= first).astype(jnp.float32) + (p >= second).astype(jnp.float32)
        col = lanes((count, 1), 0).astype(jnp.float32)
        row = lanes((1, count), 1).astype(jnp.float32)
        docs = number(col)
        self.keep = (col >= row) & (docs == number(row))
        self.same = [((col >= s) & (number(col - s) == docs)).astype(jnp.float32) for s in range(CONV)]


def shift(block, by):
    return block if by == 0 else pltpu.roll(block, by % block.shape[0], 0)


class Mixed:
    def __init__(self, spot, slot, own, maps, step_raw, taps, dt_row, rate_row):
        count = own.shape[0]
        self.spot, self.slot, self.count = spot, slot, count
        self.channels = jnp.concatenate([own[:, 256:], maps], axis=1)
        conv = taps[CONV] + sum(
            taps[CONV - 1 - s] * (shift(self.channels, s) * slot.same[s]) for s in range(CONV)
        )
        self.conv, self.sig = conv, sigmoid(conv)
        act = conv * self.sig
        self.inputs = act[:, :256]
        self.in_map, self.out_map = act[:, 256:384].astype(jnp.bfloat16), act[:, 384:].astype(jnp.bfloat16)
        self.raw = step_raw + dt_row
        self.step = jnp.where(self.raw > 20.0, self.raw, jnp.log(1.0 + jnp.exp(jnp.minimum(self.raw, 20.0))))
        lower = lanes((count, count), 0) >= lanes((count, count), 1)
        self.upper = (lanes((count, count), 0) <= lanes((count, count), 1)).astype(jnp.float32)
        self.cum = exact_dot(lower.astype(jnp.float32), self.step * rate_row)
        self.cum_t, self.step_t = self.cum.T, self.step.T
        self.inner = flat_dot(self.out_map, self.in_map, ((1,), (1,)))

    def head(self, i):
        return self.spot.q + 8 * i

    def col(self, by_head, i):
        return jnp.sum(jnp.where(lanes((1, 128), 1) == self.head(i), by_head, 0.0), axis=1, keepdims=True)

    def row(self, by_head_t, i):
        return jnp.sum(jnp.where(lanes((128, 1), 0) == self.head(i), by_head_t, 0.0), axis=0, keepdims=True)

    def decay(self, i):
        gap = jnp.where(self.slot.keep, self.col(self.cum, i) - self.row(self.cum_t, i), 0.0)
        return jnp.where(self.slot.keep, jnp.exp(gap), 0.0)


def pick_lane(row, lane):
    return jnp.sum(jnp.where(lanes(row.shape, 1) == lane, row, 0.0), axis=1, keepdims=True)


N_WIRES = 256


def forward_kernel(
    depth,
    rows_ref,
    patch_ref,
    cols_ref,
    vec_ref,
    out_ref,
    heads_ref,
    qkv,
    attn,
    gate,
    up,
    down,
    ow,
    od,
    sum_ref,
    mixed_ref,
    small_ref,
    bytes_ref,
    norm_ref,
    proj_ref,
    head_w_ref,
    own_ref,
    maps_ref,
    step_ref,
    core_ref,
    parts,
    pair,
    near,
    column,
    far,
    parts8,
    pair8,
    near8,
    send,
    recv,
    swap_send,
    swap_recv,
    local,
):
    f32, low = jnp.float32, jnp.bfloat16
    spot = Spot(depth)
    count = 128
    wires = Wires(send, recv)
    mine = pl.multiple_of(spot.me * TILE, TILE)
    bytes_ref[pl.ds(mine, TILE)] = rows_ref[:, pl.ds(pl.multiple_of(spot.me * 256, 256), 256)]
    small_ref[spot.me] = vec_ref[...]
    proj_ref[pl.ds(mine, TILE)] = cols_ref[spot.q]
    head_w_ref[spot.z] = out_ref[...]
    greet(spot)

    def lanes_of(to):
        return rows_ref.at[:, pl.ds(pl.multiple_of(to * 256, 256), 256)]

    swap_bytes = Swap(
        spot,
        swap_send.at[0],
        swap_recv.at[0],
        lanes_of,
        lambda me: bytes_ref.at[pl.ds(pl.multiple_of(me * TILE, TILE), TILE)],
    )
    swap_bytes.start()
    big = big_gather(wires, spot, ow, od, (qkv, attn, gate, up, down))
    swap_proj = Swap(
        spot,
        swap_send.at[1],
        swap_recv.at[1],
        lambda to: cols_ref.at[to % 8],
        lambda me: proj_ref.at[pl.ds(pl.multiple_of(me * TILE, TILE), TILE)],
    )
    swap_proj.start()
    small = spread_all(wires, spot, small_ref)
    next(small)
    head_w = [wires.copy(out_ref, head_w_ref.at[spot.z], spot.above(k)) for k in range(1, depth)]
    next(big)
    own_rows = []
    at = 0
    for i, ref in enumerate((qkv, attn, gate, up)):
        width = ref.shape[1]
        own_rows.append(pltpu.make_async_copy(ref, ow.at[pl.ds(mine, TILE), pl.ds(at, width)], local.at[i]))
        at += width
    deep = down.shape[0]
    own_rows.append(
        pltpu.make_async_copy(down, od.at[pl.ds(pl.multiple_of(spot.me * deep, deep), deep)], local.at[4])
    )
    for copy in own_rows:
        copy.start()
    swap_bytes.arrive()

    for b in range(4):
        block = flat_dot(bytes_ref[pl.ds(b * 256, 256)], patch_ref[...]).astype(low)
        parts[pl.ds(b * 4, 4)] = block.reshape(4, 2, TILE, D)
    total = sum_all(wires, spot, parts, pair, near, column, far, sum_ref)
    next(total)
    next(small)
    next(total)
    next(big)
    next(total)
    next(small)
    next(total)
    run(small)
    patch_sum = sum_ref[...]
    scale = lax.rsqrt(jnp.mean(patch_sum * patch_sum, axis=1, keepdims=True) + EPSILON)
    gain = gain_row(small_ref[:, TILE + 5, 0:128])
    norm_ref[spot.q] = (patch_sum * scale * gain).astype(low)
    plane = spread_plane(wires, spot, norm_ref)
    next(plane)
    next(plane)
    swap_proj.arrive()
    taps = tap_rows(spot, small_ref)
    run(plane)
    next(big)

    norm = norm_ref[...].reshape(2 * count, D)
    own_ref[...] = flat_dot(norm, proj_ref[...])
    maps_ref[...] = flat_dot(norm, small_ref[:, :TILE, 0:256].reshape(D, 256))
    step_ref[...] = flat_dot(norm, small_ref[:, :TILE, 256:384].reshape(D, 128))
    dt_row, rate_row, skip_row = heads_ref[0:1], heads_ref[1:2], heads_ref[2:3]
    got(head_w)
    gains = jnp.concatenate(
        [small_ref[spot.q + 8 * i, TILE : TILE + 16, 0:HEAD_M][6:7].astype(f32) for i in range(4)], axis=1
    )
    for x in range(2):
        at = pl.ds(x * count, count)
        slot = Slot(spot, small_ref, x, count)
        own, maps = own_ref[at], maps_ref[at]
        mix = Mixed(spot, slot, own, maps, step_ref[at], taps, dt_row, rate_row)
        outs = []
        for i in range(4):
            inputs = mix.inputs[:, i * HEAD_M : (i + 1) * HEAD_M]
            mixing = (mix.decay(i) * mix.inner * mix.row(mix.step_t, i)).astype(low)
            skip = pick_lane(skip_row, mix.head(i))
            outs.append(flat_dot(mixing, inputs.astype(low)) + skip * inputs)
        core = jnp.concatenate(outs, axis=1)
        core_ref[at] = core
        raw = own[:, :256]
        gated = core * raw * sigmoid(raw)
        part = flat_dot((gated * gains).astype(low), head_w_ref[...].reshape(256, D))
        squares = jnp.sum(gated * gated, axis=1, keepdims=True)
        parts8[pl.ds(x * 2, 2), :, :, pl.ds(0, D)] = part.astype(low).reshape(2, 2, TILE, D)
        parts8[pl.ds(x * 2, 2), :, :, pl.ds(D, 128)] = (
            jnp.broadcast_to(squares, (count, 128)).astype(low).reshape(2, 2, TILE, 128)
        )
    for total in sum_plane(wires, spot, parts8, pair8, near8):
        pass
    mixed_ref[...] = total
    for copy in own_rows:
        copy.wait()
    run(big)
    wires.drain()
    swap_bytes.leave()
    swap_proj.leave()


def forward_call(depth, n_dev, rows2, patch_proj, cols, vectors, out_proj, heads, qkv, attn, gate, up, down):
    f32, low = jnp.float32, jnp.bfloat16
    vmem = pl.BlockSpec(memory_space=pltpu.VMEM)
    anywhere = pl.BlockSpec(memory_space=pl.ANY)
    shape = jax.ShapeDtypeStruct
    plane_patches = 8 * TILE
    outs = [
        shape((D, WIDE), low),
        shape((down.shape[0] * n_dev, D), low),
        shape((TILE, D), f32),
        shape((TILE, EXT), f32),
        shape((n_dev, SMALL_ROWS, SMALL_COLS), low),
        shape((n_dev * TILE, 256), low),
        shape((8, TILE, D), low),
        shape((n_dev * TILE, 512), low),
        shape((depth, HEAD_M, D), low),
        shape((plane_patches, 512), f32),
        shape((plane_patches, 256), f32),
        shape((plane_patches, 128), f32),
        shape((plane_patches, 256), f32),
    ]
    scratch = [
        pltpu.VMEM((16, 2, TILE, D), low),
        pltpu.VMEM((16, TILE, D), low),
        pltpu.VMEM((3, depth, TILE, D), low),
        pltpu.VMEM((depth, TILE, D), low),
        pltpu.VMEM((depth - 1, TILE, D), low),
        pltpu.VMEM((4, 2, TILE, EXT), low),
        pltpu.VMEM((4, TILE, EXT), low),
        pltpu.VMEM((3, TILE, EXT), low),
        pltpu.SemaphoreType.DMA((N_WIRES,)),
        pltpu.SemaphoreType.DMA((N_WIRES,)),
        pltpu.SemaphoreType.DMA((2, n_dev)),
        pltpu.SemaphoreType.DMA((2, n_dev)),
        pltpu.SemaphoreType.DMA((5,)),
    ]
    return pl.pallas_call(
        partial(forward_kernel, depth),
        out_shape=outs,
        in_specs=[vmem] * 6 + [anywhere] * 5,
        out_specs=[anywhere] * 2 + [vmem] * 11,
        scratch_shapes=scratch,
        compiler_params=pltpu.CompilerParams(
            collective_id=0, has_side_effects=True, vmem_limit_bytes=56 * 2**20
        ),
        name="global_forward",
    )(rows2, patch_proj, cols, vectors, out_proj, heads, qkv, attn, gate, up, down)


PARTS = ((0, 3072), (3072, 1024), (4096, 4096), (8192, 4096))
STEP = 1024


def add_to(dst, sources, width):
    def one(i, carry):
        at = pl.ds(pl.multiple_of(i * STEP, STEP), STEP)
        total = sources[0](at).astype(jnp.float32)
        for source in sources[1:]:
            total = total + source(at).astype(jnp.float32)
        dst(at, total)
        return carry

    lax.fori_loop(0, width // STEP, one, 0)


def big_scatter(wires, spot, grads, bufs, outs, local):
    f32, low = jnp.float32, jnp.bfloat16
    held_w, held_d, stage_w, stage_d, near_w, near_d, last_w, last_d, ring_w, ring_d = bufs
    half, deep = WIDE // 2, held_d.shape[2]
    xn, yn, cn, zn = spot.flip(2)[0], spot.flip(1)[0], spot.sibling(), spot.above(1)
    here, xp, yp, xy = spot.plane, spot.flip(2)[1], spot.flip(1)[1], spot.flip(3)[1]
    T = [spot.column[k % spot.depth] for k in range(1, spot.depth + 1)]
    core, fetch, near, last, ring = {}, {}, {}, {}, {}
    A, B = pl.ds(0, half), pl.ds(half, half)
    DA, DB = pl.ds(0, deep // 2), pl.ds(deep // 2, deep // 2)

    def load(k):
        fetch[k] = []
        for i, ref in enumerate(grads):
            dst = stage_w.at[:, :, pl.ds(*PARTS[i])] if i < 4 else stage_d
            copy = pltpu.make_async_copy(ref.at[T[k], :, spot.c], dst, local.at[k * 5 + i])
            copy.start()
            fetch[k].append(copy)

    def open_core(k):
        core[k] = []
        for i, ref in enumerate(grads):
            dst = held_w.at[T[k], :, :, pl.ds(*PARTS[i])] if i < 4 else held_d.at[T[k]]
            core[k].append(wires.copy(ref.at[T[k], :, 1 - spot.c], dst, cn))

    def first(k):
        t = T[k]
        got(core[k])
        for copy in fetch[k]:
            copy.wait()
        for plane in range(4):

            def put_w(at, total, plane=plane):
                held_w[t, plane, :, at] = total.astype(low)

            add_to(put_w, [lambda at, p=plane: held_w[t, p, :, at], lambda at, p=plane: stage_w[p, :, at]], WIDE)
            held_d[t, plane] = (held_d[t, plane].astype(f32) + stage_d[plane].astype(f32)).astype(low)
        if k + 1 < spot.depth:
            load(k + 1)
        near[k] = []
        for x in range(2):
            src = x * 2 + (1 - spot.y)
            near[k].append(wires.copy(held_w.at[t, src, :, A], near_w.at[k, x, :, A], yn))
            near[k].append(wires.copy(held_d.at[t, src, DA], near_d.at[k, x, DA], yn))
        for y in range(2):
            src = (1 - spot.x) * 2 + y
            near[k].append(wires.copy(held_w.at[t, src, :, B], near_w.at[k, y, :, B], xn))
            near[k].append(wires.copy(held_d.at[t, src, DB], near_d.at[k, y, DB], xn))

    def second(k):
        t = T[k]
        got(near[k])
        for other in range(2):
            pa, pb = other * 2 + spot.y, spot.x * 2 + other

            def put_a(at, total, pa=pa):
                held_w[t, pa, :, at] = total.astype(low)

            def put_b(at, total, pb=pb):
                held_w[t, pb, :, pl.ds(pl.multiple_of(at.start + half, STEP), STEP)] = total.astype(low)

            shifted_by = lambda at: pl.ds(pl.multiple_of(at.start + half, STEP), STEP)
            add_to(put_a, [lambda at, p=pa: held_w[t, p, :, at], lambda at, o=other: near_w[k, o, :, at]], half)
            add_to(
                put_b,
                [
                    lambda at, p=pb: held_w[t, p, :, shifted_by(at)],
                    lambda at, o=other: near_w[k, o, :, shifted_by(at)],
                ],
                half,
            )
            held_d[t, pa, DA] = (held_d[t, pa, DA].astype(f32) + near_d[k, other, DA].astype(f32)).astype(low)
            held_d[t, pb, DB] = (held_d[t, pb, DB].astype(f32) + near_d[k, other, DB].astype(f32)).astype(low)
        last[k] = [
            wires.copy(held_w.at[t, xp, :, A], last_w.at[k, :, A], xn),
            wires.copy(held_d.at[t, xp, DA], last_d.at[k, DA], xn),
            wires.copy(held_w.at[t, yp, :, B], last_w.at[k, :, B], yn),
            wires.copy(held_d.at[t, yp, DB], last_d.at[k, DB], yn),
        ]

    def third(k):
        t = T[k]
        got(last[k])
        if k:
            got(ring[k - 1])
        terms = [lambda at: held_w[t, here, :, at], lambda at: last_w[k, :, at]]
        if k:
            terms.append(lambda at: ring_w[k - 1, :, at])
        down = held_d[t, here].astype(f32) + last_d[k].astype(f32)
        if k:
            down = down + ring_d[k - 1].astype(f32)
        if k < spot.depth - 1:

            def put_on(at, total):
                held_w[t, here, :, at] = total.astype(low)

            add_to(put_on, terms, WIDE)
            held_d[t, here] = down.astype(low)
            ring[k] = [
                wires.copy(held_w.at[t, here], ring_w.at[k], zn),
                wires.copy(held_d.at[t, here], ring_d.at[k], zn),
            ]
        else:
            for out, (begin, width) in zip(outs, PARTS):

                def put_out(at, total, out=out):
                    out[:, at] = total

                add_to(
                    put_out,
                    [
                        lambda at, f=f, b=begin: f(pl.ds(pl.multiple_of(at.start + b, STEP), STEP))
                        for f in terms
                    ],
                    width,
                )
            outs[4][...] = down

    load(0)
    for k in range(spot.depth):
        open_core(k)
    yield
    steps = [(first, 0)]
    n = spot.depth
    for k in range(1, n + 2):
        for step, lag in ((first, 0), (second, 1), (third, 2)):
            if 0 <= k - lag < n:
                steps.append((step, k - lag))
    for step, k in steps:
        step(k)
        yield


class Back:
    def __init__(self, mix, own, core, ext, d_patch, gains, head_w, heads, taps):
        f32, low = jnp.float32, jnp.bfloat16
        count = mix.count
        dt_row, rate_row, skip_row = heads[0:1], heads[1:2], heads[2:3]
        r = ext[:, 0:1] + ext[:, 2:3]
        along = ext[:, 1:2] + ext[:, 3:4]
        raw = own[:, :256]
        sig = sigmoid(raw)
        gated = core * raw * sig
        back = flat_dot(d_patch, head_w, ((1,), (1,)))
        self.norm = (gated * r * gains).astype(low)
        self.gain = jnp.sum(back * gated * r, axis=0, keepdims=True)
        d_gated = r * gains * back - gated * (r * r * r * along * (1.0 / DI))
        d_core = d_gated * raw * sig
        d_gate = d_gated * core * sig * (1.0 + raw * (1.0 - sig))
        lane = lanes((1, 128), 1)
        graph = jnp.zeros((count, count), f32)
        d_inputs = []
        direct = jnp.zeros((count, 128), f32)
        flow = jnp.zeros((count, 128), f32)
        d_skip = jnp.zeros((1, 128), f32)
        for i in range(4):
            cut = slice(i * HEAD_M, (i + 1) * HEAD_M)
            inputs, grad = mix.inputs[:, cut], d_core[:, cut]
            decay, step = mix.decay(i), mix.row(mix.step_t, i)
            kept = decay * mix.inner
            skip = pick_lane(skip_row, mix.head(i))
            d_mixing = flat_dot(grad.astype(low), inputs.astype(low), ((1,), (1,)))
            d_inputs.append(
                flat_dot((kept * step).astype(low), grad.astype(low), ((0,), (0,))) + skip * grad
            )
            graph = graph + decay * step * d_mixing
            turn = kept * d_mixing
            arrive = jnp.sum(turn.T, axis=1, keepdims=True)
            leave = jnp.sum(turn * step, axis=1, keepdims=True)
            here = lane == mix.head(i)
            direct = direct + jnp.where(here, arrive, 0.0)
            flow = flow + jnp.where(here, leave - mix.col(mix.step, i) * arrive, 0.0)
            d_skip = d_skip + jnp.where(here, jnp.sum(grad * inputs, keepdims=True).reshape(1, 1), 0.0)
        tail = exact_dot(mix.upper, flow)
        mine = own_lanes(lane, mix)
        d_step = jnp.where(mine, direct + rate_row * tail, 0.0)
        d_raw = d_step * sigmoid(mix.raw)
        self.skip = d_skip
        self.rate = jnp.sum(rate_row * mix.step * jnp.where(mine, tail, 0.0), axis=0, keepdims=True)
        self.bias = jnp.sum(d_raw, axis=0, keepdims=True)
        low_graph = graph.astype(low)
        d_out_map = flat_dot(low_graph, mix.in_map)
        d_in_map = flat_dot(low_graph, mix.out_map, ((0,), (0,)))
        d_act = jnp.concatenate(d_inputs + [d_in_map, d_out_map], axis=1)
        d_conv = d_act * (mix.sig * (1.0 + mix.conv * (1.0 - mix.sig)))
        d_channels = jnp.zeros_like(d_conv)
        self.taps = [None] * CONV + [jnp.sum(d_conv, axis=0, keepdims=True)]
        for s in range(CONV):
            kept = d_conv * mix.slot.same[s]
            d_channels = d_channels + taps[CONV - 1 - s] * shift(kept, -s)
            self.taps[CONV - 1 - s] = jnp.sum(kept * shift(mix.channels, s), axis=0, keepdims=True)
        self.rows = jnp.concatenate([d_gate, d_channels, d_raw], axis=1).astype(low)


def own_lanes(lane, mix):
    mine = lane == mix.head(0)
    for i in range(1, 4):
        mine = mine | (lane == mix.head(i))
    return mine


COLS = 512 + 256 + 128


def backward_kernel(
    depth,
    mix_ref,
    direct_ref,
    sum_ref,
    gains_ref,
    small_ref,
    bytes_ref,
    norm_ref,
    proj_ref,
    head_w_ref,
    own_ref,
    maps_ref,
    step_ref,
    core_ref,
    patch_ref,
    heads_ref,
    g_qkv,
    g_attn,
    g_gate,
    g_up,
    g_down,
    o_qkv,
    o_attn,
    o_gate,
    o_up,
    o_down,
    o_patch,
    o_rows,
    o_head,
    o_cols,
    o_maps,
    all_ref,
    mix_all,
    rows_all,
    head_sum,
    head_low,
    head_far,
    col_send,
    col_recv,
    back_send,
    parts8,
    pair8,
    near8,
    held_w,
    held_d,
    stage_w,
    stage_d,
    near_w,
    near_d,
    last_w,
    last_d,
    ring_w,
    ring_d,
    send,
    recv,
    swap_send,
    swap_recv,
    local,
):
    f32, low = jnp.float32, jnp.bfloat16
    spot = Spot(depth)
    count = 128
    wires = Wires(send, recv)
    mix_all[spot.q] = mix_ref[...]
    greet(spot)
    plane = spread_plane(wires, spot, mix_all)
    next(plane)
    big = big_scatter(
        wires,
        spot,
        (g_qkv, g_attn, g_gate, g_up, g_down),
        (held_w, held_d, stage_w, stage_d, near_w, near_d, last_w, last_d, ring_w, ring_d),
        (o_qkv, o_attn, o_gate, o_up, o_down),
        local,
    )
    next(big)
    next(plane)
    taps = tap_rows(spot, small_ref)
    heads = heads_ref[...]
    dt_row, rate_row = heads[0:1], heads[1:2]
    gains = jnp.concatenate(
        [small_ref[spot.q + 8 * i, TILE : TILE + 16, 0:HEAD_M][6:7].astype(f32) for i in range(4)], axis=1
    )
    gain = gain_row(small_ref[:, TILE + 5, 0:128])
    next(big)
    run(plane)
    sums = None
    for x in range(2):
        at = pl.ds(x * count, count)
        slot = Slot(spot, small_ref, x, count)
        mix = Mixed(spot, slot, own_ref[at], maps_ref[at], step_ref[at], taps, dt_row, rate_row)
        d_patch = mix_all[pl.ds(x * 4, 4), :, pl.ds(0, D)].reshape(count, D)
        ext = mix_all[pl.ds(x * 4, 4), :, pl.ds(D, 128)].reshape(count, 128).astype(f32)
        back = Back(
            mix, own_ref[at], core_ref[at], ext, d_patch, gains, head_w_ref[...].reshape(256, D), heads, taps
        )
        rows_all[at] = back.rows
        head = flat_dot(back.norm, d_patch, ((0,), (0,)))
        head_sum[...] = head if x == 0 else head_sum[...] + head
        new = [*back.taps, back.gain, back.bias, back.rate, back.skip]
        sums = new if sums is None else [a + b for a, b in zip(sums, new)]
        grad = flat_dot(back.rows[:, :512], proj_ref[...], ((1,), (1,)))
        grad = grad + flat_dot(
            back.rows[:, 512:], small_ref[:, :TILE, :].reshape(D, SMALL_COLS), ((1,), (1,))
        )
        parts8[pl.ds(x * 2, 2)] = grad.astype(low).reshape(2, 2, TILE, D)
        next(big)
    total8 = sum_plane(wires, spot, parts8, pair8, near8)
    next(total8)
    head_low[...] = head_sum[...].astype(low).reshape(depth, HEAD_M, D)
    head_ring = [
        wires.copy(head_low.at[(spot.z + k) % depth], head_far.at[k - 1], spot.above(k)) for k in range(1, depth)
    ]
    next(total8)
    norm = norm_ref[...].reshape(2 * count, D)
    rows = rows_all[...]
    for b in range(4):
        block = flat_dot(norm[:, b * 256 : (b + 1) * 256], rows, ((0,), (0,)))
        col_send[pl.ds(b * 8, 8)] = block.astype(low).reshape(8, TILE, COLS)
    swap_cols = Swap(
        spot, swap_send.at[0], swap_recv.at[0], lambda to: col_send.at[to], lambda me: col_recv.at[me]
    )
    grad_norm = next(total8)
    patch_sum = sum_ref[...]
    scale = lax.rsqrt(jnp.mean(patch_sum * patch_sum, axis=1, keepdims=True) + EPSILON)
    along = jnp.mean(grad_norm * gain * patch_sum, axis=1, keepdims=True)
    d_sum = direct_ref[...] + scale * gain * grad_norm - patch_sum * (scale * scale * scale * along)
    gain_sum = jnp.sum(grad_norm * patch_sum * scale, axis=0, keepdims=True)
    wide = lambda row: jnp.concatenate([row, jnp.zeros((1, D - row.shape[1]), f32)], axis=1)
    lines = [wide(row) for row in sums[: CONV + 1]]
    lines += [wide(jnp.concatenate(sums[CONV + 1 :], axis=1)), gains_ref[0:1], gains_ref[1:2], gain_sum]
    lines += [jnp.zeros((16 - len(lines), D), f32)]
    all_ref[spot.me] = jnp.concatenate([d_sum, *lines], axis=0).astype(low)
    spread = spread_all(wires, spot, all_ref)
    next(spread)
    swap_cols.start()
    col_recv[spot.me] = col_send[spot.me]
    next(big)
    next(spread)
    next(big)
    next(spread)
    run(spread)
    d_all = all_ref[:, :TILE].reshape(-1, D)
    for b in range(4):
        back_send[pl.ds(b * 8, 8)] = (
            flat_dot(d_all[b * 256 : (b + 1) * 256], patch_ref[...], ((1,), (1,))).astype(low).reshape(8, TILE, 256)
        )
    swap_rows = Swap(
        spot,
        swap_send.at[1],
        swap_recv.at[1],
        lambda to: back_send.at[to],
        lambda me: o_rows.at[:, pl.ds(pl.multiple_of(me * 256, 256), 256)],
    )
    swap_rows.start()
    o_rows[:, pl.ds(pl.multiple_of(spot.me * 256, 256), 256)] = back_send[spot.me]
    o_patch[...] = flat_dot(bytes_ref[...], d_all, ((0,), (0,)))
    got(head_ring)
    total = head_low[spot.z].astype(f32)
    for k in range(depth - 1):
        total = total + head_far[k].astype(f32)
    o_head[...] = total
    next(big)
    swap_cols.arrive()
    for q in range(8):
        total = col_recv[q, :, :512].astype(f32)
        for t in range(1, depth):
            total = total + col_recv[t * 8 + q, :, :512].astype(f32)
        o_cols[q] = total
    total = jnp.zeros((TILE, COLS - 512), f32)
    for e in range(spot.count):
        total = total + col_recv[e, :, 512:].astype(f32)
    o_maps[...] = total
    run(big)
    swap_rows.arrive()
    wires.drain()
    swap_cols.leave()
    swap_rows.leave()


def backward_call(depth, n_dev, mix, direct, patch_sum, gains, saved, patch_proj, heads, grads):
    f32, low = jnp.float32, jnp.bfloat16
    vmem = pl.BlockSpec(memory_space=pltpu.VMEM)
    anywhere = pl.BlockSpec(memory_space=pl.ANY)
    shape = jax.ShapeDtypeStruct
    deep = grads[4].shape[0] // n_dev
    cut = [g.reshape(depth, 4, 2, g.shape[0] // n_dev, g.shape[1]) for g in grads]
    outs = [shape((TILE, width), f32) for _, width in PARTS] + [
        shape((deep, D), f32),
        shape((256, D), f32),
        shape((TILE, PATCH * D), low),
        shape((HEAD_M, D), f32),
        shape((8, TILE, 512), f32),
        shape((TILE, COLS - 512), f32),
        shape((n_dev, SMALL_ROWS, D), low),
    ]
    scratch = [
        pltpu.VMEM((8, TILE, EXT), low),
        pltpu.VMEM((8 * TILE, COLS), low),
        pltpu.VMEM((256, D), f32),
        pltpu.VMEM((depth, HEAD_M, D), low),
        pltpu.VMEM((depth - 1, HEAD_M, D), low),
        pltpu.VMEM((n_dev, TILE, COLS), low),
        pltpu.VMEM((n_dev, TILE, COLS), low),
        pltpu.VMEM((n_dev, TILE, 256), low),
        pltpu.VMEM((4, 2, TILE, D), low),
        pltpu.VMEM((4, TILE, D), low),
        pltpu.VMEM((3, TILE, D), low),
        pltpu.VMEM((depth, 4, TILE, WIDE), low),
        pltpu.VMEM((depth, 4, deep, D), low),
        pltpu.VMEM((4, TILE, WIDE), low),
        pltpu.VMEM((4, deep, D), low),
        pltpu.VMEM((depth, 2, TILE, WIDE), low),
        pltpu.VMEM((depth, 2, deep, D), low),
        pltpu.VMEM((depth, TILE, WIDE), low),
        pltpu.VMEM((depth, deep, D), low),
        pltpu.VMEM((depth - 1, TILE, WIDE), low),
        pltpu.VMEM((depth - 1, deep, D), low),
        pltpu.SemaphoreType.DMA((N_WIRES,)),
        pltpu.SemaphoreType.DMA((N_WIRES,)),
        pltpu.SemaphoreType.DMA((2, n_dev)),
        pltpu.SemaphoreType.DMA((2, n_dev)),
        pltpu.SemaphoreType.DMA((5 * depth,)),
    ]
    return pl.pallas_call(
        partial(backward_kernel, depth),
        out_shape=outs,
        in_specs=[vmem] * 15 + [anywhere] * 5,
        out_specs=[vmem] * 11,
        scratch_shapes=scratch,
        compiler_params=pltpu.CompilerParams(
            collective_id=1, has_side_effects=True, vmem_limit_bytes=62 * 2**20
        ),
        name="global_backward",
    )(mix, direct, patch_sum, gains, *saved, patch_proj, heads, *cut)


BC = 2 * STATE


def split_heads(rows_by_cols):
    rows = rows_by_cols.shape[0]
    return rows_by_cols.reshape(rows // 128, 128, -1, HEAD).transpose(2, 0, 1, 3)


def join_heads(heads):
    return heads.transpose(1, 2, 0, 3).reshape(heads.shape[1] * heads.shape[2], -1)


def patch_mask():
    places = jnp.arange(128)
    return (places[:, None] >= places[None, :]) & (places[:, None] // PATCH == places[None, :] // PATCH)


def dot_f32(spec, a, b):
    return jnp.einsum(spec, a, b, preferred_element_type=jnp.float32)


def fast_body(
    depth_fsdp,
    byte_states,
    doc_lengths,
    out_grad,
    patch_proj,
    global_gain,
    in_proj,
    conv_weight,
    conv_bias,
    dt_bias,
    a_log,
    skip_weight,
    mixer_gain,
    out_proj,
    attn_gain,
    qkv_proj,
    attn_out,
    ffn_gain,
    gate_proj,
    up_proj,
    down_proj,
):
    f32, low = jnp.float32, jnp.bfloat16
    depth, n_dev = depth_fsdp[0] // 2, depth_fsdp[0] * depth_fsdp[1]
    me = lax.axis_index("dp") * depth_fsdp[1] + lax.axis_index("fsdp")
    rows = byte_states.shape[0]
    patches = rows // PATCH

    shard_rows = in_proj.shape[0]
    maps_and_steps = jnp.pad(in_proj[:, 2 * DI :], ((0, 0), (0, SMALL_COLS - BC - MHEADS)))
    lines = [conv_weight[:, k] for k in range(CONV)]
    lines += [conv_bias, global_gain, mixer_gain, attn_gain, ffn_gain, doc_lengths.reshape(-1).astype(low)]
    lines = jnp.stack([jnp.pad(line, (0, SMALL_COLS - line.shape[0])) for line in lines])
    vectors = jnp.concatenate(
        [maps_and_steps, lines, jnp.zeros((SMALL_ROWS - shard_rows - lines.shape[0], SMALL_COLS), low)]
    )
    by_place = lambda cols: cols.reshape(shard_rows, 4, 8, HEAD_M).transpose(2, 0, 1, 3).reshape(8, shard_rows, 256)
    cols = jnp.concatenate([by_place(in_proj[:, :DI]), by_place(in_proj[:, DI : 2 * DI])], axis=2)
    heads_in = jnp.pad(jnp.stack([dt_bias, -jnp.exp(a_log), skip_weight]), ((0, 5), (0, 128 - MHEADS)))
    rows2 = byte_states.reshape(patches, PATCH * D)
    (wide, deep, patch_sum, mixed, small, all_bytes, norm8, proj8, head_w, own8, maps8, step8, core8) = forward_call(
        depth, n_dev, rows2, patch_proj, cols, vectors, out_proj, heads_in, qkv_proj, attn_out, gate_proj, up_proj, down_proj
    )
    lines = small[:, shard_rows : shard_rows + 10]
    gain_g, gain_a, gain_f = (lines[:, k, : D // n_dev].reshape(-1).astype(f32) for k in (5, 7, 8))
    gain_m = lines[:, 6, : DI // n_dev].reshape(-1).astype(f32)
    my_places = lax.axis_index("fsdp") * patches + jnp.arange(patches, dtype=jnp.int32)
    live = jnp.repeat((my_places < doc_lengths[0, 0] + doc_lengths[0, 1]).astype(f32), PATCH)[:, None]
    qk, vals, attn_o = wide[:, : 2 * D], wide[:, 2 * D : 3 * D], wide[:, 3 * D : 4 * D]
    gate_w, up_w = wide[:, 4 * D : 8 * D], wide[:, 8 * D :]
    down_a, down_b = deep[:, : D // 2], deep[:, D // 2 :]
    raw_mixed = mixed[:, :D]
    mixer_r = lax.rsqrt(mixed[:, D : D + 1] / DI + EPSILON)
    mixed_patch = patch_sum + raw_mixed * mixer_r

    streams = byte_states.astype(f32) + jnp.repeat(mixed_patch, PATCH, axis=0)
    normed = rms_scale(streams, gain_a).astype(low)
    queries, key_rows = jnp.split(product(normed, qk).astype(low), 2, axis=1)
    queries, key_rows = split_heads(queries), split_heads(key_rows)
    value_rows = split_heads(product(normed, vals).astype(low))
    scale = HEAD ** (-0.5)
    scores = dot_f32("hbid,hbjd->hbij", queries, key_rows) * scale
    attn_weights = jax.nn.softmax(jnp.where(patch_mask(), scores, -1e30), axis=-1)
    attn_low = attn_weights.astype(low)
    mixed_heads = join_heads(dot_f32("hbij,hbjd->hbid", attn_low, value_rows).astype(low))
    attended = streams + product(mixed_heads, attn_o)
    ffn_low = rms_scale(attended, gain_f).astype(low)
    gate = product(ffn_low, gate_w)
    upward = product(ffn_low, up_w)
    sigma = jax.nn.sigmoid(gate)
    hidden = (gate * sigma * upward).astype(low)
    ffn_out = jnp.concatenate([product(hidden, down_a), product(hidden, down_b)], axis=1)
    block_out = (live * (attended + ffn_out)).astype(low)

    def scattered(act, grad):
        return weight_grad(act, grad).astype(low)

    grad_block = live * out_grad.astype(f32)
    down_low = grad_block.astype(low)
    grad_down = scattered(hidden, down_low)
    grad_hidden = input_grad(down_low[:, : D // 2], down_a) + input_grad(down_low[:, D // 2 :], down_b)
    grad_gate_low = (grad_hidden * upward * sigma * (1.0 + gate * (1.0 - sigma))).astype(low)
    grad_up_low = (grad_hidden * gate * sigma).astype(low)
    grad_gate = scattered(ffn_low, grad_gate_low)
    grad_up = scattered(ffn_low, grad_up_low)
    grad_ffn_in = input_grad(grad_gate_low, gate_w) + input_grad(grad_up_low, up_w)
    _, norm_back = jax.vjp(rms_scale, attended, gain_f)
    grad_attended_norm, grad_gain_f = norm_back(grad_ffn_in)
    grad_attended = grad_block + grad_attended_norm
    attn_grad_low = grad_attended.astype(low)
    grad_attn_out = scattered(mixed_heads, attn_grad_low)
    grad_mixed = split_heads(input_grad(attn_grad_low, attn_o).astype(low))
    grad_values = dot_f32("hbij,hbid->hbjd", attn_low, grad_mixed)
    grad_weights = dot_f32("hbid,hbjd->hbij", grad_mixed, value_rows)
    grad_scores = attn_weights * (
        grad_weights - jnp.sum(attn_weights * grad_weights, axis=-1, keepdims=True)
    )
    scores_low = grad_scores.astype(low)
    grad_queries = dot_f32("hbij,hbjd->hbid", scores_low, key_rows) * scale
    grad_keys = dot_f32("hbij,hbid->hbjd", scores_low, queries) * scale
    grad_qk = jnp.concatenate([join_heads(grad_queries.astype(low)), join_heads(grad_keys.astype(low))], axis=1)
    grad_v = join_heads(grad_values.astype(low))
    grad_qkv = scattered(normed, jnp.concatenate([grad_qk, grad_v], axis=1))
    grad_normed = input_grad(grad_qk, qk) + input_grad(grad_v, vals)
    _, norm_back = jax.vjp(rms_scale, streams, gain_a)
    grad_streams_norm, grad_gain_a = norm_back(grad_normed)
    grad_streams = grad_attended + grad_streams_norm

    grad_patch_mix = grad_streams.reshape(patches, PATCH, D).sum(axis=1)
    mix_low = grad_patch_mix.astype(low)
    along = jnp.sum(mix_low.astype(f32) * raw_mixed, axis=1, keepdims=True)
    pair = jnp.concatenate([mixer_r, along], axis=1)
    pair_high = pair.astype(low)
    pair_rest = (pair - pair_high.astype(f32)).astype(low)
    extra = jnp.pad(jnp.concatenate([pair_high, pair_rest], axis=1), ((0, 0), (0, 124)))
    gains = jnp.pad(jnp.stack([grad_gain_a, grad_gain_f]), ((0, 6), (0, 0)))
    saved = (small, all_bytes, norm8, proj8, head_w, own8, maps8, step8, core8)
    (g_qkv, g_attn, g_gate, g_up, g_down, g_patch, back_rows, g_out, g_cols, g_maps, everyone) = backward_call(
        depth,
        n_dev,
        jnp.concatenate([mix_low, extra], axis=1),
        grad_patch_mix,
        patch_sum,
        gains,
        saved,
        patch_proj,
        heads_in,
        (grad_qkv, grad_attn_out, grad_gate, grad_up, grad_down),
    )
    grad_states = grad_streams + back_rows.reshape(rows, D).astype(f32)

    lines = everyone[:, shard_rows : shard_rows + 9].astype(f32)
    sums = jnp.sum(lines, axis=0)
    own_part = lambda row: lax.dynamic_slice_in_dim(row, me * (D // n_dev), D // n_dev, 0)
    by_plane = jnp.sum(lines.reshape(depth, 8, 9, D), axis=0)
    by_head = lambda rows_of: rows_of.reshape(8, -1, 4, HEAD_M).transpose(1, 2, 0, 3).reshape(-1, DI)
    taps = jnp.concatenate([by_head(by_plane[:, : CONV + 1, :256]), sums[: CONV + 1, 256:512]], axis=1)
    share = CONV_CH // n_dev
    taps = lax.dynamic_slice_in_dim(taps, me * share, share, 1)
    gain_m_sum = by_head(by_plane[:, CONV + 1 : CONV + 2, :256])[0]
    gain_m_sum = lax.dynamic_slice_in_dim(gain_m_sum, me * HEAD_M, HEAD_M, 0)
    head_line = sums[CONV + 1]
    back_cols = lambda cols: cols.reshape(8, shard_rows, 4, HEAD_M).transpose(1, 2, 0, 3).reshape(shard_rows, DI)
    grad_in_proj = jnp.concatenate(
        [back_cols(g_cols[..., :256]), back_cols(g_cols[..., 256:]), g_maps[:, : BC + MHEADS]], axis=1
    )
    return (
        block_out,
        grad_states,
        g_patch,
        own_part(sums[CONV + 4]),
        grad_in_proj,
        taps[:CONV].T,
        taps[CONV],
        head_line[256 : 256 + MHEADS],
        head_line[384 : 384 + MHEADS],
        head_line[512 : 512 + MHEADS],
        gain_m_sum,
        g_out,
        own_part(sums[CONV + 2]),
        g_qkv,
        g_attn,
        own_part(sums[CONV + 3]),
        g_gate,
        g_up,
        g_down,
    )


def solution(mesh):
    in_specs = (
        P(("dp", "fsdp"), None),
        P("dp", None),
        P(("dp", "fsdp"), None),
        P(("dp", "fsdp"), None),
        P(("dp", "fsdp")),
        P(("dp", "fsdp"), None),
        P(("dp", "fsdp"), None),
        P(("dp", "fsdp")),
        P(),
        P(),
        P(),
        P(("dp", "fsdp")),
        P(("dp", "fsdp"), None),
        P(("dp", "fsdp")),
        P(("dp", "fsdp"), None),
        P(("dp", "fsdp"), None),
        P(("dp", "fsdp")),
        P(("dp", "fsdp"), None),
        P(("dp", "fsdp"), None),
        P(("dp", "fsdp"), None),
    )
    out_specs = (
        P(("dp", "fsdp"), None),
        P(("dp", "fsdp"), None),
        P(("dp", "fsdp"), None),
        P(("dp", "fsdp")),
        P(("dp", "fsdp"), None),
        P(("dp", "fsdp"), None),
        P(("dp", "fsdp")),
        P(),
        P(),
        P(),
        P(("dp", "fsdp")),
        P(("dp", "fsdp"), None),
        P(("dp", "fsdp")),
        P(("dp", "fsdp"), None),
        P(("dp", "fsdp"), None),
        P(("dp", "fsdp")),
        P(("dp", "fsdp"), None),
        P(("dp", "fsdp"), None),
        P(("dp", "fsdp"), None),
    )
    dp, fsdp = mesh.shape["dp"], mesh.shape["fsdp"]
    fast = dp * fsdp == MHEADS and fsdp == 4
    chosen = partial(fast_body, (dp, fsdp)) if fast else body
    return jax.shard_map(chosen, mesh=mesh, in_specs=in_specs, out_specs=out_specs, check_vma=False)
```

```python
from functools import partial

import jax
import jax.numpy as jnp
from jax import lax
from jax.experimental import pallas as pl
from jax.experimental.pallas import tpu as pltpu
from jax.sharding import PartitionSpec as P

D = 1024
HEAD = 64
HEAD_M = 64
STATE = 128
CONV = 4
PATCH = 8
DI = 2048
MHEADS = 32
CONV_CH = 2304


EPSILON = 1e-05
HIGHEST = lax.Precision.HIGHEST


def shifted(block, axis, distance):
    devices = range(lax.axis_size(axis))
    route = [(i - distance, i) for i in devices if i - distance in devices]
    return lax.ppermute(block, axis, route)


def prefix(value, axis, combine, identity):
    devices, place = (lax.axis_size(axis), lax.axis_index(axis))
    everything = jax.tree.map(
        lambda part, kind: lax.all_gather(part.astype(kind), axis),
        value,
        (jnp.bfloat16, jnp.bfloat16),
    )
    start = jax.tree.map(
        lambda part, zero: jnp.broadcast_to(jnp.asarray(zero, part.dtype), part.shape),
        value,
        identity,
    )

    def prefix_step(k, before):
        reached = k < place
        new = combine(
            before, jax.tree.map(lambda part, own: part[k].astype(own.dtype), everything, value)
        )
        return jax.tree.map(lambda a, b: jnp.where(reached, a, b), new, before)

    return lax.fori_loop(0, devices, prefix_step, start)


def carried_in(value, axis, combine, identity):
    devices, place = (lax.axis_size(axis), lax.axis_index(axis))
    everything = jax.tree.map(
        lambda part, kind: lax.all_gather(part.astype(kind), axis),
        value,
        jax.tree.map(lambda a: jnp.bfloat16 if a.dtype == jnp.float32 else a.dtype, value),
    )
    start = jax.tree.map(
        lambda part, zero: jnp.broadcast_to(jnp.asarray(zero, part.dtype), part.shape),
        value,
        identity,
    )

    def carried_step(k, before):
        at = devices - 1 - k
        reached = at > place
        new = combine(
            before, jax.tree.map(lambda part, own: part[at].astype(own.dtype), everything, value)
        )
        return jax.tree.map(lambda a, b: jnp.where(reached, a, b), new, before)

    return lax.fori_loop(0, devices, carried_step, start)


def product(left, right):
    return jnp.dot(left, right, preferred_element_type=jnp.float32)


def weight_grad(left, right):
    return lax.dot_general(
        left, right, (((0,), (0,)), ((), ())), preferred_element_type=jnp.float32
    )


def input_grad(grad_rows, weight):
    return lax.dot_general(
        grad_rows, weight, (((1,), (1,)), ((), ())), preferred_element_type=jnp.float32
    )


def rms_scale(value, gain):
    return value * lax.rsqrt(jnp.mean(value * value, axis=-1, keepdims=True) + EPSILON) * gain


def gated_norm(core_out, gate_raw, gain):
    count = core_out.shape[0]
    return rms_scale(core_out.reshape(count, DI) * jax.nn.silu(gate_raw), gain)


def patch_docs(doc_lengths, start, count):
    places = start + jnp.arange(count, dtype=jnp.int32)
    first_end = doc_lengths[0, 0]
    second_end = first_end + doc_lengths[0, 1]
    numbers = (places >= first_end).astype(jnp.int32) + (places >= second_end).astype(jnp.int32)
    return jnp.where(places >= 0, numbers, -1)


def chain(earlier, later):
    return (earlier[0] * later[0], later[1] + later[0][:, None, None] * earlier[1])


def mixer_core(
    channels,
    rim,
    step_raw,
    state_in,
    conv_weight,
    conv_bias,
    dt_bias,
    a_log,
    skip_weight,
    docs,
    rim_docs,
    prev_doc,
):
    count = channels.shape[0]
    padded = jnp.concatenate([rim, channels], axis=0)
    padded_docs = jnp.concatenate([rim_docs, docs])
    total = conv_bias[None, :]
    for shift_k in range(CONV):
        same_doc = (padded_docs[shift_k : shift_k + count] == docs).astype(jnp.float32)
        total = (
            total
            + padded[shift_k : shift_k + count]
            * conv_weight[:, shift_k][None, :]
            * same_doc[:, None]
        )
    activated = jax.nn.silu(total)
    inputs = activated[:, :DI].reshape(count, MHEADS, HEAD_M)
    in_map = activated[:, DI : DI + STATE]
    out_map = activated[:, DI + STATE :]
    step_size = jax.nn.softplus(step_raw + dt_bias[None, :])
    rate = -jnp.exp(a_log)
    lower = jnp.tril(jnp.ones((count, count), jnp.float32))
    cumulative = jnp.dot(lower, step_size * rate[None, :], precision=HIGHEST)
    places = jnp.arange(count, dtype=jnp.int32)
    keep = ((places[:, None] >= places[None, :]) & (docs[:, None] == docs[None, :]))[:, :, None]
    spread = cumulative[:, None, :] - cumulative[None, :, :]
    decay_table = jnp.where(keep, jnp.exp(jnp.where(keep, spread, 0.0)), 0.0)
    inner = jnp.dot(out_map, in_map.T, precision=HIGHEST, preferred_element_type=jnp.float32)
    mixing = decay_table * inner[:, :, None] * step_size[None, :, :]
    outputs = jnp.einsum("tsh,shp->thp", mixing, inputs, precision=HIGHEST)
    carry_in = jnp.where((docs == prev_doc)[:, None], jnp.exp(cumulative), 0.0)
    outputs = outputs + carry_in[:, :, None] * jnp.einsum(
        "tn,hpn->thp", out_map, state_in, precision=HIGHEST
    )
    outputs = outputs + skip_weight[None, :, None] * inputs
    last_doc = docs[count - 1]
    tail_keep = (docs == last_doc)[:, None]
    tail_gap = cumulative[count - 1][None, :] - cumulative
    tail_weight = (
        jnp.where(tail_keep, jnp.exp(jnp.where(tail_keep, tail_gap, 0.0)), 0.0) * step_size
    )
    decay_total = jnp.where(prev_doc == last_doc, jnp.exp(cumulative[count - 1]), 0.0)
    state_out = jnp.einsum("sh,shp,sn->hpn", tail_weight, inputs, in_map, precision=HIGHEST)
    state_out = state_out + decay_total[:, None, None] * state_in
    return ((outputs, state_out), (decay_total, carry_in, out_map))


def attend(qkv_low, patches):
    heads = qkv_low.reshape(patches, PATCH, 3, -1, HEAD)
    queries = heads[:, :, 0]
    key_rows = heads[:, :, 1]
    value_rows = heads[:, :, 2]
    scores = jnp.einsum(
        "pihd,pjhd->phij", queries, key_rows, preferred_element_type=jnp.float32
    ) * HEAD ** (-0.5)
    places = jnp.arange(PATCH)
    causal = places[:, None] >= places[None, :]
    scores = jnp.where(causal, scores, -1e30)
    attn_weights = jax.nn.softmax(scores, axis=-1)
    attn_low = attn_weights.astype(jnp.bfloat16)
    mixed = jnp.einsum("phij,pjhd->pihd", attn_low, value_rows, preferred_element_type=jnp.float32)
    mixed = mixed.astype(jnp.bfloat16).reshape(patches * PATCH, -1)
    return ((queries, key_rows, value_rows, attn_weights, attn_low), mixed)


def attend_back(grad_mixed_low, pieces):
    queries, key_rows, value_rows, attn_weights, attn_low = pieces
    patches = queries.shape[0]
    grad_mixed = grad_mixed_low.reshape(patches, PATCH, -1, HEAD)
    grad_values = jnp.einsum(
        "phij,pihd->pjhd", attn_low, grad_mixed, preferred_element_type=jnp.float32
    )
    grad_weights = jnp.einsum(
        "pihd,pjhd->phij", grad_mixed, value_rows, preferred_element_type=jnp.float32
    )
    grad_scores = attn_weights * (
        grad_weights - jnp.sum(attn_weights * grad_weights, axis=-1, keepdims=True)
    )
    scores_low = grad_scores.astype(jnp.bfloat16)
    scale = HEAD ** (-0.5)
    grad_queries = (
        jnp.einsum("phij,pjhd->pihd", scores_low, key_rows, preferred_element_type=jnp.float32)
        * scale
    )
    grad_keys = (
        jnp.einsum("phij,pihd->pjhd", scores_low, queries, preferred_element_type=jnp.float32)
        * scale
    )
    stacked = jnp.stack([grad_queries, grad_keys, grad_values], axis=2).reshape(patches * PATCH, -1)
    return stacked.astype(jnp.bfloat16)


def local_forward(byte_states, mixed_patch, local_set, live):
    attn_gain, qkv_proj, attn_out, ffn_gain, gate_proj, up_proj, down_proj = local_set
    rows = byte_states.shape[0]
    streams = byte_states.astype(jnp.float32) + jnp.repeat(mixed_patch, PATCH, axis=0)
    normed_low = rms_scale(streams, attn_gain.astype(jnp.float32)).astype(jnp.bfloat16)
    qkv_low = product(normed_low, qkv_proj).astype(jnp.bfloat16)
    pieces, mixed_heads = attend(qkv_low, rows // PATCH)
    attended = streams + product(mixed_heads, attn_out)
    ffn_low = rms_scale(attended, ffn_gain.astype(jnp.float32)).astype(jnp.bfloat16)
    gate = product(ffn_low, gate_proj)
    upward = product(ffn_low, up_proj)
    hidden_low = (jax.nn.silu(gate) * upward).astype(jnp.bfloat16)
    block = live * (attended + product(hidden_low, down_proj))
    cache = (streams, normed_low, pieces, mixed_heads, attended, ffn_low, gate, upward, hidden_low)
    return (block, cache)


def local_backward(grad_block, cache, local_set):
    attn_gain, qkv_proj, attn_out, ffn_gain, gate_proj, up_proj, down_proj = local_set
    streams, normed_low, pieces, mixed_heads, attended, ffn_low, gate, upward, hidden_low = cache
    down_low = grad_block.astype(jnp.bfloat16)
    grad_down = weight_grad(hidden_low, down_low)
    grad_hidden = input_grad(down_low, down_proj)
    sigma = jax.nn.sigmoid(gate)
    grad_gate_low = (grad_hidden * upward * sigma * (1.0 + gate * (1.0 - sigma))).astype(
        jnp.bfloat16
    )
    grad_up_low = (grad_hidden * gate * sigma).astype(jnp.bfloat16)
    grad_gate = weight_grad(ffn_low, grad_gate_low)
    grad_up = weight_grad(ffn_low, grad_up_low)
    grad_ffn_in = input_grad(grad_gate_low, gate_proj) + input_grad(grad_up_low, up_proj)
    _, norm_back = jax.vjp(rms_scale, attended, ffn_gain.astype(jnp.float32))
    grad_attended_norm, grad_ffn_gain = norm_back(grad_ffn_in)
    grad_attended = grad_block + grad_attended_norm
    attn_grad_low = grad_attended.astype(jnp.bfloat16)
    grad_attn_out = weight_grad(mixed_heads, attn_grad_low)
    grad_mixed_low = input_grad(attn_grad_low, attn_out).astype(jnp.bfloat16)
    grad_qkv_low = attend_back(grad_mixed_low, pieces)
    grad_qkv = weight_grad(normed_low, grad_qkv_low)
    grad_normed = input_grad(grad_qkv_low, qkv_proj)
    _, norm_back = jax.vjp(rms_scale, streams, attn_gain.astype(jnp.float32))
    grad_streams_norm, grad_attn_gain = norm_back(grad_normed)
    grad_streams = grad_attended + grad_streams_norm
    return (
        grad_streams,
        (grad_qkv, grad_attn_out, grad_gate, grad_up, grad_down, grad_attn_gain, grad_ffn_gain),
    )


def body(
    byte_states,
    doc_lengths,
    out_grad,
    patch_proj,
    global_gain,
    in_proj,
    conv_weight,
    conv_bias,
    dt_bias,
    a_log,
    skip_weight,
    mixer_gain,
    out_proj,
    attn_gain,
    qkv_proj,
    attn_out,
    ffn_gain,
    gate_proj,
    up_proj,
    down_proj,
):
    rows = byte_states.shape[0]
    patches = rows // PATCH
    share = lax.axis_index("fsdp")
    start = share * patches
    docs = patch_docs(doc_lengths, start, patches)
    rim_docs = patch_docs(doc_lengths, start - (CONV - 1), CONV - 1)
    prev_doc = patch_docs(doc_lengths, start - 1, 1)[0]
    live = jnp.repeat((docs < 2).astype(jnp.float32), PATCH)[:, None]
    all_set = (
        lax.all_gather(patch_proj, ("dp", "fsdp"), axis=0, tiled=True),
        lax.all_gather(global_gain, ("dp", "fsdp"), axis=0, tiled=True),
        lax.all_gather(in_proj, ("dp", "fsdp"), axis=0, tiled=True),
        lax.all_gather(conv_weight, ("dp", "fsdp"), axis=0, tiled=True),
        lax.all_gather(conv_bias, ("dp", "fsdp"), axis=0, tiled=True),
        lax.all_gather(mixer_gain, ("dp", "fsdp"), axis=0, tiled=True),
        lax.all_gather(out_proj, ("dp", "fsdp"), axis=0, tiled=True),
        lax.all_gather(attn_gain, ("dp", "fsdp"), axis=0, tiled=True),
        lax.all_gather(qkv_proj, ("dp", "fsdp"), axis=0, tiled=True),
        lax.all_gather(attn_out, ("dp", "fsdp"), axis=0, tiled=True),
        lax.all_gather(ffn_gain, ("dp", "fsdp"), axis=0, tiled=True),
        lax.all_gather(gate_proj, ("dp", "fsdp"), axis=0, tiled=True),
        lax.all_gather(up_proj, ("dp", "fsdp"), axis=0, tiled=True),
        lax.all_gather(down_proj, ("dp", "fsdp"), axis=0, tiled=True),
    )
    global_set = all_set[:7]
    local_set = all_set[7:]
    patch_full, gain_g_full, in_full, conv_w_full, conv_b_full, gain_m_full, out_full = global_set
    patch_rows = byte_states.reshape(patches, PATCH * D)
    patch_sum = product(patch_rows, patch_full)
    gain_g = gain_g_full.astype(jnp.float32)
    global_low = rms_scale(patch_sum, gain_g).astype(jnp.bfloat16)
    projected = product(global_low, in_full)
    gate_raw = projected[:, :DI]
    channels = projected[:, DI : DI + CONV_CH]
    step_raw = projected[:, DI + CONV_CH :]
    rim = shifted(channels[patches - (CONV - 1) :], "fsdp", 1)
    core = partial(mixer_core, docs=docs, rim_docs=rim_docs, prev_doc=prev_doc)
    conv_w = conv_w_full.astype(jnp.float32)
    conv_b = conv_b_full.astype(jnp.float32)
    empty_state = jnp.zeros((MHEADS, HEAD_M, STATE), jnp.float32)
    (partial_out, local_state), aux = core(
        channels, rim, step_raw, empty_state, conv_w, conv_b, dt_bias, a_log, skip_weight
    )
    decay_total, carry_in, out_map = aux
    identity = (jnp.ones((MHEADS,), jnp.float32), jnp.zeros((MHEADS, HEAD_M, STATE), jnp.float32))
    arrived = prefix((decay_total, local_state), "fsdp", chain, identity)
    state_in = arrived[1]
    mixer_out = partial_out + carry_in[:, :, None] * jnp.einsum(
        "tn,hpn->thp", out_map, state_in, precision=HIGHEST
    )
    gain_m = gain_m_full.astype(jnp.float32)
    mixer_low = gated_norm(mixer_out, gate_raw, gain_m).astype(jnp.bfloat16)
    mixed_patch = patch_sum + product(mixer_low, out_full)
    block, cache = local_forward(byte_states, mixed_patch, local_set, live)
    block_out = block.astype(jnp.bfloat16)
    back_set = (
        lax.all_gather(patch_proj, ("dp", "fsdp"), axis=0, tiled=True),
        lax.all_gather(global_gain, ("dp", "fsdp"), axis=0, tiled=True),
        lax.all_gather(in_proj, ("dp", "fsdp"), axis=0, tiled=True),
        lax.all_gather(conv_weight, ("dp", "fsdp"), axis=0, tiled=True),
        lax.all_gather(conv_bias, ("dp", "fsdp"), axis=0, tiled=True),
        lax.all_gather(mixer_gain, ("dp", "fsdp"), axis=0, tiled=True),
        lax.all_gather(out_proj, ("dp", "fsdp"), axis=0, tiled=True),
        lax.all_gather(attn_gain, ("dp", "fsdp"), axis=0, tiled=True),
        lax.all_gather(qkv_proj, ("dp", "fsdp"), axis=0, tiled=True),
        lax.all_gather(attn_out, ("dp", "fsdp"), axis=0, tiled=True),
        lax.all_gather(ffn_gain, ("dp", "fsdp"), axis=0, tiled=True),
        lax.all_gather(gate_proj, ("dp", "fsdp"), axis=0, tiled=True),
        lax.all_gather(up_proj, ("dp", "fsdp"), axis=0, tiled=True),
        lax.all_gather(down_proj, ("dp", "fsdp"), axis=0, tiled=True),
    )
    global_back = back_set[:7]
    local_back = back_set[7:]
    _, cache = local_forward(byte_states, mixed_patch, local_back, live)
    patch_back, _, in_back, conv_w_back, conv_b_back, _, out_back = global_back
    grad_block = live * out_grad.astype(jnp.float32)
    grad_streams, local_grads = local_backward(grad_block, cache, local_back)
    reduced_local = (
        lax.psum_scatter(local_grads[0], ("dp", "fsdp"), scatter_dimension=0, tiled=True),
        lax.psum_scatter(local_grads[1], ("dp", "fsdp"), scatter_dimension=0, tiled=True),
        lax.psum_scatter(local_grads[2], ("dp", "fsdp"), scatter_dimension=0, tiled=True),
        lax.psum_scatter(local_grads[3], ("dp", "fsdp"), scatter_dimension=0, tiled=True),
        lax.psum_scatter(local_grads[4], ("dp", "fsdp"), scatter_dimension=0, tiled=True),
        lax.psum_scatter(local_grads[5], ("dp", "fsdp"), scatter_dimension=0, tiled=True),
        lax.psum_scatter(local_grads[6], ("dp", "fsdp"), scatter_dimension=0, tiled=True),
    )
    grad_patch_mix = grad_streams.reshape(patches, PATCH, D).sum(axis=1)
    mix_low = grad_patch_mix.astype(jnp.bfloat16)
    grad_out_proj = weight_grad(mixer_low, mix_low)
    grad_mixer_low = input_grad(mix_low, out_back)
    _, norm_back = jax.vjp(gated_norm, mixer_out, gate_raw, gain_m)
    grad_core, grad_gate_raw, grad_mixer_gain = norm_back(grad_mixer_low)
    state_part = jnp.einsum("th,thp,tn->hpn", carry_in, grad_core, out_map, precision=HIGHEST)
    returned = carried_in((decay_total, state_part), "fsdp", chain, identity)
    _, core_back, _ = jax.vjp(
        core,
        channels,
        rim,
        step_raw,
        state_in,
        conv_w_back.astype(jnp.float32),
        conv_b_back.astype(jnp.float32),
        dt_bias,
        a_log,
        skip_weight,
        has_aux=True,
    )
    core_grads = core_back((grad_core, returned[1]))
    (
        grad_channels,
        grad_rim,
        grad_step,
        _,
        grad_conv_w,
        grad_conv_b,
        grad_dt_bias,
        grad_a_log,
        grad_skip,
    ) = core_grads
    rim_grad = shifted(grad_rim, "fsdp", -1)
    cut = patches - (CONV - 1)
    grad_channels = jnp.concatenate([grad_channels[:cut], grad_channels[cut:] + rim_grad], axis=0)
    proj_low = jnp.concatenate([grad_gate_raw, grad_channels, grad_step], axis=1).astype(
        jnp.bfloat16
    )
    grad_in_proj = weight_grad(global_low, proj_low)
    grad_global_norm = input_grad(proj_low, in_back)
    _, norm_back = jax.vjp(rms_scale, patch_sum, gain_g)
    grad_sum_norm, grad_global_gain = norm_back(grad_global_norm)
    sum_low = (grad_patch_mix + grad_sum_norm).astype(jnp.bfloat16)
    grad_patch_proj = weight_grad(patch_rows, sum_low)
    grad_states = grad_streams + input_grad(sum_low, patch_back).reshape(rows, D)
    reduced_global = (
        lax.psum_scatter(grad_patch_proj, ("dp", "fsdp"), scatter_dimension=0, tiled=True),
        lax.psum_scatter(grad_global_gain, ("dp", "fsdp"), scatter_dimension=0, tiled=True),
        lax.psum_scatter(grad_in_proj, ("dp", "fsdp"), scatter_dimension=0, tiled=True),
        lax.psum_scatter(grad_conv_w, ("dp", "fsdp"), scatter_dimension=0, tiled=True),
        lax.psum_scatter(grad_conv_b, ("dp", "fsdp"), scatter_dimension=0, tiled=True),
        lax.psum_scatter(grad_mixer_gain, ("dp", "fsdp"), scatter_dimension=0, tiled=True),
        lax.psum_scatter(grad_out_proj, ("dp", "fsdp"), scatter_dimension=0, tiled=True),
    )
    head_sums = lax.psum((grad_dt_bias, grad_a_log, grad_skip), ("dp", "fsdp"))
    return (
        block_out,
        grad_states,
        reduced_global[0],
        reduced_global[1],
        reduced_global[2],
        reduced_global[3],
        reduced_global[4],
        head_sums[0],
        head_sums[1],
        head_sums[2],
        reduced_global[5],
        reduced_global[6],
        reduced_local[5],
        reduced_local[0],
        reduced_local[1],
        reduced_local[6],
        reduced_local[2],
        reduced_local[3],
        reduced_local[4],
    )


MESH = pl.DeviceIdType.MESH
WIDE = 12288
TILE = 32
SMALL_ROWS, SMALL_COLS = 48, 384
EXT = D + 128


def device(z, x, y, c):
    return (z * 2 + x, y * 2 + c)


class Spot:
    def __init__(self, depth):
        dp, fs = lax.axis_index("dp"), lax.axis_index("fsdp")
        self.depth, self.count = depth, depth * 8
        self.me = dp * 4 + fs
        self.z, self.x, self.y, self.c = dp // 2, dp % 2, fs // 2, fs % 2
        self.q = self.x * 4 + self.y * 2 + self.c
        self.plane = self.x * 2 + self.y
        self.column = [(self.z + depth - j) % depth for j in range(depth)]

    def flip(self, way):
        x = 1 - self.x if way & 2 else self.x
        y = 1 - self.y if way & 1 else self.y
        return device(self.z, x, y, self.c), x * 2 + y

    def sibling(self):
        return device(self.z, self.x, self.y, 1 - self.c)

    def above(self, k):
        return device((self.z + k) % self.depth, self.x, self.y, self.c)


def greet(spot):
    barrier = pltpu.get_barrier_semaphore()

    def one(i, carry):
        to = (spot.me + i) % spot.count
        pl.semaphore_signal(barrier, inc=1, device_id=(to // 4, to % 4), device_id_type=MESH)
        return carry

    lax.fori_loop(1, spot.count, one, 0)
    pl.semaphore_wait(barrier, spot.count - 1)


class Wires:
    def __init__(self, send, recv):
        self.send, self.recv, self.used, self.open = send, recv, 0, []

    def copy(self, src, dst, to):
        i = self.used
        self.used += 1
        copy = pltpu.make_async_remote_copy(
            src_ref=src,
            dst_ref=dst,
            send_sem=self.send.at[i],
            recv_sem=self.recv.at[i],
            device_id=to,
            device_id_type=MESH,
        )
        copy.start()
        self.open.append(copy)
        return copy

    def drain(self):
        for copy in self.open:
            copy.wait_send()


def got(copies):
    for copy in copies:
        copy.wait_recv()


class Swap:
    def __init__(self, spot, send, recv, src_at, dst_at):
        self.spot, self.send, self.recv, self.src_at, self.dst_at = spot, send, recv, src_at, dst_at

    def copy(self, i):
        to = (self.spot.me + i) % self.spot.count
        return pltpu.make_async_remote_copy(
            src_ref=self.src_at(to),
            dst_ref=self.dst_at(self.spot.me),
            send_sem=self.send.at[i],
            recv_sem=self.recv.at[i],
            device_id=(to // 4, to % 4),
            device_id_type=MESH,
        )

    def each(self, act):
        def one(i, carry):
            act(self.copy(i))
            return carry

        lax.fori_loop(1, self.spot.count, one, 0)

    def start(self):
        self.each(lambda copy: copy.start())

    def arrive(self):
        self.each(lambda copy: copy.wait_recv())

    def leave(self):
        self.each(lambda copy: copy.wait_send())


def block_row(t, plane, c):
    return (t * 4 + plane) * 2 + c


def spread_all(wires, spot, buf, own=None):
    at = lambda t, plane, c: buf.at[block_row(t, plane, c)]
    mine = at(spot.z, spot.plane, spot.c)
    src = mine if own is None else own
    ring, flat, core = [], [], []
    for k in range(1, spot.depth):
        ring.append(wires.copy(src, mine, spot.above(k)))
    flat.append([wires.copy(src, mine, spot.flip(way)[0]) for way in (1, 2, 3)])
    core.append(wires.copy(src, mine, spot.sibling()))
    yield
    for j in range(1, spot.depth):
        got([ring[j - 1]])
        block = at(spot.column[j], spot.plane, spot.c)
        flat.append([wires.copy(block, block, spot.flip(way)[0]) for way in (1, 2, 3)])
        core.append(wires.copy(block, block, spot.sibling()))
    yield
    for j in range(spot.depth):
        for way in (1, 2, 3):
            got([flat[j][way - 1]])
            block = at(spot.column[j], spot.flip(way)[1], spot.c)
            core.append(wires.copy(block, block, spot.sibling()))
    yield
    got(core)


def spread_plane(wires, spot, buf):
    at = lambda plane: buf.at[plane * 2 + spot.c]
    mine = at(spot.plane)
    flat = [wires.copy(mine, mine, spot.flip(way)[0]) for way in (1, 2, 3)]
    core = [wires.copy(mine, mine, spot.sibling())]
    yield
    for way in (1, 2, 3):
        got([flat[way - 1]])
        block = at(spot.flip(way)[1])
        core.append(wires.copy(block, block, spot.sibling()))
    yield
    got(core)


def sum_plane(wires, spot, parts, pair, near):
    first = wires.copy(parts.at[:, 1 - spot.c], pair, spot.sibling())
    yield None
    got([first])
    f32 = jnp.float32
    pair[...] = (parts[:, spot.c].astype(f32) + pair[...].astype(f32)).astype(jnp.bfloat16)
    flat = [
        wires.copy(pair.at[spot.flip(way)[1]], near.at[way - 1], spot.flip(way)[0]) for way in (1, 2, 3)
    ]
    yield None
    got(flat)
    total = pair[spot.plane].astype(f32)
    for way in range(3):
        total = total + near[way].astype(f32)
    yield total


def sum_all(wires, spot, parts, pair, near, column, far, out):
    f32, low = jnp.float32, jnp.bfloat16
    half = parts.shape[-1] // 2
    cut = [pl.ds(h * half, half) for h in range(2)]
    first = [
        wires.copy(parts.at[:, 1 - spot.c, :, cut[h]], pair.at[:, :, cut[h]], spot.sibling()) for h in range(2)
    ]
    yield
    flat, ring = [], []
    rows = pair.shape[1]
    for h in range(2):
        got([first[h]])
        for b in range(4 * spot.depth):
            pair[b, :, cut[h]] = (
                parts[b, spot.c, :, cut[h]].astype(f32) + pair[b, :, cut[h]].astype(f32)
            ).astype(low)
        step = []
        for way in (1, 2, 3):
            to, plane = spot.flip(way)
            for t in range(spot.depth):
                step.append(
                    wires.copy(pair.at[t * 4 + plane, :, cut[h]], near.at[way - 1, t, :, cut[h]], to)
                )
        flat.append(step)
    yield
    for h in range(2):
        got(flat[h])
        for t in range(spot.depth):
            total = pair[t * 4 + spot.plane, :, cut[h]].astype(f32)
            for way in range(3):
                total = total + near[way, t, :, cut[h]].astype(f32)
            column[t, :, cut[h]] = total.astype(low)
        ring.append(
            [
                wires.copy(
                    column.at[(spot.z + k) % spot.depth, :, cut[h]], far.at[k - 1, :, cut[h]], spot.above(k)
                )
                for k in range(1, spot.depth)
            ]
        )
    yield
    for h in range(2):
        got(ring[h])
        total = column[spot.z, :, cut[h]].astype(f32)
        for k in range(1, spot.depth):
            total = total + far[k - 1, :, cut[h]].astype(f32)
        out[:, cut[h]] = total
    yield


def big_gather(wires, spot, ow, od, shards):
    half, down = WIDE // 2, od.shape[0] // spot.count
    xn, yn, cn, zn = spot.flip(2)[0], spot.flip(1)[0], spot.sibling(), spot.above(1)
    here, xp, yp, xy = spot.plane, spot.flip(2)[1], spot.flip(1)[1], spot.flip(3)[1]

    def refs(t, plane, part):
        r = block_row(t, plane, spot.c)
        wide, deep = pl.multiple_of(r * TILE, TILE), pl.multiple_of(r * down, down)
        if part == "A":
            return [ow.at[pl.ds(wide, TILE), pl.ds(0, half)], od.at[pl.ds(deep, down // 2)]]
        if part == "B":
            return [
                ow.at[pl.ds(wide, TILE), pl.ds(half, half)],
                od.at[pl.ds(pl.multiple_of(deep + down // 2, down // 2), down // 2)],
            ]
        return [ow.at[pl.ds(wide, TILE)], od.at[pl.ds(deep, down)]]

    def go(t, plane, part, to):
        return [wires.copy(r, r, to) for r in refs(t, plane, part)]

    qkv, attn, gate, up, deep = shards
    cols, at = [], 0
    mine = pl.multiple_of(spot.me * TILE, TILE)
    for ref, a, b in ((qkv, 0, 3072), (attn, 0, 1024), (gate, 0, 2048), (gate, 2048, 2048), (up, 0, 4096)):
        cols.append((ref.at[:, pl.ds(a, b)], ow.at[pl.ds(mine, TILE), pl.ds(at, b)]))
        at += b
    row = pl.multiple_of(spot.me * down, down)
    deeps = [
        (deep.at[pl.ds(h * down // 2, down // 2)], od.at[pl.ds(pl.multiple_of(row + h * (down // 2), down // 2), down // 2)])
        for h in range(2)
    ]

    def own(part, to):
        pairs = {"A": cols[:3] + deeps[:1], "B": cols[3:] + deeps[1:], "AB": cols + deeps}[part]
        return [wires.copy(a, b, to) for a, b in pairs]

    T = spot.column
    core, ring, fx, fy, sx, sy = [], {}, {}, {}, {}, {}

    def first(j):
        send = own if j == 0 else (lambda part, to: go(T[j], here, part, to))
        if j < spot.depth - 1:
            ring[j] = send("AB", zn)
        fx[j], fy[j] = send("A", xn), send("B", yn)
        core.append(send("AB", cn))

    def second(j):
        got(fx[j])
        sy[j] = (own("A", yn) if j == 0 else go(T[j], here, "A", yn)) + go(T[j], xp, "A", yn)
        got(fy[j])
        sx[j] = (own("B", xn) if j == 0 else go(T[j], here, "B", xn)) + go(T[j], yp, "B", xn)
        core.append(go(T[j], xp, "A", cn) + go(T[j], yp, "B", cn))

    def third(j):
        got(sy[j])
        core.append(go(T[j], yp, "A", cn) + go(T[j], xy, "A", cn))
        got(sx[j])
        core.append(go(T[j], xp, "B", cn) + go(T[j], xy, "B", cn))

    first(0)
    yield
    for j in range(1, spot.depth):
        second(j - 1)
        yield
        got(ring[j - 1])
        first(j)
        yield
        if j >= 2:
            third(j - 2)
            yield
    second(spot.depth - 1)
    yield
    third(spot.depth - 2)
    third(spot.depth - 1)
    yield
    for copies in core:
        got(copies)
    yield


def ticker(steps, plan):
    counts = iter(plan)

    def tick():
        for _ in range(next(counts)):
            next(steps, None)

    return tick


def run(steps):
    for _ in steps:
        pass


def sigmoid(v):
    return 1.0 / (1.0 + jnp.exp(-v))


def lanes(shape, axis):
    return lax.broadcasted_iota(jnp.int32, shape, axis)


def flat_dot(a, b, dims=((1,), (0,))):
    return lax.dot_general(a, b, (dims, ((), ())), preferred_element_type=jnp.float32)


def exact_dot(a, b):
    return jnp.dot(a, b, precision=HIGHEST, preferred_element_type=jnp.float32)


def gain_row(values):
    n_dev, width = values.shape[0], D // values.shape[0]
    spread = (lanes((128, D), 0) == lanes((128, D), 1) & (width - 1)).astype(jnp.bfloat16)
    rows = flat_dot(values, spread)
    return jnp.sum(jnp.where(lanes((n_dev, D), 0) == lanes((n_dev, D), 1) >> (width.bit_length() - 1), rows, 0.0), axis=0, keepdims=True)


def tap_rows(spot, small):
    n_dev = spot.count
    share = CONV_CH // n_dev
    col = lanes((1, 512), 1)
    channel = jnp.where(col < 256, (spot.q + 8 * (col >> 6)) * HEAD_M + (col & 63), DI + col - 256)
    dev = lanes((n_dev, 512), 0)
    picks = (channel >= dev * share) & (channel < dev * share + share)
    owner = jnp.sum(jnp.where(picks, dev, 0), axis=0, keepdims=True)
    within = lanes((128, 512), 0) == channel - owner * share
    rows = []
    for k in range(CONV + 1):
        values = small[:, TILE + k, 0:128]
        spread = flat_dot(values, picks.astype(jnp.bfloat16), ((0,), (0,)))
        rows.append(jnp.sum(jnp.where(within, spread, 0.0), axis=0, keepdims=True))
    return rows


def entry(block, row, lane):
    at = (lanes(block.shape, 0) == row) & (lanes(block.shape, 1) == lane)
    return jnp.sum(jnp.where(at, block.astype(jnp.float32), 0.0), keepdims=True).reshape(1, 1)


class Slot:
    def __init__(self, spot, small, x, count):
        block = small[(spot.z * 2 + x) * 4, TILE : TILE + 16, 0:128].astype(jnp.float32)
        first = entry(block, 9, 0)
        second = first + entry(block, 9, 1)
        number = lambda p: (p >= first).astype(jnp.float32) + (p >= second).astype(jnp.float32)
        col = lanes((count, 1), 0).astype(jnp.float32)
        row = lanes((1, count), 1).astype(jnp.float32)
        docs = number(col)
        self.keep = (col >= row) & (docs == number(row))
        self.same = [((col >= s) & (number(col - s) == docs)).astype(jnp.float32) for s in range(CONV)]


def shift(block, by):
    return block if by == 0 else pltpu.roll(block, by % block.shape[0], 0)


class Mixed:
    def __init__(self, spot, slot, own, maps, step_raw, taps, dt_row, rate_row):
        count = own.shape[0]
        self.spot, self.slot, self.count = spot, slot, count
        self.channels = jnp.concatenate([own[:, 256:], maps], axis=1)
        conv = taps[CONV] + sum(
            taps[CONV - 1 - s] * (shift(self.channels, s) * slot.same[s]) for s in range(CONV)
        )
        self.conv, self.sig = conv, sigmoid(conv)
        act = conv * self.sig
        self.inputs = act[:, :256]
        self.in_map, self.out_map = act[:, 256:384].astype(jnp.bfloat16), act[:, 384:].astype(jnp.bfloat16)
        self.raw = step_raw + dt_row
        self.step = jnp.where(self.raw > 20.0, self.raw, jnp.log(1.0 + jnp.exp(jnp.minimum(self.raw, 20.0))))
        lower = lanes((count, count), 0) >= lanes((count, count), 1)
        self.upper = (lanes((count, count), 0) <= lanes((count, count), 1)).astype(jnp.float32)
        self.cum = exact_dot(lower.astype(jnp.float32), self.step * rate_row)
        self.cum_t, self.step_t = self.cum.T, self.step.T
        self.inner = flat_dot(self.out_map, self.in_map, ((1,), (1,)))

    def head(self, i):
        return self.spot.q + 8 * i

    def col(self, by_head, i):
        return jnp.sum(jnp.where(lanes((1, 128), 1) == self.head(i), by_head, 0.0), axis=1, keepdims=True)

    def row(self, by_head_t, i):
        return jnp.sum(jnp.where(lanes((128, 1), 0) == self.head(i), by_head_t, 0.0), axis=0, keepdims=True)

    def decay(self, i):
        gap = jnp.where(self.slot.keep, self.col(self.cum, i) - self.row(self.cum_t, i), 0.0)
        return jnp.where(self.slot.keep, jnp.exp(gap), 0.0)


def pick_lane(row, lane):
    return jnp.sum(jnp.where(lanes(row.shape, 1) == lane, row, 0.0), axis=1, keepdims=True)


N_WIRES = 256
PLAN_F = (1, 1, 1, 0, 1, 1, 1, 1, 1, 1, 0, 1, 0, 1, 0)
PLAN_B = (1, 1, 1, 1, 1, 1, 1, 0, 1, 1, 0, 1, 1, 1, 0, 0, 0, 0, 1)


def forward_kernel(
    depth,
    rows_ref,
    patch_ref,
    cols_ref,
    vec_ref,
    out_ref,
    heads_ref,
    qkv,
    attn,
    gate,
    up,
    down,
    ow,
    od,
    sum_ref,
    mixed_ref,
    small_ref,
    bytes_ref,
    norm_ref,
    proj_ref,
    head_w_ref,
    own_ref,
    maps_ref,
    step_ref,
    core_ref,
    parts,
    pair,
    near,
    column,
    far,
    parts8,
    pair8,
    near8,
    send,
    recv,
    swap_send,
    swap_recv,
    local,
):
    f32, low = jnp.float32, jnp.bfloat16
    spot = Spot(depth)
    count = 128
    wires = Wires(send, recv)
    mine = pl.multiple_of(spot.me * TILE, TILE)
    bytes_ref[pl.ds(mine, TILE)] = rows_ref[:, pl.ds(pl.multiple_of(spot.me * 256, 256), 256)]
    small_ref[spot.me] = vec_ref[...]
    proj_ref[pl.ds(mine, TILE)] = cols_ref[spot.q]
    head_w_ref[spot.z] = out_ref[...]
    greet(spot)

    def lanes_of(to):
        return rows_ref.at[:, pl.ds(pl.multiple_of(to * 256, 256), 256)]

    swap_bytes = Swap(
        spot,
        swap_send.at[0],
        swap_recv.at[0],
        lanes_of,
        lambda me: bytes_ref.at[pl.ds(pl.multiple_of(me * TILE, TILE), TILE)],
    )
    swap_bytes.start()
    big = big_gather(wires, spot, ow, od, (qkv, attn, gate, up, down))
    swap_proj = Swap(
        spot,
        swap_send.at[1],
        swap_recv.at[1],
        lambda to: cols_ref.at[to % 8],
        lambda me: proj_ref.at[pl.ds(pl.multiple_of(me * TILE, TILE), TILE)],
    )
    swap_proj.start()
    small = spread_all(wires, spot, small_ref)
    next(small)
    head_w = [wires.copy(out_ref, head_w_ref.at[spot.z], spot.above(k)) for k in range(1, depth)]
    tick = ticker(big, PLAN_F)
    tick()
    own_rows = []
    at = 0
    for i, ref in enumerate((qkv, attn, gate, up)):
        width = ref.shape[1]
        own_rows.append(pltpu.make_async_copy(ref, ow.at[pl.ds(mine, TILE), pl.ds(at, width)], local.at[i]))
        at += width
    deep = down.shape[0]
    own_rows.append(
        pltpu.make_async_copy(down, od.at[pl.ds(pl.multiple_of(spot.me * deep, deep), deep)], local.at[4])
    )
    for copy in own_rows:
        copy.start()
    tick()
    swap_bytes.arrive()

    for b in range(4):
        block = flat_dot(bytes_ref[pl.ds(b * 256, 256)], patch_ref[...]).astype(low)
        parts[pl.ds(b * 4, 4)] = block.reshape(4, 2, TILE, D)
    tick()
    total = sum_all(wires, spot, parts, pair, near, column, far, sum_ref)
    next(total)
    next(small)
    tick()
    next(total)
    tick()
    next(total)
    next(small)
    tick()
    next(total)
    tick()
    run(small)
    patch_sum = sum_ref[...]
    scale = lax.rsqrt(jnp.mean(patch_sum * patch_sum, axis=1, keepdims=True) + EPSILON)
    gain = gain_row(small_ref[:, TILE + 5, 0:128])
    norm_ref[spot.q] = (patch_sum * scale * gain).astype(low)
    plane = spread_plane(wires, spot, norm_ref)
    next(plane)
    tick()
    next(plane)
    tick()
    swap_proj.arrive()
    taps = tap_rows(spot, small_ref)
    run(plane)
    tick()

    norm = norm_ref[...].reshape(2 * count, D)
    own_ref[...] = flat_dot(norm, proj_ref[...])
    maps_ref[...] = flat_dot(norm, small_ref[:, :TILE, 0:256].reshape(D, 256))
    step_ref[...] = flat_dot(norm, small_ref[:, :TILE, 256:384].reshape(D, 128))
    dt_row, rate_row, skip_row = heads_ref[0:1], heads_ref[1:2], heads_ref[2:3]
    tick()
    got(head_w)
    gains = jnp.concatenate(
        [small_ref[spot.q + 8 * i, TILE : TILE + 16, 0:HEAD_M][6:7].astype(f32) for i in range(4)], axis=1
    )
    for x in range(2):
        at = pl.ds(x * count, count)
        slot = Slot(spot, small_ref, x, count)
        own, maps = own_ref[at], maps_ref[at]
        mix = Mixed(spot, slot, own, maps, step_ref[at], taps, dt_row, rate_row)
        outs = []
        for i in range(4):
            inputs = mix.inputs[:, i * HEAD_M : (i + 1) * HEAD_M]
            mixing = (mix.decay(i) * mix.inner * mix.row(mix.step_t, i)).astype(low)
            skip = pick_lane(skip_row, mix.head(i))
            outs.append(flat_dot(mixing, inputs.astype(low)) + skip * inputs)
        core = jnp.concatenate(outs, axis=1)
        core_ref[at] = core
        raw = own[:, :256]
        gated = core * raw * sigmoid(raw)
        part = flat_dot((gated * gains).astype(low), head_w_ref[...].reshape(256, D))
        squares = jnp.sum(gated * gated, axis=1, keepdims=True)
        parts8[pl.ds(x * 2, 2), :, :, pl.ds(0, D)] = part.astype(low).reshape(2, 2, TILE, D)
        parts8[pl.ds(x * 2, 2), :, :, pl.ds(D, 128)] = (
            jnp.broadcast_to(squares, (count, 128)).astype(low).reshape(2, 2, TILE, 128)
        )
        tick()
    for total in sum_plane(wires, spot, parts8, pair8, near8):
        if total is None:
            tick()
    mixed_ref[...] = total
    for copy in own_rows:
        copy.wait()
    run(big)
    wires.drain()
    swap_bytes.leave()
    swap_proj.leave()


def forward_call(depth, n_dev, rows2, patch_proj, cols, vectors, out_proj, heads, qkv, attn, gate, up, down):
    f32, low = jnp.float32, jnp.bfloat16
    vmem = pl.BlockSpec(memory_space=pltpu.VMEM)
    anywhere = pl.BlockSpec(memory_space=pl.ANY)
    shape = jax.ShapeDtypeStruct
    plane_patches = 8 * TILE
    outs = [
        shape((D, WIDE), low),
        shape((down.shape[0] * n_dev, D), low),
        shape((TILE, D), f32),
        shape((TILE, EXT), f32),
        shape((n_dev, SMALL_ROWS, SMALL_COLS), low),
        shape((n_dev * TILE, 256), low),
        shape((8, TILE, D), low),
        shape((n_dev * TILE, 512), low),
        shape((depth, HEAD_M, D), low),
        shape((plane_patches, 512), f32),
        shape((plane_patches, 256), f32),
        shape((plane_patches, 128), f32),
        shape((plane_patches, 256), f32),
    ]
    scratch = [
        pltpu.VMEM((16, 2, TILE, D), low),
        pltpu.VMEM((16, TILE, D), low),
        pltpu.VMEM((3, depth, TILE, D), low),
        pltpu.VMEM((depth, TILE, D), low),
        pltpu.VMEM((depth - 1, TILE, D), low),
        pltpu.VMEM((4, 2, TILE, EXT), low),
        pltpu.VMEM((4, TILE, EXT), low),
        pltpu.VMEM((3, TILE, EXT), low),
        pltpu.SemaphoreType.DMA((N_WIRES,)),
        pltpu.SemaphoreType.DMA((N_WIRES,)),
        pltpu.SemaphoreType.DMA((2, n_dev)),
        pltpu.SemaphoreType.DMA((2, n_dev)),
        pltpu.SemaphoreType.DMA((5,)),
    ]
    return pl.pallas_call(
        partial(forward_kernel, depth),
        out_shape=outs,
        in_specs=[vmem] * 6 + [anywhere] * 5,
        out_specs=[anywhere] * 2 + [vmem] * 11,
        scratch_shapes=scratch,
        compiler_params=pltpu.CompilerParams(
            collective_id=0, has_side_effects=True, vmem_limit_bytes=56 * 2**20
        ),
        name="global_forward",
    )(rows2, patch_proj, cols, vectors, out_proj, heads, qkv, attn, gate, up, down)


PARTS = ((0, 3072), (3072, 1024), (4096, 4096), (8192, 4096))
STEP = 1024


def add_to(dst, sources, width):
    def one(i, carry):
        at = pl.ds(pl.multiple_of(i * STEP, STEP), STEP)
        total = sources[0](at).astype(jnp.float32)
        for source in sources[1:]:
            total = total + source(at).astype(jnp.float32)
        dst(at, total)
        return carry

    lax.fori_loop(0, width // STEP, one, 0)


def big_scatter(wires, spot, grads, bufs, outs, local):
    f32, low = jnp.float32, jnp.bfloat16
    held_w, held_d, stage_w, stage_d, near_w, near_d, last_w, last_d, ring_w, ring_d = bufs
    half, deep = WIDE // 2, held_d.shape[2]
    xn, yn, cn, zn = spot.flip(2)[0], spot.flip(1)[0], spot.sibling(), spot.above(1)
    here, xp, yp, xy = spot.plane, spot.flip(2)[1], spot.flip(1)[1], spot.flip(3)[1]
    T = [spot.column[k % spot.depth] for k in range(1, spot.depth + 1)]
    core, fetch, near, last, ring = {}, {}, {}, {}, {}
    A, B = pl.ds(0, half), pl.ds(half, half)
    DA, DB = pl.ds(0, deep // 2), pl.ds(deep // 2, deep // 2)

    def load(k):
        fetch[k] = []
        for i, ref in enumerate(grads):
            dst = stage_w.at[:, :, pl.ds(*PARTS[i])] if i < 4 else stage_d
            copy = pltpu.make_async_copy(ref.at[T[k], :, spot.c], dst, local.at[k * 5 + i])
            copy.start()
            fetch[k].append(copy)

    def open_core(k):
        core[k] = []
        for i, ref in enumerate(grads):
            dst = held_w.at[T[k], :, :, pl.ds(*PARTS[i])] if i < 4 else held_d.at[T[k]]
            core[k].append(wires.copy(ref.at[T[k], :, 1 - spot.c], dst, cn))

    def first(k):
        t = T[k]
        got(core[k])
        for copy in fetch[k]:
            copy.wait()
        for plane in range(4):

            def put_w(at, total, plane=plane):
                held_w[t, plane, :, at] = total.astype(low)

            add_to(put_w, [lambda at, p=plane: held_w[t, p, :, at], lambda at, p=plane: stage_w[p, :, at]], WIDE)
            held_d[t, plane] = (held_d[t, plane].astype(f32) + stage_d[plane].astype(f32)).astype(low)
        if k + 1 < spot.depth:
            load(k + 1)
        near[k] = []
        for x in range(2):
            src = x * 2 + (1 - spot.y)
            near[k].append(wires.copy(held_w.at[t, src, :, A], near_w.at[k, x, :, A], yn))
            near[k].append(wires.copy(held_d.at[t, src, DA], near_d.at[k, x, DA], yn))
        for y in range(2):
            src = (1 - spot.x) * 2 + y
            near[k].append(wires.copy(held_w.at[t, src, :, B], near_w.at[k, y, :, B], xn))
            near[k].append(wires.copy(held_d.at[t, src, DB], near_d.at[k, y, DB], xn))

    def second(k):
        t = T[k]
        got(near[k])
        for other in range(2):
            pa, pb = other * 2 + spot.y, spot.x * 2 + other

            def put_a(at, total, pa=pa):
                held_w[t, pa, :, at] = total.astype(low)

            def put_b(at, total, pb=pb):
                held_w[t, pb, :, pl.ds(pl.multiple_of(at.start + half, STEP), STEP)] = total.astype(low)

            shifted_by = lambda at: pl.ds(pl.multiple_of(at.start + half, STEP), STEP)
            add_to(put_a, [lambda at, p=pa: held_w[t, p, :, at], lambda at, o=other: near_w[k, o, :, at]], half)
            add_to(
                put_b,
                [
                    lambda at, p=pb: held_w[t, p, :, shifted_by(at)],
                    lambda at, o=other: near_w[k, o, :, shifted_by(at)],
                ],
                half,
            )
            held_d[t, pa, DA] = (held_d[t, pa, DA].astype(f32) + near_d[k, other, DA].astype(f32)).astype(low)
            held_d[t, pb, DB] = (held_d[t, pb, DB].astype(f32) + near_d[k, other, DB].astype(f32)).astype(low)
        last[k] = [
            wires.copy(held_w.at[t, xp, :, A], last_w.at[k, :, A], xn),
            wires.copy(held_d.at[t, xp, DA], last_d.at[k, DA], xn),
            wires.copy(held_w.at[t, yp, :, B], last_w.at[k, :, B], yn),
            wires.copy(held_d.at[t, yp, DB], last_d.at[k, DB], yn),
        ]

    def third(k):
        t = T[k]
        got(last[k])
        if k:
            got(ring[k - 1])
        terms = [lambda at: held_w[t, here, :, at], lambda at: last_w[k, :, at]]
        if k:
            terms.append(lambda at: ring_w[k - 1, :, at])
        down = held_d[t, here].astype(f32) + last_d[k].astype(f32)
        if k:
            down = down + ring_d[k - 1].astype(f32)
        if k < spot.depth - 1:

            def put_on(at, total):
                held_w[t, here, :, at] = total.astype(low)

            add_to(put_on, terms, WIDE)
            held_d[t, here] = down.astype(low)
            ring[k] = [
                wires.copy(held_w.at[t, here], ring_w.at[k], zn),
                wires.copy(held_d.at[t, here], ring_d.at[k], zn),
            ]
        else:
            for out, (begin, width) in zip(outs, PARTS):

                def put_out(at, total, out=out):
                    out[:, at] = total

                add_to(
                    put_out,
                    [
                        lambda at, f=f, b=begin: f(pl.ds(pl.multiple_of(at.start + b, STEP), STEP))
                        for f in terms
                    ],
                    width,
                )
            outs[4][...] = down

    load(0)
    for k in range(spot.depth):
        open_core(k)
    yield
    steps = [(first, 0)]
    n = spot.depth
    for k in range(1, n + 2):
        for step, lag in ((first, 0), (second, 1), (third, 2)):
            if 0 <= k - lag < n:
                steps.append((step, k - lag))
    for step, k in steps:
        step(k)
        yield


class Back:
    def __init__(self, mix, own, core, ext, d_patch, gains, head_w, heads, taps):
        f32, low = jnp.float32, jnp.bfloat16
        count = mix.count
        dt_row, rate_row, skip_row = heads[0:1], heads[1:2], heads[2:3]
        r = ext[:, 0:1] + ext[:, 2:3]
        along = ext[:, 1:2] + ext[:, 3:4]
        raw = own[:, :256]
        sig = sigmoid(raw)
        gated = core * raw * sig
        back = flat_dot(d_patch, head_w, ((1,), (1,)))
        self.norm = (gated * r * gains).astype(low)
        self.gain = jnp.sum(back * gated * r, axis=0, keepdims=True)
        d_gated = r * gains * back - gated * (r * r * r * along * (1.0 / DI))
        d_core = d_gated * raw * sig
        d_gate = d_gated * core * sig * (1.0 + raw * (1.0 - sig))
        lane = lanes((1, 128), 1)
        graph = jnp.zeros((count, count), f32)
        d_inputs = []
        direct = jnp.zeros((count, 128), f32)
        flow = jnp.zeros((count, 128), f32)
        d_skip = jnp.zeros((1, 128), f32)
        for i in range(4):
            cut = slice(i * HEAD_M, (i + 1) * HEAD_M)
            inputs, grad = mix.inputs[:, cut], d_core[:, cut]
            decay, step = mix.decay(i), mix.row(mix.step_t, i)
            kept = decay * mix.inner
            skip = pick_lane(skip_row, mix.head(i))
            d_mixing = flat_dot(grad.astype(low), inputs.astype(low), ((1,), (1,)))
            d_inputs.append(
                flat_dot((kept * step).astype(low), grad.astype(low), ((0,), (0,))) + skip * grad
            )
            graph = graph + decay * step * d_mixing
            turn = kept * d_mixing
            arrive = jnp.sum(turn.T, axis=1, keepdims=True)
            leave = jnp.sum(turn * step, axis=1, keepdims=True)
            here = lane == mix.head(i)
            direct = direct + jnp.where(here, arrive, 0.0)
            flow = flow + jnp.where(here, leave - mix.col(mix.step, i) * arrive, 0.0)
            d_skip = d_skip + jnp.where(here, jnp.sum(grad * inputs, keepdims=True).reshape(1, 1), 0.0)
        tail = exact_dot(mix.upper, flow)
        mine = own_lanes(lane, mix)
        d_step = jnp.where(mine, direct + rate_row * tail, 0.0)
        d_raw = d_step * sigmoid(mix.raw)
        self.skip = d_skip
        self.rate = jnp.sum(rate_row * mix.step * jnp.where(mine, tail, 0.0), axis=0, keepdims=True)
        self.bias = jnp.sum(d_raw, axis=0, keepdims=True)
        low_graph = graph.astype(low)
        d_out_map = flat_dot(low_graph, mix.in_map)
        d_in_map = flat_dot(low_graph, mix.out_map, ((0,), (0,)))
        d_act = jnp.concatenate(d_inputs + [d_in_map, d_out_map], axis=1)
        d_conv = d_act * (mix.sig * (1.0 + mix.conv * (1.0 - mix.sig)))
        d_channels = jnp.zeros_like(d_conv)
        self.taps = [None] * CONV + [jnp.sum(d_conv, axis=0, keepdims=True)]
        for s in range(CONV):
            kept = d_conv * mix.slot.same[s]
            d_channels = d_channels + taps[CONV - 1 - s] * shift(kept, -s)
            self.taps[CONV - 1 - s] = jnp.sum(kept * shift(mix.channels, s), axis=0, keepdims=True)
        self.rows = jnp.concatenate([d_gate, d_channels, d_raw], axis=1).astype(low)


def own_lanes(lane, mix):
    mine = lane == mix.head(0)
    for i in range(1, 4):
        mine = mine | (lane == mix.head(i))
    return mine


COLS = 512 + 256 + 128


def backward_kernel(
    depth,
    mix_ref,
    direct_ref,
    sum_ref,
    gains_ref,
    small_ref,
    bytes_ref,
    norm_ref,
    proj_ref,
    head_w_ref,
    own_ref,
    maps_ref,
    step_ref,
    core_ref,
    patch_ref,
    heads_ref,
    g_qkv,
    g_attn,
    g_gate,
    g_up,
    g_down,
    o_qkv,
    o_attn,
    o_gate,
    o_up,
    o_down,
    o_patch,
    o_rows,
    o_head,
    o_cols,
    o_maps,
    all_ref,
    mix_all,
    rows_all,
    head_sum,
    head_low,
    head_far,
    col_send,
    col_recv,
    back_send,
    parts8,
    pair8,
    near8,
    held_w,
    held_d,
    stage_w,
    stage_d,
    near_w,
    near_d,
    last_w,
    last_d,
    ring_w,
    ring_d,
    send,
    recv,
    swap_send,
    swap_recv,
    local,
):
    f32, low = jnp.float32, jnp.bfloat16
    spot = Spot(depth)
    count = 128
    wires = Wires(send, recv)
    mix_all[spot.q] = mix_ref[...]
    greet(spot)
    plane = spread_plane(wires, spot, mix_all)
    next(plane)
    big = big_scatter(
        wires,
        spot,
        (g_qkv, g_attn, g_gate, g_up, g_down),
        (held_w, held_d, stage_w, stage_d, near_w, near_d, last_w, last_d, ring_w, ring_d),
        (o_qkv, o_attn, o_gate, o_up, o_down),
        local,
    )
    tick = ticker(big, PLAN_B)
    tick()
    next(plane)
    tick()
    taps = tap_rows(spot, small_ref)
    heads = heads_ref[...]
    dt_row, rate_row = heads[0:1], heads[1:2]
    gains = jnp.concatenate(
        [small_ref[spot.q + 8 * i, TILE : TILE + 16, 0:HEAD_M][6:7].astype(f32) for i in range(4)], axis=1
    )
    gain = gain_row(small_ref[:, TILE + 5, 0:128])
    run(plane)
    tick()
    sums = None
    for x in range(2):
        at = pl.ds(x * count, count)
        slot = Slot(spot, small_ref, x, count)
        mix = Mixed(spot, slot, own_ref[at], maps_ref[at], step_ref[at], taps, dt_row, rate_row)
        d_patch = mix_all[pl.ds(x * 4, 4), :, pl.ds(0, D)].reshape(count, D)
        ext = mix_all[pl.ds(x * 4, 4), :, pl.ds(D, 128)].reshape(count, 128).astype(f32)
        back = Back(
            mix, own_ref[at], core_ref[at], ext, d_patch, gains, head_w_ref[...].reshape(256, D), heads, taps
        )
        rows_all[at] = back.rows
        tick()
        head = flat_dot(back.norm, d_patch, ((0,), (0,)))
        head_sum[...] = head if x == 0 else head_sum[...] + head
        new = [*back.taps, back.gain, back.bias, back.rate, back.skip]
        sums = new if sums is None else [a + b for a, b in zip(sums, new)]
        grad = flat_dot(back.rows[:, :512], proj_ref[...], ((1,), (1,)))
        grad = grad + flat_dot(
            back.rows[:, 512:], small_ref[:, :TILE, :].reshape(D, SMALL_COLS), ((1,), (1,))
        )
        parts8[pl.ds(x * 2, 2)] = grad.astype(low).reshape(2, 2, TILE, D)
        tick()
    total8 = sum_plane(wires, spot, parts8, pair8, near8)
    next(total8)
    tick()
    head_low[...] = head_sum[...].astype(low).reshape(depth, HEAD_M, D)
    head_ring = [
        wires.copy(head_low.at[(spot.z + k) % depth], head_far.at[k - 1], spot.above(k)) for k in range(1, depth)
    ]
    next(total8)
    tick()
    norm = norm_ref[...].reshape(2 * count, D)
    rows = rows_all[...]
    for b in range(4):
        block = flat_dot(norm[:, b * 256 : (b + 1) * 256], rows, ((0,), (0,)))
        col_send[pl.ds(b * 8, 8)] = block.astype(low).reshape(8, TILE, COLS)
    swap_cols = Swap(
        spot, swap_send.at[0], swap_recv.at[0], lambda to: col_send.at[to], lambda me: col_recv.at[me]
    )
    tick()
    grad_norm = next(total8)
    tick()
    patch_sum = sum_ref[...]
    scale = lax.rsqrt(jnp.mean(patch_sum * patch_sum, axis=1, keepdims=True) + EPSILON)
    along = jnp.mean(grad_norm * gain * patch_sum, axis=1, keepdims=True)
    d_sum = direct_ref[...] + scale * gain * grad_norm - patch_sum * (scale * scale * scale * along)
    gain_sum = jnp.sum(grad_norm * patch_sum * scale, axis=0, keepdims=True)
    wide = lambda row: jnp.concatenate([row, jnp.zeros((1, D - row.shape[1]), f32)], axis=1)
    lines = [wide(row) for row in sums[: CONV + 1]]
    lines += [wide(jnp.concatenate(sums[CONV + 1 :], axis=1)), gains_ref[0:1], gains_ref[1:2], gain_sum]
    lines += [jnp.zeros((16 - len(lines), D), f32)]
    all_ref[spot.me] = jnp.concatenate([d_sum, *lines], axis=0).astype(low)
    spread = spread_all(wires, spot, all_ref)
    next(spread)
    swap_cols.start()
    col_recv[spot.me] = col_send[spot.me]
    tick()
    next(spread)
    tick()
    next(spread)
    tick()
    run(spread)
    tick()
    d_all = all_ref[:, :TILE].reshape(-1, D)
    for b in range(4):
        back_send[pl.ds(b * 8, 8)] = (
            flat_dot(d_all[b * 256 : (b + 1) * 256], patch_ref[...], ((1,), (1,))).astype(low).reshape(8, TILE, 256)
        )
    swap_rows = Swap(
        spot,
        swap_send.at[1],
        swap_recv.at[1],
        lambda to: back_send.at[to],
        lambda me: o_rows.at[:, pl.ds(pl.multiple_of(me * 256, 256), 256)],
    )
    swap_rows.start()
    tick()
    o_rows[:, pl.ds(pl.multiple_of(spot.me * 256, 256), 256)] = back_send[spot.me]
    o_patch[...] = flat_dot(bytes_ref[...], d_all, ((0,), (0,)))
    tick()
    got(head_ring)
    total = head_low[spot.z].astype(f32)
    for k in range(depth - 1):
        total = total + head_far[k].astype(f32)
    o_head[...] = total
    tick()
    swap_cols.arrive()
    for q in range(8):
        total = col_recv[q, :, :512].astype(f32)
        for t in range(1, depth):
            total = total + col_recv[t * 8 + q, :, :512].astype(f32)
        o_cols[q] = total
    total = jnp.zeros((TILE, COLS - 512), f32)
    for e in range(spot.count):
        total = total + col_recv[e, :, 512:].astype(f32)
    o_maps[...] = total
    tick()
    run(big)
    swap_rows.arrive()
    wires.drain()
    swap_cols.leave()
    swap_rows.leave()


def backward_call(depth, n_dev, mix, direct, patch_sum, gains, saved, patch_proj, heads, grads):
    f32, low = jnp.float32, jnp.bfloat16
    vmem = pl.BlockSpec(memory_space=pltpu.VMEM)
    anywhere = pl.BlockSpec(memory_space=pl.ANY)
    shape = jax.ShapeDtypeStruct
    deep = grads[4].shape[0] // n_dev
    cut = [g.reshape(depth, 4, 2, g.shape[0] // n_dev, g.shape[1]) for g in grads]
    outs = [shape((TILE, width), f32) for _, width in PARTS] + [
        shape((deep, D), f32),
        shape((256, D), f32),
        shape((TILE, PATCH * D), low),
        shape((HEAD_M, D), f32),
        shape((8, TILE, 512), f32),
        shape((TILE, COLS - 512), f32),
        shape((n_dev, SMALL_ROWS, D), low),
    ]
    scratch = [
        pltpu.VMEM((8, TILE, EXT), low),
        pltpu.VMEM((8 * TILE, COLS), low),
        pltpu.VMEM((256, D), f32),
        pltpu.VMEM((depth, HEAD_M, D), low),
        pltpu.VMEM((depth - 1, HEAD_M, D), low),
        pltpu.VMEM((n_dev, TILE, COLS), low),
        pltpu.VMEM((n_dev, TILE, COLS), low),
        pltpu.VMEM((n_dev, TILE, 256), low),
        pltpu.VMEM((4, 2, TILE, D), low),
        pltpu.VMEM((4, TILE, D), low),
        pltpu.VMEM((3, TILE, D), low),
        pltpu.VMEM((depth, 4, TILE, WIDE), low),
        pltpu.VMEM((depth, 4, deep, D), low),
        pltpu.VMEM((4, TILE, WIDE), low),
        pltpu.VMEM((4, deep, D), low),
        pltpu.VMEM((depth, 2, TILE, WIDE), low),
        pltpu.VMEM((depth, 2, deep, D), low),
        pltpu.VMEM((depth, TILE, WIDE), low),
        pltpu.VMEM((depth, deep, D), low),
        pltpu.VMEM((depth - 1, TILE, WIDE), low),
        pltpu.VMEM((depth - 1, deep, D), low),
        pltpu.SemaphoreType.DMA((N_WIRES,)),
        pltpu.SemaphoreType.DMA((N_WIRES,)),
        pltpu.SemaphoreType.DMA((2, n_dev)),
        pltpu.SemaphoreType.DMA((2, n_dev)),
        pltpu.SemaphoreType.DMA((5 * depth,)),
    ]
    return pl.pallas_call(
        partial(backward_kernel, depth),
        out_shape=outs,
        in_specs=[vmem] * 15 + [anywhere] * 5,
        out_specs=[vmem] * 11,
        scratch_shapes=scratch,
        compiler_params=pltpu.CompilerParams(
            collective_id=1, has_side_effects=True, vmem_limit_bytes=62 * 2**20
        ),
        name="global_backward",
    )(mix, direct, patch_sum, gains, *saved, patch_proj, heads, *cut)


def patch_pairs(count):
    i, j = lanes((count, count), 0), lanes((count, count), 1)
    return (i >= j) & ((i >> 3) == (j >> 3))


def rms_back(value, gain, grad):
    scale = lax.rsqrt(jnp.mean(value * value, axis=1, keepdims=True) + EPSILON)
    along = jnp.mean(grad * gain * value, axis=1, keepdims=True)
    d_value = scale * gain * grad - value * (scale * scale * scale * along)
    return d_value, jnp.sum(grad * value * scale, axis=0, keepdims=True)


def halves_of(block):
    left = lanes(block.shape, 1) < HEAD
    return left, [jnp.where(left, block, 0), jnp.where(left, 0, block)]


def local_kernel(
    lengths,
    bytes_ref,
    grad_ref,
    sum_ref,
    mixed_ref,
    small_ref,
    wide,
    deep,
    o_block,
    o_streams,
    o_mix,
    o_direct,
    o_gains,
    g_qkv,
    g_attn,
    g_gate,
    g_up,
    g_down,
    attn_w,
    ffn_w,
    g_buf,
    streams,
    normed,
    qkv,
    weights,
    heads,
    attended,
    ffn_low,
    ffn_t,
    total,
    d_ffn,
    d_down,
    load_sem,
    ffn_sem,
    g_sem,
):
    f32, low = jnp.float32, jnp.bfloat16
    rows = bytes_ref.shape[0]
    scale = HEAD ** (-0.5)
    load = pltpu.make_async_copy(wide.at[:, pl.ds(0, 4 * D)], attn_w, load_sem.at[0])
    load.start()

    def ffn_loads(j, slot):
        at = lambda base: pl.ds(pl.multiple_of(base + j * D, D), D)
        return [
            pltpu.make_async_copy(wide.at[:, at(4 * D)], ffn_w.at[slot, 0], ffn_sem.at[slot, 0]),
            pltpu.make_async_copy(wide.at[:, at(8 * D)], ffn_w.at[slot, 1], ffn_sem.at[slot, 1]),
            pltpu.make_async_copy(deep.at[at(0)], ffn_w.at[slot, 2], ffn_sem.at[slot, 2]),
        ]

    for copy in ffn_loads(0, 0):
        copy.start()
    gain_a = gain_row(small_ref[:, TILE + 7, 0:128])
    gain_f = gain_row(small_ref[:, TILE + 8, 0:128])
    place = lax.axis_index("fsdp") * (rows // PATCH) + (lanes((rows, 1), 0) >> 3)
    live = (place < lengths[0, 0] + lengths[0, 1]).astype(f32)
    raw = mixed_ref[:, pl.ds(0, D)]
    mixer_r = lax.rsqrt(mixed_ref[:, pl.ds(D, 128)] * (1.0 / DI) + EPSILON)[:, 0:1]
    patch = sum_ref[...] + raw * mixer_r
    patch = jnp.broadcast_to(patch[:, None, :], (rows // PATCH, PATCH, D)).reshape(rows, D)
    streams[...] = bytes_ref[...].astype(f32) + patch
    normed[...] = rms_scale(streams[...], gain_a).astype(low)
    d_down[...] = (live * grad_ref[...].astype(f32)).astype(low)
    load.wait()
    for i in range(3):
        at = pl.ds(i * D, D)
        qkv[:, at] = flat_dot(normed[...], attn_w[:, at]).astype(low)
    pairs = patch_pairs(128)

    def blocks(p, b):
        row = pl.ds(b * 128, 128)
        return row, [pl.ds(pl.multiple_of(base + p * 128, 128), 128) for base in (0, D, 2 * D)]

    def attend(p, carry):
        for b in range(rows // 128):
            row, (qa, ka, va) = blocks(p, b)
            k, v = qkv[row, ka], qkv[row, va]
            left, queries = halves_of(qkv[row, qa])
            outs = []
            for h in range(2):
                scores = flat_dot(queries[h], k, ((1,), (1,))) * scale
                scores = jnp.where(pairs, scores, -1e30)
                e = jnp.exp(scores - jnp.max(scores, axis=1, keepdims=True))
                w = e / jnp.sum(e, axis=1, keepdims=True)
                weights[p, b, h] = w
                outs.append(flat_dot(w.astype(low), v))
            heads[row, qa] = jnp.where(left, outs[0], outs[1]).astype(low)
        return carry

    lax.fori_loop(0, D // 128, attend, 0)
    attended[...] = streams[...] + flat_dot(heads[...], attn_w[:, pl.ds(3 * D, D)])
    ffn_low[...] = rms_scale(attended[...], gain_f).astype(low)
    ffn_t[...] = ffn_low[...].astype(f32).T.astype(low)
    total[...] = attended[...]
    d_ffn[...] = jnp.zeros_like(d_ffn)
    n_ffn = deep.shape[0] // D

    def stores(j):
        at = pl.ds(pl.multiple_of(j * D, D), D)
        return [
            pltpu.make_async_copy(g_buf.at[0], g_gate.at[:, at], g_sem.at[0]),
            pltpu.make_async_copy(g_buf.at[1], g_up.at[:, at], g_sem.at[1]),
            pltpu.make_async_copy(g_buf.at[2], g_down.at[at], g_sem.at[2]),
        ]

    def feed(j, carry):
        slot = lax.rem(j, 2)
        for copy in ffn_loads(j, slot):
            copy.wait()

        @pl.when(j + 1 < n_ffn)
        def _():
            for copy in ffn_loads(j + 1, 1 - slot):
                copy.start()

        gate = flat_dot(ffn_low[...], ffn_w[slot, 0])
        upward = flat_dot(ffn_low[...], ffn_w[slot, 1])
        sig = sigmoid(gate)
        act = gate * sig
        hidden = (act * upward).astype(low)
        total[...] += flat_dot(hidden, ffn_w[slot, 2])
        d_hidden = flat_dot(d_down[...], ffn_w[slot, 2], ((1,), (1,)))
        d_gate = (d_hidden * upward * (sig + act * (1.0 - sig))).astype(low)
        d_up = (d_hidden * act).astype(low)
        d_ffn[...] += flat_dot(d_gate, ffn_w[slot, 0], ((1,), (1,)))
        d_ffn[...] += flat_dot(d_up, ffn_w[slot, 1], ((1,), (1,)))

        @pl.when(j > 0)
        def _():
            for copy in stores(j - 1):
                copy.wait()

        g_buf[0] = flat_dot(ffn_t[...], d_gate).astype(low)
        g_buf[1] = flat_dot(ffn_t[...], d_up).astype(low)
        g_buf[2] = flat_dot(hidden.astype(f32).T.astype(low), d_down[...]).astype(low)
        for copy in stores(j):
            copy.start()
        return carry

    lax.fori_loop(0, n_ffn, feed, 0)
    o_block[...] = (live * total[...]).astype(low)
    d_norm, gain_f_sum = rms_back(attended[...], gain_f, d_ffn[...])
    d_attended = live * grad_ref[...].astype(f32) + d_norm
    total[...] = d_attended
    d_low = d_attended.astype(low)
    for copy in stores(n_ffn - 1):
        copy.wait()
    d_down[...] = flat_dot(d_low, attn_w[:, pl.ds(3 * D, D)], ((1,), (1,))).astype(low)
    g_buf[0] = flat_dot(heads[...].astype(f32).T.astype(low), d_low).astype(low)
    last = [pltpu.make_async_copy(g_buf.at[0], g_attn, g_sem.at[0])]
    last[0].start()

    def attend_back(p, carry):
        for b in range(rows // 128):
            row, (qa, ka, va) = blocks(p, b)
            q, k, v = qkv[row, qa], qkv[row, ka], qkv[row, va]
            grad = d_down[row, qa]
            left, grads = halves_of(grad)
            dq, dk, dv = [], [], []
            for h in range(2):
                w = weights[p, b, h]
                dv.append(flat_dot(w.T.astype(low), grad))
                d_w = flat_dot(grads[h], v, ((1,), (1,)))
                d_s = w * (d_w - jnp.sum(w * d_w, axis=1, keepdims=True))
                dq.append(flat_dot(d_s.astype(low), k) * scale)
                dk.append(flat_dot(d_s.T.astype(low), q) * scale)
            qkv[row, qa] = jnp.where(left, dq[0], dq[1]).astype(low)
            qkv[row, ka] = jnp.where(left, dk[0], dk[1]).astype(low)
            qkv[row, va] = jnp.where(left, dv[0], dv[1]).astype(low)
        return carry

    lax.fori_loop(0, D // 128, attend_back, 0)
    ffn_t[...] = normed[...].astype(f32).T.astype(low)
    for i in range(3):
        at = pl.ds(i * D, D)
        if i == 2:
            last[0].wait()
        buf = (i + 1) % 3
        g_buf[buf] = flat_dot(ffn_t[...], qkv[:, at]).astype(low)
        copy = pltpu.make_async_copy(g_buf.at[buf], g_qkv.at[:, at], g_sem.at[buf])
        copy.start()
        last.append(copy)
    d_ffn[...] = flat_dot(qkv[...], attn_w[:, pl.ds(0, 3 * D)], ((1,), (1,)))
    d_norm, gain_a_sum = rms_back(streams[...], gain_a, d_ffn[...])
    d_streams = total[...] + d_norm
    o_streams[...] = d_streams
    direct = jnp.sum(d_streams.reshape(rows // PATCH, PATCH, D), axis=1)
    o_direct[...] = direct
    mix = direct.astype(low)
    along = jnp.sum(mix.astype(f32) * raw, axis=1, keepdims=True)
    high_r, high_a = (v.astype(low).astype(f32) for v in (mixer_r, along))
    lane = lanes((rows // PATCH, 128), 1)
    ext = jnp.zeros((rows // PATCH, 128), f32)
    for i, v in enumerate((high_r, high_a, mixer_r - high_r, along - high_a)):
        ext = jnp.where(lane == i, v, ext)
    o_mix[:, pl.ds(0, D)] = mix
    o_mix[:, pl.ds(D, 128)] = ext.astype(low)
    o_gains[...] = jnp.concatenate([gain_a_sum, gain_f_sum, jnp.zeros((6, D), f32)], axis=0)
    for copy in last[1:]:
        copy.wait()


def local_call(lengths, byte_states, out_grad, patch_sum, mixed, small, wide, deep):
    f32, low = jnp.float32, jnp.bfloat16
    vmem = pl.BlockSpec(memory_space=pltpu.VMEM)
    anywhere = pl.BlockSpec(memory_space=pl.ANY)
    shape = jax.ShapeDtypeStruct
    rows = byte_states.shape[0]
    outs = [
        shape((rows, D), low),
        shape((rows, D), f32),
        shape((rows // PATCH, EXT), low),
        shape((rows // PATCH, D), f32),
        shape((8, D), f32),
        shape((D, 3 * D), low),
        shape((D, D), low),
        shape((D, deep.shape[0]), low),
        shape((D, deep.shape[0]), low),
        shape(deep.shape, low),
    ]
    scratch = [
        pltpu.VMEM((D, 4 * D), low),
        pltpu.VMEM((2, 3, D, D), low),
        pltpu.VMEM((3, D, D), low),
        pltpu.VMEM((rows, D), f32),
        pltpu.VMEM((rows, D), low),
        pltpu.VMEM((rows, 3 * D), low),
        pltpu.VMEM((D // 128, rows // 128, 2, 128, 128), f32),
        pltpu.VMEM((rows, D), low),
        pltpu.VMEM((rows, D), f32),
        pltpu.VMEM((rows, D), low),
        pltpu.VMEM((D, rows), low),
        pltpu.VMEM((rows, D), f32),
        pltpu.VMEM((rows, D), f32),
        pltpu.VMEM((rows, D), low),
        pltpu.SemaphoreType.DMA((1,)),
        pltpu.SemaphoreType.DMA((2, 3)),
        pltpu.SemaphoreType.DMA((3,)),
    ]
    return pl.pallas_call(
        local_kernel,
        out_shape=outs,
        in_specs=[pl.BlockSpec(memory_space=pltpu.SMEM)] + [vmem] * 5 + [anywhere] * 2,
        out_specs=[vmem] * 5 + [anywhere] * 5,
        scratch_shapes=scratch,
        compiler_params=pltpu.CompilerParams(vmem_limit_bytes=60 * 2**20),
        name="local_block",
    )(lengths, byte_states, out_grad, patch_sum, mixed, small, wide, deep)


BC = 2 * STATE


def fast_body(
    depth_fsdp,
    byte_states,
    doc_lengths,
    out_grad,
    patch_proj,
    global_gain,
    in_proj,
    conv_weight,
    conv_bias,
    dt_bias,
    a_log,
    skip_weight,
    mixer_gain,
    out_proj,
    attn_gain,
    qkv_proj,
    attn_out,
    ffn_gain,
    gate_proj,
    up_proj,
    down_proj,
):
    f32, low = jnp.float32, jnp.bfloat16
    depth, n_dev = depth_fsdp[0] // 2, depth_fsdp[0] * depth_fsdp[1]
    me = lax.axis_index("dp") * depth_fsdp[1] + lax.axis_index("fsdp")
    rows = byte_states.shape[0]
    patches = rows // PATCH

    shard_rows = in_proj.shape[0]
    maps_and_steps = jnp.pad(in_proj[:, 2 * DI :], ((0, 0), (0, SMALL_COLS - BC - MHEADS)))
    lines = [conv_weight[:, k] for k in range(CONV)]
    lines += [conv_bias, global_gain, mixer_gain, attn_gain, ffn_gain, doc_lengths.reshape(-1).astype(low)]
    lines = jnp.stack([jnp.pad(line, (0, SMALL_COLS - line.shape[0])) for line in lines])
    vectors = jnp.concatenate(
        [maps_and_steps, lines, jnp.zeros((SMALL_ROWS - shard_rows - lines.shape[0], SMALL_COLS), low)]
    )
    by_place = lambda cols: cols.reshape(shard_rows, 4, 8, HEAD_M).transpose(2, 0, 1, 3).reshape(8, shard_rows, 256)
    cols = jnp.concatenate([by_place(in_proj[:, :DI]), by_place(in_proj[:, DI : 2 * DI])], axis=2)
    heads_in = jnp.pad(jnp.stack([dt_bias, -jnp.exp(a_log), skip_weight]), ((0, 5), (0, 128 - MHEADS)))
    rows2 = byte_states.reshape(patches, PATCH * D)
    (wide, deep, patch_sum, mixed, small, all_bytes, norm8, proj8, head_w, own8, maps8, step8, core8) = forward_call(
        depth, n_dev, rows2, patch_proj, cols, vectors, out_proj, heads_in, qkv_proj, attn_out, gate_proj, up_proj, down_proj
    )
    block_out, grad_streams, mix, direct, gains, *grads = local_call(
        doc_lengths, byte_states, out_grad, patch_sum, mixed, small, wide, deep
    )
    saved = (small, all_bytes, norm8, proj8, head_w, own8, maps8, step8, core8)
    (g_qkv, g_attn, g_gate, g_up, g_down, g_patch, back_rows, g_out, g_cols, g_maps, everyone) = backward_call(
        depth,
        n_dev,
        mix,
        direct,
        patch_sum,
        gains,
        saved,
        patch_proj,
        heads_in,
        grads,
    )
    grad_states = grad_streams + back_rows.reshape(rows, D).astype(f32)

    lines = everyone[:, shard_rows : shard_rows + 9].astype(f32)
    sums = jnp.sum(lines, axis=0)
    own_part = lambda row: lax.dynamic_slice_in_dim(row, me * (D // n_dev), D // n_dev, 0)
    by_plane = jnp.sum(lines.reshape(depth, 8, 9, D), axis=0)
    by_head = lambda rows_of: rows_of.reshape(8, -1, 4, HEAD_M).transpose(1, 2, 0, 3).reshape(-1, DI)
    taps = jnp.concatenate([by_head(by_plane[:, : CONV + 1, :256]), sums[: CONV + 1, 256:512]], axis=1)
    share = CONV_CH // n_dev
    taps = lax.dynamic_slice_in_dim(taps, me * share, share, 1)
    gain_m_sum = by_head(by_plane[:, CONV + 1 : CONV + 2, :256])[0]
    gain_m_sum = lax.dynamic_slice_in_dim(gain_m_sum, me * HEAD_M, HEAD_M, 0)
    head_line = sums[CONV + 1]
    back_cols = lambda cols: cols.reshape(8, shard_rows, 4, HEAD_M).transpose(1, 2, 0, 3).reshape(shard_rows, DI)
    grad_in_proj = jnp.concatenate(
        [back_cols(g_cols[..., :256]), back_cols(g_cols[..., 256:]), g_maps[:, : BC + MHEADS]], axis=1
    )
    return (
        block_out,
        grad_states,
        g_patch,
        own_part(sums[CONV + 4]),
        grad_in_proj,
        taps[:CONV].T,
        taps[CONV],
        head_line[256 : 256 + MHEADS],
        head_line[384 : 384 + MHEADS],
        head_line[512 : 512 + MHEADS],
        gain_m_sum,
        g_out,
        own_part(sums[CONV + 2]),
        g_qkv,
        g_attn,
        own_part(sums[CONV + 3]),
        g_gate,
        g_up,
        g_down,
    )


def solution(mesh):
    in_specs = (
        P(("dp", "fsdp"), None),
        P("dp", None),
        P(("dp", "fsdp"), None),
        P(("dp", "fsdp"), None),
        P(("dp", "fsdp")),
        P(("dp", "fsdp"), None),
        P(("dp", "fsdp"), None),
        P(("dp", "fsdp")),
        P(),
        P(),
        P(),
        P(("dp", "fsdp")),
        P(("dp", "fsdp"), None),
        P(("dp", "fsdp")),
        P(("dp", "fsdp"), None),
        P(("dp", "fsdp"), None),
        P(("dp", "fsdp")),
        P(("dp", "fsdp"), None),
        P(("dp", "fsdp"), None),
        P(("dp", "fsdp"), None),
    )
    out_specs = (
        P(("dp", "fsdp"), None),
        P(("dp", "fsdp"), None),
        P(("dp", "fsdp"), None),
        P(("dp", "fsdp")),
        P(("dp", "fsdp"), None),
        P(("dp", "fsdp"), None),
        P(("dp", "fsdp")),
        P(),
        P(),
        P(),
        P(("dp", "fsdp")),
        P(("dp", "fsdp"), None),
        P(("dp", "fsdp")),
        P(("dp", "fsdp"), None),
        P(("dp", "fsdp"), None),
        P(("dp", "fsdp")),
        P(("dp", "fsdp"), None),
        P(("dp", "fsdp"), None),
        P(("dp", "fsdp"), None),
    )
    dp, fsdp = mesh.shape["dp"], mesh.shape["fsdp"]
    fast = dp * fsdp == MHEADS and fsdp == 4
    chosen = partial(fast_body, (dp, fsdp)) if fast else body
    return jax.shard_map(chosen, mesh=mesh, in_specs=in_specs, out_specs=out_specs, check_vma=False)
```

```python
from functools import partial

import jax
import jax.numpy as jnp
from jax import lax
from jax.experimental import pallas as pl
from jax.experimental.pallas import tpu as pltpu
from jax.sharding import PartitionSpec as P

D = 1024
HEAD = 64
HEAD_M = 64
STATE = 128
CONV = 4
PATCH = 8
DI = 2048
MHEADS = 32
CONV_CH = 2304


EPSILON = 1e-05
HIGHEST = lax.Precision.HIGHEST


def shifted(block, axis, distance):
    devices = range(lax.axis_size(axis))
    route = [(i - distance, i) for i in devices if i - distance in devices]
    return lax.ppermute(block, axis, route)


def prefix(value, axis, combine, identity):
    devices, place = (lax.axis_size(axis), lax.axis_index(axis))
    everything = jax.tree.map(
        lambda part, kind: lax.all_gather(part.astype(kind), axis),
        value,
        (jnp.bfloat16, jnp.bfloat16),
    )
    start = jax.tree.map(
        lambda part, zero: jnp.broadcast_to(jnp.asarray(zero, part.dtype), part.shape),
        value,
        identity,
    )

    def prefix_step(k, before):
        reached = k < place
        new = combine(
            before, jax.tree.map(lambda part, own: part[k].astype(own.dtype), everything, value)
        )
        return jax.tree.map(lambda a, b: jnp.where(reached, a, b), new, before)

    return lax.fori_loop(0, devices, prefix_step, start)


def carried_in(value, axis, combine, identity):
    devices, place = (lax.axis_size(axis), lax.axis_index(axis))
    everything = jax.tree.map(
        lambda part, kind: lax.all_gather(part.astype(kind), axis),
        value,
        jax.tree.map(lambda a: jnp.bfloat16 if a.dtype == jnp.float32 else a.dtype, value),
    )
    start = jax.tree.map(
        lambda part, zero: jnp.broadcast_to(jnp.asarray(zero, part.dtype), part.shape),
        value,
        identity,
    )

    def carried_step(k, before):
        at = devices - 1 - k
        reached = at > place
        new = combine(
            before, jax.tree.map(lambda part, own: part[at].astype(own.dtype), everything, value)
        )
        return jax.tree.map(lambda a, b: jnp.where(reached, a, b), new, before)

    return lax.fori_loop(0, devices, carried_step, start)


def product(left, right):
    return jnp.dot(left, right, preferred_element_type=jnp.float32)


def weight_grad(left, right):
    return lax.dot_general(
        left, right, (((0,), (0,)), ((), ())), preferred_element_type=jnp.float32
    )


def input_grad(grad_rows, weight):
    return lax.dot_general(
        grad_rows, weight, (((1,), (1,)), ((), ())), preferred_element_type=jnp.float32
    )


def rms_scale(value, gain):
    return value * lax.rsqrt(jnp.mean(value * value, axis=-1, keepdims=True) + EPSILON) * gain


def gated_norm(core_out, gate_raw, gain):
    count = core_out.shape[0]
    return rms_scale(core_out.reshape(count, DI) * jax.nn.silu(gate_raw), gain)


def patch_docs(doc_lengths, start, count):
    places = start + jnp.arange(count, dtype=jnp.int32)
    first_end = doc_lengths[0, 0]
    second_end = first_end + doc_lengths[0, 1]
    numbers = (places >= first_end).astype(jnp.int32) + (places >= second_end).astype(jnp.int32)
    return jnp.where(places >= 0, numbers, -1)


def chain(earlier, later):
    return (earlier[0] * later[0], later[1] + later[0][:, None, None] * earlier[1])


def mixer_core(
    channels,
    rim,
    step_raw,
    state_in,
    conv_weight,
    conv_bias,
    dt_bias,
    a_log,
    skip_weight,
    docs,
    rim_docs,
    prev_doc,
):
    count = channels.shape[0]
    padded = jnp.concatenate([rim, channels], axis=0)
    padded_docs = jnp.concatenate([rim_docs, docs])
    total = conv_bias[None, :]
    for shift_k in range(CONV):
        same_doc = (padded_docs[shift_k : shift_k + count] == docs).astype(jnp.float32)
        total = (
            total
            + padded[shift_k : shift_k + count]
            * conv_weight[:, shift_k][None, :]
            * same_doc[:, None]
        )
    activated = jax.nn.silu(total)
    inputs = activated[:, :DI].reshape(count, MHEADS, HEAD_M)
    in_map = activated[:, DI : DI + STATE]
    out_map = activated[:, DI + STATE :]
    step_size = jax.nn.softplus(step_raw + dt_bias[None, :])
    rate = -jnp.exp(a_log)
    lower = jnp.tril(jnp.ones((count, count), jnp.float32))
    cumulative = jnp.dot(lower, step_size * rate[None, :], precision=HIGHEST)
    places = jnp.arange(count, dtype=jnp.int32)
    keep = ((places[:, None] >= places[None, :]) & (docs[:, None] == docs[None, :]))[:, :, None]
    spread = cumulative[:, None, :] - cumulative[None, :, :]
    decay_table = jnp.where(keep, jnp.exp(jnp.where(keep, spread, 0.0)), 0.0)
    inner = jnp.dot(out_map, in_map.T, precision=HIGHEST, preferred_element_type=jnp.float32)
    mixing = decay_table * inner[:, :, None] * step_size[None, :, :]
    outputs = jnp.einsum("tsh,shp->thp", mixing, inputs, precision=HIGHEST)
    carry_in = jnp.where((docs == prev_doc)[:, None], jnp.exp(cumulative), 0.0)
    outputs = outputs + carry_in[:, :, None] * jnp.einsum(
        "tn,hpn->thp", out_map, state_in, precision=HIGHEST
    )
    outputs = outputs + skip_weight[None, :, None] * inputs
    last_doc = docs[count - 1]
    tail_keep = (docs == last_doc)[:, None]
    tail_gap = cumulative[count - 1][None, :] - cumulative
    tail_weight = (
        jnp.where(tail_keep, jnp.exp(jnp.where(tail_keep, tail_gap, 0.0)), 0.0) * step_size
    )
    decay_total = jnp.where(prev_doc == last_doc, jnp.exp(cumulative[count - 1]), 0.0)
    state_out = jnp.einsum("sh,shp,sn->hpn", tail_weight, inputs, in_map, precision=HIGHEST)
    state_out = state_out + decay_total[:, None, None] * state_in
    return ((outputs, state_out), (decay_total, carry_in, out_map))


def attend(qkv_low, patches):
    heads = qkv_low.reshape(patches, PATCH, 3, -1, HEAD)
    queries = heads[:, :, 0]
    key_rows = heads[:, :, 1]
    value_rows = heads[:, :, 2]
    scores = jnp.einsum(
        "pihd,pjhd->phij", queries, key_rows, preferred_element_type=jnp.float32
    ) * HEAD ** (-0.5)
    places = jnp.arange(PATCH)
    causal = places[:, None] >= places[None, :]
    scores = jnp.where(causal, scores, -1e30)
    attn_weights = jax.nn.softmax(scores, axis=-1)
    attn_low = attn_weights.astype(jnp.bfloat16)
    mixed = jnp.einsum("phij,pjhd->pihd", attn_low, value_rows, preferred_element_type=jnp.float32)
    mixed = mixed.astype(jnp.bfloat16).reshape(patches * PATCH, -1)
    return ((queries, key_rows, value_rows, attn_weights, attn_low), mixed)


def attend_back(grad_mixed_low, pieces):
    queries, key_rows, value_rows, attn_weights, attn_low = pieces
    patches = queries.shape[0]
    grad_mixed = grad_mixed_low.reshape(patches, PATCH, -1, HEAD)
    grad_values = jnp.einsum(
        "phij,pihd->pjhd", attn_low, grad_mixed, preferred_element_type=jnp.float32
    )
    grad_weights = jnp.einsum(
        "pihd,pjhd->phij", grad_mixed, value_rows, preferred_element_type=jnp.float32
    )
    grad_scores = attn_weights * (
        grad_weights - jnp.sum(attn_weights * grad_weights, axis=-1, keepdims=True)
    )
    scores_low = grad_scores.astype(jnp.bfloat16)
    scale = HEAD ** (-0.5)
    grad_queries = (
        jnp.einsum("phij,pjhd->pihd", scores_low, key_rows, preferred_element_type=jnp.float32)
        * scale
    )
    grad_keys = (
        jnp.einsum("phij,pihd->pjhd", scores_low, queries, preferred_element_type=jnp.float32)
        * scale
    )
    stacked = jnp.stack([grad_queries, grad_keys, grad_values], axis=2).reshape(patches * PATCH, -1)
    return stacked.astype(jnp.bfloat16)


def local_forward(byte_states, mixed_patch, local_set, live):
    attn_gain, qkv_proj, attn_out, ffn_gain, gate_proj, up_proj, down_proj = local_set
    rows = byte_states.shape[0]
    streams = byte_states.astype(jnp.float32) + jnp.repeat(mixed_patch, PATCH, axis=0)
    normed_low = rms_scale(streams, attn_gain.astype(jnp.float32)).astype(jnp.bfloat16)
    qkv_low = product(normed_low, qkv_proj).astype(jnp.bfloat16)
    pieces, mixed_heads = attend(qkv_low, rows // PATCH)
    attended = streams + product(mixed_heads, attn_out)
    ffn_low = rms_scale(attended, ffn_gain.astype(jnp.float32)).astype(jnp.bfloat16)
    gate = product(ffn_low, gate_proj)
    upward = product(ffn_low, up_proj)
    hidden_low = (jax.nn.silu(gate) * upward).astype(jnp.bfloat16)
    block = live * (attended + product(hidden_low, down_proj))
    cache = (streams, normed_low, pieces, mixed_heads, attended, ffn_low, gate, upward, hidden_low)
    return (block, cache)


def local_backward(grad_block, cache, local_set):
    attn_gain, qkv_proj, attn_out, ffn_gain, gate_proj, up_proj, down_proj = local_set
    streams, normed_low, pieces, mixed_heads, attended, ffn_low, gate, upward, hidden_low = cache
    down_low = grad_block.astype(jnp.bfloat16)
    grad_down = weight_grad(hidden_low, down_low)
    grad_hidden = input_grad(down_low, down_proj)
    sigma = jax.nn.sigmoid(gate)
    grad_gate_low = (grad_hidden * upward * sigma * (1.0 + gate * (1.0 - sigma))).astype(
        jnp.bfloat16
    )
    grad_up_low = (grad_hidden * gate * sigma).astype(jnp.bfloat16)
    grad_gate = weight_grad(ffn_low, grad_gate_low)
    grad_up = weight_grad(ffn_low, grad_up_low)
    grad_ffn_in = input_grad(grad_gate_low, gate_proj) + input_grad(grad_up_low, up_proj)
    _, norm_back = jax.vjp(rms_scale, attended, ffn_gain.astype(jnp.float32))
    grad_attended_norm, grad_ffn_gain = norm_back(grad_ffn_in)
    grad_attended = grad_block + grad_attended_norm
    attn_grad_low = grad_attended.astype(jnp.bfloat16)
    grad_attn_out = weight_grad(mixed_heads, attn_grad_low)
    grad_mixed_low = input_grad(attn_grad_low, attn_out).astype(jnp.bfloat16)
    grad_qkv_low = attend_back(grad_mixed_low, pieces)
    grad_qkv = weight_grad(normed_low, grad_qkv_low)
    grad_normed = input_grad(grad_qkv_low, qkv_proj)
    _, norm_back = jax.vjp(rms_scale, streams, attn_gain.astype(jnp.float32))
    grad_streams_norm, grad_attn_gain = norm_back(grad_normed)
    grad_streams = grad_attended + grad_streams_norm
    return (
        grad_streams,
        (grad_qkv, grad_attn_out, grad_gate, grad_up, grad_down, grad_attn_gain, grad_ffn_gain),
    )


def body(
    byte_states,
    doc_lengths,
    out_grad,
    patch_proj,
    global_gain,
    in_proj,
    conv_weight,
    conv_bias,
    dt_bias,
    a_log,
    skip_weight,
    mixer_gain,
    out_proj,
    attn_gain,
    qkv_proj,
    attn_out,
    ffn_gain,
    gate_proj,
    up_proj,
    down_proj,
):
    rows = byte_states.shape[0]
    patches = rows // PATCH
    share = lax.axis_index("fsdp")
    start = share * patches
    docs = patch_docs(doc_lengths, start, patches)
    rim_docs = patch_docs(doc_lengths, start - (CONV - 1), CONV - 1)
    prev_doc = patch_docs(doc_lengths, start - 1, 1)[0]
    live = jnp.repeat((docs < 2).astype(jnp.float32), PATCH)[:, None]
    all_set = (
        lax.all_gather(patch_proj, ("dp", "fsdp"), axis=0, tiled=True),
        lax.all_gather(global_gain, ("dp", "fsdp"), axis=0, tiled=True),
        lax.all_gather(in_proj, ("dp", "fsdp"), axis=0, tiled=True),
        lax.all_gather(conv_weight, ("dp", "fsdp"), axis=0, tiled=True),
        lax.all_gather(conv_bias, ("dp", "fsdp"), axis=0, tiled=True),
        lax.all_gather(mixer_gain, ("dp", "fsdp"), axis=0, tiled=True),
        lax.all_gather(out_proj, ("dp", "fsdp"), axis=0, tiled=True),
        lax.all_gather(attn_gain, ("dp", "fsdp"), axis=0, tiled=True),
        lax.all_gather(qkv_proj, ("dp", "fsdp"), axis=0, tiled=True),
        lax.all_gather(attn_out, ("dp", "fsdp"), axis=0, tiled=True),
        lax.all_gather(ffn_gain, ("dp", "fsdp"), axis=0, tiled=True),
        lax.all_gather(gate_proj, ("dp", "fsdp"), axis=0, tiled=True),
        lax.all_gather(up_proj, ("dp", "fsdp"), axis=0, tiled=True),
        lax.all_gather(down_proj, ("dp", "fsdp"), axis=0, tiled=True),
    )
    global_set = all_set[:7]
    local_set = all_set[7:]
    patch_full, gain_g_full, in_full, conv_w_full, conv_b_full, gain_m_full, out_full = global_set
    patch_rows = byte_states.reshape(patches, PATCH * D)
    patch_sum = product(patch_rows, patch_full)
    gain_g = gain_g_full.astype(jnp.float32)
    global_low = rms_scale(patch_sum, gain_g).astype(jnp.bfloat16)
    projected = product(global_low, in_full)
    gate_raw = projected[:, :DI]
    channels = projected[:, DI : DI + CONV_CH]
    step_raw = projected[:, DI + CONV_CH :]
    rim = shifted(channels[patches - (CONV - 1) :], "fsdp", 1)
    core = partial(mixer_core, docs=docs, rim_docs=rim_docs, prev_doc=prev_doc)
    conv_w = conv_w_full.astype(jnp.float32)
    conv_b = conv_b_full.astype(jnp.float32)
    empty_state = jnp.zeros((MHEADS, HEAD_M, STATE), jnp.float32)
    (partial_out, local_state), aux = core(
        channels, rim, step_raw, empty_state, conv_w, conv_b, dt_bias, a_log, skip_weight
    )
    decay_total, carry_in, out_map = aux
    identity = (jnp.ones((MHEADS,), jnp.float32), jnp.zeros((MHEADS, HEAD_M, STATE), jnp.float32))
    arrived = prefix((decay_total, local_state), "fsdp", chain, identity)
    state_in = arrived[1]
    mixer_out = partial_out + carry_in[:, :, None] * jnp.einsum(
        "tn,hpn->thp", out_map, state_in, precision=HIGHEST
    )
    gain_m = gain_m_full.astype(jnp.float32)
    mixer_low = gated_norm(mixer_out, gate_raw, gain_m).astype(jnp.bfloat16)
    mixed_patch = patch_sum + product(mixer_low, out_full)
    block, cache = local_forward(byte_states, mixed_patch, local_set, live)
    block_out = block.astype(jnp.bfloat16)
    back_set = (
        lax.all_gather(patch_proj, ("dp", "fsdp"), axis=0, tiled=True),
        lax.all_gather(global_gain, ("dp", "fsdp"), axis=0, tiled=True),
        lax.all_gather(in_proj, ("dp", "fsdp"), axis=0, tiled=True),
        lax.all_gather(conv_weight, ("dp", "fsdp"), axis=0, tiled=True),
        lax.all_gather(conv_bias, ("dp", "fsdp"), axis=0, tiled=True),
        lax.all_gather(mixer_gain, ("dp", "fsdp"), axis=0, tiled=True),
        lax.all_gather(out_proj, ("dp", "fsdp"), axis=0, tiled=True),
        lax.all_gather(attn_gain, ("dp", "fsdp"), axis=0, tiled=True),
        lax.all_gather(qkv_proj, ("dp", "fsdp"), axis=0, tiled=True),
        lax.all_gather(attn_out, ("dp", "fsdp"), axis=0, tiled=True),
        lax.all_gather(ffn_gain, ("dp", "fsdp"), axis=0, tiled=True),
        lax.all_gather(gate_proj, ("dp", "fsdp"), axis=0, tiled=True),
        lax.all_gather(up_proj, ("dp", "fsdp"), axis=0, tiled=True),
        lax.all_gather(down_proj, ("dp", "fsdp"), axis=0, tiled=True),
    )
    global_back = back_set[:7]
    local_back = back_set[7:]
    _, cache = local_forward(byte_states, mixed_patch, local_back, live)
    patch_back, _, in_back, conv_w_back, conv_b_back, _, out_back = global_back
    grad_block = live * out_grad.astype(jnp.float32)
    grad_streams, local_grads = local_backward(grad_block, cache, local_back)
    reduced_local = (
        lax.psum_scatter(local_grads[0], ("dp", "fsdp"), scatter_dimension=0, tiled=True),
        lax.psum_scatter(local_grads[1], ("dp", "fsdp"), scatter_dimension=0, tiled=True),
        lax.psum_scatter(local_grads[2], ("dp", "fsdp"), scatter_dimension=0, tiled=True),
        lax.psum_scatter(local_grads[3], ("dp", "fsdp"), scatter_dimension=0, tiled=True),
        lax.psum_scatter(local_grads[4], ("dp", "fsdp"), scatter_dimension=0, tiled=True),
        lax.psum_scatter(local_grads[5], ("dp", "fsdp"), scatter_dimension=0, tiled=True),
        lax.psum_scatter(local_grads[6], ("dp", "fsdp"), scatter_dimension=0, tiled=True),
    )
    grad_patch_mix = grad_streams.reshape(patches, PATCH, D).sum(axis=1)
    mix_low = grad_patch_mix.astype(jnp.bfloat16)
    grad_out_proj = weight_grad(mixer_low, mix_low)
    grad_mixer_low = input_grad(mix_low, out_back)
    _, norm_back = jax.vjp(gated_norm, mixer_out, gate_raw, gain_m)
    grad_core, grad_gate_raw, grad_mixer_gain = norm_back(grad_mixer_low)
    state_part = jnp.einsum("th,thp,tn->hpn", carry_in, grad_core, out_map, precision=HIGHEST)
    returned = carried_in((decay_total, state_part), "fsdp", chain, identity)
    _, core_back, _ = jax.vjp(
        core,
        channels,
        rim,
        step_raw,
        state_in,
        conv_w_back.astype(jnp.float32),
        conv_b_back.astype(jnp.float32),
        dt_bias,
        a_log,
        skip_weight,
        has_aux=True,
    )
    core_grads = core_back((grad_core, returned[1]))
    (
        grad_channels,
        grad_rim,
        grad_step,
        _,
        grad_conv_w,
        grad_conv_b,
        grad_dt_bias,
        grad_a_log,
        grad_skip,
    ) = core_grads
    rim_grad = shifted(grad_rim, "fsdp", -1)
    cut = patches - (CONV - 1)
    grad_channels = jnp.concatenate([grad_channels[:cut], grad_channels[cut:] + rim_grad], axis=0)
    proj_low = jnp.concatenate([grad_gate_raw, grad_channels, grad_step], axis=1).astype(
        jnp.bfloat16
    )
    grad_in_proj = weight_grad(global_low, proj_low)
    grad_global_norm = input_grad(proj_low, in_back)
    _, norm_back = jax.vjp(rms_scale, patch_sum, gain_g)
    grad_sum_norm, grad_global_gain = norm_back(grad_global_norm)
    sum_low = (grad_patch_mix + grad_sum_norm).astype(jnp.bfloat16)
    grad_patch_proj = weight_grad(patch_rows, sum_low)
    grad_states = grad_streams + input_grad(sum_low, patch_back).reshape(rows, D)
    reduced_global = (
        lax.psum_scatter(grad_patch_proj, ("dp", "fsdp"), scatter_dimension=0, tiled=True),
        lax.psum_scatter(grad_global_gain, ("dp", "fsdp"), scatter_dimension=0, tiled=True),
        lax.psum_scatter(grad_in_proj, ("dp", "fsdp"), scatter_dimension=0, tiled=True),
        lax.psum_scatter(grad_conv_w, ("dp", "fsdp"), scatter_dimension=0, tiled=True),
        lax.psum_scatter(grad_conv_b, ("dp", "fsdp"), scatter_dimension=0, tiled=True),
        lax.psum_scatter(grad_mixer_gain, ("dp", "fsdp"), scatter_dimension=0, tiled=True),
        lax.psum_scatter(grad_out_proj, ("dp", "fsdp"), scatter_dimension=0, tiled=True),
    )
    head_sums = lax.psum((grad_dt_bias, grad_a_log, grad_skip), ("dp", "fsdp"))
    return (
        block_out,
        grad_states,
        reduced_global[0],
        reduced_global[1],
        reduced_global[2],
        reduced_global[3],
        reduced_global[4],
        head_sums[0],
        head_sums[1],
        head_sums[2],
        reduced_global[5],
        reduced_global[6],
        reduced_local[5],
        reduced_local[0],
        reduced_local[1],
        reduced_local[6],
        reduced_local[2],
        reduced_local[3],
        reduced_local[4],
    )


MESH = pl.DeviceIdType.MESH
WIDE = 12288
PARTS = ((0, 3072), (3072, 1024), (4096, 4096), (8192, 4096))
STEP = 1024
FAR_F, FAR_B = 2048, 2048
CUTS = (2048, 2048, 1024)
CUTS_F = (1024, 1024, 1024)
TILE = 32
SMALL_ROWS, SMALL_COLS = 48, 384
EXT = D + 128


def device(z, x, y, c):
    return (z * 2 + x, y * 2 + c)


class Spot:
    def __init__(self, depth):
        dp, fs = lax.axis_index("dp"), lax.axis_index("fsdp")
        self.depth, self.count = depth, depth * 8
        self.me = dp * 4 + fs
        self.z, self.x, self.y, self.c = dp // 2, dp % 2, fs // 2, fs % 2
        self.q = self.x * 4 + self.y * 2 + self.c
        self.plane = self.x * 2 + self.y
        self.column = [(self.z + depth - j) % depth for j in range(depth)]

    def flip(self, way):
        x = 1 - self.x if way & 2 else self.x
        y = 1 - self.y if way & 1 else self.y
        return device(self.z, x, y, self.c), x * 2 + y

    def sibling(self):
        return device(self.z, self.x, self.y, 1 - self.c)

    def above(self, k):
        return device((self.z + k) % self.depth, self.x, self.y, self.c)


def greet(spot):
    barrier = pltpu.get_barrier_semaphore()

    def one(i, carry):
        to = (spot.me + i) % spot.count
        pl.semaphore_signal(barrier, inc=1, device_id=(to // 4, to % 4), device_id_type=MESH)
        return carry

    lax.fori_loop(1, spot.count, one, 0)
    pl.semaphore_wait(barrier, spot.count - 1)


class Wires:
    def __init__(self, send, recv):
        self.send, self.recv, self.used, self.open = send, recv, 0, []

    def copy(self, src, dst, to):
        i = self.used
        self.used += 1
        copy = pltpu.make_async_remote_copy(
            src_ref=src,
            dst_ref=dst,
            send_sem=self.send.at[i],
            recv_sem=self.recv.at[i],
            device_id=to,
            device_id_type=MESH,
        )
        copy.start()
        self.open.append(copy)
        return copy

    def drain(self):
        for copy in self.open:
            copy.wait_send()


def got(copies):
    for copy in copies:
        copy.wait_recv()


class Swap:
    def __init__(self, spot, send, recv, src_at, dst_at):
        self.spot, self.send, self.recv, self.src_at, self.dst_at = spot, send, recv, src_at, dst_at

    def copy(self, i):
        to = (self.spot.me + i) % self.spot.count
        return pltpu.make_async_remote_copy(
            src_ref=self.src_at(to),
            dst_ref=self.dst_at(self.spot.me),
            send_sem=self.send.at[i],
            recv_sem=self.recv.at[i],
            device_id=(to // 4, to % 4),
            device_id_type=MESH,
        )

    def each(self, act):
        def one(i, carry):
            act(self.copy(i))
            return carry

        lax.fori_loop(1, self.spot.count, one, 0)

    def start(self):
        self.each(lambda copy: copy.start())

    def arrive(self):
        self.each(lambda copy: copy.wait_recv())

    def leave(self):
        self.each(lambda copy: copy.wait_send())


def plane_swap(wires, spot, src_at, dst_at):
    copies = []
    for way in range(4):
        for other in range(2):
            if way or other:
                x = spot.x ^ (way >> 1)
                y = spot.y ^ (way & 1)
                c = spot.c ^ other
                copies.append(
                    wires.copy(src_at(x * 4 + y * 2 + c), dst_at(spot.q), device(spot.z, x, y, c))
                )
    return copies


def block_row(t, plane, c):
    return (t * 4 + plane) * 2 + c


def spread_all(wires, spot, buf, own=None):
    at = lambda t, plane, c: buf.at[block_row(t, plane, c)]
    mine = at(spot.z, spot.plane, spot.c)
    src = mine if own is None else own
    ring, flat, core = [], [], []
    for k in range(1, spot.depth):
        ring.append(wires.copy(src, mine, spot.above(k)))
    flat.append([wires.copy(src, mine, spot.flip(way)[0]) for way in (1, 2, 3)])
    core.append(wires.copy(src, mine, spot.sibling()))
    yield
    for j in range(1, spot.depth):
        got([ring[j - 1]])
        block = at(spot.column[j], spot.plane, spot.c)
        flat.append([wires.copy(block, block, spot.flip(way)[0]) for way in (1, 2, 3)])
        core.append(wires.copy(block, block, spot.sibling()))
    yield
    for j in range(spot.depth):
        for way in (1, 2, 3):
            got([flat[j][way - 1]])
            block = at(spot.column[j], spot.flip(way)[1], spot.c)
            core.append(wires.copy(block, block, spot.sibling()))
    yield
    got(core)


def spread_plane(wires, spot, buf):
    at = lambda plane: buf.at[plane * 2 + spot.c]
    mine = at(spot.plane)
    flat = [wires.copy(mine, mine, spot.flip(way)[0]) for way in (1, 2, 3)]
    core = [wires.copy(mine, mine, spot.sibling())]
    yield
    for way in (1, 2, 3):
        got([flat[way - 1]])
        block = at(spot.flip(way)[1])
        core.append(wires.copy(block, block, spot.sibling()))
    yield
    got(core)


def sum_plane(wires, spot, parts, pair, near):
    first = wires.copy(parts.at[:, 1 - spot.c], pair, spot.sibling())
    yield None
    got([first])
    f32 = jnp.float32
    pair[...] = (parts[:, spot.c].astype(f32) + pair[...].astype(f32)).astype(jnp.bfloat16)
    flat = [
        wires.copy(pair.at[spot.flip(way)[1]], near.at[way - 1], spot.flip(way)[0]) for way in (1, 2, 3)
    ]
    yield None
    got(flat)
    total = pair[spot.plane].astype(f32)
    for way in range(3):
        total = total + near[way].astype(f32)
    yield total


def sum_all(wires, spot, parts, pair, near, column, far, out):
    f32, low = jnp.float32, jnp.bfloat16
    half = parts.shape[-1] // 2
    cut = [pl.ds(h * half, half) for h in range(2)]
    first = [
        wires.copy(parts.at[:, 1 - spot.c, :, cut[h]], pair.at[:, :, cut[h]], spot.sibling()) for h in range(2)
    ]
    yield
    flat, ring = [], []
    rows = pair.shape[1]
    for h in range(2):
        got([first[h]])
        for b in range(4 * spot.depth):
            pair[b, :, cut[h]] = (
                parts[b, spot.c, :, cut[h]].astype(f32) + pair[b, :, cut[h]].astype(f32)
            ).astype(low)
        step = []
        for way in (1, 2, 3):
            to, plane = spot.flip(way)
            for t in range(spot.depth):
                step.append(
                    wires.copy(pair.at[t * 4 + plane, :, cut[h]], near.at[way - 1, t, :, cut[h]], to)
                )
        flat.append(step)
    yield
    for h in range(2):
        got(flat[h])
        for t in range(spot.depth):
            total = pair[t * 4 + spot.plane, :, cut[h]].astype(f32)
            for way in range(3):
                total = total + near[way, t, :, cut[h]].astype(f32)
            column[t, :, cut[h]] = total.astype(low)
        ring.append(
            [
                wires.copy(
                    column.at[(spot.z + k) % spot.depth, :, cut[h]], far.at[k - 1, :, cut[h]], spot.above(k)
                )
                for k in range(1, spot.depth)
            ]
        )
    yield
    for h in range(2):
        got(ring[h])
        total = column[spot.z, :, cut[h]].astype(f32)
        for k in range(1, spot.depth):
            total = total + far[k - 1, :, cut[h]].astype(f32)
        out[:, cut[h]] = total
    yield


def big_gather(wires, spot, ow, od, shards):
    down = od.shape[0] // spot.count
    xn, yn, cn, zn = spot.flip(2)[0], spot.flip(1)[0], spot.sibling(), spot.above(1)
    here, xp, yp, xy = spot.plane, spot.flip(2)[1], spot.flip(1)[1], spot.flip(3)[1]
    parts = {"C": (WIDE - FAR_F, FAR_F, None), ("A", 0): (0, 2 * D, None), ("B", 0): (2 * D, 2 * D, None)}
    begin, side, at = 4 * D, (WIDE - FAR_F - 4 * D) // 2, 0
    for i, width in enumerate(CUTS_F, 1):
        last = i == len(CUTS_F)
        parts["A", i] = (begin + at, width, (0, down // 2) if last else None)
        parts["B", i] = (begin + side + at, width, (down // 2, down // 2) if last else None)
        at += width
    assert at == side
    mine = pl.multiple_of(spot.me * TILE, TILE)
    row = pl.multiple_of(spot.me * down, down)

    def refs(t, plane, part):
        begin, width, deep = parts[part]
        r = block_row(t, plane, spot.c)
        found = [ow.at[pl.ds(pl.multiple_of(r * TILE, TILE), TILE), pl.ds(begin, width)]]
        if deep:
            found.append(od.at[pl.ds(pl.multiple_of(r * down + deep[0], deep[1]), deep[1])])
        return found

    def go(t, plane, part, to):
        return [wires.copy(r, r, to) for r in refs(t, plane, part)]

    def own(part, to):
        begin, width, deep = parts[part]
        pairs = []
        for ref, (base, size) in zip(shards[:4], PARTS):
            low, high = max(begin, base), min(begin + width, base + size)
            if low < high:
                pairs.append(
                    (ref.at[:, pl.ds(low - base, high - low)], ow.at[pl.ds(mine, TILE), pl.ds(low, high - low)])
                )
        if deep:
            pairs.append(
                (shards[4].at[pl.ds(*deep)], od.at[pl.ds(pl.multiple_of(row + deep[0], deep[1]), deep[1])])
            )
        return [wires.copy(a, b, to) for a, b in pairs]

    T = spot.column
    core, ring, fx, fy, sx, sy = {i: [] for i in range(len(CUTS_F) + 2)}, {}, {}, {}, {}, {}

    def arrived(j, i):
        if (j - 1, i) in ring:
            got(ring.pop((j - 1, i)))

    def climb_on(j, i):
        send = own if j == 0 else (lambda part, to: go(T[j], here, part, to))
        arrived(j, i)
        ring[j, i] = send(("A", i), zn) + send(("B", i), zn)

    def first(j, i):
        send = own if j == 0 else (lambda part, to: go(T[j], here, part, to))
        arrived(j, i)
        fx[j, i], fy[j, i] = send(("A", i), xn), send(("B", i), yn)
        core[i].append(send(("A", i), cn) + send(("B", i), cn))

    def second(j, i):
        send = own if j == 0 else (lambda part, to: go(T[j], here, part, to))
        got(fx[j, i])
        sy[j, i] = send(("A", i), yn) + go(T[j], xp, ("A", i), yn)
        got(fy[j, i])
        sx[j, i] = send(("B", i), xn) + go(T[j], yp, ("B", i), xn)
        core[i].append(go(T[j], xp, ("A", i), cn) + go(T[j], yp, ("B", i), cn))

    def third(j, i):
        got(sy[j, i])
        core[i].append(go(T[j], yp, ("A", i), cn) + go(T[j], xy, ("A", i), cn))
        got(sx[j, i])
        core[i].append(go(T[j], xp, ("B", i), cn) + go(T[j], xy, ("B", i), cn))

    flat, climb = [], {}

    def far(j):
        if j < 0:
            flat.extend(own("C", spot.flip(way)[0]) for way in (1, 2, 3))
            core[len(CUTS_F) + 1].append(own("C", cn))
            return
        if j == 0:
            for copies in flat:
                got(copies)
        else:
            got(climb[j - 1])
        if j < spot.depth - 1:
            climb[j] = own("C", zn) if j == 0 else go(T[j], here, "C", zn)
            for plane in (xp, yp, xy):
                climb[j] += go(T[j], plane, "C", zn)
        for plane in (xp, yp, xy) + ((here,) if j else ()):
            core[len(CUTS_F) + 1].append(go(T[j], plane, "C", cn))

    chunks, n = range(len(CUTS_F) + 1), spot.depth
    steps = {"C%d" % j: partial(far, j) for j in range(-1, n)}
    for i in chunks:
        for j in range(n):
            steps["r%d%d" % (j, i)] = partial(climb_on, j, i)
            steps["a%d%d" % (j, i)] = partial(first, j, i)
            steps["b%d%d" % (j, i)] = partial(second, j, i)
            steps["c%d%d" % (j, i)] = partial(third, j, i)
        del steps["r%d%d" % (n - 1, i)]

    def close(which):
        for part in which:
            for copies in core.pop(part):
                got(copies)

    return steps, close


class Ticker:
    def __init__(self, steps, plan):
        self.steps, self.plan = dict(steps), iter(plan)

    def __call__(self):
        for name in next(self.plan):
            self.steps.pop(name)()

    def rest(self, order):
        for name in order:
            if name in self.steps:
                self.steps.pop(name)()
        assert not self.steps


def run(steps):
    for _ in steps:
        pass


def sigmoid(v):
    return 1.0 / (1.0 + jnp.exp(-v))


def lanes(shape, axis):
    return lax.broadcasted_iota(jnp.int32, shape, axis)


def flat_dot(a, b, dims=((1,), (0,))):
    return lax.dot_general(a, b, (dims, ((), ())), preferred_element_type=jnp.float32)


def exact_dot(a, b):
    return jnp.dot(a, b, precision=HIGHEST, preferred_element_type=jnp.float32)


def gain_row(values):
    n_dev, width = values.shape[0], D // values.shape[0]
    spread = (lanes((128, D), 0) == lanes((128, D), 1) & (width - 1)).astype(jnp.bfloat16)
    rows = flat_dot(values, spread)
    return jnp.sum(jnp.where(lanes((n_dev, D), 0) == lanes((n_dev, D), 1) >> (width.bit_length() - 1), rows, 0.0), axis=0, keepdims=True)


def tap_rows(spot, small):
    n_dev = spot.count
    share = CONV_CH // n_dev
    col = lanes((1, 512), 1)
    channel = jnp.where(col < 256, (spot.q + 8 * (col >> 6)) * HEAD_M + (col & 63), DI + col - 256)
    dev = lanes((n_dev, 512), 0)
    picks = (channel >= dev * share) & (channel < dev * share + share)
    owner = jnp.sum(jnp.where(picks, dev, 0), axis=0, keepdims=True)
    within = lanes((128, 512), 0) == channel - owner * share
    rows = []
    for k in range(CONV + 1):
        values = small[:, TILE + k, 0:128]
        spread = flat_dot(values, picks.astype(jnp.bfloat16), ((0,), (0,)))
        rows.append(jnp.sum(jnp.where(within, spread, 0.0), axis=0, keepdims=True))
    return rows


def entry(block, row, lane):
    at = (lanes(block.shape, 0) == row) & (lanes(block.shape, 1) == lane)
    return jnp.sum(jnp.where(at, block.astype(jnp.float32), 0.0), keepdims=True).reshape(1, 1)


class Slot:
    def __init__(self, spot, small, x, count):
        block = small[(spot.z * 2 + x) * 4, TILE : TILE + 16, 0:128].astype(jnp.float32)
        first = entry(block, 9, 0)
        second = first + entry(block, 9, 1)
        number = lambda p: (p >= first).astype(jnp.float32) + (p >= second).astype(jnp.float32)
        col = lanes((count, 1), 0).astype(jnp.float32)
        row = lanes((1, count), 1).astype(jnp.float32)
        docs = number(col)
        self.keep = (col >= row) & (docs == number(row))
        self.same = [((col >= s) & (number(col - s) == docs)).astype(jnp.float32) for s in range(CONV)]


def shift(block, by):
    return block if by == 0 else pltpu.roll(block, by % block.shape[0], 0)


class Mixed:
    def __init__(self, spot, slot, own, maps, step_raw, taps, dt_row, rate_row):
        count = own.shape[0]
        self.spot, self.slot, self.count = spot, slot, count
        self.channels = jnp.concatenate([own[:, 256:], maps], axis=1)
        conv = taps[CONV] + sum(
            taps[CONV - 1 - s] * (shift(self.channels, s) * slot.same[s]) for s in range(CONV)
        )
        self.conv, self.sig = conv, sigmoid(conv)
        act = conv * self.sig
        self.inputs = act[:, :256]
        self.in_map, self.out_map = act[:, 256:384].astype(jnp.bfloat16), act[:, 384:].astype(jnp.bfloat16)
        self.raw = step_raw + dt_row
        self.step = jnp.where(self.raw > 20.0, self.raw, jnp.log(1.0 + jnp.exp(jnp.minimum(self.raw, 20.0))))
        lower = lanes((count, count), 0) >= lanes((count, count), 1)
        self.upper = (lanes((count, count), 0) <= lanes((count, count), 1)).astype(jnp.float32)
        self.cum = exact_dot(lower.astype(jnp.float32), self.step * rate_row)
        self.cum_t, self.step_t = self.cum.T, self.step.T
        self.inner = flat_dot(self.out_map, self.in_map, ((1,), (1,)))

    def head(self, i):
        return self.spot.q + 8 * i

    def col(self, by_head, i):
        return jnp.sum(jnp.where(lanes((1, 128), 1) == self.head(i), by_head, 0.0), axis=1, keepdims=True)

    def row(self, by_head_t, i):
        return jnp.sum(jnp.where(lanes((128, 1), 0) == self.head(i), by_head_t, 0.0), axis=0, keepdims=True)

    def decay(self, i):
        gap = jnp.where(self.slot.keep, self.col(self.cum, i) - self.row(self.cum_t, i), 0.0)
        return jnp.where(self.slot.keep, jnp.exp(gap), 0.0)


def pick_lane(row, lane):
    return jnp.sum(jnp.where(lanes(row.shape, 1) == lane, row, 0.0), axis=1, keepdims=True)


def patch_pairs(count):
    i, j = lanes((count, count), 0), lanes((count, count), 1)
    return (i >= j) & ((i >> 3) == (j >> 3))


def rms_back(value, gain, grad):
    scale = lax.rsqrt(jnp.mean(value * value, axis=1, keepdims=True) + EPSILON)
    along = jnp.mean(grad * gain * value, axis=1, keepdims=True)
    d_value = scale * gain * grad - value * (scale * scale * scale * along)
    return d_value, jnp.sum(grad * value * scale, axis=0, keepdims=True)


def halves_of(block):
    left = lanes(block.shape, 1) < HEAD
    return left, [jnp.where(left, block, 0), jnp.where(left, 0, block)]


def local_block(
    tick,
    ready,
    whole,
    lengths,
    bytes_ref,
    grad_ref,
    sum_ref,
    mixed_ref,
    small_ref,
    wide,
    deep,
    o_block,
    o_streams,
    o_mix,
    o_direct,
    o_gains,
    g_qkv,
    g_attn,
    g_gate,
    g_up,
    g_down,
    attn_w,
    ffn_w,
    g_buf,
    streams,
    normed,
    qkv,
    weights,
    heads,
    attended,
    ffn_low,
    ffn_t,
    total,
    d_ffn,
    d_down,
    load_sem,
    ffn_sem,
    g_sem,
):
    f32, low = jnp.float32, jnp.bfloat16
    rows = bytes_ref.shape[0]
    scale = HEAD ** (-0.5)
    ready()
    load = pltpu.make_async_copy(wide.at[:, pl.ds(0, 4 * D)], attn_w, load_sem.at[0])
    load.start()

    def ffn_loads(j, slot):
        at = lambda base: pl.ds(pl.multiple_of(base + j * D, D), D)
        return [
            pltpu.make_async_copy(wide.at[:, at(4 * D)], ffn_w.at[slot, 0], ffn_sem.at[slot, 0]),
            pltpu.make_async_copy(wide.at[:, at(8 * D)], ffn_w.at[slot, 1], ffn_sem.at[slot, 1]),
            pltpu.make_async_copy(deep.at[at(0)], ffn_w.at[slot, 2], ffn_sem.at[slot, 2]),
        ]

    gain_a = gain_row(small_ref[:, TILE + 7, 0:128])
    gain_f = gain_row(small_ref[:, TILE + 8, 0:128])
    place = lax.axis_index("fsdp") * (rows // PATCH) + (lanes((rows, 1), 0) >> 3)
    live = (place < lengths[0, 0] + lengths[0, 1]).astype(f32)
    raw = mixed_ref[:, pl.ds(0, D)]
    mixer_r = lax.rsqrt(mixed_ref[:, pl.ds(D, 128)] * (1.0 / DI) + EPSILON)[:, 0:1]
    patch = sum_ref[...] + raw * mixer_r
    patch = jnp.broadcast_to(patch[:, None, :], (rows // PATCH, PATCH, D)).reshape(rows, D)
    streams[...] = bytes_ref[...].astype(f32) + patch
    normed[...] = rms_scale(streams[...], gain_a).astype(low)
    d_down[...] = (live * grad_ref[...].astype(f32)).astype(low)
    load.wait()
    for i in range(3):
        at = pl.ds(i * D, D)
        qkv[:, at] = flat_dot(normed[...], attn_w[:, at]).astype(low)
        tick()
    pairs = patch_pairs(128)

    def blocks(p, b):
        row = pl.ds(b * 128, 128)
        return row, [pl.ds(pl.multiple_of(base + p * 128, 128), 128) for base in (0, D, 2 * D)]

    def attend(p, carry):
        for b in range(rows // 128):
            row, (qa, ka, va) = blocks(p, b)
            k, v = qkv[row, ka], qkv[row, va]
            left, queries = halves_of(qkv[row, qa])
            outs = []
            for h in range(2):
                scores = flat_dot(queries[h], k, ((1,), (1,))) * scale
                scores = jnp.where(pairs, scores, -1e30)
                e = jnp.exp(scores - jnp.max(scores, axis=1, keepdims=True))
                w = e / jnp.sum(e, axis=1, keepdims=True)
                weights[p, b, h] = w
                outs.append(flat_dot(w.astype(low), v))
            heads[row, qa] = jnp.where(left, outs[0], outs[1]).astype(low)
        return carry

    for begin in range(0, D // 128, 2):
        lax.fori_loop(begin, begin + 2, attend, 0)
        tick()
    attended[...] = streams[...] + flat_dot(heads[...], attn_w[:, pl.ds(3 * D, D)])
    ffn_low[...] = rms_scale(attended[...], gain_f).astype(low)
    whole()
    for copy in ffn_loads(0, 0):
        copy.start()
    ffn_t[...] = ffn_low[...].astype(f32).T.astype(low)
    total[...] = attended[...]
    d_ffn[...] = jnp.zeros_like(d_ffn)
    n_ffn = deep.shape[0] // D

    def stores(j):
        at = pl.ds(pl.multiple_of(j * D, D), D)
        return [
            pltpu.make_async_copy(g_buf.at[0], g_gate.at[:, at], g_sem.at[0]),
            pltpu.make_async_copy(g_buf.at[1], g_up.at[:, at], g_sem.at[1]),
            pltpu.make_async_copy(g_buf.at[2], g_down.at[at], g_sem.at[2]),
        ]

    def feed(j, carry):
        slot = lax.rem(j, 2)
        for copy in ffn_loads(j, slot):
            copy.wait()

        @pl.when(j + 1 < n_ffn)
        def _():
            for copy in ffn_loads(j + 1, 1 - slot):
                copy.start()

        gate = flat_dot(ffn_low[...], ffn_w[slot, 0])
        upward = flat_dot(ffn_low[...], ffn_w[slot, 1])
        sig = sigmoid(gate)
        act = gate * sig
        hidden = (act * upward).astype(low)
        total[...] += flat_dot(hidden, ffn_w[slot, 2])
        d_hidden = flat_dot(d_down[...], ffn_w[slot, 2], ((1,), (1,)))
        d_gate = (d_hidden * upward * (sig + act * (1.0 - sig))).astype(low)
        d_up = (d_hidden * act).astype(low)
        d_ffn[...] += flat_dot(d_gate, ffn_w[slot, 0], ((1,), (1,)))
        d_ffn[...] += flat_dot(d_up, ffn_w[slot, 1], ((1,), (1,)))

        @pl.when(j > 0)
        def _():
            for copy in stores(j - 1):
                copy.wait()

        g_buf[0] = flat_dot(ffn_t[...], d_gate).astype(low)
        g_buf[1] = flat_dot(ffn_t[...], d_up).astype(low)
        g_buf[2] = flat_dot(hidden.astype(f32).T.astype(low), d_down[...]).astype(low)
        for copy in stores(j):
            copy.start()
        return carry

    lax.fori_loop(0, n_ffn, feed, 0)
    o_block[...] = (live * total[...]).astype(low)
    d_norm, gain_f_sum = rms_back(attended[...], gain_f, d_ffn[...])
    d_attended = live * grad_ref[...].astype(f32) + d_norm
    total[...] = d_attended
    d_low = d_attended.astype(low)
    for copy in stores(n_ffn - 1):
        copy.wait()
    d_down[...] = flat_dot(d_low, attn_w[:, pl.ds(3 * D, D)], ((1,), (1,))).astype(low)
    g_buf[0] = flat_dot(heads[...].astype(f32).T.astype(low), d_low).astype(low)
    last = [pltpu.make_async_copy(g_buf.at[0], g_attn, g_sem.at[0])]
    last[0].start()

    def attend_back(p, carry):
        for b in range(rows // 128):
            row, (qa, ka, va) = blocks(p, b)
            q, k, v = qkv[row, qa], qkv[row, ka], qkv[row, va]
            grad = d_down[row, qa]
            left, grads = halves_of(grad)
            dq, dk, dv = [], [], []
            for h in range(2):
                w = weights[p, b, h]
                dv.append(flat_dot(w.T.astype(low), grad))
                d_w = flat_dot(grads[h], v, ((1,), (1,)))
                d_s = w * (d_w - jnp.sum(w * d_w, axis=1, keepdims=True))
                dq.append(flat_dot(d_s.astype(low), k) * scale)
                dk.append(flat_dot(d_s.T.astype(low), q) * scale)
            qkv[row, qa] = jnp.where(left, dq[0], dq[1]).astype(low)
            qkv[row, ka] = jnp.where(left, dk[0], dk[1]).astype(low)
            qkv[row, va] = jnp.where(left, dv[0], dv[1]).astype(low)
        return carry

    lax.fori_loop(0, D // 128, attend_back, 0)
    ffn_t[...] = normed[...].astype(f32).T.astype(low)
    for i in range(3):
        at = pl.ds(i * D, D)
        if i == 2:
            last[0].wait()
        buf = (i + 1) % 3
        g_buf[buf] = flat_dot(ffn_t[...], qkv[:, at]).astype(low)
        copy = pltpu.make_async_copy(g_buf.at[buf], g_qkv.at[:, at], g_sem.at[buf])
        copy.start()
        last.append(copy)
    d_ffn[...] = flat_dot(qkv[...], attn_w[:, pl.ds(0, 3 * D)], ((1,), (1,)))
    d_norm, gain_a_sum = rms_back(streams[...], gain_a, d_ffn[...])
    d_streams = total[...] + d_norm
    o_streams[...] = d_streams
    direct = jnp.sum(d_streams.reshape(rows // PATCH, PATCH, D), axis=1)
    o_direct[...] = direct
    mix = direct.astype(low)
    along = jnp.sum(mix.astype(f32) * raw, axis=1, keepdims=True)
    high_r, high_a = (v.astype(low).astype(f32) for v in (mixer_r, along))
    lane = lanes((rows // PATCH, 128), 1)
    ext = jnp.zeros((rows // PATCH, 128), f32)
    for i, v in enumerate((high_r, high_a, mixer_r - high_r, along - high_a)):
        ext = jnp.where(lane == i, v, ext)
    o_mix[:, pl.ds(0, D)] = mix
    o_mix[:, pl.ds(D, 128)] = ext.astype(low)
    o_gains[...] = jnp.concatenate([gain_a_sum, gain_f_sum, jnp.zeros((6, D), f32)], axis=0)
    for copy in last[1:]:
        copy.wait()


N_WIRES = 512
PLAN_F = (
    ("C-1", "r00", "a00"),
    (),
    (),
    (),
    ("b00", "a01"),
    ("r10", "a10", "r01"),
    (),
    ("b10", "a02", "r20"),
    ("c00",),
    ("a20", "b01"),
    ("b20", "r02", "r03", "a03"),
    ("c10",),
    ("b02",),
    ("a30",),
    ("r11", "a11"),
    ("C0",),
    ("b30",),
    ("c20",),
    ("r12", "a12"),
    ("b03",),
    ("r13", "a13"),
    (),
    ("c30", "b11", "b12"),
    ("r21", "a21"),
    ("b13", "r22", "a22"),
    ("C1", "c01", "c02"),
    ("r23", "a23", "b21"),
    ("b22", "c03", "c11"),
    ("a31", "b23", "c12"),
    ("C2", "a32", "c13"),
)
REST_F = (
    "b31",
    "a33",
    "b32",
    "b33",
    "C3",
    "c21",
    "c22",
    "c23",
    "c31",
    "c32",
    "c33",
)
PLAN_B = (
    (),
    (),
    ("a00",),
    ("a01", "a02"),
    ("C0",),
    ("a10",),
    (),
    ("C1",),
    ("a11",),
    ("b00",),
    ("a20",),
    ("C2",),
    ("c00",),
    (),
    (),
    (),
    ("b01", "a12"),
    (),
    (),
    ("b02",),
    ("b10", "a21"),
    (),
    (),
    ("a22", "c01", "b11", "c10"),
    ("a30", "b12", "c02"),
    ("a31", "b20"),
    ("c11", "a32", "b21", "C3"),
)
REST_B = (
    "c12",
    "b22",
    "c20",
    "b30",
    "c21",
    "b31",
    "c22",
    "b32",
    "C4",
    "c30",
    "c31",
    "c32",
)


def forward_kernel(
    depth,
    rows_ref,
    patch_ref,
    cols_ref,
    vec_ref,
    out_ref,
    heads_ref,
    lengths,
    states_ref,
    grad_ref,
    qkv,
    attn,
    gate,
    up,
    down,
    ow,
    od,
    o_block,
    o_streams,
    o_mix,
    o_direct,
    o_gains,
    g_qkv,
    g_attn,
    g_gate,
    g_up,
    g_down,
    sum_ref,
    small_ref,
    bytes_ref,
    norm_ref,
    proj_ref,
    head_w_ref,
    own_ref,
    maps_ref,
    step_ref,
    core_ref,
    mixed_ref,
    attn_w,
    ffn_w,
    g_buf,
    streams,
    normed,
    qkv_low,
    weights,
    mixed_heads,
    attended,
    ffn_low,
    ffn_t,
    total_ref,
    d_ffn,
    d_down,
    load_sem,
    ffn_sem,
    g_sem,
    parts,
    pair,
    near,
    column,
    far,
    parts8,
    pair8,
    near8,
    send,
    recv,
    swap_send,
    swap_recv,
    local,
):
    f32, low = jnp.float32, jnp.bfloat16
    spot = Spot(depth)
    count = 128
    wires = Wires(send, recv)
    mine = pl.multiple_of(spot.me * TILE, TILE)
    bytes_ref[pl.ds(mine, TILE)] = rows_ref[:, pl.ds(pl.multiple_of(spot.me * 256, 256), 256)]
    small_ref[spot.me] = vec_ref[...]
    proj_ref[pl.ds(mine, TILE)] = cols_ref[spot.q]
    head_w_ref[spot.z] = out_ref[...]
    greet(spot)

    def lanes_of(to):
        return rows_ref.at[:, pl.ds(pl.multiple_of(to * 256, 256), 256)]

    swap_bytes = Swap(
        spot,
        swap_send,
        swap_recv,
        lanes_of,
        lambda me: bytes_ref.at[pl.ds(pl.multiple_of(me * TILE, TILE), TILE)],
    )
    swap_bytes.start()
    steps, close = big_gather(wires, spot, ow, od, (qkv, attn, gate, up, down))
    near_proj = plane_swap(
        wires,
        spot,
        lambda q: cols_ref.at[q],
        lambda q: proj_ref.at[pl.ds(pl.multiple_of((spot.z * 8 + q) * TILE, TILE), TILE)],
    )
    small = spread_all(wires, spot, small_ref)
    next(small)
    tick = Ticker(steps, PLAN_F)
    tick()
    own_rows = []
    at = 0
    for i, ref in enumerate((qkv, attn, gate, up)):
        width = ref.shape[1]
        own_rows.append(pltpu.make_async_copy(ref, ow.at[pl.ds(mine, TILE), pl.ds(at, width)], local.at[i]))
        at += width
    deep = down.shape[0]
    own_rows.append(
        pltpu.make_async_copy(down, od.at[pl.ds(pl.multiple_of(spot.me * deep, deep), deep)], local.at[4])
    )
    for copy in own_rows:
        copy.start()
    tick()
    swap_bytes.arrive()
    got(near_proj)
    layer = proj_ref.at[pl.ds(pl.multiple_of(spot.z * 8 * TILE, 8 * TILE), 8 * TILE)]
    far_proj = [wires.copy(layer, layer, spot.above(k)) for k in range(1, depth)]

    for b in range(4):
        block = flat_dot(bytes_ref[pl.ds(b * 256, 256)], patch_ref[...]).astype(low)
        parts[pl.ds(b * 4, 4)] = block.reshape(4, 2, TILE, D)
    tick()
    total = sum_all(wires, spot, parts, pair, near, column, far, sum_ref)
    next(total)
    next(small)
    tick()
    next(total)
    tick()
    next(total)
    next(small)
    tick()
    head_w = [wires.copy(out_ref, head_w_ref.at[spot.z], spot.above(k)) for k in range(1, depth)]
    next(total)
    tick()
    run(small)
    patch_sum = sum_ref[...]
    scale = lax.rsqrt(jnp.mean(patch_sum * patch_sum, axis=1, keepdims=True) + EPSILON)
    gain = gain_row(small_ref[:, TILE + 5, 0:128])
    norm_ref[spot.q] = (patch_sum * scale * gain).astype(low)
    plane = spread_plane(wires, spot, norm_ref)
    next(plane)
    tick()
    next(plane)
    tick()
    got(far_proj)
    taps = tap_rows(spot, small_ref)
    run(plane)
    tick()

    norm = norm_ref[...].reshape(2 * count, D)
    own_ref[...] = flat_dot(norm, proj_ref[...])
    maps_ref[...] = flat_dot(norm, small_ref[:, :TILE, 0:256].reshape(D, 256))
    step_ref[...] = flat_dot(norm, small_ref[:, :TILE, 256:384].reshape(D, 128))
    dt_row, rate_row, skip_row = heads_ref[0:1], heads_ref[1:2], heads_ref[2:3]
    tick()
    got(head_w)
    gains = jnp.concatenate(
        [small_ref[spot.q + 8 * i, TILE : TILE + 16, 0:HEAD_M][6:7].astype(f32) for i in range(4)], axis=1
    )
    for x in range(2):
        at = pl.ds(x * count, count)
        slot = Slot(spot, small_ref, x, count)
        own, maps = own_ref[at], maps_ref[at]
        mix = Mixed(spot, slot, own, maps, step_ref[at], taps, dt_row, rate_row)
        outs = []
        for i in range(4):
            tick()
            inputs = mix.inputs[:, i * HEAD_M : (i + 1) * HEAD_M]
            mixing = (mix.decay(i) * mix.inner * mix.row(mix.step_t, i)).astype(low)
            skip = pick_lane(skip_row, mix.head(i))
            outs.append(flat_dot(mixing, inputs.astype(low)) + skip * inputs)
        core = jnp.concatenate(outs, axis=1)
        core_ref[at] = core
        raw = own[:, :256]
        gated = core * raw * sigmoid(raw)
        part = flat_dot((gated * gains).astype(low), head_w_ref[...].reshape(256, D))
        squares = jnp.sum(gated * gated, axis=1, keepdims=True)
        parts8[pl.ds(x * 2, 2), :, :, pl.ds(0, D)] = part.astype(low).reshape(2, 2, TILE, D)
        parts8[pl.ds(x * 2, 2), :, :, pl.ds(D, 128)] = (
            jnp.broadcast_to(squares, (count, 128)).astype(low).reshape(2, 2, TILE, 128)
        )
        tick()
    for total in sum_plane(wires, spot, parts8, pair8, near8):
        if total is None:
            tick()
    mixed_ref[...] = total

    def ready():
        for copy in own_rows:
            copy.wait()
        close([0])

    def whole():
        tick.rest(REST_F)
        close(range(1, len(CUTS_F) + 2))

    local_block(
        tick,
        ready,
        whole,
        lengths,
        states_ref,
        grad_ref,
        sum_ref,
        mixed_ref,
        small_ref,
        ow,
        od,
        o_block,
        o_streams,
        o_mix,
        o_direct,
        o_gains,
        g_qkv,
        g_attn,
        g_gate,
        g_up,
        g_down,
        attn_w,
        ffn_w,
        g_buf,
        streams,
        normed,
        qkv_low,
        weights,
        mixed_heads,
        attended,
        ffn_low,
        ffn_t,
        total_ref,
        d_ffn,
        d_down,
        load_sem,
        ffn_sem,
        g_sem,
    )
    wires.drain()
    swap_bytes.leave()


def forward_call(
    depth,
    n_dev,
    rows2,
    patch_proj,
    cols,
    vectors,
    out_proj,
    heads,
    lengths,
    byte_states,
    out_grad,
    qkv,
    attn,
    gate,
    up,
    down,
):
    f32, low = jnp.float32, jnp.bfloat16
    vmem = pl.BlockSpec(memory_space=pltpu.VMEM)
    anywhere = pl.BlockSpec(memory_space=pl.ANY)
    smem = pl.BlockSpec(memory_space=pltpu.SMEM)
    shape = jax.ShapeDtypeStruct
    plane_patches = 8 * TILE
    rows, hidden = byte_states.shape[0], down.shape[0] * n_dev
    outs = [
        shape((D, WIDE), low),
        shape((hidden, D), low),
        shape((rows, D), low),
        shape((rows, D), f32),
        shape((rows // PATCH, EXT), low),
        shape((rows // PATCH, D), f32),
        shape((8, D), f32),
        shape((D, 3 * D), low),
        shape((D, D), low),
        shape((D, hidden), low),
        shape((D, hidden), low),
        shape((hidden, D), low),
        shape((TILE, D), f32),
        shape((n_dev, SMALL_ROWS, SMALL_COLS), low),
        shape((n_dev * TILE, 256), low),
        shape((8, TILE, D), low),
        shape((n_dev * TILE, 512), low),
        shape((depth, HEAD_M, D), low),
        shape((plane_patches, 512), f32),
        shape((plane_patches, 256), f32),
        shape((plane_patches, 128), f32),
        shape((plane_patches, 256), f32),
    ]
    scratch = [
        pltpu.VMEM((TILE, EXT), f32),
        pltpu.VMEM((D, 4 * D), low),
        pltpu.VMEM((2, 3, D, D), low),
        pltpu.VMEM((3, D, D), low),
        pltpu.VMEM((rows, D), f32),
        pltpu.VMEM((rows, D), low),
        pltpu.VMEM((rows, 3 * D), low),
        pltpu.VMEM((D // 128, rows // 128, 2, 128, 128), f32),
        pltpu.VMEM((rows, D), low),
        pltpu.VMEM((rows, D), f32),
        pltpu.VMEM((rows, D), low),
        pltpu.VMEM((D, rows), low),
        pltpu.VMEM((rows, D), f32),
        pltpu.VMEM((rows, D), f32),
        pltpu.VMEM((rows, D), low),
        pltpu.SemaphoreType.DMA((1,)),
        pltpu.SemaphoreType.DMA((2, 3)),
        pltpu.SemaphoreType.DMA((3,)),
        pltpu.VMEM((16, 2, TILE, D), low),
        pltpu.VMEM((16, TILE, D), low),
        pltpu.VMEM((3, depth, TILE, D), low),
        pltpu.VMEM((depth, TILE, D), low),
        pltpu.VMEM((depth - 1, TILE, D), low),
        pltpu.VMEM((4, 2, TILE, EXT), low),
        pltpu.VMEM((4, TILE, EXT), low),
        pltpu.VMEM((3, TILE, EXT), low),
        pltpu.SemaphoreType.DMA((N_WIRES,)),
        pltpu.SemaphoreType.DMA((N_WIRES,)),
        pltpu.SemaphoreType.DMA((n_dev,)),
        pltpu.SemaphoreType.DMA((n_dev,)),
        pltpu.SemaphoreType.DMA((5,)),
    ]
    found = pl.pallas_call(
        partial(forward_kernel, depth),
        out_shape=outs,
        in_specs=[vmem] * 6 + [smem] + [vmem] * 2 + [anywhere] * 5,
        out_specs=[anywhere] * 2 + [vmem] * 5 + [anywhere] * 5 + [vmem] * 10,
        scratch_shapes=scratch,
        compiler_params=pltpu.CompilerParams(
            collective_id=0, has_side_effects=True, vmem_limit_bytes=62 * 2**20
        ),
        name="global_forward",
    )(rows2, patch_proj, cols, vectors, out_proj, heads, lengths, byte_states, out_grad, qkv, attn, gate, up, down)
    block, streams, mix, direct, gains, *rest = found[2:]
    return (block, streams, mix, direct, gains), rest[:5], rest[5], rest[6:]


def add_to(dst, sources, width):
    def one(i, carry):
        at = pl.ds(pl.multiple_of(i * STEP, STEP), STEP)
        total = sources[0](at).astype(jnp.float32)
        for source in sources[1:]:
            total = total + source(at).astype(jnp.float32)
        dst(at, total)
        return carry

    lax.fori_loop(0, width // STEP, one, 0)


def big_scatter(wires, spot, grads, bufs, outs, local):
    f32, low = jnp.float32, jnp.bfloat16
    held_w, held_d, stage_w, stage_d, near_w, near_d, last_w, last_d, ring_w, ring_d, climb_c, flat_c = bufs
    half, deep = (WIDE - FAR_B) // 2, held_d.shape[2]
    xn, yn, cn, zn = spot.flip(2)[0], spot.flip(1)[0], spot.sibling(), spot.above(1)
    here, xp, yp, xy = spot.plane, spot.flip(2)[1], spot.flip(1)[1], spot.flip(3)[1]
    T = [spot.column[k % spot.depth] for k in range(1, spot.depth + 1)]
    core, fetch, near, last, ring = {}, {}, {}, {}, {}
    A, B, C = pl.ds(0, half), pl.ds(half, half), pl.ds(2 * half, FAR_B)
    AB = pl.ds(0, 2 * half)
    climb, flat = {}, []
    DA, DB = pl.ds(0, deep // 2), pl.ds(deep // 2, deep // 2)

    def load(k):
        fetch[k] = []
        for i, ref in enumerate(grads):
            dst = stage_w.at[:, :, pl.ds(*PARTS[i])] if i < 4 else stage_d
            copy = pltpu.make_async_copy(ref.at[T[k], :, spot.c], dst, local.at[k * 5 + i])
            copy.start()
            fetch[k].append(copy)

    def open_core(k):
        core[k] = []
        for i, ref in enumerate(grads):
            dst = held_w.at[T[k], :, :, pl.ds(*PARTS[i])] if i < 4 else held_d.at[T[k]]
            core[k].append(wires.copy(ref.at[T[k], :, 1 - spot.c], dst, cn))

    def join(k):
        t = T[k]
        got(core[k])
        for copy in fetch[k]:
            copy.wait()
        for plane in range(4):

            def put_w(at, total, plane=plane):
                held_w[t, plane, :, at] = total.astype(low)

            add_to(put_w, [lambda at, p=plane: held_w[t, p, :, at], lambda at, p=plane: stage_w[p, :, at]], WIDE)
            held_d[t, plane] = (held_d[t, plane].astype(f32) + stage_d[plane].astype(f32)).astype(low)
        if k + 1 < spot.depth:
            load(k + 1)

    parts, at = [], 0
    for i, width in enumerate(CUTS):
        end = i == len(CUTS) - 1
        width = half - at if end else width
        parts.append((at, width, end))
        at += width

    def spans(i):
        at, width, end = parts[i]
        found = [(pl.ds(at, width), pl.ds(half + at, width))]
        return found, end

    def near_sends(k, i):
        t = T[k]
        [(a, b)], end = spans(i)
        sends = []
        for x in range(2):
            src = x * 2 + (1 - spot.y)
            sends.append(wires.copy(held_w.at[t, src, :, a], near_w.at[k, x, :, a], yn))
            if end:
                sends.append(wires.copy(held_d.at[t, src, DA], near_d.at[k, x, DA], yn))
        for y in range(2):
            src = (1 - spot.x) * 2 + y
            sends.append(wires.copy(held_w.at[t, src, :, b], near_w.at[k, y, :, b], xn))
            if end:
                sends.append(wires.copy(held_d.at[t, src, DB], near_d.at[k, y, DB], xn))
        near[k, i] = sends

    def first(k, i):
        if i == 0:
            join(k)
        near_sends(k, i)

    def second(k, i):
        t = T[k]
        got(near[k, i])
        at, width, end = parts[i]
        for other in range(2):
            for plane, base in ((other * 2 + spot.y, at), (spot.x * 2 + other, half + at)):
                moved = lambda c, base=base: pl.ds(pl.multiple_of(c.start + base, STEP), STEP)

                def put(c, total, plane=plane, moved=moved):
                    held_w[t, plane, :, moved(c)] = total.astype(low)

                add_to(
                    put,
                    [
                        lambda c, p=plane, m=moved: held_w[t, p, :, m(c)],
                        lambda c, o=other, m=moved: near_w[k, o, :, m(c)],
                    ],
                    width,
                )
            if end:
                pa, pb = other * 2 + spot.y, spot.x * 2 + other
                held_d[t, pa, DA] = (held_d[t, pa, DA].astype(f32) + near_d[k, other, DA].astype(f32)).astype(low)
                held_d[t, pb, DB] = (held_d[t, pb, DB].astype(f32) + near_d[k, other, DB].astype(f32)).astype(low)
        [(a, b)], _ = spans(i)
        sends = [
            wires.copy(held_w.at[t, xp, :, a], last_w.at[k, :, a], xn),
            wires.copy(held_w.at[t, yp, :, b], last_w.at[k, :, b], yn),
        ]
        if end:
            sends.append(wires.copy(held_d.at[t, xp, DA], last_d.at[k, DA], xn))
            sends.append(wires.copy(held_d.at[t, yp, DB], last_d.at[k, DB], yn))
        last[k, i] = sends

    def finish(terms, begin, end):
        for out, (base, size) in zip(outs, PARTS):
            a, b = max(begin, base), min(end, base + size)

            def put_out(at, total, out=out, shift_by=a - base):
                out[:, pl.ds(pl.multiple_of(at.start + shift_by, STEP), STEP)] = total

            if a < b:
                moved = [
                    lambda at, f=f, a=a: f(pl.ds(pl.multiple_of(at.start + a, STEP), STEP)) for f in terms
                ]
                add_to(put_out, moved, b - a)

    def far(k):
        t = T[k]
        if k:
            got(climb[k - 1])
            for plane in range(4):
                base = lambda at: pl.ds(pl.multiple_of(at.start + 2 * half, STEP), STEP)

                def put_far(at, total, plane=plane):
                    held_w[t, plane, :, base(at)] = total.astype(low)

                terms = [
                    lambda at, p=plane: held_w[t, p, :, base(at)],
                    lambda at, p=plane: climb_c[k - 1, p, :, at],
                ]
                add_to(put_far, terms, FAR_B)
        if k < spot.depth - 1:
            climb[k] = [wires.copy(held_w.at[t, :, :, C], climb_c.at[k], zn)]
        else:
            for way in (1, 2, 3):
                to, plane = spot.flip(way)
                flat.append(wires.copy(held_w.at[t, plane, :, C], flat_c.at[way - 1], to))

    def far_end():
        got(flat)
        terms = [lambda at: held_w[T[-1], here, :, at]]
        for way in range(3):
            terms.append(
                lambda at, w=way: flat_c[w, :, pl.ds(pl.multiple_of(at.start - 2 * half, STEP), STEP)]
            )
        finish(terms, 2 * half, WIDE)

    def third(k, i):
        t = T[k]
        got(last[k, i])
        if k:
            got(ring[k - 1, i])
        at, width, end = parts[i]
        [(a, b)], _ = spans(i)
        terms = [lambda c: held_w[t, here, :, c], lambda c: last_w[k, :, c]]
        if k:
            terms.append(lambda c: ring_w[k - 1, :, c])
        if end:
            down = held_d[t, here].astype(f32) + last_d[k].astype(f32)
            if k:
                down = down + ring_d[k - 1].astype(f32)
        if k == spot.depth - 1:
            finish(terms, at, at + width)
            finish(terms, half + at, half + at + width)
            if end:
                outs[4][...] = down
            return
        for base in (at, half + at):
            moved = lambda c, base=base: pl.ds(pl.multiple_of(c.start + base, STEP), STEP)

            def put_on(c, total, moved=moved):
                held_w[t, here, :, moved(c)] = total.astype(low)

            add_to(put_on, [lambda c, f=f, m=moved: f(m(c)) for f in terms], width)
        ring[k, i] = [wires.copy(held_w.at[t, here, :, c], ring_w.at[k, :, c], zn) for c in (a, b)]
        if end:
            held_d[t, here] = down.astype(low)
            ring[k, i].append(wires.copy(held_d.at[t, here], ring_d.at[k], zn))

    load(0)
    for k in range(spot.depth):
        open_core(k)
    steps = {"C%d" % k: partial(far, k) for k in range(spot.depth)}
    steps["C%d" % spot.depth] = far_end
    for i in range(len(CUTS)):
        for k in range(spot.depth):
            steps["a%d%d" % (k, i)] = partial(first, k, i)
            steps["b%d%d" % (k, i)] = partial(second, k, i)
            steps["c%d%d" % (k, i)] = partial(third, k, i)
    return steps


class Back:
    def __init__(self, mix, own, core, ext, d_patch, gains, head_w, heads, taps, tick):
        f32, low = jnp.float32, jnp.bfloat16
        count = mix.count
        dt_row, rate_row, skip_row = heads[0:1], heads[1:2], heads[2:3]
        r = ext[:, 0:1] + ext[:, 2:3]
        along = ext[:, 1:2] + ext[:, 3:4]
        raw = own[:, :256]
        sig = sigmoid(raw)
        gated = core * raw * sig
        back = flat_dot(d_patch, head_w, ((1,), (1,)))
        self.norm = (gated * r * gains).astype(low)
        self.gain = jnp.sum(back * gated * r, axis=0, keepdims=True)
        d_gated = r * gains * back - gated * (r * r * r * along * (1.0 / DI))
        d_core = d_gated * raw * sig
        d_gate = d_gated * core * sig * (1.0 + raw * (1.0 - sig))
        lane = lanes((1, 128), 1)
        graph = jnp.zeros((count, count), f32)
        d_inputs = []
        direct = jnp.zeros((count, 128), f32)
        flow = jnp.zeros((count, 128), f32)
        d_skip = jnp.zeros((1, 128), f32)
        for i in range(4):
            tick()
            cut = slice(i * HEAD_M, (i + 1) * HEAD_M)
            inputs, grad = mix.inputs[:, cut], d_core[:, cut]
            decay, step = mix.decay(i), mix.row(mix.step_t, i)
            kept = decay * mix.inner
            skip = pick_lane(skip_row, mix.head(i))
            d_mixing = flat_dot(grad.astype(low), inputs.astype(low), ((1,), (1,)))
            d_inputs.append(
                flat_dot((kept * step).astype(low), grad.astype(low), ((0,), (0,))) + skip * grad
            )
            graph = graph + decay * step * d_mixing
            turn = kept * d_mixing
            arrive = jnp.sum(turn.T, axis=1, keepdims=True)
            leave = jnp.sum(turn * step, axis=1, keepdims=True)
            here = lane == mix.head(i)
            direct = direct + jnp.where(here, arrive, 0.0)
            flow = flow + jnp.where(here, leave - mix.col(mix.step, i) * arrive, 0.0)
            d_skip = d_skip + jnp.where(here, jnp.sum(grad * inputs, keepdims=True).reshape(1, 1), 0.0)
        tail = exact_dot(mix.upper, flow)
        mine = own_lanes(lane, mix)
        d_step = jnp.where(mine, direct + rate_row * tail, 0.0)
        d_raw = d_step * sigmoid(mix.raw)
        self.skip = d_skip
        self.rate = jnp.sum(rate_row * mix.step * jnp.where(mine, tail, 0.0), axis=0, keepdims=True)
        self.bias = jnp.sum(d_raw, axis=0, keepdims=True)
        low_graph = graph.astype(low)
        d_out_map = flat_dot(low_graph, mix.in_map)
        d_in_map = flat_dot(low_graph, mix.out_map, ((0,), (0,)))
        d_act = jnp.concatenate(d_inputs + [d_in_map, d_out_map], axis=1)
        d_conv = d_act * (mix.sig * (1.0 + mix.conv * (1.0 - mix.sig)))
        d_channels = jnp.zeros_like(d_conv)
        self.taps = [None] * CONV + [jnp.sum(d_conv, axis=0, keepdims=True)]
        for s in range(CONV):
            kept = d_conv * mix.slot.same[s]
            d_channels = d_channels + taps[CONV - 1 - s] * shift(kept, -s)
            self.taps[CONV - 1 - s] = jnp.sum(kept * shift(mix.channels, s), axis=0, keepdims=True)
        self.rows = jnp.concatenate([d_gate, d_channels, d_raw], axis=1).astype(low)


def own_lanes(lane, mix):
    mine = lane == mix.head(0)
    for i in range(1, 4):
        mine = mine | (lane == mix.head(i))
    return mine


COLS = 512 + 256 + 128


def backward_kernel(
    depth,
    mix_ref,
    direct_ref,
    sum_ref,
    gains_ref,
    small_ref,
    bytes_ref,
    norm_ref,
    proj_ref,
    head_w_ref,
    own_ref,
    maps_ref,
    step_ref,
    core_ref,
    patch_ref,
    heads_ref,
    g_qkv,
    g_attn,
    g_gate,
    g_up,
    g_down,
    o_qkv,
    o_attn,
    o_gate,
    o_up,
    o_down,
    o_patch,
    o_rows,
    o_head,
    o_cols,
    o_maps,
    all_ref,
    mix_all,
    rows_all,
    head_sum,
    head_low,
    head_far,
    col_send,
    col_recv,
    col_far,
    col_sum,
    back_send,
    parts8,
    pair8,
    near8,
    held_w,
    held_d,
    stage_w,
    stage_d,
    near_w,
    near_d,
    last_w,
    last_d,
    ring_w,
    ring_d,
    climb_c,
    flat_c,
    send,
    recv,
    swap_send,
    swap_recv,
    local,
):
    f32, low = jnp.float32, jnp.bfloat16
    spot = Spot(depth)
    count = 128
    wires = Wires(send, recv)
    mix_all[spot.q] = mix_ref[...]
    greet(spot)
    plane = spread_plane(wires, spot, mix_all)
    next(plane)
    steps = big_scatter(
        wires,
        spot,
        (g_qkv, g_attn, g_gate, g_up, g_down),
        (held_w, held_d, stage_w, stage_d, near_w, near_d, last_w, last_d, ring_w, ring_d, climb_c, flat_c),
        (o_qkv, o_attn, o_gate, o_up, o_down),
        local,
    )
    tick = Ticker(steps, PLAN_B)
    tick()
    next(plane)
    tick()
    taps = tap_rows(spot, small_ref)
    heads = heads_ref[...]
    dt_row, rate_row = heads[0:1], heads[1:2]
    gains = jnp.concatenate(
        [small_ref[spot.q + 8 * i, TILE : TILE + 16, 0:HEAD_M][6:7].astype(f32) for i in range(4)], axis=1
    )
    gain = gain_row(small_ref[:, TILE + 5, 0:128])
    run(plane)
    tick()
    sums = None
    for x in range(2):
        at = pl.ds(x * count, count)
        slot = Slot(spot, small_ref, x, count)
        mix = Mixed(spot, slot, own_ref[at], maps_ref[at], step_ref[at], taps, dt_row, rate_row)
        d_patch = mix_all[pl.ds(x * 4, 4), :, pl.ds(0, D)].reshape(count, D)
        ext = mix_all[pl.ds(x * 4, 4), :, pl.ds(D, 128)].reshape(count, 128).astype(f32)
        back = Back(
            mix, own_ref[at], core_ref[at], ext, d_patch, gains, head_w_ref[...].reshape(256, D), heads, taps, tick
        )
        rows_all[at] = back.rows
        tick()
        head = flat_dot(back.norm, d_patch, ((0,), (0,)))
        head_sum[...] = head if x == 0 else head_sum[...] + head
        new = [*back.taps, back.gain, back.bias, back.rate, back.skip]
        sums = new if sums is None else [a + b for a, b in zip(sums, new)]
        grad = flat_dot(back.rows[:, :512], proj_ref[...], ((1,), (1,)))
        grad = grad + flat_dot(
            back.rows[:, 512:], small_ref[:, :TILE, :].reshape(D, SMALL_COLS), ((1,), (1,))
        )
        parts8[pl.ds(x * 2, 2)] = grad.astype(low).reshape(2, 2, TILE, D)
        tick()
    total8 = sum_plane(wires, spot, parts8, pair8, near8)
    next(total8)
    tick()
    head_low[...] = head_sum[...].astype(low).reshape(depth, HEAD_M, D)
    next(total8)
    tick()
    norm = norm_ref[...].reshape(2 * count, D)
    rows = rows_all[...]
    for b in range(4):
        block = flat_dot(norm[:, b * 256 : (b + 1) * 256], rows, ((0,), (0,)))
        col_send[pl.ds(b * 8, 8)] = block.astype(low).reshape(8, TILE, COLS)
    tick()
    grad_norm = next(total8)
    tick()
    patch_sum = sum_ref[...]
    scale = lax.rsqrt(jnp.mean(patch_sum * patch_sum, axis=1, keepdims=True) + EPSILON)
    along = jnp.mean(grad_norm * gain * patch_sum, axis=1, keepdims=True)
    d_sum = direct_ref[...] + scale * gain * grad_norm - patch_sum * (scale * scale * scale * along)
    gain_sum = jnp.sum(grad_norm * patch_sum * scale, axis=0, keepdims=True)
    wide = lambda row: jnp.concatenate([row, jnp.zeros((1, D - row.shape[1]), f32)], axis=1)
    lines = [wide(row) for row in sums[: CONV + 1]]
    lines += [wide(jnp.concatenate(sums[CONV + 1 :], axis=1)), gains_ref[0:1], gains_ref[1:2], gain_sum]
    lines += [jnp.zeros((16 - len(lines), D), f32)]
    all_ref[spot.me] = jnp.concatenate([d_sum, *lines], axis=0).astype(low)
    spread = spread_all(wires, spot, all_ref)
    next(spread)
    col_ring = [
        wires.copy(col_send.at[pl.ds(((spot.z + k) % depth) * 8, 8)], col_far.at[k - 1], spot.above(k))
        for k in range(1, depth)
    ]
    head_ring = [
        wires.copy(head_low.at[(spot.z + k) % depth], head_far.at[k - 1], spot.above(k)) for k in range(1, depth)
    ]
    tick()
    next(spread)
    tick()
    next(spread)
    tick()
    run(spread)
    tick()
    d_all = all_ref[:, :TILE].reshape(-1, D)
    for b in range(4):
        back_send[pl.ds(b * 8, 8)] = (
            flat_dot(d_all[b * 256 : (b + 1) * 256], patch_ref[...], ((1,), (1,))).astype(low).reshape(8, TILE, 256)
        )
    swap_rows = Swap(
        spot,
        swap_send,
        swap_recv,
        lambda to: back_send.at[to],
        lambda me: o_rows.at[:, pl.ds(pl.multiple_of(me * 256, 256), 256)],
    )
    swap_rows.start()
    got(col_ring)
    for q in range(8):
        total = col_send[spot.z * 8 + q].astype(f32)
        for k in range(depth - 1):
            total = total + col_far[k, q].astype(f32)
        col_sum[q] = total.astype(low)
    col_plane = plane_swap(wires, spot, lambda q: col_sum.at[q], lambda q: col_recv.at[q])
    col_recv[spot.q] = col_sum[spot.q]
    tick()
    o_rows[:, pl.ds(pl.multiple_of(spot.me * 256, 256), 256)] = back_send[spot.me]
    o_patch[...] = flat_dot(bytes_ref[...], d_all, ((0,), (0,)))
    tick()
    got(head_ring)
    total = head_low[spot.z].astype(f32)
    for k in range(depth - 1):
        total = total + head_far[k].astype(f32)
    o_head[...] = total
    tick()
    got(col_plane)
    total = jnp.zeros((TILE, COLS - 512), f32)
    for q in range(8):
        o_cols[q] = col_recv[q, :, :512].astype(f32)
        total = total + col_recv[q, :, 512:].astype(f32)
    o_maps[...] = total
    tick()
    tick.rest(REST_B)
    swap_rows.arrive()
    wires.drain()
    swap_rows.leave()


def backward_call(depth, n_dev, mix, direct, patch_sum, gains, saved, patch_proj, heads, grads):
    f32, low = jnp.float32, jnp.bfloat16
    vmem = pl.BlockSpec(memory_space=pltpu.VMEM)
    anywhere = pl.BlockSpec(memory_space=pl.ANY)
    shape = jax.ShapeDtypeStruct
    deep = grads[4].shape[0] // n_dev
    cut = [g.reshape(depth, 4, 2, g.shape[0] // n_dev, g.shape[1]) for g in grads]
    outs = [shape((TILE, width), f32) for _, width in PARTS] + [
        shape((deep, D), f32),
        shape((256, D), f32),
        shape((TILE, PATCH * D), low),
        shape((HEAD_M, D), f32),
        shape((8, TILE, 512), f32),
        shape((TILE, COLS - 512), f32),
        shape((n_dev, SMALL_ROWS, D), low),
    ]
    scratch = [
        pltpu.VMEM((8, TILE, EXT), low),
        pltpu.VMEM((8 * TILE, COLS), low),
        pltpu.VMEM((256, D), f32),
        pltpu.VMEM((depth, HEAD_M, D), low),
        pltpu.VMEM((depth - 1, HEAD_M, D), low),
        pltpu.VMEM((n_dev, TILE, COLS), low),
        pltpu.VMEM((8, TILE, COLS), low),
        pltpu.VMEM((depth - 1, 8, TILE, COLS), low),
        pltpu.VMEM((8, TILE, COLS), low),
        pltpu.VMEM((n_dev, TILE, 256), low),
        pltpu.VMEM((4, 2, TILE, D), low),
        pltpu.VMEM((4, TILE, D), low),
        pltpu.VMEM((3, TILE, D), low),
        pltpu.VMEM((depth, 4, TILE, WIDE), low),
        pltpu.VMEM((depth, 4, deep, D), low),
        pltpu.VMEM((4, TILE, WIDE), low),
        pltpu.VMEM((4, deep, D), low),
        pltpu.VMEM((depth, 2, TILE, WIDE - FAR_B), low),
        pltpu.VMEM((depth, 2, deep, D), low),
        pltpu.VMEM((depth, TILE, WIDE - FAR_B), low),
        pltpu.VMEM((depth, deep, D), low),
        pltpu.VMEM((depth - 1, TILE, WIDE - FAR_B), low),
        pltpu.VMEM((depth - 1, deep, D), low),
        pltpu.VMEM((depth - 1, 4, TILE, FAR_B), low),
        pltpu.VMEM((3, TILE, FAR_B), low),
        pltpu.SemaphoreType.DMA((N_WIRES,)),
        pltpu.SemaphoreType.DMA((N_WIRES,)),
        pltpu.SemaphoreType.DMA((n_dev,)),
        pltpu.SemaphoreType.DMA((n_dev,)),
        pltpu.SemaphoreType.DMA((5 * depth,)),
    ]
    return pl.pallas_call(
        partial(backward_kernel, depth),
        out_shape=outs,
        in_specs=[vmem] * 15 + [anywhere] * 5,
        out_specs=[vmem] * 11,
        scratch_shapes=scratch,
        compiler_params=pltpu.CompilerParams(
            collective_id=1, has_side_effects=True, vmem_limit_bytes=62 * 2**20
        ),
        name="global_backward",
    )(mix, direct, patch_sum, gains, *saved, patch_proj, heads, *cut)


BC = 2 * STATE


def fast_body(
    depth_fsdp,
    byte_states,
    doc_lengths,
    out_grad,
    patch_proj,
    global_gain,
    in_proj,
    conv_weight,
    conv_bias,
    dt_bias,
    a_log,
    skip_weight,
    mixer_gain,
    out_proj,
    attn_gain,
    qkv_proj,
    attn_out,
    ffn_gain,
    gate_proj,
    up_proj,
    down_proj,
):
    f32, low = jnp.float32, jnp.bfloat16
    depth, n_dev = depth_fsdp[0] // 2, depth_fsdp[0] * depth_fsdp[1]
    me = lax.axis_index("dp") * depth_fsdp[1] + lax.axis_index("fsdp")
    rows = byte_states.shape[0]
    patches = rows // PATCH

    shard_rows = in_proj.shape[0]
    maps_and_steps = jnp.pad(in_proj[:, 2 * DI :], ((0, 0), (0, SMALL_COLS - BC - MHEADS)))
    lines = [conv_weight[:, k] for k in range(CONV)]
    lines += [conv_bias, global_gain, mixer_gain, attn_gain, ffn_gain, doc_lengths.reshape(-1).astype(low)]
    lines = jnp.stack([jnp.pad(line, (0, SMALL_COLS - line.shape[0])) for line in lines])
    vectors = jnp.concatenate(
        [maps_and_steps, lines, jnp.zeros((SMALL_ROWS - shard_rows - lines.shape[0], SMALL_COLS), low)]
    )
    by_place = lambda cols: cols.reshape(shard_rows, 4, 8, HEAD_M).transpose(2, 0, 1, 3).reshape(8, shard_rows, 256)
    cols = jnp.concatenate([by_place(in_proj[:, :DI]), by_place(in_proj[:, DI : 2 * DI])], axis=2)
    heads_in = jnp.pad(jnp.stack([dt_bias, -jnp.exp(a_log), skip_weight]), ((0, 5), (0, 128 - MHEADS)))
    rows2 = byte_states.reshape(patches, PATCH * D)
    (block_out, grad_streams, mix, direct, gains), grads, patch_sum, saved = forward_call(
        depth,
        n_dev,
        rows2,
        patch_proj,
        cols,
        vectors,
        out_proj,
        heads_in,
        doc_lengths,
        byte_states,
        out_grad,
        qkv_proj,
        attn_out,
        gate_proj,
        up_proj,
        down_proj,
    )
    (g_qkv, g_attn, g_gate, g_up, g_down, g_patch, back_rows, g_out, g_cols, g_maps, everyone) = backward_call(
        depth,
        n_dev,
        mix,
        direct,
        patch_sum,
        gains,
        saved,
        patch_proj,
        heads_in,
        grads,
    )
    grad_states = grad_streams + back_rows.reshape(rows, D).astype(f32)

    lines = everyone[:, shard_rows : shard_rows + 9].astype(f32)
    sums = jnp.sum(lines, axis=0)
    own_part = lambda row: lax.dynamic_slice_in_dim(row, me * (D // n_dev), D // n_dev, 0)
    by_plane = jnp.sum(lines.reshape(depth, 8, 9, D), axis=0)
    by_head = lambda rows_of: rows_of.reshape(8, -1, 4, HEAD_M).transpose(1, 2, 0, 3).reshape(-1, DI)
    taps = jnp.concatenate([by_head(by_plane[:, : CONV + 1, :256]), sums[: CONV + 1, 256:512]], axis=1)
    share = CONV_CH // n_dev
    taps = lax.dynamic_slice_in_dim(taps, me * share, share, 1)
    gain_m_sum = by_head(by_plane[:, CONV + 1 : CONV + 2, :256])[0]
    gain_m_sum = lax.dynamic_slice_in_dim(gain_m_sum, me * HEAD_M, HEAD_M, 0)
    head_line = sums[CONV + 1]
    back_cols = lambda cols: cols.reshape(8, shard_rows, 4, HEAD_M).transpose(1, 2, 0, 3).reshape(shard_rows, DI)
    grad_in_proj = jnp.concatenate(
        [back_cols(g_cols[..., :256]), back_cols(g_cols[..., 256:]), g_maps[:, : BC + MHEADS]], axis=1
    )
    return (
        block_out,
        grad_states,
        g_patch,
        own_part(sums[CONV + 4]),
        grad_in_proj,
        taps[:CONV].T,
        taps[CONV],
        head_line[256 : 256 + MHEADS],
        head_line[384 : 384 + MHEADS],
        head_line[512 : 512 + MHEADS],
        gain_m_sum,
        g_out,
        own_part(sums[CONV + 2]),
        g_qkv,
        g_attn,
        own_part(sums[CONV + 3]),
        g_gate,
        g_up,
        g_down,
    )


def solution(mesh):
    in_specs = (
        P(("dp", "fsdp"), None),
        P("dp", None),
        P(("dp", "fsdp"), None),
        P(("dp", "fsdp"), None),
        P(("dp", "fsdp")),
        P(("dp", "fsdp"), None),
        P(("dp", "fsdp"), None),
        P(("dp", "fsdp")),
        P(),
        P(),
        P(),
        P(("dp", "fsdp")),
        P(("dp", "fsdp"), None),
        P(("dp", "fsdp")),
        P(("dp", "fsdp"), None),
        P(("dp", "fsdp"), None),
        P(("dp", "fsdp")),
        P(("dp", "fsdp"), None),
        P(("dp", "fsdp"), None),
        P(("dp", "fsdp"), None),
    )
    out_specs = (
        P(("dp", "fsdp"), None),
        P(("dp", "fsdp"), None),
        P(("dp", "fsdp"), None),
        P(("dp", "fsdp")),
        P(("dp", "fsdp"), None),
        P(("dp", "fsdp"), None),
        P(("dp", "fsdp")),
        P(),
        P(),
        P(),
        P(("dp", "fsdp")),
        P(("dp", "fsdp"), None),
        P(("dp", "fsdp")),
        P(("dp", "fsdp"), None),
        P(("dp", "fsdp"), None),
        P(("dp", "fsdp")),
        P(("dp", "fsdp"), None),
        P(("dp", "fsdp"), None),
        P(("dp", "fsdp"), None),
    )
    dp, fsdp = mesh.shape["dp"], mesh.shape["fsdp"]
    fast = dp * fsdp == MHEADS and fsdp == 4
    chosen = partial(fast_body, (dp, fsdp)) if fast else body
    return jax.shard_map(chosen, mesh=mesh, in_specs=in_specs, out_specs=out_specs, check_vma=False)
```

```python
from functools import partial

import jax
import jax.numpy as jnp
from jax import lax
from jax.experimental import pallas as pl
from jax.experimental.pallas import tpu as pltpu
from jax.sharding import PartitionSpec as P

D = 1024
HEAD = 64
HEAD_M = 64
STATE = 128
CONV = 4
PATCH = 8
DI = 2048
MHEADS = 32
CONV_CH = 2304


EPSILON = 1e-05
HIGHEST = lax.Precision.HIGHEST


def shifted(block, axis, distance):
    devices = range(lax.axis_size(axis))
    route = [(i - distance, i) for i in devices if i - distance in devices]
    return lax.ppermute(block, axis, route)


def prefix(value, axis, combine, identity):
    devices, place = (lax.axis_size(axis), lax.axis_index(axis))
    everything = jax.tree.map(
        lambda part, kind: lax.all_gather(part.astype(kind), axis),
        value,
        (jnp.bfloat16, jnp.bfloat16),
    )
    start = jax.tree.map(
        lambda part, zero: jnp.broadcast_to(jnp.asarray(zero, part.dtype), part.shape),
        value,
        identity,
    )

    def prefix_step(k, before):
        reached = k < place
        new = combine(
            before, jax.tree.map(lambda part, own: part[k].astype(own.dtype), everything, value)
        )
        return jax.tree.map(lambda a, b: jnp.where(reached, a, b), new, before)

    return lax.fori_loop(0, devices, prefix_step, start)


def carried_in(value, axis, combine, identity):
    devices, place = (lax.axis_size(axis), lax.axis_index(axis))
    everything = jax.tree.map(
        lambda part, kind: lax.all_gather(part.astype(kind), axis),
        value,
        jax.tree.map(lambda a: jnp.bfloat16 if a.dtype == jnp.float32 else a.dtype, value),
    )
    start = jax.tree.map(
        lambda part, zero: jnp.broadcast_to(jnp.asarray(zero, part.dtype), part.shape),
        value,
        identity,
    )

    def carried_step(k, before):
        at = devices - 1 - k
        reached = at > place
        new = combine(
            before, jax.tree.map(lambda part, own: part[at].astype(own.dtype), everything, value)
        )
        return jax.tree.map(lambda a, b: jnp.where(reached, a, b), new, before)

    return lax.fori_loop(0, devices, carried_step, start)


def product(left, right):
    return jnp.dot(left, right, preferred_element_type=jnp.float32)


def weight_grad(left, right):
    return lax.dot_general(
        left, right, (((0,), (0,)), ((), ())), preferred_element_type=jnp.float32
    )


def input_grad(grad_rows, weight):
    return lax.dot_general(
        grad_rows, weight, (((1,), (1,)), ((), ())), preferred_element_type=jnp.float32
    )


def rms_scale(value, gain):
    return value * lax.rsqrt(jnp.mean(value * value, axis=-1, keepdims=True) + EPSILON) * gain


def gated_norm(core_out, gate_raw, gain):
    count = core_out.shape[0]
    return rms_scale(core_out.reshape(count, DI) * jax.nn.silu(gate_raw), gain)


def patch_docs(doc_lengths, start, count):
    places = start + jnp.arange(count, dtype=jnp.int32)
    first_end = doc_lengths[0, 0]
    second_end = first_end + doc_lengths[0, 1]
    numbers = (places >= first_end).astype(jnp.int32) + (places >= second_end).astype(jnp.int32)
    return jnp.where(places >= 0, numbers, -1)


def chain(earlier, later):
    return (earlier[0] * later[0], later[1] + later[0][:, None, None] * earlier[1])


def mixer_core(
    channels,
    rim,
    step_raw,
    state_in,
    conv_weight,
    conv_bias,
    dt_bias,
    a_log,
    skip_weight,
    docs,
    rim_docs,
    prev_doc,
):
    count = channels.shape[0]
    padded = jnp.concatenate([rim, channels], axis=0)
    padded_docs = jnp.concatenate([rim_docs, docs])
    total = conv_bias[None, :]
    for shift_k in range(CONV):
        same_doc = (padded_docs[shift_k : shift_k + count] == docs).astype(jnp.float32)
        total = (
            total
            + padded[shift_k : shift_k + count]
            * conv_weight[:, shift_k][None, :]
            * same_doc[:, None]
        )
    activated = jax.nn.silu(total)
    inputs = activated[:, :DI].reshape(count, MHEADS, HEAD_M)
    in_map = activated[:, DI : DI + STATE]
    out_map = activated[:, DI + STATE :]
    step_size = jax.nn.softplus(step_raw + dt_bias[None, :])
    rate = -jnp.exp(a_log)
    lower = jnp.tril(jnp.ones((count, count), jnp.float32))
    cumulative = jnp.dot(lower, step_size * rate[None, :], precision=HIGHEST)
    places = jnp.arange(count, dtype=jnp.int32)
    keep = ((places[:, None] >= places[None, :]) & (docs[:, None] == docs[None, :]))[:, :, None]
    spread = cumulative[:, None, :] - cumulative[None, :, :]
    decay_table = jnp.where(keep, jnp.exp(jnp.where(keep, spread, 0.0)), 0.0)
    inner = jnp.dot(out_map, in_map.T, precision=HIGHEST, preferred_element_type=jnp.float32)
    mixing = decay_table * inner[:, :, None] * step_size[None, :, :]
    outputs = jnp.einsum("tsh,shp->thp", mixing, inputs, precision=HIGHEST)
    carry_in = jnp.where((docs == prev_doc)[:, None], jnp.exp(cumulative), 0.0)
    outputs = outputs + carry_in[:, :, None] * jnp.einsum(
        "tn,hpn->thp", out_map, state_in, precision=HIGHEST
    )
    outputs = outputs + skip_weight[None, :, None] * inputs
    last_doc = docs[count - 1]
    tail_keep = (docs == last_doc)[:, None]
    tail_gap = cumulative[count - 1][None, :] - cumulative
    tail_weight = (
        jnp.where(tail_keep, jnp.exp(jnp.where(tail_keep, tail_gap, 0.0)), 0.0) * step_size
    )
    decay_total = jnp.where(prev_doc == last_doc, jnp.exp(cumulative[count - 1]), 0.0)
    state_out = jnp.einsum("sh,shp,sn->hpn", tail_weight, inputs, in_map, precision=HIGHEST)
    state_out = state_out + decay_total[:, None, None] * state_in
    return ((outputs, state_out), (decay_total, carry_in, out_map))


def attend(qkv_low, patches):
    heads = qkv_low.reshape(patches, PATCH, 3, -1, HEAD)
    queries = heads[:, :, 0]
    key_rows = heads[:, :, 1]
    value_rows = heads[:, :, 2]
    scores = jnp.einsum(
        "pihd,pjhd->phij", queries, key_rows, preferred_element_type=jnp.float32
    ) * HEAD ** (-0.5)
    places = jnp.arange(PATCH)
    causal = places[:, None] >= places[None, :]
    scores = jnp.where(causal, scores, -1e30)
    attn_weights = jax.nn.softmax(scores, axis=-1)
    attn_low = attn_weights.astype(jnp.bfloat16)
    mixed = jnp.einsum("phij,pjhd->pihd", attn_low, value_rows, preferred_element_type=jnp.float32)
    mixed = mixed.astype(jnp.bfloat16).reshape(patches * PATCH, -1)
    return ((queries, key_rows, value_rows, attn_weights, attn_low), mixed)


def attend_back(grad_mixed_low, pieces):
    queries, key_rows, value_rows, attn_weights, attn_low = pieces
    patches = queries.shape[0]
    grad_mixed = grad_mixed_low.reshape(patches, PATCH, -1, HEAD)
    grad_values = jnp.einsum(
        "phij,pihd->pjhd", attn_low, grad_mixed, preferred_element_type=jnp.float32
    )
    grad_weights = jnp.einsum(
        "pihd,pjhd->phij", grad_mixed, value_rows, preferred_element_type=jnp.float32
    )
    grad_scores = attn_weights * (
        grad_weights - jnp.sum(attn_weights * grad_weights, axis=-1, keepdims=True)
    )
    scores_low = grad_scores.astype(jnp.bfloat16)
    scale = HEAD ** (-0.5)
    grad_queries = (
        jnp.einsum("phij,pjhd->pihd", scores_low, key_rows, preferred_element_type=jnp.float32)
        * scale
    )
    grad_keys = (
        jnp.einsum("phij,pihd->pjhd", scores_low, queries, preferred_element_type=jnp.float32)
        * scale
    )
    stacked = jnp.stack([grad_queries, grad_keys, grad_values], axis=2).reshape(patches * PATCH, -1)
    return stacked.astype(jnp.bfloat16)


def local_forward(byte_states, mixed_patch, local_set, live):
    attn_gain, qkv_proj, attn_out, ffn_gain, gate_proj, up_proj, down_proj = local_set
    rows = byte_states.shape[0]
    streams = byte_states.astype(jnp.float32) + jnp.repeat(mixed_patch, PATCH, axis=0)
    normed_low = rms_scale(streams, attn_gain.astype(jnp.float32)).astype(jnp.bfloat16)
    qkv_low = product(normed_low, qkv_proj).astype(jnp.bfloat16)
    pieces, mixed_heads = attend(qkv_low, rows // PATCH)
    attended = streams + product(mixed_heads, attn_out)
    ffn_low = rms_scale(attended, ffn_gain.astype(jnp.float32)).astype(jnp.bfloat16)
    gate = product(ffn_low, gate_proj)
    upward = product(ffn_low, up_proj)
    hidden_low = (jax.nn.silu(gate) * upward).astype(jnp.bfloat16)
    block = live * (attended + product(hidden_low, down_proj))
    cache = (streams, normed_low, pieces, mixed_heads, attended, ffn_low, gate, upward, hidden_low)
    return (block, cache)


def local_backward(grad_block, cache, local_set):
    attn_gain, qkv_proj, attn_out, ffn_gain, gate_proj, up_proj, down_proj = local_set
    streams, normed_low, pieces, mixed_heads, attended, ffn_low, gate, upward, hidden_low = cache
    down_low = grad_block.astype(jnp.bfloat16)
    grad_down = weight_grad(hidden_low, down_low)
    grad_hidden = input_grad(down_low, down_proj)
    sigma = jax.nn.sigmoid(gate)
    grad_gate_low = (grad_hidden * upward * sigma * (1.0 + gate * (1.0 - sigma))).astype(
        jnp.bfloat16
    )
    grad_up_low = (grad_hidden * gate * sigma).astype(jnp.bfloat16)
    grad_gate = weight_grad(ffn_low, grad_gate_low)
    grad_up = weight_grad(ffn_low, grad_up_low)
    grad_ffn_in = input_grad(grad_gate_low, gate_proj) + input_grad(grad_up_low, up_proj)
    _, norm_back = jax.vjp(rms_scale, attended, ffn_gain.astype(jnp.float32))
    grad_attended_norm, grad_ffn_gain = norm_back(grad_ffn_in)
    grad_attended = grad_block + grad_attended_norm
    attn_grad_low = grad_attended.astype(jnp.bfloat16)
    grad_attn_out = weight_grad(mixed_heads, attn_grad_low)
    grad_mixed_low = input_grad(attn_grad_low, attn_out).astype(jnp.bfloat16)
    grad_qkv_low = attend_back(grad_mixed_low, pieces)
    grad_qkv = weight_grad(normed_low, grad_qkv_low)
    grad_normed = input_grad(grad_qkv_low, qkv_proj)
    _, norm_back = jax.vjp(rms_scale, streams, attn_gain.astype(jnp.float32))
    grad_streams_norm, grad_attn_gain = norm_back(grad_normed)
    grad_streams = grad_attended + grad_streams_norm
    return (
        grad_streams,
        (grad_qkv, grad_attn_out, grad_gate, grad_up, grad_down, grad_attn_gain, grad_ffn_gain),
    )


def body(
    byte_states,
    doc_lengths,
    out_grad,
    patch_proj,
    global_gain,
    in_proj,
    conv_weight,
    conv_bias,
    dt_bias,
    a_log,
    skip_weight,
    mixer_gain,
    out_proj,
    attn_gain,
    qkv_proj,
    attn_out,
    ffn_gain,
    gate_proj,
    up_proj,
    down_proj,
):
    rows = byte_states.shape[0]
    patches = rows // PATCH
    share = lax.axis_index("fsdp")
    start = share * patches
    docs = patch_docs(doc_lengths, start, patches)
    rim_docs = patch_docs(doc_lengths, start - (CONV - 1), CONV - 1)
    prev_doc = patch_docs(doc_lengths, start - 1, 1)[0]
    live = jnp.repeat((docs < 2).astype(jnp.float32), PATCH)[:, None]
    all_set = (
        lax.all_gather(patch_proj, ("dp", "fsdp"), axis=0, tiled=True),
        lax.all_gather(global_gain, ("dp", "fsdp"), axis=0, tiled=True),
        lax.all_gather(in_proj, ("dp", "fsdp"), axis=0, tiled=True),
        lax.all_gather(conv_weight, ("dp", "fsdp"), axis=0, tiled=True),
        lax.all_gather(conv_bias, ("dp", "fsdp"), axis=0, tiled=True),
        lax.all_gather(mixer_gain, ("dp", "fsdp"), axis=0, tiled=True),
        lax.all_gather(out_proj, ("dp", "fsdp"), axis=0, tiled=True),
        lax.all_gather(attn_gain, ("dp", "fsdp"), axis=0, tiled=True),
        lax.all_gather(qkv_proj, ("dp", "fsdp"), axis=0, tiled=True),
        lax.all_gather(attn_out, ("dp", "fsdp"), axis=0, tiled=True),
        lax.all_gather(ffn_gain, ("dp", "fsdp"), axis=0, tiled=True),
        lax.all_gather(gate_proj, ("dp", "fsdp"), axis=0, tiled=True),
        lax.all_gather(up_proj, ("dp", "fsdp"), axis=0, tiled=True),
        lax.all_gather(down_proj, ("dp", "fsdp"), axis=0, tiled=True),
    )
    global_set = all_set[:7]
    local_set = all_set[7:]
    patch_full, gain_g_full, in_full, conv_w_full, conv_b_full, gain_m_full, out_full = global_set
    patch_rows = byte_states.reshape(patches, PATCH * D)
    patch_sum = product(patch_rows, patch_full)
    gain_g = gain_g_full.astype(jnp.float32)
    global_low = rms_scale(patch_sum, gain_g).astype(jnp.bfloat16)
    projected = product(global_low, in_full)
    gate_raw = projected[:, :DI]
    channels = projected[:, DI : DI + CONV_CH]
    step_raw = projected[:, DI + CONV_CH :]
    rim = shifted(channels[patches - (CONV - 1) :], "fsdp", 1)
    core = partial(mixer_core, docs=docs, rim_docs=rim_docs, prev_doc=prev_doc)
    conv_w = conv_w_full.astype(jnp.float32)
    conv_b = conv_b_full.astype(jnp.float32)
    empty_state = jnp.zeros((MHEADS, HEAD_M, STATE), jnp.float32)
    (partial_out, local_state), aux = core(
        channels, rim, step_raw, empty_state, conv_w, conv_b, dt_bias, a_log, skip_weight
    )
    decay_total, carry_in, out_map = aux
    identity = (jnp.ones((MHEADS,), jnp.float32), jnp.zeros((MHEADS, HEAD_M, STATE), jnp.float32))
    arrived = prefix((decay_total, local_state), "fsdp", chain, identity)
    state_in = arrived[1]
    mixer_out = partial_out + carry_in[:, :, None] * jnp.einsum(
        "tn,hpn->thp", out_map, state_in, precision=HIGHEST
    )
    gain_m = gain_m_full.astype(jnp.float32)
    mixer_low = gated_norm(mixer_out, gate_raw, gain_m).astype(jnp.bfloat16)
    mixed_patch = patch_sum + product(mixer_low, out_full)
    block, cache = local_forward(byte_states, mixed_patch, local_set, live)
    block_out = block.astype(jnp.bfloat16)
    back_set = (
        lax.all_gather(patch_proj, ("dp", "fsdp"), axis=0, tiled=True),
        lax.all_gather(global_gain, ("dp", "fsdp"), axis=0, tiled=True),
        lax.all_gather(in_proj, ("dp", "fsdp"), axis=0, tiled=True),
        lax.all_gather(conv_weight, ("dp", "fsdp"), axis=0, tiled=True),
        lax.all_gather(conv_bias, ("dp", "fsdp"), axis=0, tiled=True),
        lax.all_gather(mixer_gain, ("dp", "fsdp"), axis=0, tiled=True),
        lax.all_gather(out_proj, ("dp", "fsdp"), axis=0, tiled=True),
        lax.all_gather(attn_gain, ("dp", "fsdp"), axis=0, tiled=True),
        lax.all_gather(qkv_proj, ("dp", "fsdp"), axis=0, tiled=True),
        lax.all_gather(attn_out, ("dp", "fsdp"), axis=0, tiled=True),
        lax.all_gather(ffn_gain, ("dp", "fsdp"), axis=0, tiled=True),
        lax.all_gather(gate_proj, ("dp", "fsdp"), axis=0, tiled=True),
        lax.all_gather(up_proj, ("dp", "fsdp"), axis=0, tiled=True),
        lax.all_gather(down_proj, ("dp", "fsdp"), axis=0, tiled=True),
    )
    global_back = back_set[:7]
    local_back = back_set[7:]
    _, cache = local_forward(byte_states, mixed_patch, local_back, live)
    patch_back, _, in_back, conv_w_back, conv_b_back, _, out_back = global_back
    grad_block = live * out_grad.astype(jnp.float32)
    grad_streams, local_grads = local_backward(grad_block, cache, local_back)
    reduced_local = (
        lax.psum_scatter(local_grads[0], ("dp", "fsdp"), scatter_dimension=0, tiled=True),
        lax.psum_scatter(local_grads[1], ("dp", "fsdp"), scatter_dimension=0, tiled=True),
        lax.psum_scatter(local_grads[2], ("dp", "fsdp"), scatter_dimension=0, tiled=True),
        lax.psum_scatter(local_grads[3], ("dp", "fsdp"), scatter_dimension=0, tiled=True),
        lax.psum_scatter(local_grads[4], ("dp", "fsdp"), scatter_dimension=0, tiled=True),
        lax.psum_scatter(local_grads[5], ("dp", "fsdp"), scatter_dimension=0, tiled=True),
        lax.psum_scatter(local_grads[6], ("dp", "fsdp"), scatter_dimension=0, tiled=True),
    )
    grad_patch_mix = grad_streams.reshape(patches, PATCH, D).sum(axis=1)
    mix_low = grad_patch_mix.astype(jnp.bfloat16)
    grad_out_proj = weight_grad(mixer_low, mix_low)
    grad_mixer_low = input_grad(mix_low, out_back)
    _, norm_back = jax.vjp(gated_norm, mixer_out, gate_raw, gain_m)
    grad_core, grad_gate_raw, grad_mixer_gain = norm_back(grad_mixer_low)
    state_part = jnp.einsum("th,thp,tn->hpn", carry_in, grad_core, out_map, precision=HIGHEST)
    returned = carried_in((decay_total, state_part), "fsdp", chain, identity)
    _, core_back, _ = jax.vjp(
        core,
        channels,
        rim,
        step_raw,
        state_in,
        conv_w_back.astype(jnp.float32),
        conv_b_back.astype(jnp.float32),
        dt_bias,
        a_log,
        skip_weight,
        has_aux=True,
    )
    core_grads = core_back((grad_core, returned[1]))
    (
        grad_channels,
        grad_rim,
        grad_step,
        _,
        grad_conv_w,
        grad_conv_b,
        grad_dt_bias,
        grad_a_log,
        grad_skip,
    ) = core_grads
    rim_grad = shifted(grad_rim, "fsdp", -1)
    cut = patches - (CONV - 1)
    grad_channels = jnp.concatenate([grad_channels[:cut], grad_channels[cut:] + rim_grad], axis=0)
    proj_low = jnp.concatenate([grad_gate_raw, grad_channels, grad_step], axis=1).astype(
        jnp.bfloat16
    )
    grad_in_proj = weight_grad(global_low, proj_low)
    grad_global_norm = input_grad(proj_low, in_back)
    _, norm_back = jax.vjp(rms_scale, patch_sum, gain_g)
    grad_sum_norm, grad_global_gain = norm_back(grad_global_norm)
    sum_low = (grad_patch_mix + grad_sum_norm).astype(jnp.bfloat16)
    grad_patch_proj = weight_grad(patch_rows, sum_low)
    grad_states = grad_streams + input_grad(sum_low, patch_back).reshape(rows, D)
    reduced_global = (
        lax.psum_scatter(grad_patch_proj, ("dp", "fsdp"), scatter_dimension=0, tiled=True),
        lax.psum_scatter(grad_global_gain, ("dp", "fsdp"), scatter_dimension=0, tiled=True),
        lax.psum_scatter(grad_in_proj, ("dp", "fsdp"), scatter_dimension=0, tiled=True),
        lax.psum_scatter(grad_conv_w, ("dp", "fsdp"), scatter_dimension=0, tiled=True),
        lax.psum_scatter(grad_conv_b, ("dp", "fsdp"), scatter_dimension=0, tiled=True),
        lax.psum_scatter(grad_mixer_gain, ("dp", "fsdp"), scatter_dimension=0, tiled=True),
        lax.psum_scatter(grad_out_proj, ("dp", "fsdp"), scatter_dimension=0, tiled=True),
    )
    head_sums = lax.psum((grad_dt_bias, grad_a_log, grad_skip), ("dp", "fsdp"))
    return (
        block_out,
        grad_states,
        reduced_global[0],
        reduced_global[1],
        reduced_global[2],
        reduced_global[3],
        reduced_global[4],
        head_sums[0],
        head_sums[1],
        head_sums[2],
        reduced_global[5],
        reduced_global[6],
        reduced_local[5],
        reduced_local[0],
        reduced_local[1],
        reduced_local[6],
        reduced_local[2],
        reduced_local[3],
        reduced_local[4],
    )


MESH = pl.DeviceIdType.MESH
WIDE = 12288
PARTS = ((0, 3072), (3072, 1024), (4096, 4096), (8192, 4096))
STEP = 1024
FAR_F, FAR_B = 2048, 2048
CUTS = (2048, 2048, 1024)
CUTS_F = (1024, 1024, 1024)
TILE = 32
SMALL_ROWS, SMALL_COLS = 48, 384
EXT = D + 128


def device(z, x, y, c):
    return (z * 2 + x, y * 2 + c)


class Spot:
    def __init__(self, depth):
        dp, fs = lax.axis_index("dp"), lax.axis_index("fsdp")
        self.depth, self.count = depth, depth * 8
        self.me = dp * 4 + fs
        self.z, self.x, self.y, self.c = dp // 2, dp % 2, fs // 2, fs % 2
        self.q = self.x * 4 + self.y * 2 + self.c
        self.plane = self.x * 2 + self.y
        swap = lambda place: place + (place // 2) * (1 - 2 * (place % 2))
        self.turn = swap(self.z)
        self.column = [swap((self.turn + depth - j) % depth) for j in range(depth)]

    def flip(self, way):
        x = 1 - self.x if way & 2 else self.x
        y = 1 - self.y if way & 1 else self.y
        return device(self.z, x, y, self.c), x * 2 + y

    def sibling(self):
        return device(self.z, self.x, self.y, 1 - self.c)

    def onward(self):
        place = (self.turn + 1) % self.depth
        return device(place + (place // 2) * (1 - 2 * (place % 2)), self.x, self.y, self.c)

    def above(self, k):
        return device((self.z + k) % self.depth, self.x, self.y, self.c)


def greet(spot):
    barrier = pltpu.get_barrier_semaphore()

    def one(i, carry):
        to = (spot.me + i) % spot.count
        pl.semaphore_signal(barrier, inc=1, device_id=(to // 4, to % 4), device_id_type=MESH)
        return carry

    lax.fori_loop(1, spot.count, one, 0)
    pl.semaphore_wait(barrier, spot.count - 1)


class Wires:
    def __init__(self, send, recv):
        self.send, self.recv, self.used, self.open = send, recv, 0, []

    def copy(self, src, dst, to):
        i = self.used
        self.used += 1
        copy = pltpu.make_async_remote_copy(
            src_ref=src,
            dst_ref=dst,
            send_sem=self.send.at[i],
            recv_sem=self.recv.at[i],
            device_id=to,
            device_id_type=MESH,
        )
        copy.start()
        self.open.append(copy)
        return copy

    def drain(self):
        for copy in self.open:
            copy.wait_send()


def got(copies):
    for copy in copies:
        copy.wait_recv()


class Swap:
    def __init__(self, spot, send, recv, src_at, dst_at):
        self.spot, self.send, self.recv, self.src_at, self.dst_at = spot, send, recv, src_at, dst_at

    def copy(self, i):
        to = (self.spot.me + i) % self.spot.count
        return pltpu.make_async_remote_copy(
            src_ref=self.src_at(to),
            dst_ref=self.dst_at(self.spot.me),
            send_sem=self.send.at[i],
            recv_sem=self.recv.at[i],
            device_id=(to // 4, to % 4),
            device_id_type=MESH,
        )

    def each(self, act):
        def one(i, carry):
            act(self.copy(i))
            return carry

        lax.fori_loop(1, self.spot.count, one, 0)

    def start(self):
        self.each(lambda copy: copy.start())

    def arrive(self):
        self.each(lambda copy: copy.wait_recv())

    def leave(self):
        self.each(lambda copy: copy.wait_send())


def plane_swap(wires, spot, src_at, dst_at):
    copies = []
    for way in range(4):
        for other in range(2):
            if way or other:
                x = spot.x ^ (way >> 1)
                y = spot.y ^ (way & 1)
                c = spot.c ^ other
                copies.append(
                    wires.copy(src_at(x * 4 + y * 2 + c), dst_at(spot.q), device(spot.z, x, y, c))
                )
    return copies


def block_row(t, plane, c):
    return (t * 4 + plane) * 2 + c


def spread_all(wires, spot, buf, own=None):
    at = lambda t, plane, c: buf.at[block_row(t, plane, c)]
    mine = at(spot.z, spot.plane, spot.c)
    src = mine if own is None else own
    ring, flat, core = [], [], []
    for k in range(1, spot.depth):
        ring.append(wires.copy(src, mine, spot.above(k)))
    flat.append([wires.copy(src, mine, spot.flip(way)[0]) for way in (1, 2, 3)])
    core.append(wires.copy(src, mine, spot.sibling()))
    yield
    for j in range(1, spot.depth):
        got([ring[j - 1]])
        block = at((spot.z + spot.depth - j) % spot.depth, spot.plane, spot.c)
        flat.append([wires.copy(block, block, spot.flip(way)[0]) for way in (1, 2, 3)])
        core.append(wires.copy(block, block, spot.sibling()))
    yield
    for j in range(spot.depth):
        for way in (1, 2, 3):
            got([flat[j][way - 1]])
            block = at((spot.z + spot.depth - j) % spot.depth, spot.flip(way)[1], spot.c)
            core.append(wires.copy(block, block, spot.sibling()))
    yield
    got(core)


def spread_plane(wires, spot, buf):
    at = lambda plane: buf.at[plane * 2 + spot.c]
    mine = at(spot.plane)
    flat = [wires.copy(mine, mine, spot.flip(way)[0]) for way in (1, 2, 3)]
    core = [wires.copy(mine, mine, spot.sibling())]
    yield
    for way in (1, 2, 3):
        got([flat[way - 1]])
        block = at(spot.flip(way)[1])
        core.append(wires.copy(block, block, spot.sibling()))
    yield
    got(core)


def sum_plane(wires, spot, parts, pair, near):
    first = wires.copy(parts.at[:, 1 - spot.c], pair, spot.sibling())
    yield None
    got([first])
    f32 = jnp.float32
    pair[...] = (parts[:, spot.c].astype(f32) + pair[...].astype(f32)).astype(jnp.bfloat16)
    flat = [
        wires.copy(pair.at[spot.flip(way)[1]], near.at[way - 1], spot.flip(way)[0]) for way in (1, 2, 3)
    ]
    yield None
    got(flat)
    total = pair[spot.plane].astype(f32)
    for way in range(3):
        total = total + near[way].astype(f32)
    yield total


def sum_all(wires, spot, parts, pair, near, column, far, out):
    f32, low = jnp.float32, jnp.bfloat16
    half = parts.shape[-1] // 2
    cut = [pl.ds(h * half, half) for h in range(2)]
    first = [
        wires.copy(parts.at[:, 1 - spot.c, :, cut[h]], pair.at[:, :, cut[h]], spot.sibling()) for h in range(2)
    ]
    yield
    flat, ring = [], []
    rows = pair.shape[1]
    for h in range(2):
        got([first[h]])
        for b in range(4 * spot.depth):
            pair[b, :, cut[h]] = (
                parts[b, spot.c, :, cut[h]].astype(f32) + pair[b, :, cut[h]].astype(f32)
            ).astype(low)
        step = []
        for way in (1, 2, 3):
            to, plane = spot.flip(way)
            for t in range(spot.depth):
                step.append(
                    wires.copy(pair.at[t * 4 + plane, :, cut[h]], near.at[way - 1, t, :, cut[h]], to)
                )
        flat.append(step)
    yield
    for h in range(2):
        got(flat[h])
        for t in range(spot.depth):
            total = pair[t * 4 + spot.plane, :, cut[h]].astype(f32)
            for way in range(3):
                total = total + near[way, t, :, cut[h]].astype(f32)
            column[t, :, cut[h]] = total.astype(low)
        ring.append(
            [
                wires.copy(
                    column.at[(spot.z + k) % spot.depth, :, cut[h]], far.at[k - 1, :, cut[h]], spot.above(k)
                )
                for k in range(1, spot.depth)
            ]
        )
    yield
    for h in range(2):
        got(ring[h])
        total = column[spot.z, :, cut[h]].astype(f32)
        for k in range(1, spot.depth):
            total = total + far[k - 1, :, cut[h]].astype(f32)
        out[:, cut[h]] = total
    yield


def big_gather(wires, spot, ow, od, shards):
    down = od.shape[0] // spot.count
    xn, yn, cn, zn = spot.flip(2)[0], spot.flip(1)[0], spot.sibling(), spot.onward()
    here, xp, yp, xy = spot.plane, spot.flip(2)[1], spot.flip(1)[1], spot.flip(3)[1]
    parts = {"C": (WIDE - FAR_F, FAR_F, None), ("A", 0): (0, 2 * D, None), ("B", 0): (2 * D, 2 * D, None)}
    begin, side, at = 4 * D, (WIDE - FAR_F - 4 * D) // 2, 0
    for i, width in enumerate(CUTS_F, 1):
        last = i == len(CUTS_F)
        parts["A", i] = (begin + at, width, (0, down // 2) if last else None)
        parts["B", i] = (begin + side + at, width, (down // 2, down // 2) if last else None)
        at += width
    assert at == side
    mine = pl.multiple_of(spot.me * TILE, TILE)
    row = pl.multiple_of(spot.me * down, down)

    def refs(t, plane, part):
        begin, width, deep = parts[part]
        r = block_row(t, plane, spot.c)
        found = [ow.at[pl.ds(pl.multiple_of(r * TILE, TILE), TILE), pl.ds(begin, width)]]
        if deep:
            found.append(od.at[pl.ds(pl.multiple_of(r * down + deep[0], deep[1]), deep[1])])
        return found

    def go(t, plane, part, to):
        return [wires.copy(r, r, to) for r in refs(t, plane, part)]

    def own(part, to):
        begin, width, deep = parts[part]
        pairs = []
        for ref, (base, size) in zip(shards[:4], PARTS):
            low, high = max(begin, base), min(begin + width, base + size)
            if low < high:
                pairs.append(
                    (ref.at[:, pl.ds(low - base, high - low)], ow.at[pl.ds(mine, TILE), pl.ds(low, high - low)])
                )
        if deep:
            pairs.append(
                (shards[4].at[pl.ds(*deep)], od.at[pl.ds(pl.multiple_of(row + deep[0], deep[1]), deep[1])])
            )
        return [wires.copy(a, b, to) for a, b in pairs]

    T = spot.column
    core, ring, fx, fy, sx, sy = {i: [] for i in range(len(CUTS_F) + 2)}, {}, {}, {}, {}, {}

    def arrived(j, i):
        if (j - 1, i) in ring:
            got(ring.pop((j - 1, i)))

    def climb_on(j, i):
        send = own if j == 0 else (lambda part, to: go(T[j], here, part, to))
        arrived(j, i)
        ring[j, i] = send(("A", i), zn) + send(("B", i), zn)

    def first(j, i):
        send = own if j == 0 else (lambda part, to: go(T[j], here, part, to))
        arrived(j, i)
        fx[j, i], fy[j, i] = send(("A", i), xn), send(("B", i), yn)
        core[i].append(send(("A", i), cn) + send(("B", i), cn))

    def second(j, i):
        send = own if j == 0 else (lambda part, to: go(T[j], here, part, to))
        got(fx[j, i])
        sy[j, i] = send(("A", i), yn) + go(T[j], xp, ("A", i), yn)
        got(fy[j, i])
        sx[j, i] = send(("B", i), xn) + go(T[j], yp, ("B", i), xn)
        core[i].append(go(T[j], xp, ("A", i), cn) + go(T[j], yp, ("B", i), cn))

    def third(j, i):
        got(sy[j, i])
        core[i].append(go(T[j], yp, ("A", i), cn) + go(T[j], xy, ("A", i), cn))
        got(sx[j, i])
        core[i].append(go(T[j], xp, ("B", i), cn) + go(T[j], xy, ("B", i), cn))

    flat, climb = [], {}

    def far(j):
        if j < 0:
            flat.extend(own("C", spot.flip(way)[0]) for way in (1, 2, 3))
            core[len(CUTS_F) + 1].append(own("C", cn))
            return
        if j == 0:
            for copies in flat:
                got(copies)
        else:
            got(climb[j - 1])
        if j < spot.depth - 1:
            climb[j] = own("C", zn) if j == 0 else go(T[j], here, "C", zn)
            for plane in (xp, yp, xy):
                climb[j] += go(T[j], plane, "C", zn)
        for plane in (xp, yp, xy) + ((here,) if j else ()):
            core[len(CUTS_F) + 1].append(go(T[j], plane, "C", cn))

    chunks, n = range(len(CUTS_F) + 1), spot.depth
    steps = {far_step(j): partial(far, j) for j in range(-1, n)}
    for i in chunks:
        for j in range(n):
            for kind, act in enumerate((climb_on, first, second, third), 1):
                if act is not climb_on or j < n - 1:
                    steps[100 * kind + 10 * j + i] = partial(act, j, i)

    def close(which):
        for part in which:
            for copies in core.pop(part):
                got(copies)

    return steps, close


def far_step(j):
    return 510 + 10 * j


class Ticker:
    def __init__(self, steps, plan):
        self.steps, self.plan = dict(steps), iter(plan)

    def __call__(self):
        for name in next(self.plan):
            self.steps.pop(name)()

    def rest(self, order):
        for name in order:
            if name in self.steps:
                self.steps.pop(name)()
        assert not self.steps


def run(steps):
    for _ in steps:
        pass


def sigmoid(v):
    return 1.0 / (1.0 + jnp.exp(-v))


def lanes(shape, axis):
    return lax.broadcasted_iota(jnp.int32, shape, axis)


def flat_dot(a, b, dims=((1,), (0,))):
    return lax.dot_general(a, b, (dims, ((), ())), preferred_element_type=jnp.float32)


def exact_dot(a, b):
    return jnp.dot(a, b, precision=HIGHEST, preferred_element_type=jnp.float32)


def gain_row(values):
    n_dev, width = values.shape[0], D // values.shape[0]
    spread = (lanes((128, D), 0) == lanes((128, D), 1) & (width - 1)).astype(jnp.bfloat16)
    rows = flat_dot(values, spread)
    return jnp.sum(jnp.where(lanes((n_dev, D), 0) == lanes((n_dev, D), 1) >> (width.bit_length() - 1), rows, 0.0), axis=0, keepdims=True)


def tap_rows(spot, small):
    n_dev = spot.count
    share = CONV_CH // n_dev
    col = lanes((1, 512), 1)
    channel = jnp.where(col < 256, (spot.q + 8 * (col >> 6)) * HEAD_M + (col & 63), DI + col - 256)
    dev = lanes((n_dev, 512), 0)
    picks = (channel >= dev * share) & (channel < dev * share + share)
    owner = jnp.sum(jnp.where(picks, dev, 0), axis=0, keepdims=True)
    within = lanes((128, 512), 0) == channel - owner * share
    rows = []
    for k in range(CONV + 1):
        values = small[:, TILE + k, 0:128]
        spread = flat_dot(values, picks.astype(jnp.bfloat16), ((0,), (0,)))
        rows.append(jnp.sum(jnp.where(within, spread, 0.0), axis=0, keepdims=True))
    return rows


def entry(block, row, lane):
    at = (lanes(block.shape, 0) == row) & (lanes(block.shape, 1) == lane)
    return jnp.sum(jnp.where(at, block.astype(jnp.float32), 0.0), keepdims=True).reshape(1, 1)


class Slot:
    def __init__(self, spot, small, x, count):
        block = small[(spot.z * 2 + x) * 4, TILE : TILE + 16, 0:128].astype(jnp.float32)
        first = entry(block, 9, 0)
        second = first + entry(block, 9, 1)
        number = lambda p: (p >= first).astype(jnp.float32) + (p >= second).astype(jnp.float32)
        col = lanes((count, 1), 0).astype(jnp.float32)
        row = lanes((1, count), 1).astype(jnp.float32)
        docs = number(col)
        self.keep = (col >= row) & (docs == number(row))
        self.same = [((col >= s) & (number(col - s) == docs)).astype(jnp.float32) for s in range(CONV)]


def shift(block, by):
    return block if by == 0 else pltpu.roll(block, by % block.shape[0], 0)


class Mixed:
    def __init__(self, spot, slot, own, maps, step_raw, taps, dt_row, rate_row):
        count = own.shape[0]
        self.spot, self.slot, self.count = spot, slot, count
        self.channels = jnp.concatenate([own[:, 256:], maps], axis=1)
        conv = taps[CONV] + sum(
            taps[CONV - 1 - s] * (shift(self.channels, s) * slot.same[s]) for s in range(CONV)
        )
        self.conv, self.sig = conv, sigmoid(conv)
        act = conv * self.sig
        self.inputs = act[:, :256]
        self.in_map, self.out_map = act[:, 256:384].astype(jnp.bfloat16), act[:, 384:].astype(jnp.bfloat16)
        self.raw = step_raw + dt_row
        self.step = jnp.where(self.raw > 20.0, self.raw, jnp.log(1.0 + jnp.exp(jnp.minimum(self.raw, 20.0))))
        lower = lanes((count, count), 0) >= lanes((count, count), 1)
        self.upper = (lanes((count, count), 0) <= lanes((count, count), 1)).astype(jnp.float32)
        self.cum = exact_dot(lower.astype(jnp.float32), self.step * rate_row)
        self.cum_t, self.step_t = self.cum.T, self.step.T
        self.inner = flat_dot(self.out_map, self.in_map, ((1,), (1,)))

    def head(self, i):
        return self.spot.q + 8 * i

    def col(self, by_head, i):
        return jnp.sum(jnp.where(lanes((1, 128), 1) == self.head(i), by_head, 0.0), axis=1, keepdims=True)

    def row(self, by_head_t, i):
        return jnp.sum(jnp.where(lanes((128, 1), 0) == self.head(i), by_head_t, 0.0), axis=0, keepdims=True)

    def decay(self, i):
        gap = jnp.where(self.slot.keep, self.col(self.cum, i) - self.row(self.cum_t, i), 0.0)
        return jnp.where(self.slot.keep, jnp.exp(gap), 0.0)


def pick_lane(row, lane):
    return jnp.sum(jnp.where(lanes(row.shape, 1) == lane, row, 0.0), axis=1, keepdims=True)


def patch_pairs(count):
    i, j = lanes((count, count), 0), lanes((count, count), 1)
    return (i >= j) & ((i >> 3) == (j >> 3))


def rms_back(value, gain, grad):
    scale = lax.rsqrt(jnp.mean(value * value, axis=1, keepdims=True) + EPSILON)
    along = jnp.mean(grad * gain * value, axis=1, keepdims=True)
    d_value = scale * gain * grad - value * (scale * scale * scale * along)
    return d_value, jnp.sum(grad * value * scale, axis=0, keepdims=True)


def halves_of(block):
    left = lanes(block.shape, 1) < HEAD
    return left, [jnp.where(left, block, 0), jnp.where(left, 0, block)]


def local_block(
    tick,
    ready,
    whole,
    lengths,
    bytes_ref,
    grad_ref,
    sum_ref,
    mixed_ref,
    small_ref,
    wide,
    deep,
    o_block,
    o_streams,
    o_mix,
    o_direct,
    o_gains,
    g_qkv,
    g_attn,
    g_gate,
    g_up,
    g_down,
    attn_w,
    ffn_w,
    g_buf,
    streams,
    normed,
    qkv,
    weights,
    heads,
    attended,
    ffn_low,
    ffn_t,
    total,
    d_ffn,
    d_down,
    load_sem,
    ffn_sem,
    g_sem,
):
    f32, low = jnp.float32, jnp.bfloat16
    rows = bytes_ref.shape[0]
    scale = HEAD ** (-0.5)
    ready()
    load = pltpu.make_async_copy(wide.at[:, pl.ds(0, 4 * D)], attn_w, load_sem.at[0])
    load.start()

    def ffn_loads(j, slot):
        at = lambda base: pl.ds(pl.multiple_of(base + j * D, D), D)
        return [
            pltpu.make_async_copy(wide.at[:, at(4 * D)], ffn_w.at[slot, 0], ffn_sem.at[slot, 0]),
            pltpu.make_async_copy(wide.at[:, at(8 * D)], ffn_w.at[slot, 1], ffn_sem.at[slot, 1]),
            pltpu.make_async_copy(deep.at[at(0)], ffn_w.at[slot, 2], ffn_sem.at[slot, 2]),
        ]

    gain_a = gain_row(small_ref[:, TILE + 7, 0:128])
    gain_f = gain_row(small_ref[:, TILE + 8, 0:128])
    place = lax.axis_index("fsdp") * (rows // PATCH) + (lanes((rows, 1), 0) >> 3)
    live = (place < lengths[0, 0] + lengths[0, 1]).astype(f32)
    raw = mixed_ref[:, pl.ds(0, D)]
    mixer_r = lax.rsqrt(mixed_ref[:, pl.ds(D, 128)] * (1.0 / DI) + EPSILON)[:, 0:1]
    patch = sum_ref[...] + raw * mixer_r
    patch = jnp.broadcast_to(patch[:, None, :], (rows // PATCH, PATCH, D)).reshape(rows, D)
    streams[...] = bytes_ref[...].astype(f32) + patch
    normed[...] = rms_scale(streams[...], gain_a).astype(low)
    d_down[...] = (live * grad_ref[...].astype(f32)).astype(low)
    load.wait()
    for i in range(3):
        at = pl.ds(i * D, D)
        qkv[:, at] = flat_dot(normed[...], attn_w[:, at]).astype(low)
        tick()
    pairs = patch_pairs(128)

    def blocks(p, b):
        row = pl.ds(b * 128, 128)
        return row, [pl.ds(pl.multiple_of(base + p * 128, 128), 128) for base in (0, D, 2 * D)]

    def attend(p, carry):
        for b in range(rows // 128):
            row, (qa, ka, va) = blocks(p, b)
            k, v = qkv[row, ka], qkv[row, va]
            left, queries = halves_of(qkv[row, qa])
            outs = []
            for h in range(2):
                scores = flat_dot(queries[h], k, ((1,), (1,))) * scale
                scores = jnp.where(pairs, scores, -1e30)
                e = jnp.exp(scores - jnp.max(scores, axis=1, keepdims=True))
                w = e / jnp.sum(e, axis=1, keepdims=True)
                weights[p, b, h] = w
                outs.append(flat_dot(w.astype(low), v))
            heads[row, qa] = jnp.where(left, outs[0], outs[1]).astype(low)
        return carry

    for begin in range(0, D // 128, 2):
        lax.fori_loop(begin, begin + 2, attend, 0)
        tick()
    attended[...] = streams[...] + flat_dot(heads[...], attn_w[:, pl.ds(3 * D, D)])
    ffn_low[...] = rms_scale(attended[...], gain_f).astype(low)
    whole()
    for copy in ffn_loads(0, 0):
        copy.start()
    ffn_t[...] = ffn_low[...].astype(f32).T.astype(low)
    total[...] = attended[...]
    d_ffn[...] = jnp.zeros_like(d_ffn)
    n_ffn = deep.shape[0] // D

    def stores(j):
        at = pl.ds(pl.multiple_of(j * D, D), D)
        return [
            pltpu.make_async_copy(g_buf.at[0], g_gate.at[:, at], g_sem.at[0]),
            pltpu.make_async_copy(g_buf.at[1], g_up.at[:, at], g_sem.at[1]),
            pltpu.make_async_copy(g_buf.at[2], g_down.at[at], g_sem.at[2]),
        ]

    def feed(j, carry):
        slot = lax.rem(j, 2)
        for copy in ffn_loads(j, slot):
            copy.wait()

        @pl.when(j + 1 < n_ffn)
        def _():
            for copy in ffn_loads(j + 1, 1 - slot):
                copy.start()

        gate = flat_dot(ffn_low[...], ffn_w[slot, 0])
        upward = flat_dot(ffn_low[...], ffn_w[slot, 1])
        sig = sigmoid(gate)
        act = gate * sig
        hidden = (act * upward).astype(low)
        total[...] += flat_dot(hidden, ffn_w[slot, 2])
        d_hidden = flat_dot(d_down[...], ffn_w[slot, 2], ((1,), (1,)))
        d_gate = (d_hidden * upward * (sig + act * (1.0 - sig))).astype(low)
        d_up = (d_hidden * act).astype(low)
        d_ffn[...] += flat_dot(d_gate, ffn_w[slot, 0], ((1,), (1,)))
        d_ffn[...] += flat_dot(d_up, ffn_w[slot, 1], ((1,), (1,)))

        @pl.when(j > 0)
        def _():
            for copy in stores(j - 1):
                copy.wait()

        g_buf[0] = flat_dot(ffn_t[...], d_gate).astype(low)
        g_buf[1] = flat_dot(ffn_t[...], d_up).astype(low)
        g_buf[2] = flat_dot(hidden.astype(f32).T.astype(low), d_down[...]).astype(low)
        for copy in stores(j):
            copy.start()
        return carry

    lax.fori_loop(0, n_ffn, feed, 0)
    o_block[...] = (live * total[...]).astype(low)
    d_norm, gain_f_sum = rms_back(attended[...], gain_f, d_ffn[...])
    d_attended = live * grad_ref[...].astype(f32) + d_norm
    total[...] = d_attended
    d_low = d_attended.astype(low)
    for copy in stores(n_ffn - 1):
        copy.wait()
    d_down[...] = flat_dot(d_low, attn_w[:, pl.ds(3 * D, D)], ((1,), (1,))).astype(low)
    g_buf[0] = flat_dot(heads[...].astype(f32).T.astype(low), d_low).astype(low)
    last = [pltpu.make_async_copy(g_buf.at[0], g_attn, g_sem.at[0])]
    last[0].start()

    def attend_back(p, carry):
        for b in range(rows // 128):
            row, (qa, ka, va) = blocks(p, b)
            q, k, v = qkv[row, qa], qkv[row, ka], qkv[row, va]
            grad = d_down[row, qa]
            left, grads = halves_of(grad)
            dq, dk, dv = [], [], []
            for h in range(2):
                w = weights[p, b, h]
                dv.append(flat_dot(w.T.astype(low), grad))
                d_w = flat_dot(grads[h], v, ((1,), (1,)))
                d_s = w * (d_w - jnp.sum(w * d_w, axis=1, keepdims=True))
                dq.append(flat_dot(d_s.astype(low), k) * scale)
                dk.append(flat_dot(d_s.T.astype(low), q) * scale)
            qkv[row, qa] = jnp.where(left, dq[0], dq[1]).astype(low)
            qkv[row, ka] = jnp.where(left, dk[0], dk[1]).astype(low)
            qkv[row, va] = jnp.where(left, dv[0], dv[1]).astype(low)
        return carry

    lax.fori_loop(0, D // 128, attend_back, 0)
    ffn_t[...] = normed[...].astype(f32).T.astype(low)
    for i in range(3):
        at = pl.ds(i * D, D)
        if i == 2:
            last[0].wait()
        buf = (i + 1) % 3
        g_buf[buf] = flat_dot(ffn_t[...], qkv[:, at]).astype(low)
        copy = pltpu.make_async_copy(g_buf.at[buf], g_qkv.at[:, at], g_sem.at[buf])
        copy.start()
        last.append(copy)
    d_ffn[...] = flat_dot(qkv[...], attn_w[:, pl.ds(0, 3 * D)], ((1,), (1,)))
    d_norm, gain_a_sum = rms_back(streams[...], gain_a, d_ffn[...])
    d_streams = total[...] + d_norm
    o_streams[...] = d_streams
    direct = jnp.sum(d_streams.reshape(rows // PATCH, PATCH, D), axis=1)
    o_direct[...] = direct
    mix = direct.astype(low)
    along = jnp.sum(mix.astype(f32) * raw, axis=1, keepdims=True)
    high_r, high_a = (v.astype(low).astype(f32) for v in (mixer_r, along))
    lane = lanes((rows // PATCH, 128), 1)
    ext = jnp.zeros((rows // PATCH, 128), f32)
    for i, v in enumerate((high_r, high_a, mixer_r - high_r, along - high_a)):
        ext = jnp.where(lane == i, v, ext)
    o_mix[:, pl.ds(0, D)] = mix
    o_mix[:, pl.ds(D, 128)] = ext.astype(low)
    o_gains[...] = jnp.concatenate([gain_a_sum, gain_f_sum, jnp.zeros((6, D), f32)], axis=0)
    for copy in last[1:]:
        copy.wait()


N_WIRES = 512
PLAN_F = (
    (500, 100, 200),
    (),
    (),
    (),
    (300, 201),
    (110, 210, 101),
    (),
    (310, 202, 120),
    (400,),
    (220, 301),
    (320, 102, 103, 203),
    (410,),
    (302,),
    (230,),
    (111, 211),
    (510,),
    (330,),
    (420,),
    (112, 212),
    (303,),
    (113, 213),
    (),
    (430, 311, 312),
    (121, 221),
    (313, 122, 222),
    (520, 401, 402),
    (123, 223, 321),
    (322, 403, 411),
    (231, 323, 412),
    (530, 232, 413),
)
REST_F = (
    331,
    233,
    332,
    333,
    540,
    421,
    422,
    423,
    431,
    432,
    433,
)
PLAN_B = (
    (),
    (),
    (200,),
    (201, 202),
    (510,),
    (210,),
    (),
    (520,),
    (211,),
    (300,),
    (220,),
    (530,),
    (400,),
    (),
    (),
    (),
    (301, 212),
    (),
    (),
    (302,),
    (310, 221),
    (),
    (),
    (222, 401, 311, 410),
    (230, 312, 402),
    (231, 320),
    (411, 232, 321, 540),
)
REST_B = (
    412,
    322,
    420,
    330,
    421,
    331,
    422,
    332,
    550,
    430,
    431,
    432,
)


def forward_kernel(
    depth,
    rows_ref,
    patch_ref,
    cols_ref,
    vec_ref,
    out_ref,
    heads_ref,
    lengths,
    states_ref,
    grad_ref,
    qkv,
    attn,
    gate,
    up,
    down,
    ow,
    od,
    o_block,
    o_streams,
    o_mix,
    o_direct,
    o_gains,
    g_qkv,
    g_attn,
    g_gate,
    g_up,
    g_down,
    sum_ref,
    small_ref,
    bytes_ref,
    norm_ref,
    proj_ref,
    head_w_ref,
    own_ref,
    maps_ref,
    step_ref,
    core_ref,
    mixed_ref,
    attn_w,
    ffn_w,
    g_buf,
    streams,
    normed,
    qkv_low,
    weights,
    mixed_heads,
    attended,
    ffn_low,
    ffn_t,
    total_ref,
    d_ffn,
    d_down,
    load_sem,
    ffn_sem,
    g_sem,
    parts,
    pair,
    near,
    column,
    far,
    parts8,
    pair8,
    near8,
    send,
    recv,
    swap_send,
    swap_recv,
    local,
):
    f32, low = jnp.float32, jnp.bfloat16
    spot = Spot(depth)
    count = 128
    wires = Wires(send, recv)
    mine = pl.multiple_of(spot.me * TILE, TILE)
    bytes_ref[pl.ds(mine, TILE)] = rows_ref[:, pl.ds(pl.multiple_of(spot.me * 256, 256), 256)]
    small_ref[spot.me] = vec_ref[...]
    proj_ref[pl.ds(mine, TILE)] = cols_ref[spot.q]
    head_w_ref[spot.z] = out_ref[...]
    greet(spot)

    def lanes_of(to):
        return rows_ref.at[:, pl.ds(pl.multiple_of(to * 256, 256), 256)]

    swap_bytes = Swap(
        spot,
        swap_send,
        swap_recv,
        lanes_of,
        lambda me: bytes_ref.at[pl.ds(pl.multiple_of(me * TILE, TILE), TILE)],
    )
    swap_bytes.start()
    steps, close = big_gather(wires, spot, ow, od, (qkv, attn, gate, up, down))
    near_proj = plane_swap(
        wires,
        spot,
        lambda q: cols_ref.at[q],
        lambda q: proj_ref.at[pl.ds(pl.multiple_of((spot.z * 8 + q) * TILE, TILE), TILE)],
    )
    small = spread_all(wires, spot, small_ref)
    next(small)
    tick = Ticker(steps, PLAN_F)
    tick()
    own_rows = []
    at = 0
    for i, ref in enumerate((qkv, attn, gate, up)):
        width = ref.shape[1]
        own_rows.append(pltpu.make_async_copy(ref, ow.at[pl.ds(mine, TILE), pl.ds(at, width)], local.at[i]))
        at += width
    deep = down.shape[0]
    own_rows.append(
        pltpu.make_async_copy(down, od.at[pl.ds(pl.multiple_of(spot.me * deep, deep), deep)], local.at[4])
    )
    for copy in own_rows:
        copy.start()
    tick()
    swap_bytes.arrive()
    got(near_proj)
    layer = proj_ref.at[pl.ds(pl.multiple_of(spot.z * 8 * TILE, 8 * TILE), 8 * TILE)]
    far_proj = [wires.copy(layer, layer, spot.above(k)) for k in range(1, depth)]

    for b in range(4):
        block = flat_dot(bytes_ref[pl.ds(b * 256, 256)], patch_ref[...]).astype(low)
        parts[pl.ds(b * 4, 4)] = block.reshape(4, 2, TILE, D)
    tick()
    total = sum_all(wires, spot, parts, pair, near, column, far, sum_ref)
    next(total)
    next(small)
    tick()
    next(total)
    tick()
    next(total)
    next(small)
    tick()
    head_w = [wires.copy(out_ref, head_w_ref.at[spot.z], spot.above(k)) for k in range(1, depth)]
    next(total)
    tick()
    run(small)
    patch_sum = sum_ref[...]
    scale = lax.rsqrt(jnp.mean(patch_sum * patch_sum, axis=1, keepdims=True) + EPSILON)
    gain = gain_row(small_ref[:, TILE + 5, 0:128])
    norm_ref[spot.q] = (patch_sum * scale * gain).astype(low)
    plane = spread_plane(wires, spot, norm_ref)
    next(plane)
    tick()
    next(plane)
    tick()
    got(far_proj)
    taps = tap_rows(spot, small_ref)
    run(plane)
    tick()

    norm = norm_ref[...].reshape(2 * count, D)
    own_ref[...] = flat_dot(norm, proj_ref[...])
    maps_ref[...] = flat_dot(norm, small_ref[:, :TILE, 0:256].reshape(D, 256))
    step_ref[...] = flat_dot(norm, small_ref[:, :TILE, 256:384].reshape(D, 128))
    dt_row, rate_row, skip_row = heads_ref[0:1], heads_ref[1:2], heads_ref[2:3]
    tick()
    got(head_w)
    gains = jnp.concatenate(
        [small_ref[spot.q + 8 * i, TILE : TILE + 16, 0:HEAD_M][6:7].astype(f32) for i in range(4)], axis=1
    )
    for x in range(2):
        at = pl.ds(x * count, count)
        slot = Slot(spot, small_ref, x, count)
        own, maps = own_ref[at], maps_ref[at]
        mix = Mixed(spot, slot, own, maps, step_ref[at], taps, dt_row, rate_row)
        outs = []
        for i in range(4):
            tick()
            inputs = mix.inputs[:, i * HEAD_M : (i + 1) * HEAD_M]
            mixing = (mix.decay(i) * mix.inner * mix.row(mix.step_t, i)).astype(low)
            skip = pick_lane(skip_row, mix.head(i))
            outs.append(flat_dot(mixing, inputs.astype(low)) + skip * inputs)
        core = jnp.concatenate(outs, axis=1)
        core_ref[at] = core
        raw = own[:, :256]
        gated = core * raw * sigmoid(raw)
        part = flat_dot((gated * gains).astype(low), head_w_ref[...].reshape(256, D))
        squares = jnp.sum(gated * gated, axis=1, keepdims=True)
        parts8[pl.ds(x * 2, 2), :, :, pl.ds(0, D)] = part.astype(low).reshape(2, 2, TILE, D)
        parts8[pl.ds(x * 2, 2), :, :, pl.ds(D, 128)] = (
            jnp.broadcast_to(squares, (count, 128)).astype(low).reshape(2, 2, TILE, 128)
        )
        tick()
    for total in sum_plane(wires, spot, parts8, pair8, near8):
        if total is None:
            tick()
    mixed_ref[...] = total

    def ready():
        for copy in own_rows:
            copy.wait()
        close([0])

    def whole():
        tick.rest(REST_F)
        close(range(1, len(CUTS_F) + 2))

    local_block(
        tick,
        ready,
        whole,
        lengths,
        states_ref,
        grad_ref,
        sum_ref,
        mixed_ref,
        small_ref,
        ow,
        od,
        o_block,
        o_streams,
        o_mix,
        o_direct,
        o_gains,
        g_qkv,
        g_attn,
        g_gate,
        g_up,
        g_down,
        attn_w,
        ffn_w,
        g_buf,
        streams,
        normed,
        qkv_low,
        weights,
        mixed_heads,
        attended,
        ffn_low,
        ffn_t,
        total_ref,
        d_ffn,
        d_down,
        load_sem,
        ffn_sem,
        g_sem,
    )
    wires.drain()
    swap_bytes.leave()


def forward_call(
    depth,
    n_dev,
    rows2,
    patch_proj,
    cols,
    vectors,
    out_proj,
    heads,
    lengths,
    byte_states,
    out_grad,
    qkv,
    attn,
    gate,
    up,
    down,
):
    f32, low = jnp.float32, jnp.bfloat16
    vmem = pl.BlockSpec(memory_space=pltpu.VMEM)
    anywhere = pl.BlockSpec(memory_space=pl.ANY)
    smem = pl.BlockSpec(memory_space=pltpu.SMEM)
    shape = jax.ShapeDtypeStruct
    plane_patches = 8 * TILE
    rows, hidden = byte_states.shape[0], down.shape[0] * n_dev
    outs = [
        shape((D, WIDE), low),
        shape((hidden, D), low),
        shape((rows, D), low),
        shape((rows, D), f32),
        shape((rows // PATCH, EXT), low),
        shape((rows // PATCH, D), f32),
        shape((8, D), f32),
        shape((D, 3 * D), low),
        shape((D, D), low),
        shape((D, hidden), low),
        shape((D, hidden), low),
        shape((hidden, D), low),
        shape((TILE, D), f32),
        shape((n_dev, SMALL_ROWS, SMALL_COLS), low),
        shape((n_dev * TILE, 256), low),
        shape((8, TILE, D), low),
        shape((n_dev * TILE, 512), low),
        shape((depth, HEAD_M, D), low),
        shape((plane_patches, 512), f32),
        shape((plane_patches, 256), f32),
        shape((plane_patches, 128), f32),
        shape((plane_patches, 256), f32),
    ]
    scratch = [
        pltpu.VMEM((TILE, EXT), f32),
        pltpu.VMEM((D, 4 * D), low),
        pltpu.VMEM((2, 3, D, D), low),
        pltpu.VMEM((3, D, D), low),
        pltpu.VMEM((rows, D), f32),
        pltpu.VMEM((rows, D), low),
        pltpu.VMEM((rows, 3 * D), low),
        pltpu.VMEM((D // 128, rows // 128, 2, 128, 128), f32),
        pltpu.VMEM((rows, D), low),
        pltpu.VMEM((rows, D), f32),
        pltpu.VMEM((rows, D), low),
        pltpu.VMEM((D, rows), low),
        pltpu.VMEM((rows, D), f32),
        pltpu.VMEM((rows, D), f32),
        pltpu.VMEM((rows, D), low),
        pltpu.SemaphoreType.DMA((1,)),
        pltpu.SemaphoreType.DMA((2, 3)),
        pltpu.SemaphoreType.DMA((3,)),
        pltpu.VMEM((16, 2, TILE, D), low),
        pltpu.VMEM((16, TILE, D), low),
        pltpu.VMEM((3, depth, TILE, D), low),
        pltpu.VMEM((depth, TILE, D), low),
        pltpu.VMEM((depth - 1, TILE, D), low),
        pltpu.VMEM((4, 2, TILE, EXT), low),
        pltpu.VMEM((4, TILE, EXT), low),
        pltpu.VMEM((3, TILE, EXT), low),
        pltpu.SemaphoreType.DMA((N_WIRES,)),
        pltpu.SemaphoreType.DMA((N_WIRES,)),
        pltpu.SemaphoreType.DMA((n_dev,)),
        pltpu.SemaphoreType.DMA((n_dev,)),
        pltpu.SemaphoreType.DMA((5,)),
    ]
    found = pl.pallas_call(
        partial(forward_kernel, depth),
        out_shape=outs,
        in_specs=[vmem] * 6 + [smem] + [vmem] * 2 + [anywhere] * 5,
        out_specs=[anywhere] * 2 + [vmem] * 5 + [anywhere] * 5 + [vmem] * 10,
        scratch_shapes=scratch,
        compiler_params=pltpu.CompilerParams(
            collective_id=0, has_side_effects=True, vmem_limit_bytes=62 * 2**20
        ),
        name="global_forward",
    )(rows2, patch_proj, cols, vectors, out_proj, heads, lengths, byte_states, out_grad, qkv, attn, gate, up, down)
    block, streams, mix, direct, gains, *rest = found[2:]
    return (block, streams, mix, direct, gains), rest[:5], rest[5], rest[6:]


def add_to(dst, sources, width):
    def one(i, carry):
        at = pl.ds(pl.multiple_of(i * STEP, STEP), STEP)
        total = sources[0](at).astype(jnp.float32)
        for source in sources[1:]:
            total = total + source(at).astype(jnp.float32)
        dst(at, total)
        return carry

    lax.fori_loop(0, width // STEP, one, 0)


def big_scatter(wires, spot, grads, bufs, outs, local):
    f32, low = jnp.float32, jnp.bfloat16
    held_w, held_d, stage_w, stage_d, near_w, near_d, last_w, last_d, ring_w, ring_d, climb_c, flat_c = bufs
    half, deep = (WIDE - FAR_B) // 2, held_d.shape[2]
    xn, yn, cn, zn = spot.flip(2)[0], spot.flip(1)[0], spot.sibling(), spot.onward()
    here, xp, yp, xy = spot.plane, spot.flip(2)[1], spot.flip(1)[1], spot.flip(3)[1]
    T = [spot.column[k % spot.depth] for k in range(1, spot.depth + 1)]
    core, fetch, near, last, ring = {}, {}, {}, {}, {}
    A, B, C = pl.ds(0, half), pl.ds(half, half), pl.ds(2 * half, FAR_B)
    AB = pl.ds(0, 2 * half)
    climb, flat = {}, []
    DA, DB = pl.ds(0, deep // 2), pl.ds(deep // 2, deep // 2)

    def load(k, side):
        fetch[k, side] = []
        for i, ref in enumerate(grads):
            dst = stage_w.at[:, :, pl.ds(*PARTS[i])] if i < 4 else stage_d
            copy = pltpu.make_async_copy(ref.at[T[k], pl.ds(2 * side, 2), spot.c], dst, local.at[k * 5 + i])
            copy.start()
            fetch[k, side].append(copy)

    def open_core(k):
        core[k] = []
        for i, ref in enumerate(grads):
            dst = held_w.at[T[k], :, :, pl.ds(*PARTS[i])] if i < 4 else held_d.at[T[k]]
            core[k].append(wires.copy(ref.at[T[k], :, 1 - spot.c], dst, cn))

    def join(k):
        t = T[k]
        got(core[k])
        for side in range(2):
            for copy in fetch[k, side]:
                copy.wait()
            for half_at in range(2):
                plane = 2 * side + half_at

                def put_w(at, total, plane=plane):
                    held_w[t, plane, :, at] = total.astype(low)

                add_to(
                    put_w,
                    [lambda at, p=plane: held_w[t, p, :, at], lambda at, h=half_at: stage_w[h, :, at]],
                    WIDE,
                )
                held_d[t, plane] = (held_d[t, plane].astype(f32) + stage_d[half_at].astype(f32)).astype(low)
            if side == 0:
                load(k, 1)
            elif k + 1 < spot.depth:
                load(k + 1, 0)

    parts, at = [], 0
    for i, width in enumerate(CUTS):
        end = i == len(CUTS) - 1
        width = half - at if end else width
        parts.append((at, width, end))
        at += width

    def spans(i):
        at, width, end = parts[i]
        found = [(pl.ds(at, width), pl.ds(half + at, width))]
        return found, end

    def near_sends(k, i):
        t = T[k]
        [(a, b)], end = spans(i)
        sends = []
        for x in range(2):
            src = x * 2 + (1 - spot.y)
            sends.append(wires.copy(held_w.at[t, src, :, a], near_w.at[k, x, :, a], yn))
            if end:
                sends.append(wires.copy(held_d.at[t, src, DA], near_d.at[k, x, DA], yn))
        for y in range(2):
            src = (1 - spot.x) * 2 + y
            sends.append(wires.copy(held_w.at[t, src, :, b], near_w.at[k, y, :, b], xn))
            if end:
                sends.append(wires.copy(held_d.at[t, src, DB], near_d.at[k, y, DB], xn))
        near[k, i] = sends

    def first(k, i):
        if i == 0:
            join(k)
        near_sends(k, i)

    def second(k, i):
        t = T[k]
        got(near[k, i])
        at, width, end = parts[i]
        for other in range(2):
            for plane, base in ((other * 2 + spot.y, at), (spot.x * 2 + other, half + at)):
                moved = lambda c, base=base: pl.ds(pl.multiple_of(c.start + base, STEP), STEP)

                def put(c, total, plane=plane, moved=moved):
                    held_w[t, plane, :, moved(c)] = total.astype(low)

                add_to(
                    put,
                    [
                        lambda c, p=plane, m=moved: held_w[t, p, :, m(c)],
                        lambda c, o=other, m=moved: near_w[k, o, :, m(c)],
                    ],
                    width,
                )
            if end:
                pa, pb = other * 2 + spot.y, spot.x * 2 + other
                held_d[t, pa, DA] = (held_d[t, pa, DA].astype(f32) + near_d[k, other, DA].astype(f32)).astype(low)
                held_d[t, pb, DB] = (held_d[t, pb, DB].astype(f32) + near_d[k, other, DB].astype(f32)).astype(low)
        [(a, b)], _ = spans(i)
        sends = [
            wires.copy(held_w.at[t, xp, :, a], last_w.at[k, :, a], xn),
            wires.copy(held_w.at[t, yp, :, b], last_w.at[k, :, b], yn),
        ]
        if end:
            sends.append(wires.copy(held_d.at[t, xp, DA], last_d.at[k, DA], xn))
            sends.append(wires.copy(held_d.at[t, yp, DB], last_d.at[k, DB], yn))
        last[k, i] = sends

    def finish(terms, begin, end):
        for out, (base, size) in zip(outs, PARTS):
            a, b = max(begin, base), min(end, base + size)

            def put_out(at, total, out=out, shift_by=a - base):
                out[:, pl.ds(pl.multiple_of(at.start + shift_by, STEP), STEP)] = total

            if a < b:
                moved = [
                    lambda at, f=f, a=a: f(pl.ds(pl.multiple_of(at.start + a, STEP), STEP)) for f in terms
                ]
                add_to(put_out, moved, b - a)

    def far(k):
        t = T[k]
        if k:
            got(climb[k - 1])
            for plane in range(4):
                base = lambda at: pl.ds(pl.multiple_of(at.start + 2 * half, STEP), STEP)

                def put_far(at, total, plane=plane):
                    held_w[t, plane, :, base(at)] = total.astype(low)

                terms = [
                    lambda at, p=plane: held_w[t, p, :, base(at)],
                    lambda at, p=plane: climb_c[k - 1, p, :, at],
                ]
                add_to(put_far, terms, FAR_B)
        if k < spot.depth - 1:
            climb[k] = [wires.copy(held_w.at[t, :, :, C], climb_c.at[k], zn)]
        else:
            for way in (1, 2, 3):
                to, plane = spot.flip(way)
                flat.append(wires.copy(held_w.at[t, plane, :, C], flat_c.at[way - 1], to))

    def far_end():
        got(flat)
        terms = [lambda at: held_w[T[-1], here, :, at]]
        for way in range(3):
            terms.append(
                lambda at, w=way: flat_c[w, :, pl.ds(pl.multiple_of(at.start - 2 * half, STEP), STEP)]
            )
        finish(terms, 2 * half, WIDE)

    def third(k, i):
        t = T[k]
        got(last[k, i])
        if k:
            got(ring[k - 1, i])
        at, width, end = parts[i]
        [(a, b)], _ = spans(i)
        terms = [lambda c: held_w[t, here, :, c], lambda c: last_w[k, :, c]]
        if k:
            terms.append(lambda c: ring_w[k - 1, :, c])
        if end:
            down = held_d[t, here].astype(f32) + last_d[k].astype(f32)
            if k:
                down = down + ring_d[k - 1].astype(f32)
        if k == spot.depth - 1:
            finish(terms, at, at + width)
            finish(terms, half + at, half + at + width)
            if end:
                outs[4][...] = down
            return
        for base in (at, half + at):
            moved = lambda c, base=base: pl.ds(pl.multiple_of(c.start + base, STEP), STEP)

            def put_on(c, total, moved=moved):
                held_w[t, here, :, moved(c)] = total.astype(low)

            add_to(put_on, [lambda c, f=f, m=moved: f(m(c)) for f in terms], width)
        ring[k, i] = [wires.copy(held_w.at[t, here, :, c], ring_w.at[k, :, c], zn) for c in (a, b)]
        if end:
            held_d[t, here] = down.astype(low)
            ring[k, i].append(wires.copy(held_d.at[t, here], ring_d.at[k], zn))

    load(0, 0)
    for k in range(spot.depth):
        open_core(k)
    steps = {far_step(k): partial(far, k) for k in range(spot.depth)}
    steps[far_step(spot.depth)] = far_end
    for i in range(len(CUTS)):
        for k in range(spot.depth):
            for kind, act in enumerate((first, second, third), 2):
                steps[100 * kind + 10 * k + i] = partial(act, k, i)
    return steps


class Back:
    def __init__(self, mix, own, core, ext, d_patch, gains, head_w, heads, taps, tick):
        f32, low = jnp.float32, jnp.bfloat16
        count = mix.count
        dt_row, rate_row, skip_row = heads[0:1], heads[1:2], heads[2:3]
        r = ext[:, 0:1] + ext[:, 2:3]
        along = ext[:, 1:2] + ext[:, 3:4]
        raw = own[:, :256]
        sig = sigmoid(raw)
        gated = core * raw * sig
        back = flat_dot(d_patch, head_w, ((1,), (1,)))
        self.norm = (gated * r * gains).astype(low)
        self.gain = jnp.sum(back * gated * r, axis=0, keepdims=True)
        d_gated = r * gains * back - gated * (r * r * r * along * (1.0 / DI))
        d_core = d_gated * raw * sig
        d_gate = d_gated * core * sig * (1.0 + raw * (1.0 - sig))
        lane = lanes((1, 128), 1)
        graph = jnp.zeros((count, count), f32)
        d_inputs = []
        direct = jnp.zeros((count, 128), f32)
        flow = jnp.zeros((count, 128), f32)
        d_skip = jnp.zeros((1, 128), f32)
        for i in range(4):
            tick()
            cut = slice(i * HEAD_M, (i + 1) * HEAD_M)
            inputs, grad = mix.inputs[:, cut], d_core[:, cut]
            decay, step = mix.decay(i), mix.row(mix.step_t, i)
            kept = decay * mix.inner
            skip = pick_lane(skip_row, mix.head(i))
            d_mixing = flat_dot(grad.astype(low), inputs.astype(low), ((1,), (1,)))
            d_inputs.append(
                flat_dot((kept * step).astype(low), grad.astype(low), ((0,), (0,))) + skip * grad
            )
            graph = graph + decay * step * d_mixing
            turn = kept * d_mixing
            arrive = jnp.sum(turn.T, axis=1, keepdims=True)
            leave = jnp.sum(turn * step, axis=1, keepdims=True)
            here = lane == mix.head(i)
            direct = direct + jnp.where(here, arrive, 0.0)
            flow = flow + jnp.where(here, leave - mix.col(mix.step, i) * arrive, 0.0)
            d_skip = d_skip + jnp.where(here, jnp.sum(grad * inputs, keepdims=True).reshape(1, 1), 0.0)
        tail = exact_dot(mix.upper, flow)
        mine = own_lanes(lane, mix)
        d_step = jnp.where(mine, direct + rate_row * tail, 0.0)
        d_raw = d_step * sigmoid(mix.raw)
        self.skip = d_skip
        self.rate = jnp.sum(rate_row * mix.step * jnp.where(mine, tail, 0.0), axis=0, keepdims=True)
        self.bias = jnp.sum(d_raw, axis=0, keepdims=True)
        low_graph = graph.astype(low)
        d_out_map = flat_dot(low_graph, mix.in_map)
        d_in_map = flat_dot(low_graph, mix.out_map, ((0,), (0,)))
        d_act = jnp.concatenate(d_inputs + [d_in_map, d_out_map], axis=1)
        d_conv = d_act * (mix.sig * (1.0 + mix.conv * (1.0 - mix.sig)))
        d_channels = jnp.zeros_like(d_conv)
        self.taps = [None] * CONV + [jnp.sum(d_conv, axis=0, keepdims=True)]
        for s in range(CONV):
            kept = d_conv * mix.slot.same[s]
            d_channels = d_channels + taps[CONV - 1 - s] * shift(kept, -s)
            self.taps[CONV - 1 - s] = jnp.sum(kept * shift(mix.channels, s), axis=0, keepdims=True)
        self.rows = jnp.concatenate([d_gate, d_channels, d_raw], axis=1).astype(low)


def own_lanes(lane, mix):
    mine = lane == mix.head(0)
    for i in range(1, 4):
        mine = mine | (lane == mix.head(i))
    return mine


COLS = 512 + 256 + 128


def backward_kernel(
    depth,
    mix_ref,
    direct_ref,
    streams_ref,
    sum_ref,
    gains_ref,
    small_ref,
    bytes_ref,
    norm_ref,
    proj_ref,
    head_w_ref,
    own_ref,
    maps_ref,
    step_ref,
    core_ref,
    patch_ref,
    heads_ref,
    g_qkv,
    g_attn,
    g_gate,
    g_up,
    g_down,
    o_qkv,
    o_attn,
    o_gate,
    o_up,
    o_down,
    o_patch,
    o_states,
    o_head,
    o_cols,
    o_maps,
    all_ref,
    o_rows,
    mix_all,
    rows_all,
    head_sum,
    head_low,
    head_far,
    col_send,
    col_recv,
    col_far,
    col_sum,
    back_send,
    parts8,
    pair8,
    near8,
    held_w,
    held_d,
    stage_w,
    stage_d,
    near_w,
    near_d,
    last_w,
    last_d,
    ring_w,
    ring_d,
    climb_c,
    flat_c,
    send,
    recv,
    swap_send,
    swap_recv,
    local,
):
    f32, low = jnp.float32, jnp.bfloat16
    spot = Spot(depth)
    count = 128
    wires = Wires(send, recv)
    mix_all[spot.q] = mix_ref[...]
    greet(spot)
    plane = spread_plane(wires, spot, mix_all)
    next(plane)
    steps = big_scatter(
        wires,
        spot,
        (g_qkv, g_attn, g_gate, g_up, g_down),
        (held_w, held_d, stage_w, stage_d, near_w, near_d, last_w, last_d, ring_w, ring_d, climb_c, flat_c),
        (o_qkv, o_attn, o_gate, o_up, o_down),
        local,
    )
    tick = Ticker(steps, PLAN_B)
    tick()
    next(plane)
    tick()
    taps = tap_rows(spot, small_ref)
    heads = heads_ref[...]
    dt_row, rate_row = heads[0:1], heads[1:2]
    gains = jnp.concatenate(
        [small_ref[spot.q + 8 * i, TILE : TILE + 16, 0:HEAD_M][6:7].astype(f32) for i in range(4)], axis=1
    )
    gain = gain_row(small_ref[:, TILE + 5, 0:128])
    run(plane)
    tick()
    sums = None
    for x in range(2):
        at = pl.ds(x * count, count)
        slot = Slot(spot, small_ref, x, count)
        mix = Mixed(spot, slot, own_ref[at], maps_ref[at], step_ref[at], taps, dt_row, rate_row)
        d_patch = mix_all[pl.ds(x * 4, 4), :, pl.ds(0, D)].reshape(count, D)
        ext = mix_all[pl.ds(x * 4, 4), :, pl.ds(D, 128)].reshape(count, 128).astype(f32)
        back = Back(
            mix, own_ref[at], core_ref[at], ext, d_patch, gains, head_w_ref[...].reshape(256, D), heads, taps, tick
        )
        rows_all[at] = back.rows
        tick()
        head = flat_dot(back.norm, d_patch, ((0,), (0,)))
        head = head.reshape(TILE, PATCH, D)
        head_sum[...] = head if x == 0 else head_sum[...] + head
        new = [*back.taps, back.gain, back.bias, back.rate, back.skip]
        sums = new if sums is None else [a + b for a, b in zip(sums, new)]
        grad = flat_dot(back.rows[:, :512], proj_ref[...], ((1,), (1,)))
        grad = grad + flat_dot(
            back.rows[:, 512:], small_ref[:, :TILE, :].reshape(D, SMALL_COLS), ((1,), (1,))
        )
        parts8[pl.ds(x * 2, 2)] = grad.astype(low).reshape(2, 2, TILE, D)
        tick()
    total8 = sum_plane(wires, spot, parts8, pair8, near8)
    next(total8)
    tick()
    head_low[...] = head_sum[...].reshape(256, D).astype(low).reshape(depth, HEAD_M, D)
    fetch = pltpu.make_async_copy(streams_ref, head_sum, local.at[5 * depth])
    fetch.start()
    next(total8)
    tick()
    norm = norm_ref[...].reshape(2 * count, D)
    rows = rows_all[...]
    for b in range(4):
        block = flat_dot(norm[:, b * 256 : (b + 1) * 256], rows, ((0,), (0,)))
        col_send[pl.ds(b * 8, 8)] = block.astype(low).reshape(8, TILE, COLS)
    tick()
    grad_norm = next(total8)
    tick()
    patch_sum = sum_ref[...]
    scale = lax.rsqrt(jnp.mean(patch_sum * patch_sum, axis=1, keepdims=True) + EPSILON)
    along = jnp.mean(grad_norm * gain * patch_sum, axis=1, keepdims=True)
    d_sum = direct_ref[...] + scale * gain * grad_norm - patch_sum * (scale * scale * scale * along)
    gain_sum = jnp.sum(grad_norm * patch_sum * scale, axis=0, keepdims=True)
    wide = lambda row: jnp.concatenate([row, jnp.zeros((1, D - row.shape[1]), f32)], axis=1)
    lines = [wide(row) for row in sums[: CONV + 1]]
    lines += [wide(jnp.concatenate(sums[CONV + 1 :], axis=1)), gains_ref[0:1], gains_ref[1:2], gain_sum]
    lines += [jnp.zeros((16 - len(lines), D), f32)]
    all_ref[spot.me] = jnp.concatenate([d_sum, *lines], axis=0).astype(low)
    spread = spread_all(wires, spot, all_ref)
    next(spread)
    col_ring = [
        wires.copy(col_send.at[pl.ds(((spot.z + k) % depth) * 8, 8)], col_far.at[k - 1], spot.above(k))
        for k in range(1, depth)
    ]
    head_ring = [
        wires.copy(head_low.at[(spot.z + k) % depth], head_far.at[k - 1], spot.above(k)) for k in range(1, depth)
    ]
    tick()
    next(spread)
    tick()
    next(spread)
    tick()
    run(spread)
    tick()
    d_all = all_ref[:, :TILE].reshape(-1, D)
    for b in range(4):
        back_send[pl.ds(b * 8, 8)] = (
            flat_dot(d_all[b * 256 : (b + 1) * 256], patch_ref[...], ((1,), (1,))).astype(low).reshape(8, TILE, 256)
        )
    swap_rows = Swap(
        spot,
        swap_send,
        swap_recv,
        lambda to: back_send.at[to],
        lambda me: o_rows.at[:, pl.ds(pl.multiple_of(me * 256, 256), 256)],
    )
    swap_rows.start()
    got(col_ring)
    for q in range(8):
        total = col_send[spot.z * 8 + q].astype(f32)
        for k in range(depth - 1):
            total = total + col_far[k, q].astype(f32)
        col_sum[q] = total.astype(low)
    col_plane = plane_swap(wires, spot, lambda q: col_sum.at[q], lambda q: col_recv.at[q])
    col_recv[spot.q] = col_sum[spot.q]
    tick()
    o_rows[:, pl.ds(pl.multiple_of(spot.me * 256, 256), 256)] = back_send[spot.me]
    o_patch[...] = flat_dot(bytes_ref[...], d_all, ((0,), (0,)))
    tick()
    got(head_ring)
    total = head_low[spot.z].astype(f32)
    for k in range(depth - 1):
        total = total + head_far[k].astype(f32)
    o_head[...] = total
    tick()
    got(col_plane)
    total = jnp.zeros((TILE, COLS - 512), f32)
    for q in range(8):
        o_cols[q] = col_recv[q, :, :512].astype(f32)
        total = total + col_recv[q, :, 512:].astype(f32)
    o_maps[...] = total
    tick()
    tick.rest(REST_B)
    swap_rows.arrive()
    fetch.wait()
    for j in range(PATCH):
        o_states[:, j] = head_sum[:, j] + o_rows[:, j * D : (j + 1) * D].astype(f32)
    wires.drain()
    swap_rows.leave()


def backward_call(depth, n_dev, mix, direct, streams, patch_sum, gains, saved, patch_proj, heads, grads):
    f32, low = jnp.float32, jnp.bfloat16
    vmem = pl.BlockSpec(memory_space=pltpu.VMEM)
    anywhere = pl.BlockSpec(memory_space=pl.ANY)
    shape = jax.ShapeDtypeStruct
    deep = grads[4].shape[0] // n_dev
    cut = [g.reshape(depth, 4, 2, g.shape[0] // n_dev, g.shape[1]) for g in grads]
    outs = [shape((TILE, width), f32) for _, width in PARTS] + [
        shape((deep, D), f32),
        shape((256, D), f32),
        shape((TILE, PATCH, D), f32),
        shape((HEAD_M, D), f32),
        shape((8, TILE, 512), f32),
        shape((TILE, COLS - 512), f32),
        shape((n_dev, SMALL_ROWS, D), low),
    ]
    scratch = [
        pltpu.VMEM((TILE, PATCH * D), low),
        pltpu.VMEM((8, TILE, EXT), low),
        pltpu.VMEM((8 * TILE, COLS), low),
        pltpu.VMEM((TILE, PATCH, D), f32),
        pltpu.VMEM((depth, HEAD_M, D), low),
        pltpu.VMEM((depth - 1, HEAD_M, D), low),
        pltpu.VMEM((n_dev, TILE, COLS), low),
        pltpu.VMEM((8, TILE, COLS), low),
        pltpu.VMEM((depth - 1, 8, TILE, COLS), low),
        pltpu.VMEM((8, TILE, COLS), low),
        pltpu.VMEM((n_dev, TILE, 256), low),
        pltpu.VMEM((4, 2, TILE, D), low),
        pltpu.VMEM((4, TILE, D), low),
        pltpu.VMEM((3, TILE, D), low),
        pltpu.VMEM((depth, 4, TILE, WIDE), low),
        pltpu.VMEM((depth, 4, deep, D), low),
        pltpu.VMEM((2, TILE, WIDE), low),
        pltpu.VMEM((2, deep, D), low),
        pltpu.VMEM((depth, 2, TILE, WIDE - FAR_B), low),
        pltpu.VMEM((depth, 2, deep, D), low),
        pltpu.VMEM((depth, TILE, WIDE - FAR_B), low),
        pltpu.VMEM((depth, deep, D), low),
        pltpu.VMEM((depth - 1, TILE, WIDE - FAR_B), low),
        pltpu.VMEM((depth - 1, deep, D), low),
        pltpu.VMEM((depth - 1, 4, TILE, FAR_B), low),
        pltpu.VMEM((3, TILE, FAR_B), low),
        pltpu.SemaphoreType.DMA((N_WIRES,)),
        pltpu.SemaphoreType.DMA((N_WIRES,)),
        pltpu.SemaphoreType.DMA((n_dev,)),
        pltpu.SemaphoreType.DMA((n_dev,)),
        pltpu.SemaphoreType.DMA((5 * depth + 1,)),
    ]
    return pl.pallas_call(
        partial(backward_kernel, depth),
        out_shape=outs,
        in_specs=[vmem] * 2 + [anywhere] + [vmem] * 13 + [anywhere] * 5,
        out_specs=[vmem] * 11,
        scratch_shapes=scratch,
        compiler_params=pltpu.CompilerParams(
            collective_id=1, has_side_effects=True, vmem_limit_bytes=62 * 2**20
        ),
        name="global_backward",
    )(mix, direct, streams.reshape(TILE, PATCH, D), patch_sum, gains, *saved, patch_proj, heads, *cut)


BC = 2 * STATE


def fast_body(
    depth_fsdp,
    byte_states,
    doc_lengths,
    out_grad,
    patch_proj,
    global_gain,
    in_proj,
    conv_weight,
    conv_bias,
    dt_bias,
    a_log,
    skip_weight,
    mixer_gain,
    out_proj,
    attn_gain,
    qkv_proj,
    attn_out,
    ffn_gain,
    gate_proj,
    up_proj,
    down_proj,
):
    f32, low = jnp.float32, jnp.bfloat16
    depth, n_dev = depth_fsdp[0] // 2, depth_fsdp[0] * depth_fsdp[1]
    me = lax.axis_index("dp") * depth_fsdp[1] + lax.axis_index("fsdp")
    rows = byte_states.shape[0]
    patches = rows // PATCH

    shard_rows = in_proj.shape[0]
    maps_and_steps = jnp.pad(in_proj[:, 2 * DI :], ((0, 0), (0, SMALL_COLS - BC - MHEADS)))
    lines = []
    for line in (conv_bias, global_gain, mixer_gain, attn_gain, ffn_gain, doc_lengths.reshape(-1).astype(low)):
        lines += [line, jnp.zeros((SMALL_COLS - line.shape[0],), low)]
    lines = jnp.concatenate(lines + [jnp.zeros((6 * SMALL_COLS,), low)]).reshape(-1, SMALL_COLS)
    taps = jnp.pad(conv_weight.T, ((0, 0), (0, SMALL_COLS - conv_weight.shape[0])))
    vectors = jnp.concatenate([maps_and_steps, taps, lines])
    by_place = lambda cols: cols.reshape(shard_rows, 4, 8, HEAD_M).transpose(2, 0, 1, 3).reshape(8, shard_rows, 256)
    cols = jnp.concatenate([by_place(in_proj[:, :DI]), by_place(in_proj[:, DI : 2 * DI])], axis=2)
    heads_in = jnp.pad(jnp.stack([dt_bias, -jnp.exp(a_log), skip_weight]), ((0, 5), (0, 128 - MHEADS)))
    rows2 = byte_states.reshape(patches, PATCH * D)
    (block_out, grad_streams, mix, direct, gains), grads, patch_sum, saved = forward_call(
        depth,
        n_dev,
        rows2,
        patch_proj,
        cols,
        vectors,
        out_proj,
        heads_in,
        doc_lengths,
        byte_states,
        out_grad,
        qkv_proj,
        attn_out,
        gate_proj,
        up_proj,
        down_proj,
    )
    (g_qkv, g_attn, g_gate, g_up, g_down, g_patch, grad_states, g_out, g_cols, g_maps, everyone) = backward_call(
        depth,
        n_dev,
        mix,
        direct,
        grad_streams,
        patch_sum,
        gains,
        saved,
        patch_proj,
        heads_in,
        grads,
    )

    lines = everyone[:, shard_rows : shard_rows + 9].astype(f32)
    sums = jnp.sum(lines, axis=0)
    own_part = lambda row: lax.dynamic_slice_in_dim(row, me * (D // n_dev), D // n_dev, 0)
    by_plane = jnp.sum(lines.reshape(depth, 8, 9, D), axis=0)
    by_head = lambda rows_of: rows_of.reshape(8, -1, 4, HEAD_M).transpose(1, 2, 0, 3).reshape(-1, DI)
    taps = jnp.concatenate([by_head(by_plane[:, : CONV + 1, :256]), sums[: CONV + 1, 256:512]], axis=1)
    share = CONV_CH // n_dev
    taps = lax.dynamic_slice_in_dim(taps, me * share, share, 1)
    gain_m_sum = by_head(by_plane[:, CONV + 1 : CONV + 2, :256])[0]
    gain_m_sum = lax.dynamic_slice_in_dim(gain_m_sum, me * HEAD_M, HEAD_M, 0)
    head_line = sums[CONV + 1]
    back_cols = lambda cols: cols.reshape(8, shard_rows, 4, HEAD_M).transpose(1, 2, 0, 3).reshape(shard_rows, DI)
    grad_in_proj = jnp.concatenate(
        [back_cols(g_cols[..., :256]), back_cols(g_cols[..., 256:]), g_maps[:, : BC + MHEADS]], axis=1
    )
    return (
        block_out,
        grad_states.reshape(rows, D),
        g_patch,
        own_part(sums[CONV + 4]),
        grad_in_proj,
        taps[:CONV].T,
        taps[CONV],
        head_line[256 : 256 + MHEADS],
        head_line[384 : 384 + MHEADS],
        head_line[512 : 512 + MHEADS],
        gain_m_sum,
        g_out,
        own_part(sums[CONV + 2]),
        g_qkv,
        g_attn,
        own_part(sums[CONV + 3]),
        g_gate,
        g_up,
        g_down,
    )


def solution(mesh):
    in_specs = (
        P(("dp", "fsdp"), None),
        P("dp", None),
        P(("dp", "fsdp"), None),
        P(("dp", "fsdp"), None),
        P(("dp", "fsdp")),
        P(("dp", "fsdp"), None),
        P(("dp", "fsdp"), None),
        P(("dp", "fsdp")),
        P(),
        P(),
        P(),
        P(("dp", "fsdp")),
        P(("dp", "fsdp"), None),
        P(("dp", "fsdp")),
        P(("dp", "fsdp"), None),
        P(("dp", "fsdp"), None),
        P(("dp", "fsdp")),
        P(("dp", "fsdp"), None),
        P(("dp", "fsdp"), None),
        P(("dp", "fsdp"), None),
    )
    out_specs = (
        P(("dp", "fsdp"), None),
        P(("dp", "fsdp"), None),
        P(("dp", "fsdp"), None),
        P(("dp", "fsdp")),
        P(("dp", "fsdp"), None),
        P(("dp", "fsdp"), None),
        P(("dp", "fsdp")),
        P(),
        P(),
        P(),
        P(("dp", "fsdp")),
        P(("dp", "fsdp"), None),
        P(("dp", "fsdp")),
        P(("dp", "fsdp"), None),
        P(("dp", "fsdp"), None),
        P(("dp", "fsdp")),
        P(("dp", "fsdp"), None),
        P(("dp", "fsdp"), None),
        P(("dp", "fsdp"), None),
    )
    dp, fsdp = mesh.shape["dp"], mesh.shape["fsdp"]
    fast = dp * fsdp == MHEADS and fsdp == 4
    chosen = partial(fast_body, (dp, fsdp)) if fast else body
    return jax.shard_map(chosen, mesh=mesh, in_specs=in_specs, out_specs=out_specs, check_vma=False)
```

```python
from functools import partial

import jax
import jax.numpy as jnp
from jax import lax
from jax.experimental import pallas as pl
from jax.experimental.pallas import tpu as pltpu
from jax.sharding import PartitionSpec as P

D = 1024
HEAD = 64
HEAD_M = 64
STATE = 128
CONV = 4
PATCH = 8
DI = 2048
MHEADS = 32
CONV_CH = 2304


EPSILON = 1e-05
HIGHEST = lax.Precision.HIGHEST


def shifted(block, axis, distance):
    devices = range(lax.axis_size(axis))
    route = [(i - distance, i) for i in devices if i - distance in devices]
    return lax.ppermute(block, axis, route)


def prefix(value, axis, combine, identity):
    devices, place = (lax.axis_size(axis), lax.axis_index(axis))
    everything = jax.tree.map(
        lambda part, kind: lax.all_gather(part.astype(kind), axis),
        value,
        (jnp.bfloat16, jnp.bfloat16),
    )
    start = jax.tree.map(
        lambda part, zero: jnp.broadcast_to(jnp.asarray(zero, part.dtype), part.shape),
        value,
        identity,
    )

    def prefix_step(k, before):
        reached = k < place
        new = combine(
            before, jax.tree.map(lambda part, own: part[k].astype(own.dtype), everything, value)
        )
        return jax.tree.map(lambda a, b: jnp.where(reached, a, b), new, before)

    return lax.fori_loop(0, devices, prefix_step, start)


def carried_in(value, axis, combine, identity):
    devices, place = (lax.axis_size(axis), lax.axis_index(axis))
    everything = jax.tree.map(
        lambda part, kind: lax.all_gather(part.astype(kind), axis),
        value,
        jax.tree.map(lambda a: jnp.bfloat16 if a.dtype == jnp.float32 else a.dtype, value),
    )
    start = jax.tree.map(
        lambda part, zero: jnp.broadcast_to(jnp.asarray(zero, part.dtype), part.shape),
        value,
        identity,
    )

    def carried_step(k, before):
        at = devices - 1 - k
        reached = at > place
        new = combine(
            before, jax.tree.map(lambda part, own: part[at].astype(own.dtype), everything, value)
        )
        return jax.tree.map(lambda a, b: jnp.where(reached, a, b), new, before)

    return lax.fori_loop(0, devices, carried_step, start)


def product(left, right):
    return jnp.dot(left, right, preferred_element_type=jnp.float32)


def weight_grad(left, right):
    return lax.dot_general(
        left, right, (((0,), (0,)), ((), ())), preferred_element_type=jnp.float32
    )


def input_grad(grad_rows, weight):
    return lax.dot_general(
        grad_rows, weight, (((1,), (1,)), ((), ())), preferred_element_type=jnp.float32
    )


def rms_scale(value, gain):
    return value * lax.rsqrt(jnp.mean(value * value, axis=-1, keepdims=True) + EPSILON) * gain


def gated_norm(core_out, gate_raw, gain):
    count = core_out.shape[0]
    return rms_scale(core_out.reshape(count, DI) * jax.nn.silu(gate_raw), gain)


def patch_docs(doc_lengths, start, count):
    places = start + jnp.arange(count, dtype=jnp.int32)
    first_end = doc_lengths[0, 0]
    second_end = first_end + doc_lengths[0, 1]
    numbers = (places >= first_end).astype(jnp.int32) + (places >= second_end).astype(jnp.int32)
    return jnp.where(places >= 0, numbers, -1)


def chain(earlier, later):
    return (earlier[0] * later[0], later[1] + later[0][:, None, None] * earlier[1])


def mixer_core(
    channels,
    rim,
    step_raw,
    state_in,
    conv_weight,
    conv_bias,
    dt_bias,
    a_log,
    skip_weight,
    docs,
    rim_docs,
    prev_doc,
):
    count = channels.shape[0]
    padded = jnp.concatenate([rim, channels], axis=0)
    padded_docs = jnp.concatenate([rim_docs, docs])
    total = conv_bias[None, :]
    for shift_k in range(CONV):
        same_doc = (padded_docs[shift_k : shift_k + count] == docs).astype(jnp.float32)
        total = (
            total
            + padded[shift_k : shift_k + count]
            * conv_weight[:, shift_k][None, :]
            * same_doc[:, None]
        )
    activated = jax.nn.silu(total)
    inputs = activated[:, :DI].reshape(count, MHEADS, HEAD_M)
    in_map = activated[:, DI : DI + STATE]
    out_map = activated[:, DI + STATE :]
    step_size = jax.nn.softplus(step_raw + dt_bias[None, :])
    rate = -jnp.exp(a_log)
    lower = jnp.tril(jnp.ones((count, count), jnp.float32))
    cumulative = jnp.dot(lower, step_size * rate[None, :], precision=HIGHEST)
    places = jnp.arange(count, dtype=jnp.int32)
    keep = ((places[:, None] >= places[None, :]) & (docs[:, None] == docs[None, :]))[:, :, None]
    spread = cumulative[:, None, :] - cumulative[None, :, :]
    decay_table = jnp.where(keep, jnp.exp(jnp.where(keep, spread, 0.0)), 0.0)
    inner = jnp.dot(out_map, in_map.T, precision=HIGHEST, preferred_element_type=jnp.float32)
    mixing = decay_table * inner[:, :, None] * step_size[None, :, :]
    outputs = jnp.einsum("tsh,shp->thp", mixing, inputs, precision=HIGHEST)
    carry_in = jnp.where((docs == prev_doc)[:, None], jnp.exp(cumulative), 0.0)
    outputs = outputs + carry_in[:, :, None] * jnp.einsum(
        "tn,hpn->thp", out_map, state_in, precision=HIGHEST
    )
    outputs = outputs + skip_weight[None, :, None] * inputs
    last_doc = docs[count - 1]
    tail_keep = (docs == last_doc)[:, None]
    tail_gap = cumulative[count - 1][None, :] - cumulative
    tail_weight = (
        jnp.where(tail_keep, jnp.exp(jnp.where(tail_keep, tail_gap, 0.0)), 0.0) * step_size
    )
    decay_total = jnp.where(prev_doc == last_doc, jnp.exp(cumulative[count - 1]), 0.0)
    state_out = jnp.einsum("sh,shp,sn->hpn", tail_weight, inputs, in_map, precision=HIGHEST)
    state_out = state_out + decay_total[:, None, None] * state_in
    return ((outputs, state_out), (decay_total, carry_in, out_map))


def attend(qkv_low, patches):
    heads = qkv_low.reshape(patches, PATCH, 3, -1, HEAD)
    queries = heads[:, :, 0]
    key_rows = heads[:, :, 1]
    value_rows = heads[:, :, 2]
    scores = jnp.einsum(
        "pihd,pjhd->phij", queries, key_rows, preferred_element_type=jnp.float32
    ) * HEAD ** (-0.5)
    places = jnp.arange(PATCH)
    causal = places[:, None] >= places[None, :]
    scores = jnp.where(causal, scores, -1e30)
    attn_weights = jax.nn.softmax(scores, axis=-1)
    attn_low = attn_weights.astype(jnp.bfloat16)
    mixed = jnp.einsum("phij,pjhd->pihd", attn_low, value_rows, preferred_element_type=jnp.float32)
    mixed = mixed.astype(jnp.bfloat16).reshape(patches * PATCH, -1)
    return ((queries, key_rows, value_rows, attn_weights, attn_low), mixed)


def attend_back(grad_mixed_low, pieces):
    queries, key_rows, value_rows, attn_weights, attn_low = pieces
    patches = queries.shape[0]
    grad_mixed = grad_mixed_low.reshape(patches, PATCH, -1, HEAD)
    grad_values = jnp.einsum(
        "phij,pihd->pjhd", attn_low, grad_mixed, preferred_element_type=jnp.float32
    )
    grad_weights = jnp.einsum(
        "pihd,pjhd->phij", grad_mixed, value_rows, preferred_element_type=jnp.float32
    )
    grad_scores = attn_weights * (
        grad_weights - jnp.sum(attn_weights * grad_weights, axis=-1, keepdims=True)
    )
    scores_low = grad_scores.astype(jnp.bfloat16)
    scale = HEAD ** (-0.5)
    grad_queries = (
        jnp.einsum("phij,pjhd->pihd", scores_low, key_rows, preferred_element_type=jnp.float32)
        * scale
    )
    grad_keys = (
        jnp.einsum("phij,pihd->pjhd", scores_low, queries, preferred_element_type=jnp.float32)
        * scale
    )
    stacked = jnp.stack([grad_queries, grad_keys, grad_values], axis=2).reshape(patches * PATCH, -1)
    return stacked.astype(jnp.bfloat16)


def local_forward(byte_states, mixed_patch, local_set, live):
    attn_gain, qkv_proj, attn_out, ffn_gain, gate_proj, up_proj, down_proj = local_set
    rows = byte_states.shape[0]
    streams = byte_states.astype(jnp.float32) + jnp.repeat(mixed_patch, PATCH, axis=0)
    normed_low = rms_scale(streams, attn_gain.astype(jnp.float32)).astype(jnp.bfloat16)
    qkv_low = product(normed_low, qkv_proj).astype(jnp.bfloat16)
    pieces, mixed_heads = attend(qkv_low, rows // PATCH)
    attended = streams + product(mixed_heads, attn_out)
    ffn_low = rms_scale(attended, ffn_gain.astype(jnp.float32)).astype(jnp.bfloat16)
    gate = product(ffn_low, gate_proj)
    upward = product(ffn_low, up_proj)
    hidden_low = (jax.nn.silu(gate) * upward).astype(jnp.bfloat16)
    block = live * (attended + product(hidden_low, down_proj))
    cache = (streams, normed_low, pieces, mixed_heads, attended, ffn_low, gate, upward, hidden_low)
    return (block, cache)


def local_backward(grad_block, cache, local_set):
    attn_gain, qkv_proj, attn_out, ffn_gain, gate_proj, up_proj, down_proj = local_set
    streams, normed_low, pieces, mixed_heads, attended, ffn_low, gate, upward, hidden_low = cache
    down_low = grad_block.astype(jnp.bfloat16)
    grad_down = weight_grad(hidden_low, down_low)
    grad_hidden = input_grad(down_low, down_proj)
    sigma = jax.nn.sigmoid(gate)
    grad_gate_low = (grad_hidden * upward * sigma * (1.0 + gate * (1.0 - sigma))).astype(
        jnp.bfloat16
    )
    grad_up_low = (grad_hidden * gate * sigma).astype(jnp.bfloat16)
    grad_gate = weight_grad(ffn_low, grad_gate_low)
    grad_up = weight_grad(ffn_low, grad_up_low)
    grad_ffn_in = input_grad(grad_gate_low, gate_proj) + input_grad(grad_up_low, up_proj)
    _, norm_back = jax.vjp(rms_scale, attended, ffn_gain.astype(jnp.float32))
    grad_attended_norm, grad_ffn_gain = norm_back(grad_ffn_in)
    grad_attended = grad_block + grad_attended_norm
    attn_grad_low = grad_attended.astype(jnp.bfloat16)
    grad_attn_out = weight_grad(mixed_heads, attn_grad_low)
    grad_mixed_low = input_grad(attn_grad_low, attn_out).astype(jnp.bfloat16)
    grad_qkv_low = attend_back(grad_mixed_low, pieces)
    grad_qkv = weight_grad(normed_low, grad_qkv_low)
    grad_normed = input_grad(grad_qkv_low, qkv_proj)
    _, norm_back = jax.vjp(rms_scale, streams, attn_gain.astype(jnp.float32))
    grad_streams_norm, grad_attn_gain = norm_back(grad_normed)
    grad_streams = grad_attended + grad_streams_norm
    return (
        grad_streams,
        (grad_qkv, grad_attn_out, grad_gate, grad_up, grad_down, grad_attn_gain, grad_ffn_gain),
    )


def body(
    byte_states,
    doc_lengths,
    out_grad,
    patch_proj,
    global_gain,
    in_proj,
    conv_weight,
    conv_bias,
    dt_bias,
    a_log,
    skip_weight,
    mixer_gain,
    out_proj,
    attn_gain,
    qkv_proj,
    attn_out,
    ffn_gain,
    gate_proj,
    up_proj,
    down_proj,
):
    rows = byte_states.shape[0]
    patches = rows // PATCH
    share = lax.axis_index("fsdp")
    start = share * patches
    docs = patch_docs(doc_lengths, start, patches)
    rim_docs = patch_docs(doc_lengths, start - (CONV - 1), CONV - 1)
    prev_doc = patch_docs(doc_lengths, start - 1, 1)[0]
    live = jnp.repeat((docs < 2).astype(jnp.float32), PATCH)[:, None]
    all_set = (
        lax.all_gather(patch_proj, ("dp", "fsdp"), axis=0, tiled=True),
        lax.all_gather(global_gain, ("dp", "fsdp"), axis=0, tiled=True),
        lax.all_gather(in_proj, ("dp", "fsdp"), axis=0, tiled=True),
        lax.all_gather(conv_weight, ("dp", "fsdp"), axis=0, tiled=True),
        lax.all_gather(conv_bias, ("dp", "fsdp"), axis=0, tiled=True),
        lax.all_gather(mixer_gain, ("dp", "fsdp"), axis=0, tiled=True),
        lax.all_gather(out_proj, ("dp", "fsdp"), axis=0, tiled=True),
        lax.all_gather(attn_gain, ("dp", "fsdp"), axis=0, tiled=True),
        lax.all_gather(qkv_proj, ("dp", "fsdp"), axis=0, tiled=True),
        lax.all_gather(attn_out, ("dp", "fsdp"), axis=0, tiled=True),
        lax.all_gather(ffn_gain, ("dp", "fsdp"), axis=0, tiled=True),
        lax.all_gather(gate_proj, ("dp", "fsdp"), axis=0, tiled=True),
        lax.all_gather(up_proj, ("dp", "fsdp"), axis=0, tiled=True),
        lax.all_gather(down_proj, ("dp", "fsdp"), axis=0, tiled=True),
    )
    global_set = all_set[:7]
    local_set = all_set[7:]
    patch_full, gain_g_full, in_full, conv_w_full, conv_b_full, gain_m_full, out_full = global_set
    patch_rows = byte_states.reshape(patches, PATCH * D)
    patch_sum = product(patch_rows, patch_full)
    gain_g = gain_g_full.astype(jnp.float32)
    global_low = rms_scale(patch_sum, gain_g).astype(jnp.bfloat16)
    projected = product(global_low, in_full)
    gate_raw = projected[:, :DI]
    channels = projected[:, DI : DI + CONV_CH]
    step_raw = projected[:, DI + CONV_CH :]
    rim = shifted(channels[patches - (CONV - 1) :], "fsdp", 1)
    core = partial(mixer_core, docs=docs, rim_docs=rim_docs, prev_doc=prev_doc)
    conv_w = conv_w_full.astype(jnp.float32)
    conv_b = conv_b_full.astype(jnp.float32)
    empty_state = jnp.zeros((MHEADS, HEAD_M, STATE), jnp.float32)
    (partial_out, local_state), aux = core(
        channels, rim, step_raw, empty_state, conv_w, conv_b, dt_bias, a_log, skip_weight
    )
    decay_total, carry_in, out_map = aux
    identity = (jnp.ones((MHEADS,), jnp.float32), jnp.zeros((MHEADS, HEAD_M, STATE), jnp.float32))
    arrived = prefix((decay_total, local_state), "fsdp", chain, identity)
    state_in = arrived[1]
    mixer_out = partial_out + carry_in[:, :, None] * jnp.einsum(
        "tn,hpn->thp", out_map, state_in, precision=HIGHEST
    )
    gain_m = gain_m_full.astype(jnp.float32)
    mixer_low = gated_norm(mixer_out, gate_raw, gain_m).astype(jnp.bfloat16)
    mixed_patch = patch_sum + product(mixer_low, out_full)
    block, cache = local_forward(byte_states, mixed_patch, local_set, live)
    block_out = block.astype(jnp.bfloat16)
    back_set = (
        lax.all_gather(patch_proj, ("dp", "fsdp"), axis=0, tiled=True),
        lax.all_gather(global_gain, ("dp", "fsdp"), axis=0, tiled=True),
        lax.all_gather(in_proj, ("dp", "fsdp"), axis=0, tiled=True),
        lax.all_gather(conv_weight, ("dp", "fsdp"), axis=0, tiled=True),
        lax.all_gather(conv_bias, ("dp", "fsdp"), axis=0, tiled=True),
        lax.all_gather(mixer_gain, ("dp", "fsdp"), axis=0, tiled=True),
        lax.all_gather(out_proj, ("dp", "fsdp"), axis=0, tiled=True),
        lax.all_gather(attn_gain, ("dp", "fsdp"), axis=0, tiled=True),
        lax.all_gather(qkv_proj, ("dp", "fsdp"), axis=0, tiled=True),
        lax.all_gather(attn_out, ("dp", "fsdp"), axis=0, tiled=True),
        lax.all_gather(ffn_gain, ("dp", "fsdp"), axis=0, tiled=True),
        lax.all_gather(gate_proj, ("dp", "fsdp"), axis=0, tiled=True),
        lax.all_gather(up_proj, ("dp", "fsdp"), axis=0, tiled=True),
        lax.all_gather(down_proj, ("dp", "fsdp"), axis=0, tiled=True),
    )
    global_back = back_set[:7]
    local_back = back_set[7:]
    _, cache = local_forward(byte_states, mixed_patch, local_back, live)
    patch_back, _, in_back, conv_w_back, conv_b_back, _, out_back = global_back
    grad_block = live * out_grad.astype(jnp.float32)
    grad_streams, local_grads = local_backward(grad_block, cache, local_back)
    reduced_local = (
        lax.psum_scatter(local_grads[0], ("dp", "fsdp"), scatter_dimension=0, tiled=True),
        lax.psum_scatter(local_grads[1], ("dp", "fsdp"), scatter_dimension=0, tiled=True),
        lax.psum_scatter(local_grads[2], ("dp", "fsdp"), scatter_dimension=0, tiled=True),
        lax.psum_scatter(local_grads[3], ("dp", "fsdp"), scatter_dimension=0, tiled=True),
        lax.psum_scatter(local_grads[4], ("dp", "fsdp"), scatter_dimension=0, tiled=True),
        lax.psum_scatter(local_grads[5], ("dp", "fsdp"), scatter_dimension=0, tiled=True),
        lax.psum_scatter(local_grads[6], ("dp", "fsdp"), scatter_dimension=0, tiled=True),
    )
    grad_patch_mix = grad_streams.reshape(patches, PATCH, D).sum(axis=1)
    mix_low = grad_patch_mix.astype(jnp.bfloat16)
    grad_out_proj = weight_grad(mixer_low, mix_low)
    grad_mixer_low = input_grad(mix_low, out_back)
    _, norm_back = jax.vjp(gated_norm, mixer_out, gate_raw, gain_m)
    grad_core, grad_gate_raw, grad_mixer_gain = norm_back(grad_mixer_low)
    state_part = jnp.einsum("th,thp,tn->hpn", carry_in, grad_core, out_map, precision=HIGHEST)
    returned = carried_in((decay_total, state_part), "fsdp", chain, identity)
    _, core_back, _ = jax.vjp(
        core,
        channels,
        rim,
        step_raw,
        state_in,
        conv_w_back.astype(jnp.float32),
        conv_b_back.astype(jnp.float32),
        dt_bias,
        a_log,
        skip_weight,
        has_aux=True,
    )
    core_grads = core_back((grad_core, returned[1]))
    (
        grad_channels,
        grad_rim,
        grad_step,
        _,
        grad_conv_w,
        grad_conv_b,
        grad_dt_bias,
        grad_a_log,
        grad_skip,
    ) = core_grads
    rim_grad = shifted(grad_rim, "fsdp", -1)
    cut = patches - (CONV - 1)
    grad_channels = jnp.concatenate([grad_channels[:cut], grad_channels[cut:] + rim_grad], axis=0)
    proj_low = jnp.concatenate([grad_gate_raw, grad_channels, grad_step], axis=1).astype(
        jnp.bfloat16
    )
    grad_in_proj = weight_grad(global_low, proj_low)
    grad_global_norm = input_grad(proj_low, in_back)
    _, norm_back = jax.vjp(rms_scale, patch_sum, gain_g)
    grad_sum_norm, grad_global_gain = norm_back(grad_global_norm)
    sum_low = (grad_patch_mix + grad_sum_norm).astype(jnp.bfloat16)
    grad_patch_proj = weight_grad(patch_rows, sum_low)
    grad_states = grad_streams + input_grad(sum_low, patch_back).reshape(rows, D)
    reduced_global = (
        lax.psum_scatter(grad_patch_proj, ("dp", "fsdp"), scatter_dimension=0, tiled=True),
        lax.psum_scatter(grad_global_gain, ("dp", "fsdp"), scatter_dimension=0, tiled=True),
        lax.psum_scatter(grad_in_proj, ("dp", "fsdp"), scatter_dimension=0, tiled=True),
        lax.psum_scatter(grad_conv_w, ("dp", "fsdp"), scatter_dimension=0, tiled=True),
        lax.psum_scatter(grad_conv_b, ("dp", "fsdp"), scatter_dimension=0, tiled=True),
        lax.psum_scatter(grad_mixer_gain, ("dp", "fsdp"), scatter_dimension=0, tiled=True),
        lax.psum_scatter(grad_out_proj, ("dp", "fsdp"), scatter_dimension=0, tiled=True),
    )
    head_sums = lax.psum((grad_dt_bias, grad_a_log, grad_skip), ("dp", "fsdp"))
    return (
        block_out,
        grad_states,
        reduced_global[0],
        reduced_global[1],
        reduced_global[2],
        reduced_global[3],
        reduced_global[4],
        head_sums[0],
        head_sums[1],
        head_sums[2],
        reduced_global[5],
        reduced_global[6],
        reduced_local[5],
        reduced_local[0],
        reduced_local[1],
        reduced_local[6],
        reduced_local[2],
        reduced_local[3],
        reduced_local[4],
    )


MESH = pl.DeviceIdType.MESH
WIDE = 12288
PARTS = ((0, 3072), (3072, 1024), (4096, 4096), (8192, 4096))
STEP = 1024
FAR_F, FAR_B = 2048, 2048
CUTS = (2048, 2048, 1024)
CUTS_F = (1536, 1024, 512)
TILE = 32
SMALL_ROWS, SMALL_COLS = 48, 384
EXT = D + 128


def device(z, x, y, c):
    return (z * 2 + x, y * 2 + c)


class Spot:
    def __init__(self, depth):
        dp, fs = lax.axis_index("dp"), lax.axis_index("fsdp")
        self.depth, self.count = depth, depth * 8
        self.me = dp * 4 + fs
        self.z, self.x, self.y, self.c = dp // 2, dp % 2, fs // 2, fs % 2
        self.q = self.x * 4 + self.y * 2 + self.c
        self.plane = self.x * 2 + self.y
        swap = lambda place: place + (place // 2) * (1 - 2 * (place % 2))
        self.turn = swap(self.z)
        self.column = [swap((self.turn + depth - j) % depth) for j in range(depth)]

    def flip(self, way):
        x = 1 - self.x if way & 2 else self.x
        y = 1 - self.y if way & 1 else self.y
        return device(self.z, x, y, self.c), x * 2 + y

    def sibling(self):
        return device(self.z, self.x, self.y, 1 - self.c)

    def onward(self):
        place = (self.turn + 1) % self.depth
        return device(place + (place // 2) * (1 - 2 * (place % 2)), self.x, self.y, self.c)

    def above(self, k):
        return device((self.z + k) % self.depth, self.x, self.y, self.c)


def greet(spot):
    barrier = pltpu.get_barrier_semaphore()

    def one(i, carry):
        to = (spot.me + i) % spot.count
        pl.semaphore_signal(barrier, inc=1, device_id=(to // 4, to % 4), device_id_type=MESH)
        return carry

    lax.fori_loop(1, spot.count, one, 0)
    pl.semaphore_wait(barrier, spot.count - 1)


class Wires:
    def __init__(self, send, recv):
        self.send, self.recv, self.used, self.open = send, recv, 0, []

    def copy(self, src, dst, to):
        i = self.used
        self.used += 1
        copy = pltpu.make_async_remote_copy(
            src_ref=src,
            dst_ref=dst,
            send_sem=self.send.at[i],
            recv_sem=self.recv.at[i],
            device_id=to,
            device_id_type=MESH,
        )
        copy.start()
        self.open.append(copy)
        return copy

    def drain(self):
        for copy in self.open:
            copy.wait_send()


def got(copies):
    for copy in copies:
        copy.wait_recv()


class Swap:
    def __init__(self, spot, send, recv, src_at, dst_at):
        self.spot, self.send, self.recv, self.src_at, self.dst_at = spot, send, recv, src_at, dst_at

    def copy(self, i):
        to = (self.spot.me + i) % self.spot.count
        return pltpu.make_async_remote_copy(
            src_ref=self.src_at(to),
            dst_ref=self.dst_at(self.spot.me),
            send_sem=self.send.at[i],
            recv_sem=self.recv.at[i],
            device_id=(to // 4, to % 4),
            device_id_type=MESH,
        )

    def each(self, act):
        def one(i, carry):
            act(self.copy(i))
            return carry

        lax.fori_loop(1, self.spot.count, one, 0)

    def start(self):
        self.each(lambda copy: copy.start())

    def arrive(self):
        self.each(lambda copy: copy.wait_recv())

    def leave(self):
        self.each(lambda copy: copy.wait_send())


def plane_swap(wires, spot, src_at, dst_at):
    copies = []
    for way in range(4):
        for other in range(2):
            if way or other:
                x = spot.x ^ (way >> 1)
                y = spot.y ^ (way & 1)
                c = spot.c ^ other
                copies.append(
                    wires.copy(src_at(x * 4 + y * 2 + c), dst_at(spot.q), device(spot.z, x, y, c))
                )
    return copies


def block_row(t, plane, c):
    return (t * 4 + plane) * 2 + c


def spread_all(wires, spot, buf, own=None):
    at = lambda t, plane, c: buf.at[block_row(t, plane, c)]
    mine = at(spot.z, spot.plane, spot.c)
    src = mine if own is None else own
    ring, flat, core = [], [], []
    for k in range(1, spot.depth):
        ring.append(wires.copy(src, mine, spot.above(k)))
    flat.append([wires.copy(src, mine, spot.flip(way)[0]) for way in (1, 2, 3)])
    core.append(wires.copy(src, mine, spot.sibling()))
    yield
    for j in range(1, spot.depth):
        got([ring[j - 1]])
        block = at((spot.z + spot.depth - j) % spot.depth, spot.plane, spot.c)
        flat.append([wires.copy(block, block, spot.flip(way)[0]) for way in (1, 2, 3)])
        core.append(wires.copy(block, block, spot.sibling()))
    yield
    for j in range(spot.depth):
        for way in (1, 2, 3):
            got([flat[j][way - 1]])
            block = at((spot.z + spot.depth - j) % spot.depth, spot.flip(way)[1], spot.c)
            core.append(wires.copy(block, block, spot.sibling()))
    yield
    got(core)


def spread_plane(wires, spot, buf):
    at = lambda plane: buf.at[plane * 2 + spot.c]
    mine = at(spot.plane)
    flat = [wires.copy(mine, mine, spot.flip(way)[0]) for way in (1, 2, 3)]
    core = [wires.copy(mine, mine, spot.sibling())]
    yield
    for way in (1, 2, 3):
        got([flat[way - 1]])
        block = at(spot.flip(way)[1])
        core.append(wires.copy(block, block, spot.sibling()))
    yield
    got(core)


def sum_plane(wires, spot, parts, pair, near):
    first = wires.copy(parts.at[:, 1 - spot.c], pair, spot.sibling())
    yield None
    got([first])
    f32 = jnp.float32
    pair[...] = (parts[:, spot.c].astype(f32) + pair[...].astype(f32)).astype(jnp.bfloat16)
    flat = [
        wires.copy(pair.at[spot.flip(way)[1]], near.at[way - 1], spot.flip(way)[0]) for way in (1, 2, 3)
    ]
    yield None
    got(flat)
    total = pair[spot.plane].astype(f32)
    for way in range(3):
        total = total + near[way].astype(f32)
    yield total


def sum_all(wires, spot, parts, pair, near, column, far, out):
    f32, low = jnp.float32, jnp.bfloat16
    half = parts.shape[-1] // 2
    cut = [pl.ds(h * half, half) for h in range(2)]
    first = [
        wires.copy(parts.at[:, 1 - spot.c, :, cut[h]], pair.at[:, :, cut[h]], spot.sibling()) for h in range(2)
    ]
    yield
    flat, ring = [], []
    rows = pair.shape[1]
    for h in range(2):
        got([first[h]])
        for b in range(4 * spot.depth):
            pair[b, :, cut[h]] = (
                parts[b, spot.c, :, cut[h]].astype(f32) + pair[b, :, cut[h]].astype(f32)
            ).astype(low)
        step = []
        for way in (1, 2, 3):
            to, plane = spot.flip(way)
            for t in range(spot.depth):
                step.append(
                    wires.copy(pair.at[t * 4 + plane, :, cut[h]], near.at[way - 1, t, :, cut[h]], to)
                )
        flat.append(step)
    yield
    for h in range(2):
        got(flat[h])
        for t in range(spot.depth):
            total = pair[t * 4 + spot.plane, :, cut[h]].astype(f32)
            for way in range(3):
                total = total + near[way, t, :, cut[h]].astype(f32)
            column[t, :, cut[h]] = total.astype(low)
        ring.append(
            [
                wires.copy(
                    column.at[(spot.z + k) % spot.depth, :, cut[h]], far.at[k - 1, :, cut[h]], spot.above(k)
                )
                for k in range(1, spot.depth)
            ]
        )
    yield
    for h in range(2):
        got(ring[h])
        total = column[spot.z, :, cut[h]].astype(f32)
        for k in range(1, spot.depth):
            total = total + far[k - 1, :, cut[h]].astype(f32)
        out[:, cut[h]] = total
    yield


def big_gather(wires, spot, ow, od, shards):
    down = od.shape[0] // spot.count
    xn, yn, cn, zn = spot.flip(2)[0], spot.flip(1)[0], spot.sibling(), spot.onward()
    here, xp, yp, xy = spot.plane, spot.flip(2)[1], spot.flip(1)[1], spot.flip(3)[1]
    parts = {"C": (WIDE - FAR_F, FAR_F, None), ("A", 0): (0, 2 * D, None), ("B", 0): (2 * D, 2 * D, None)}
    begin, side, at = 4 * D, (WIDE - FAR_F - 4 * D) // 2, 0
    for i, width in enumerate(CUTS_F, 1):
        last = i == len(CUTS_F)
        parts["A", i] = (begin + at, width, (0, down // 2) if last else None)
        parts["B", i] = (begin + side + at, width, (down // 2, down // 2) if last else None)
        at += width
    assert at == side
    mine = pl.multiple_of(spot.me * TILE, TILE)
    row = pl.multiple_of(spot.me * down, down)

    def refs(t, plane, part):
        begin, width, deep = parts[part]
        r = block_row(t, plane, spot.c)
        found = [ow.at[pl.ds(pl.multiple_of(r * TILE, TILE), TILE), pl.ds(begin, width)]]
        if deep:
            found.append(od.at[pl.ds(pl.multiple_of(r * down + deep[0], deep[1]), deep[1])])
        return found

    def go(t, plane, part, to):
        return [wires.copy(r, r, to) for r in refs(t, plane, part)]

    def own(part, to):
        begin, width, deep = parts[part]
        pairs = []
        for ref, (base, size) in zip(shards[:4], PARTS):
            low, high = max(begin, base), min(begin + width, base + size)
            if low < high:
                pairs.append(
                    (ref.at[:, pl.ds(low - base, high - low)], ow.at[pl.ds(mine, TILE), pl.ds(low, high - low)])
                )
        if deep:
            pairs.append(
                (shards[4].at[pl.ds(*deep)], od.at[pl.ds(pl.multiple_of(row + deep[0], deep[1]), deep[1])])
            )
        return [wires.copy(a, b, to) for a, b in pairs]

    T = spot.column
    core, ring, fx, fy, sx, sy = {i: [] for i in range(len(CUTS_F) + 2)}, {}, {}, {}, {}, {}

    landed = set()

    def arrived(j, i):
        if j and (j, i) not in landed:
            got(ring[j - 1, i])
            landed.add((j, i))

    def climb_on(j, i):
        send = own if j == 0 else (lambda part, to: go(T[j], here, part, to))
        arrived(j, i)
        ring[j, i] = send(("A", i), zn) + send(("B", i), zn)

    def first(j, i):
        send = own if j == 0 else (lambda part, to: go(T[j], here, part, to))
        arrived(j, i)
        fx[j, i], fy[j, i] = send(("A", i), xn), send(("B", i), yn)
        core[i].append(send(("A", i), cn) + send(("B", i), cn))

    def second(j, i):
        send = own if j == 0 else (lambda part, to: go(T[j], here, part, to))
        got(fx[j, i])
        sy[j, i] = send(("A", i), yn) + go(T[j], xp, ("A", i), yn)
        got(fy[j, i])
        sx[j, i] = send(("B", i), xn) + go(T[j], yp, ("B", i), xn)
        core[i].append(go(T[j], xp, ("A", i), cn) + go(T[j], yp, ("B", i), cn))

    def third(j, i):
        got(sy[j, i])
        core[i].append(go(T[j], yp, ("A", i), cn) + go(T[j], xy, ("A", i), cn))
        got(sx[j, i])
        core[i].append(go(T[j], xp, ("B", i), cn) + go(T[j], xy, ("B", i), cn))

    flat, climb = [], {}

    def far(j):
        if j < 0:
            flat.extend(own("C", spot.flip(way)[0]) for way in (1, 2, 3))
            core[len(CUTS_F) + 1].append(own("C", cn))
            return
        if j == 0:
            assert flat
            for copies in flat:
                got(copies)
        else:
            got(climb[j - 1])
        if j < spot.depth - 1:
            climb[j] = own("C", zn) if j == 0 else go(T[j], here, "C", zn)
            for plane in (xp, yp, xy):
                climb[j] += go(T[j], plane, "C", zn)
        for plane in (xp, yp, xy) + ((here,) if j else ()):
            core[len(CUTS_F) + 1].append(go(T[j], plane, "C", cn))

    chunks, n = range(len(CUTS_F) + 1), spot.depth
    steps = {far_step(j): partial(far, j) for j in range(-1, n)}
    for i in chunks:
        for j in range(n):
            for kind, act in enumerate((climb_on, first, second, third), 1):
                if act is not climb_on or j < n - 1:
                    steps[100 * kind + 10 * j + i] = partial(act, j, i)

    def close(which):
        for part in which:
            for copies in core.pop(part):
                got(copies)

    return steps, close


def far_step(j):
    return 510 + 10 * j


class Ticker:
    def __init__(self, steps, plan):
        self.steps, self.plan = dict(steps), iter(plan)

    def __call__(self):
        for name in next(self.plan):
            self.steps.pop(name)()

    def rest(self, order):
        for name in order:
            if name in self.steps:
                self.steps.pop(name)()
        assert not self.steps


def run(steps):
    for _ in steps:
        pass


def sigmoid(v):
    return 1.0 / (1.0 + jnp.exp(-v))


def lanes(shape, axis):
    return lax.broadcasted_iota(jnp.int32, shape, axis)


def flat_dot(a, b, dims=((1,), (0,))):
    return lax.dot_general(a, b, (dims, ((), ())), preferred_element_type=jnp.float32)


def exact_dot(a, b):
    return jnp.dot(a, b, precision=HIGHEST, preferred_element_type=jnp.float32)


def gain_row(values):
    n_dev, width = values.shape[0], D // values.shape[0]
    spread = (lanes((128, D), 0) == lanes((128, D), 1) & (width - 1)).astype(jnp.bfloat16)
    rows = flat_dot(values, spread)
    return jnp.sum(jnp.where(lanes((n_dev, D), 0) == lanes((n_dev, D), 1) >> (width.bit_length() - 1), rows, 0.0), axis=0, keepdims=True)


def tap_rows(spot, small):
    n_dev = spot.count
    share = CONV_CH // n_dev
    col = lanes((1, 512), 1)
    channel = jnp.where(col < 256, (spot.q + 8 * (col >> 6)) * HEAD_M + (col & 63), DI + col - 256)
    dev = lanes((n_dev, 512), 0)
    picks = (channel >= dev * share) & (channel < dev * share + share)
    owner = jnp.sum(jnp.where(picks, dev, 0), axis=0, keepdims=True)
    within = lanes((128, 512), 0) == channel - owner * share
    rows = []
    for k in range(CONV + 1):
        values = small[:, TILE + k, 0:128]
        spread = flat_dot(values, picks.astype(jnp.bfloat16), ((0,), (0,)))
        rows.append(jnp.sum(jnp.where(within, spread, 0.0), axis=0, keepdims=True))
    return rows


def entry(block, row, lane):
    at = (lanes(block.shape, 0) == row) & (lanes(block.shape, 1) == lane)
    return jnp.sum(jnp.where(at, block.astype(jnp.float32), 0.0), keepdims=True).reshape(1, 1)


class Slot:
    def __init__(self, spot, small, x, count):
        block = small[(spot.z * 2 + x) * 4, TILE : TILE + 16, 0:128].astype(jnp.float32)
        first = entry(block, 9, 0)
        second = first + entry(block, 9, 1)
        number = lambda p: (p >= first).astype(jnp.float32) + (p >= second).astype(jnp.float32)
        col = lanes((count, 1), 0).astype(jnp.float32)
        row = lanes((1, count), 1).astype(jnp.float32)
        docs = number(col)
        self.keep = (col >= row) & (docs == number(row))
        self.same = [((col >= s) & (number(col - s) == docs)).astype(jnp.float32) for s in range(CONV)]


def shift(block, by):
    return block if by == 0 else pltpu.roll(block, by % block.shape[0], 0)


class Mixed:
    def __init__(self, spot, slot, own, maps, step_raw, taps, dt_row, rate_row):
        count = own.shape[0]
        self.spot, self.slot, self.count = spot, slot, count
        self.channels = jnp.concatenate([own[:, 256:], maps], axis=1)
        conv = taps[CONV] + sum(
            taps[CONV - 1 - s] * (shift(self.channels, s) * slot.same[s]) for s in range(CONV)
        )
        self.conv, self.sig = conv, sigmoid(conv)
        act = conv * self.sig
        self.inputs = act[:, :256]
        self.in_map, self.out_map = act[:, 256:384].astype(jnp.bfloat16), act[:, 384:].astype(jnp.bfloat16)
        self.raw = step_raw + dt_row
        self.step = jnp.where(self.raw > 20.0, self.raw, jnp.log(1.0 + jnp.exp(jnp.minimum(self.raw, 20.0))))
        lower = lanes((count, count), 0) >= lanes((count, count), 1)
        self.upper = (lanes((count, count), 0) <= lanes((count, count), 1)).astype(jnp.float32)
        self.cum = exact_dot(lower.astype(jnp.float32), self.step * rate_row)
        self.cum_t, self.step_t = self.cum.T, self.step.T
        self.inner = flat_dot(self.out_map, self.in_map, ((1,), (1,)))

    def head(self, i):
        return self.spot.q + 8 * i

    def col(self, by_head, i):
        return jnp.sum(jnp.where(lanes((1, 128), 1) == self.head(i), by_head, 0.0), axis=1, keepdims=True)

    def row(self, by_head_t, i):
        return jnp.sum(jnp.where(lanes((128, 1), 0) == self.head(i), by_head_t, 0.0), axis=0, keepdims=True)

    def decay(self, i):
        gap = jnp.where(self.slot.keep, self.col(self.cum, i) - self.row(self.cum_t, i), 0.0)
        return jnp.where(self.slot.keep, jnp.exp(gap), 0.0)


def pick_lane(row, lane):
    return jnp.sum(jnp.where(lanes(row.shape, 1) == lane, row, 0.0), axis=1, keepdims=True)


def patch_pairs(count):
    i, j = lanes((count, count), 0), lanes((count, count), 1)
    return (i >= j) & ((i >> 3) == (j >> 3))


def rms_back(value, gain, grad):
    scale = lax.rsqrt(jnp.mean(value * value, axis=1, keepdims=True) + EPSILON)
    along = jnp.mean(grad * gain * value, axis=1, keepdims=True)
    d_value = scale * gain * grad - value * (scale * scale * scale * along)
    return d_value, jnp.sum(grad * value * scale, axis=0, keepdims=True)


def halves_of(block):
    left = lanes(block.shape, 1) < HEAD
    return left, [jnp.where(left, block, 0), jnp.where(left, 0, block)]


def local_block(
    tick,
    ready,
    whole,
    lengths,
    bytes_ref,
    grad_ref,
    sum_ref,
    mixed_ref,
    small_ref,
    wide,
    deep,
    o_block,
    o_streams,
    o_mix,
    o_direct,
    o_gains,
    g_qkv,
    g_attn,
    g_gate,
    g_up,
    g_down,
    attn_w,
    ffn_w,
    g_buf,
    streams,
    normed,
    qkv,
    weights,
    heads,
    attended,
    ffn_low,
    ffn_t,
    total,
    d_ffn,
    d_down,
    load_sem,
    ffn_sem,
    g_sem,
):
    f32, low = jnp.float32, jnp.bfloat16
    rows = bytes_ref.shape[0]
    scale = HEAD ** (-0.5)
    ready()
    load = pltpu.make_async_copy(wide.at[:, pl.ds(0, 4 * D)], attn_w, load_sem.at[0])
    load.start()

    def ffn_loads(j, slot):
        at = lambda base: pl.ds(pl.multiple_of(base + j * D, D), D)
        return [
            pltpu.make_async_copy(wide.at[:, at(4 * D)], ffn_w.at[slot, 0], ffn_sem.at[slot, 0]),
            pltpu.make_async_copy(wide.at[:, at(8 * D)], ffn_w.at[slot, 1], ffn_sem.at[slot, 1]),
            pltpu.make_async_copy(deep.at[at(0)], ffn_w.at[slot, 2], ffn_sem.at[slot, 2]),
        ]

    gain_a = gain_row(small_ref[:, TILE + 7, 0:128])
    gain_f = gain_row(small_ref[:, TILE + 8, 0:128])
    place = lax.axis_index("fsdp") * (rows // PATCH) + (lanes((rows, 1), 0) >> 3)
    live = (place < lengths[0, 0] + lengths[0, 1]).astype(f32)
    raw = mixed_ref[:, pl.ds(0, D)]
    mixer_r = lax.rsqrt(mixed_ref[:, pl.ds(D, 128)] * (1.0 / DI) + EPSILON)[:, 0:1]
    patch = sum_ref[...] + raw * mixer_r
    patch = jnp.broadcast_to(patch[:, None, :], (rows // PATCH, PATCH, D)).reshape(rows, D)
    streams[...] = bytes_ref[...].astype(f32) + patch
    normed[...] = rms_scale(streams[...], gain_a).astype(low)
    d_down[...] = (live * grad_ref[...].astype(f32)).astype(low)
    load.wait()
    for i in range(3):
        at = pl.ds(i * D, D)
        qkv[:, at] = flat_dot(normed[...], attn_w[:, at]).astype(low)
        tick()
    pairs = patch_pairs(128)

    def blocks(p, b):
        row = pl.ds(b * 128, 128)
        return row, [pl.ds(pl.multiple_of(base + p * 128, 128), 128) for base in (0, D, 2 * D)]

    def attend(p, carry):
        for b in range(rows // 128):
            row, (qa, ka, va) = blocks(p, b)
            k, v = qkv[row, ka], qkv[row, va]
            left, queries = halves_of(qkv[row, qa])
            outs = []
            for h in range(2):
                scores = flat_dot(queries[h], k, ((1,), (1,))) * scale
                scores = jnp.where(pairs, scores, -1e30)
                e = jnp.exp(scores - jnp.max(scores, axis=1, keepdims=True))
                w = e / jnp.sum(e, axis=1, keepdims=True)
                weights[p, b, h] = w
                outs.append(flat_dot(w.astype(low), v))
            heads[row, qa] = jnp.where(left, outs[0], outs[1]).astype(low)
        return carry

    for begin in range(0, D // 128, 2):
        lax.fori_loop(begin, begin + 2, attend, 0)
        tick()
    attended[...] = streams[...] + flat_dot(heads[...], attn_w[:, pl.ds(3 * D, D)])
    ffn_low[...] = rms_scale(attended[...], gain_f).astype(low)
    whole()
    for copy in ffn_loads(0, 0):
        copy.start()
    ffn_t[...] = ffn_low[...].astype(f32).T.astype(low)
    total[...] = attended[...]
    d_ffn[...] = jnp.zeros_like(d_ffn)
    n_ffn = deep.shape[0] // D

    def stores(j):
        at = pl.ds(pl.multiple_of(j * D, D), D)
        return [
            pltpu.make_async_copy(g_buf.at[0], g_gate.at[:, at], g_sem.at[0]),
            pltpu.make_async_copy(g_buf.at[1], g_up.at[:, at], g_sem.at[1]),
            pltpu.make_async_copy(g_buf.at[2], g_down.at[at], g_sem.at[2]),
        ]

    def feed(j, carry):
        slot = lax.rem(j, 2)
        for copy in ffn_loads(j, slot):
            copy.wait()

        @pl.when(j + 1 < n_ffn)
        def _():
            for copy in ffn_loads(j + 1, 1 - slot):
                copy.start()

        gate = flat_dot(ffn_low[...], ffn_w[slot, 0])
        upward = flat_dot(ffn_low[...], ffn_w[slot, 1])
        sig = sigmoid(gate)
        act = gate * sig
        hidden = (act * upward).astype(low)
        total[...] += flat_dot(hidden, ffn_w[slot, 2])
        d_hidden = flat_dot(d_down[...], ffn_w[slot, 2], ((1,), (1,)))
        d_gate = (d_hidden * upward * (sig + act * (1.0 - sig))).astype(low)
        d_up = (d_hidden * act).astype(low)
        d_ffn[...] += flat_dot(d_gate, ffn_w[slot, 0], ((1,), (1,)))
        d_ffn[...] += flat_dot(d_up, ffn_w[slot, 1], ((1,), (1,)))

        @pl.when(j > 0)
        def _():
            for copy in stores(j - 1):
                copy.wait()

        g_buf[0] = flat_dot(ffn_t[...], d_gate).astype(low)
        g_buf[1] = flat_dot(ffn_t[...], d_up).astype(low)
        g_buf[2] = flat_dot(hidden.astype(f32).T.astype(low), d_down[...]).astype(low)
        for copy in stores(j):
            copy.start()
        return carry

    lax.fori_loop(0, n_ffn, feed, 0)
    o_block[...] = (live * total[...]).astype(low)
    d_norm, gain_f_sum = rms_back(attended[...], gain_f, d_ffn[...])
    d_attended = live * grad_ref[...].astype(f32) + d_norm
    total[...] = d_attended
    d_low = d_attended.astype(low)
    for copy in stores(n_ffn - 1):
        copy.wait()
    d_down[...] = flat_dot(d_low, attn_w[:, pl.ds(3 * D, D)], ((1,), (1,))).astype(low)
    g_buf[0] = flat_dot(heads[...].astype(f32).T.astype(low), d_low).astype(low)
    last = [pltpu.make_async_copy(g_buf.at[0], g_attn, g_sem.at[0])]
    last[0].start()

    def attend_back(p, carry):
        for b in range(rows // 128):
            row, (qa, ka, va) = blocks(p, b)
            q, k, v = qkv[row, qa], qkv[row, ka], qkv[row, va]
            grad = d_down[row, qa]
            left, grads = halves_of(grad)
            dq, dk, dv = [], [], []
            for h in range(2):
                w = weights[p, b, h]
                dv.append(flat_dot(w.T.astype(low), grad))
                d_w = flat_dot(grads[h], v, ((1,), (1,)))
                d_s = w * (d_w - jnp.sum(w * d_w, axis=1, keepdims=True))
                dq.append(flat_dot(d_s.astype(low), k) * scale)
                dk.append(flat_dot(d_s.T.astype(low), q) * scale)
            qkv[row, qa] = jnp.where(left, dq[0], dq[1]).astype(low)
            qkv[row, ka] = jnp.where(left, dk[0], dk[1]).astype(low)
            qkv[row, va] = jnp.where(left, dv[0], dv[1]).astype(low)
        return carry

    lax.fori_loop(0, D // 128, attend_back, 0)
    ffn_t[...] = normed[...].astype(f32).T.astype(low)
    for i in range(3):
        at = pl.ds(i * D, D)
        if i == 2:
            last[0].wait()
        buf = (i + 1) % 3
        g_buf[buf] = flat_dot(ffn_t[...], qkv[:, at]).astype(low)
        copy = pltpu.make_async_copy(g_buf.at[buf], g_qkv.at[:, at], g_sem.at[buf])
        copy.start()
        last.append(copy)
    d_ffn[...] = flat_dot(qkv[...], attn_w[:, pl.ds(0, 3 * D)], ((1,), (1,)))
    d_norm, gain_a_sum = rms_back(streams[...], gain_a, d_ffn[...])
    d_streams = total[...] + d_norm
    o_streams[...] = d_streams
    direct = jnp.sum(d_streams.reshape(rows // PATCH, PATCH, D), axis=1)
    o_direct[...] = direct
    mix = direct.astype(low)
    along = jnp.sum(mix.astype(f32) * raw, axis=1, keepdims=True)
    high_r, high_a = (v.astype(low).astype(f32) for v in (mixer_r, along))
    lane = lanes((rows // PATCH, 128), 1)
    ext = jnp.zeros((rows // PATCH, 128), f32)
    for i, v in enumerate((high_r, high_a, mixer_r - high_r, along - high_a)):
        ext = jnp.where(lane == i, v, ext)
    o_mix[:, pl.ds(0, D)] = mix
    o_mix[:, pl.ds(D, 128)] = ext.astype(low)
    o_gains[...] = jnp.concatenate([gain_a_sum, gain_f_sum, jnp.zeros((6, D), f32)], axis=0)
    for copy in last[1:]:
        copy.wait()


N_WIRES = 512
PLAN_F = (
    (500, 100, 200),
    (),
    (),
    (),
    (300, 201),
    (110, 210, 101),
    (),
    (310, 202, 120),
    (400,),
    (220, 301),
    (320, 102, 103, 203),
    (410,),
    (302,),
    (230,),
    (111, 211),
    (510,),
    (330,),
    (420,),
    (112, 212),
    (303,),
    (113, 213),
    (),
    (430, 311, 312),
    (121, 221),
    (313, 122, 222),
    (520, 401, 402),
    (123, 223, 321),
    (322, 403, 411),
    (231, 323, 412),
    (530, 232, 413),
)
REST_F = (
    331,
    233,
    332,
    333,
    540,
    421,
    422,
    423,
    431,
    432,
    433,
)
PLAN_B = (
    (),
    (),
    (200, 210),
    (201, 202),
    (510, 520),
    (211,),
    (300,),
    (220,),
    (530,),
    (),
    (),
    (),
    (400,),
    (),
    (),
    (),
    (301, 212),
    (),
    (),
    (302,),
    (310, 221),
    (),
    (),
    (222, 401, 311, 410),
    (230, 312, 402),
    (231, 320),
    (411, 232, 321, 540),
)
REST_B = (
    412,
    322,
    420,
    330,
    421,
    331,
    422,
    332,
    430,
    550,
    431,
    432,
)


def forward_kernel(
    depth,
    rows_ref,
    patch_ref,
    cols_ref,
    vec_ref,
    out_ref,
    heads_ref,
    lengths,
    states_ref,
    grad_ref,
    qkv,
    attn,
    gate,
    up,
    down,
    ow,
    od,
    o_block,
    o_streams,
    o_mix,
    o_direct,
    o_gains,
    g_qkv,
    g_attn,
    g_gate,
    g_up,
    g_down,
    sum_ref,
    small_ref,
    bytes_ref,
    norm_ref,
    proj_ref,
    head_w_ref,
    own_ref,
    maps_ref,
    step_ref,
    core_ref,
    mixed_ref,
    attn_w,
    ffn_w,
    g_buf,
    streams,
    normed,
    qkv_low,
    weights,
    mixed_heads,
    attended,
    ffn_low,
    ffn_t,
    total_ref,
    d_ffn,
    d_down,
    load_sem,
    ffn_sem,
    g_sem,
    parts,
    pair,
    near,
    column,
    far,
    parts8,
    pair8,
    near8,
    send,
    recv,
    swap_send,
    swap_recv,
    local,
):
    f32, low = jnp.float32, jnp.bfloat16
    spot = Spot(depth)
    count = 128
    wires = Wires(send, recv)
    mine = pl.multiple_of(spot.me * TILE, TILE)
    bytes_ref[pl.ds(mine, TILE)] = rows_ref[:, pl.ds(pl.multiple_of(spot.me * 256, 256), 256)]
    small_ref[spot.me] = vec_ref[...]
    proj_ref[pl.ds(mine, TILE)] = cols_ref[spot.q]
    head_w_ref[spot.z] = out_ref[...]
    greet(spot)

    def lanes_of(to):
        return rows_ref.at[:, pl.ds(pl.multiple_of(to * 256, 256), 256)]

    swap_bytes = Swap(
        spot,
        swap_send,
        swap_recv,
        lanes_of,
        lambda me: bytes_ref.at[pl.ds(pl.multiple_of(me * TILE, TILE), TILE)],
    )
    swap_bytes.start()
    steps, close = big_gather(wires, spot, ow, od, (qkv, attn, gate, up, down))
    near_proj = plane_swap(
        wires,
        spot,
        lambda q: cols_ref.at[q],
        lambda q: proj_ref.at[pl.ds(pl.multiple_of((spot.z * 8 + q) * TILE, TILE), TILE)],
    )
    small = spread_all(wires, spot, small_ref)
    next(small)
    tick = Ticker(steps, PLAN_F)
    tick()
    own_rows = []
    at = 0
    for i, ref in enumerate((qkv, attn, gate, up)):
        width = ref.shape[1]
        own_rows.append(pltpu.make_async_copy(ref, ow.at[pl.ds(mine, TILE), pl.ds(at, width)], local.at[i]))
        at += width
    deep = down.shape[0]
    own_rows.append(
        pltpu.make_async_copy(down, od.at[pl.ds(pl.multiple_of(spot.me * deep, deep), deep)], local.at[4])
    )
    for copy in own_rows:
        copy.start()
    tick()
    swap_bytes.arrive()
    got(near_proj)
    layer = proj_ref.at[pl.ds(pl.multiple_of(spot.z * 8 * TILE, 8 * TILE), 8 * TILE)]
    far_proj = [wires.copy(layer, layer, spot.above(k)) for k in range(1, depth)]

    for b in range(4):
        block = flat_dot(bytes_ref[pl.ds(b * 256, 256)], patch_ref[...]).astype(low)
        parts[pl.ds(b * 4, 4)] = block.reshape(4, 2, TILE, D)
    tick()
    total = sum_all(wires, spot, parts, pair, near, column, far, sum_ref)
    next(total)
    next(small)
    tick()
    next(total)
    tick()
    next(total)
    next(small)
    tick()
    head_w = [wires.copy(out_ref, head_w_ref.at[spot.z], spot.above(k)) for k in range(1, depth)]
    next(total)
    tick()
    run(small)
    patch_sum = sum_ref[...]
    scale = lax.rsqrt(jnp.mean(patch_sum * patch_sum, axis=1, keepdims=True) + EPSILON)
    gain = gain_row(small_ref[:, TILE + 5, 0:128])
    norm_ref[spot.q] = (patch_sum * scale * gain).astype(low)
    plane = spread_plane(wires, spot, norm_ref)
    next(plane)
    tick()
    next(plane)
    tick()
    got(far_proj)
    taps = tap_rows(spot, small_ref)
    run(plane)
    tick()

    norm = norm_ref[...].reshape(2 * count, D)
    own_ref[...] = flat_dot(norm, proj_ref[...])
    maps_ref[...] = flat_dot(norm, small_ref[:, :TILE, 0:256].reshape(D, 256))
    step_ref[...] = flat_dot(norm, small_ref[:, :TILE, 256:384].reshape(D, 128))
    dt_row, rate_row, skip_row = heads_ref[0:1], heads_ref[1:2], heads_ref[2:3]
    tick()
    got(head_w)
    gains = jnp.concatenate(
        [small_ref[spot.q + 8 * i, TILE : TILE + 16, 0:HEAD_M][6:7].astype(f32) for i in range(4)], axis=1
    )
    for x in range(2):
        at = pl.ds(x * count, count)
        slot = Slot(spot, small_ref, x, count)
        own, maps = own_ref[at], maps_ref[at]
        mix = Mixed(spot, slot, own, maps, step_ref[at], taps, dt_row, rate_row)
        outs = []
        for i in range(4):
            tick()
            inputs = mix.inputs[:, i * HEAD_M : (i + 1) * HEAD_M]
            mixing = (mix.decay(i) * mix.inner * mix.row(mix.step_t, i)).astype(low)
            skip = pick_lane(skip_row, mix.head(i))
            outs.append(flat_dot(mixing, inputs.astype(low)) + skip * inputs)
        core = jnp.concatenate(outs, axis=1)
        core_ref[at] = core
        raw = own[:, :256]
        gated = core * raw * sigmoid(raw)
        part = flat_dot((gated * gains).astype(low), head_w_ref[...].reshape(256, D))
        squares = jnp.sum(gated * gated, axis=1, keepdims=True)
        parts8[pl.ds(x * 2, 2), :, :, pl.ds(0, D)] = part.astype(low).reshape(2, 2, TILE, D)
        parts8[pl.ds(x * 2, 2), :, :, pl.ds(D, 128)] = (
            jnp.broadcast_to(squares, (count, 128)).astype(low).reshape(2, 2, TILE, 128)
        )
        tick()
    for total in sum_plane(wires, spot, parts8, pair8, near8):
        if total is None:
            tick()
    mixed_ref[...] = total

    def ready():
        for copy in own_rows:
            copy.wait()
        close([0])

    def whole():
        tick.rest(REST_F)
        close(range(1, len(CUTS_F) + 2))

    local_block(
        tick,
        ready,
        whole,
        lengths,
        states_ref,
        grad_ref,
        sum_ref,
        mixed_ref,
        small_ref,
        ow,
        od,
        o_block,
        o_streams,
        o_mix,
        o_direct,
        o_gains,
        g_qkv,
        g_attn,
        g_gate,
        g_up,
        g_down,
        attn_w,
        ffn_w,
        g_buf,
        streams,
        normed,
        qkv_low,
        weights,
        mixed_heads,
        attended,
        ffn_low,
        ffn_t,
        total_ref,
        d_ffn,
        d_down,
        load_sem,
        ffn_sem,
        g_sem,
    )
    wires.drain()
    swap_bytes.leave()


def forward_call(
    depth,
    n_dev,
    rows2,
    patch_proj,
    cols,
    vectors,
    out_proj,
    heads,
    lengths,
    byte_states,
    out_grad,
    qkv,
    attn,
    gate,
    up,
    down,
):
    f32, low = jnp.float32, jnp.bfloat16
    vmem = pl.BlockSpec(memory_space=pltpu.VMEM)
    anywhere = pl.BlockSpec(memory_space=pl.ANY)
    smem = pl.BlockSpec(memory_space=pltpu.SMEM)
    shape = jax.ShapeDtypeStruct
    plane_patches = 8 * TILE
    rows, hidden = byte_states.shape[0], down.shape[0] * n_dev
    outs = [
        shape((D, WIDE), low),
        shape((hidden, D), low),
        shape((rows, D), low),
        shape((rows, D), f32),
        shape((rows // PATCH, EXT), low),
        shape((rows // PATCH, D), f32),
        shape((8, D), f32),
        shape((D, 3 * D), low),
        shape((D, D), low),
        shape((D, hidden), low),
        shape((D, hidden), low),
        shape((hidden, D), low),
        shape((TILE, D), f32),
        shape((n_dev, SMALL_ROWS, SMALL_COLS), low),
        shape((n_dev * TILE, 256), low),
        shape((8, TILE, D), low),
        shape((n_dev * TILE, 512), low),
        shape((depth, HEAD_M, D), low),
        shape((plane_patches, 512), f32),
        shape((plane_patches, 256), f32),
        shape((plane_patches, 128), f32),
        shape((plane_patches, 256), f32),
    ]
    scratch = [
        pltpu.VMEM((TILE, EXT), f32),
        pltpu.VMEM((D, 4 * D), low),
        pltpu.VMEM((2, 3, D, D), low),
        pltpu.VMEM((3, D, D), low),
        pltpu.VMEM((rows, D), f32),
        pltpu.VMEM((rows, D), low),
        pltpu.VMEM((rows, 3 * D), low),
        pltpu.VMEM((D // 128, rows // 128, 2, 128, 128), f32),
        pltpu.VMEM((rows, D), low),
        pltpu.VMEM((rows, D), f32),
        pltpu.VMEM((rows, D), low),
        pltpu.VMEM((D, rows), low),
        pltpu.VMEM((rows, D), f32),
        pltpu.VMEM((rows, D), f32),
        pltpu.VMEM((rows, D), low),
        pltpu.SemaphoreType.DMA((1,)),
        pltpu.SemaphoreType.DMA((2, 3)),
        pltpu.SemaphoreType.DMA((3,)),
        pltpu.VMEM((16, 2, TILE, D), low),
        pltpu.VMEM((16, TILE, D), low),
        pltpu.VMEM((3, depth, TILE, D), low),
        pltpu.VMEM((depth, TILE, D), low),
        pltpu.VMEM((depth - 1, TILE, D), low),
        pltpu.VMEM((4, 2, TILE, EXT), low),
        pltpu.VMEM((4, TILE, EXT), low),
        pltpu.VMEM((3, TILE, EXT), low),
        pltpu.SemaphoreType.DMA((N_WIRES,)),
        pltpu.SemaphoreType.DMA((N_WIRES,)),
        pltpu.SemaphoreType.DMA((n_dev,)),
        pltpu.SemaphoreType.DMA((n_dev,)),
        pltpu.SemaphoreType.DMA((5,)),
    ]
    found = pl.pallas_call(
        partial(forward_kernel, depth),
        out_shape=outs,
        in_specs=[vmem] * 6 + [smem] + [vmem] * 2 + [anywhere] * 5,
        out_specs=[anywhere] * 2 + [vmem] * 5 + [anywhere] * 5 + [vmem] * 10,
        scratch_shapes=scratch,
        compiler_params=pltpu.CompilerParams(
            collective_id=0, has_side_effects=True, vmem_limit_bytes=58 * 2**20
        ),
        name="global_forward",
    )(rows2, patch_proj, cols, vectors, out_proj, heads, lengths, byte_states, out_grad, qkv, attn, gate, up, down)
    block, streams, mix, direct, gains, *rest = found[2:]
    return (block, streams, mix, direct, gains), rest[:5], rest[5], rest[6:]


def add_to(dst, sources, width):
    def one(i, carry):
        at = pl.ds(pl.multiple_of(i * STEP, STEP), STEP)
        total = sources[0](at).astype(jnp.float32)
        for source in sources[1:]:
            total = total + source(at).astype(jnp.float32)
        dst(at, total)
        return carry

    lax.fori_loop(0, width // STEP, one, 0)


def big_scatter(wires, spot, grads, bufs, outs, local):
    f32, low = jnp.float32, jnp.bfloat16
    held_w, held_d, stage_w, stage_d, near_w, near_d, last_w, last_d, ring_w, ring_d, climb_c, flat_c = bufs
    half, deep = (WIDE - FAR_B) // 2, held_d.shape[2]
    xn, yn, cn, zn = spot.flip(2)[0], spot.flip(1)[0], spot.sibling(), spot.onward()
    here, xp, yp, xy = spot.plane, spot.flip(2)[1], spot.flip(1)[1], spot.flip(3)[1]
    T = [spot.column[k % spot.depth] for k in range(1, spot.depth + 1)]
    core, fetch, near, last, ring = {}, {}, {}, {}, {}
    A, B, C = pl.ds(0, half), pl.ds(half, half), pl.ds(2 * half, FAR_B)
    AB = pl.ds(0, 2 * half)
    climb, flat = {}, []
    DA, DB = pl.ds(0, deep // 2), pl.ds(deep // 2, deep // 2)

    def load(k, side):
        fetch[k, side] = []
        for i, ref in enumerate(grads):
            dst = stage_w.at[:, :, pl.ds(*PARTS[i])] if i < 4 else stage_d
            copy = pltpu.make_async_copy(ref.at[T[k], pl.ds(2 * side, 2), spot.c], dst, local.at[k * 5 + i])
            copy.start()
            fetch[k, side].append(copy)

    def open_core(k):
        core[k] = []
        for i, ref in enumerate(grads):
            dst = held_w.at[T[k], :, :, pl.ds(*PARTS[i])] if i < 4 else held_d.at[T[k]]
            core[k].append(wires.copy(ref.at[T[k], :, 1 - spot.c], dst, cn))

    def join(k):
        if k not in core:
            return
        t = T[k]
        got(core.pop(k))
        for side in range(2):
            for copy in fetch[k, side]:
                copy.wait()
            for half_at in range(2):
                plane = 2 * side + half_at

                def put_w(at, total, plane=plane):
                    held_w[t, plane, :, at] = total.astype(low)

                add_to(
                    put_w,
                    [lambda at, p=plane: held_w[t, p, :, at], lambda at, h=half_at: stage_w[h, :, at]],
                    WIDE,
                )
                held_d[t, plane] = (held_d[t, plane].astype(f32) + stage_d[half_at].astype(f32)).astype(low)
            if side == 0:
                load(k, 1)
            elif k + 1 < spot.depth:
                load(k + 1, 0)

    parts, at = [], 0
    for i, width in enumerate(CUTS):
        end = i == len(CUTS) - 1
        width = half - at if end else width
        parts.append((at, width, end))
        at += width

    def spans(i):
        at, width, end = parts[i]
        found = [(pl.ds(at, width), pl.ds(half + at, width))]
        return found, end

    def near_sends(k, i):
        t = T[k]
        [(a, b)], end = spans(i)
        sends = []
        for x in range(2):
            src = x * 2 + (1 - spot.y)
            sends.append(wires.copy(held_w.at[t, src, :, a], near_w.at[k, x, :, a], yn))
            if end:
                sends.append(wires.copy(held_d.at[t, src, DA], near_d.at[k, x, DA], yn))
        for y in range(2):
            src = (1 - spot.x) * 2 + y
            sends.append(wires.copy(held_w.at[t, src, :, b], near_w.at[k, y, :, b], xn))
            if end:
                sends.append(wires.copy(held_d.at[t, src, DB], near_d.at[k, y, DB], xn))
        near[k, i] = sends

    def first(k, i):
        join(k)
        near_sends(k, i)

    def second(k, i):
        t = T[k]
        got(near[k, i])
        at, width, end = parts[i]
        for other in range(2):
            for plane, base in ((other * 2 + spot.y, at), (spot.x * 2 + other, half + at)):
                moved = lambda c, base=base: pl.ds(pl.multiple_of(c.start + base, STEP), STEP)

                def put(c, total, plane=plane, moved=moved):
                    held_w[t, plane, :, moved(c)] = total.astype(low)

                add_to(
                    put,
                    [
                        lambda c, p=plane, m=moved: held_w[t, p, :, m(c)],
                        lambda c, o=other, m=moved: near_w[k, o, :, m(c)],
                    ],
                    width,
                )
            if end:
                pa, pb = other * 2 + spot.y, spot.x * 2 + other
                held_d[t, pa, DA] = (held_d[t, pa, DA].astype(f32) + near_d[k, other, DA].astype(f32)).astype(low)
                held_d[t, pb, DB] = (held_d[t, pb, DB].astype(f32) + near_d[k, other, DB].astype(f32)).astype(low)
        [(a, b)], _ = spans(i)
        sends = [
            wires.copy(held_w.at[t, xp, :, a], last_w.at[k, :, a], xn),
            wires.copy(held_w.at[t, yp, :, b], last_w.at[k, :, b], yn),
        ]
        if end:
            sends.append(wires.copy(held_d.at[t, xp, DA], last_d.at[k, DA], xn))
            sends.append(wires.copy(held_d.at[t, yp, DB], last_d.at[k, DB], yn))
        last[k, i] = sends

    def finish(terms, begin, end):
        for out, (base, size) in zip(outs, PARTS):
            a, b = max(begin, base), min(end, base + size)

            def put_out(at, total, out=out, shift_by=a - base):
                out[:, pl.ds(pl.multiple_of(at.start + shift_by, STEP), STEP)] = total

            if a < b:
                moved = [
                    lambda at, f=f, a=a: f(pl.ds(pl.multiple_of(at.start + a, STEP), STEP)) for f in terms
                ]
                add_to(put_out, moved, b - a)

    def far(k):
        join(k)
        t = T[k]
        if k:
            got(climb[k - 1])
            for plane in range(4):
                base = lambda at: pl.ds(pl.multiple_of(at.start + 2 * half, STEP), STEP)

                def put_far(at, total, plane=plane):
                    held_w[t, plane, :, base(at)] = total.astype(low)

                terms = [
                    lambda at, p=plane: held_w[t, p, :, base(at)],
                    lambda at, p=plane: climb_c[k - 1, p, :, at],
                ]
                add_to(put_far, terms, FAR_B)
        if k < spot.depth - 1:
            climb[k] = [wires.copy(held_w.at[t, :, :, C], climb_c.at[k], zn)]
        else:
            for way in (1, 2, 3):
                to, plane = spot.flip(way)
                flat.append(wires.copy(held_w.at[t, plane, :, C], flat_c.at[way - 1], to))

    def far_end():
        assert flat
        got(flat)
        terms = [lambda at: held_w[T[-1], here, :, at]]
        for way in range(3):
            terms.append(
                lambda at, w=way: flat_c[w, :, pl.ds(pl.multiple_of(at.start - 2 * half, STEP), STEP)]
            )
        finish(terms, 2 * half, WIDE)

    def third(k, i):
        t = T[k]
        got(last[k, i])
        if k:
            got(ring[k - 1, i])
        at, width, end = parts[i]
        [(a, b)], _ = spans(i)
        terms = [lambda c: held_w[t, here, :, c], lambda c: last_w[k, :, c]]
        if k:
            terms.append(lambda c: ring_w[k - 1, :, c])
        if end:
            down = held_d[t, here].astype(f32) + last_d[k].astype(f32)
            if k:
                down = down + ring_d[k - 1].astype(f32)
        if k == spot.depth - 1:
            finish(terms, at, at + width)
            finish(terms, half + at, half + at + width)
            if end:
                outs[4][...] = down
            return
        for base in (at, half + at):
            moved = lambda c, base=base: pl.ds(pl.multiple_of(c.start + base, STEP), STEP)

            def put_on(c, total, moved=moved):
                held_w[t, here, :, moved(c)] = total.astype(low)

            add_to(put_on, [lambda c, f=f, m=moved: f(m(c)) for f in terms], width)
        ring[k, i] = [wires.copy(held_w.at[t, here, :, c], ring_w.at[k, :, c], zn) for c in (a, b)]
        if end:
            held_d[t, here] = down.astype(low)
            ring[k, i].append(wires.copy(held_d.at[t, here], ring_d.at[k], zn))

    load(0, 0)
    for k in range(spot.depth):
        open_core(k)
    steps = {far_step(k): partial(far, k) for k in range(spot.depth)}
    steps[far_step(spot.depth)] = far_end
    for i in range(len(CUTS)):
        for k in range(spot.depth):
            for kind, act in enumerate((first, second, third), 2):
                steps[100 * kind + 10 * k + i] = partial(act, k, i)
    return steps


class Back:
    def __init__(self, mix, own, core, ext, d_patch, gains, head_w, heads, taps, tick):
        f32, low = jnp.float32, jnp.bfloat16
        count = mix.count
        dt_row, rate_row, skip_row = heads[0:1], heads[1:2], heads[2:3]
        r = ext[:, 0:1] + ext[:, 2:3]
        along = ext[:, 1:2] + ext[:, 3:4]
        raw = own[:, :256]
        sig = sigmoid(raw)
        gated = core * raw * sig
        back = flat_dot(d_patch, head_w, ((1,), (1,)))
        self.norm = (gated * r * gains).astype(low)
        self.gain = jnp.sum(back * gated * r, axis=0, keepdims=True)
        d_gated = r * gains * back - gated * (r * r * r * along * (1.0 / DI))
        d_core = d_gated * raw * sig
        d_gate = d_gated * core * sig * (1.0 + raw * (1.0 - sig))
        lane = lanes((1, 128), 1)
        graph = jnp.zeros((count, count), f32)
        d_inputs = []
        direct = jnp.zeros((count, 128), f32)
        flow = jnp.zeros((count, 128), f32)
        d_skip = jnp.zeros((1, 128), f32)
        for i in range(4):
            tick()
            cut = slice(i * HEAD_M, (i + 1) * HEAD_M)
            inputs, grad = mix.inputs[:, cut], d_core[:, cut]
            decay, step = mix.decay(i), mix.row(mix.step_t, i)
            kept = decay * mix.inner
            skip = pick_lane(skip_row, mix.head(i))
            d_mixing = flat_dot(grad.astype(low), inputs.astype(low), ((1,), (1,)))
            d_inputs.append(
                flat_dot((kept * step).astype(low), grad.astype(low), ((0,), (0,))) + skip * grad
            )
            graph = graph + decay * step * d_mixing
            turn = kept * d_mixing
            arrive = jnp.sum(turn.T, axis=1, keepdims=True)
            leave = jnp.sum(turn * step, axis=1, keepdims=True)
            here = lane == mix.head(i)
            direct = direct + jnp.where(here, arrive, 0.0)
            flow = flow + jnp.where(here, leave - mix.col(mix.step, i) * arrive, 0.0)
            d_skip = d_skip + jnp.where(here, jnp.sum(grad * inputs, keepdims=True).reshape(1, 1), 0.0)
        tail = exact_dot(mix.upper, flow)
        mine = own_lanes(lane, mix)
        d_step = jnp.where(mine, direct + rate_row * tail, 0.0)
        d_raw = d_step * sigmoid(mix.raw)
        self.skip = d_skip
        self.rate = jnp.sum(rate_row * mix.step * jnp.where(mine, tail, 0.0), axis=0, keepdims=True)
        self.bias = jnp.sum(d_raw, axis=0, keepdims=True)
        low_graph = graph.astype(low)
        d_out_map = flat_dot(low_graph, mix.in_map)
        d_in_map = flat_dot(low_graph, mix.out_map, ((0,), (0,)))
        d_act = jnp.concatenate(d_inputs + [d_in_map, d_out_map], axis=1)
        d_conv = d_act * (mix.sig * (1.0 + mix.conv * (1.0 - mix.sig)))
        d_channels = jnp.zeros_like(d_conv)
        self.taps = [None] * CONV + [jnp.sum(d_conv, axis=0, keepdims=True)]
        for s in range(CONV):
            kept = d_conv * mix.slot.same[s]
            d_channels = d_channels + taps[CONV - 1 - s] * shift(kept, -s)
            self.taps[CONV - 1 - s] = jnp.sum(kept * shift(mix.channels, s), axis=0, keepdims=True)
        self.rows = jnp.concatenate([d_gate, d_channels, d_raw], axis=1).astype(low)


def own_lanes(lane, mix):
    mine = lane == mix.head(0)
    for i in range(1, 4):
        mine = mine | (lane == mix.head(i))
    return mine


COLS = 512 + 256 + 128


def backward_kernel(
    depth,
    mix_ref,
    direct_ref,
    streams_ref,
    sum_ref,
    gains_ref,
    small_ref,
    bytes_ref,
    norm_ref,
    proj_ref,
    head_w_ref,
    own_ref,
    maps_ref,
    step_ref,
    core_ref,
    patch_ref,
    heads_ref,
    g_qkv,
    g_attn,
    g_gate,
    g_up,
    g_down,
    o_qkv,
    o_attn,
    o_gate,
    o_up,
    o_down,
    o_patch,
    o_states,
    o_head,
    o_cols,
    o_maps,
    extra_ref,
    all_ref,
    map_send,
    map_near,
    map_sum,
    map_far,
    o_rows,
    mix_all,
    rows_all,
    head_sum,
    head_low,
    head_far,
    col_send,
    col_recv,
    col_far,
    col_sum,
    back_send,
    parts8,
    pair8,
    near8,
    held_w,
    held_d,
    stage_w,
    stage_d,
    near_w,
    near_d,
    last_w,
    last_d,
    ring_w,
    ring_d,
    climb_c,
    flat_c,
    send,
    recv,
    swap_send,
    swap_recv,
    local,
):
    f32, low = jnp.float32, jnp.bfloat16
    spot = Spot(depth)
    count = 128
    wires = Wires(send, recv)
    mix_all[spot.q] = mix_ref[...]
    greet(spot)
    plane = spread_plane(wires, spot, mix_all)
    next(plane)
    steps = big_scatter(
        wires,
        spot,
        (g_qkv, g_attn, g_gate, g_up, g_down),
        (held_w, held_d, stage_w, stage_d, near_w, near_d, last_w, last_d, ring_w, ring_d, climb_c, flat_c),
        (o_qkv, o_attn, o_gate, o_up, o_down),
        local,
    )
    tick = Ticker(steps, PLAN_B)
    tick()
    next(plane)
    tick()
    taps = tap_rows(spot, small_ref)
    heads = heads_ref[...]
    dt_row, rate_row = heads[0:1], heads[1:2]
    gains = jnp.concatenate(
        [small_ref[spot.q + 8 * i, TILE : TILE + 16, 0:HEAD_M][6:7].astype(f32) for i in range(4)], axis=1
    )
    gain = gain_row(small_ref[:, TILE + 5, 0:128])
    run(plane)
    tick()
    sums = None
    for x in range(2):
        at = pl.ds(x * count, count)
        slot = Slot(spot, small_ref, x, count)
        mix = Mixed(spot, slot, own_ref[at], maps_ref[at], step_ref[at], taps, dt_row, rate_row)
        d_patch = mix_all[pl.ds(x * 4, 4), :, pl.ds(0, D)].reshape(count, D)
        ext = mix_all[pl.ds(x * 4, 4), :, pl.ds(D, 128)].reshape(count, 128).astype(f32)
        back = Back(
            mix, own_ref[at], core_ref[at], ext, d_patch, gains, head_w_ref[...].reshape(256, D), heads, taps, tick
        )
        rows_all[at] = back.rows
        tick()
        head = flat_dot(back.norm, d_patch, ((0,), (0,)))
        head = head.reshape(TILE, PATCH, D)
        head_sum[...] = head if x == 0 else head_sum[...] + head
        new = [*back.taps, back.gain, back.bias, back.rate, back.skip]
        sums = new if sums is None else [a + b for a, b in zip(sums, new)]
        grad = flat_dot(back.rows[:, :512], proj_ref[...], ((1,), (1,)))
        grad = grad + flat_dot(
            back.rows[:, 512:], small_ref[:, :TILE, :].reshape(D, SMALL_COLS), ((1,), (1,))
        )
        parts8[pl.ds(x * 2, 2)] = grad.astype(low).reshape(2, 2, TILE, D)
        tick()
    total8 = sum_plane(wires, spot, parts8, pair8, near8)
    next(total8)
    tick()
    head_low[...] = head_sum[...].reshape(256, D).astype(low).reshape(depth, HEAD_M, D)
    fetch = pltpu.make_async_copy(streams_ref, head_sum, local.at[5 * depth])
    fetch.start()
    next(total8)
    tick()
    norm = norm_ref[...].reshape(2 * count, D)
    rows = rows_all[...]
    for b in range(4):
        block = flat_dot(norm[:, b * 256 : (b + 1) * 256], rows, ((0,), (0,)))
        block = block.astype(low).reshape(8, TILE, COLS)
        col_send[pl.ds(b * 8, 8)] = block[:, :, :512]
        map_send[b] = block[:, :, 512:]
    tick()
    grad_norm = next(total8)
    tick()
    patch_sum = sum_ref[...]
    scale = lax.rsqrt(jnp.mean(patch_sum * patch_sum, axis=1, keepdims=True) + EPSILON)
    along = jnp.mean(grad_norm * gain * patch_sum, axis=1, keepdims=True)
    d_sum = direct_ref[...] + scale * gain * grad_norm - patch_sum * (scale * scale * scale * along)
    gain_sum = jnp.sum(grad_norm * patch_sum * scale, axis=0, keepdims=True)
    lines = sums[: CONV + 1]
    for row in (jnp.concatenate([*sums[CONV + 1 :], jnp.zeros((1, 384), f32)], axis=1), gains_ref[0:1], gains_ref[1:2], gain_sum):
        lines += [row[:, :512], row[:, 512:]]
    lines += [jnp.zeros((16 - len(lines), 512), f32)]
    all_ref[spot.me] = d_sum.astype(low)
    extra_ref[spot.me] = jnp.concatenate(lines, axis=0).astype(low)
    spread = spread_all(wires, spot, all_ref)
    next(spread)
    col_ring = [
        wires.copy(col_send.at[pl.ds(((spot.z + k) % depth) * 8, 8)], col_far.at[k - 1], spot.above(k))
        for k in range(1, depth)
    ]
    tick()
    next(spread)
    map_plane = plane_swap(wires, spot, lambda q: map_send.at[:, q], lambda q: map_near.at[q])
    tick()
    next(spread)
    tick()
    run(spread)
    tick()
    d_all = all_ref[...].reshape(-1, D)
    for b in range(4):
        back_send[pl.ds(b * 8, 8)] = (
            flat_dot(d_all[b * 256 : (b + 1) * 256], patch_ref[...], ((1,), (1,))).astype(low).reshape(8, TILE, 256)
        )
    swap_rows = Swap(
        spot,
        swap_send,
        swap_recv,
        lambda to: back_send.at[to],
        lambda me: o_rows.at[:, pl.ds(pl.multiple_of(me * 256, 256), 256)],
    )
    swap_rows.start()
    extra = spread_all(wires, spot, extra_ref)
    next(extra)
    tick()
    o_rows[:, pl.ds(pl.multiple_of(spot.me * 256, 256), 256)] = back_send[spot.me]
    o_patch[...] = flat_dot(bytes_ref[...], d_all, ((0,), (0,)))
    got(col_ring)
    for q in range(8):
        total = col_send[spot.z * 8 + q].astype(f32)
        for k in range(depth - 1):
            total = total + col_far[k, q].astype(f32)
        col_sum[q] = total.astype(low)
    col_plane = plane_swap(wires, spot, lambda q: col_sum.at[q], lambda q: col_recv.at[q])
    col_recv[spot.q] = col_sum[spot.q]
    got(map_plane)
    map_near[spot.q] = map_send[:, spot.q]
    for t in range(depth):
        total = map_near[0, t].astype(f32)
        for q in range(1, 8):
            total = total + map_near[q, t].astype(f32)
        map_sum[t] = total.astype(low)
    map_ring = [
        wires.copy(map_sum.at[(spot.z + k) % depth], map_far.at[k - 1], spot.above(k)) for k in range(1, depth)
    ]
    head_ring = [
        wires.copy(head_low.at[(spot.z + k) % depth], head_far.at[k - 1], spot.above(k)) for k in range(1, depth)
    ]
    next(extra)
    tick()
    next(extra)
    tick()
    tick()
    tick.rest(REST_B)
    got(head_ring)
    total = head_low[spot.z].astype(f32)
    for k in range(depth - 1):
        total = total + head_far[k].astype(f32)
    o_head[...] = total
    got(col_plane)
    for q in range(8):
        o_cols[q] = col_recv[q].astype(f32)
    got(map_ring)
    total = map_sum[spot.z].astype(f32)
    for k in range(depth - 1):
        total = total + map_far[k].astype(f32)
    o_maps[...] = total
    run(extra)
    swap_rows.arrive()
    fetch.wait()
    for j in range(PATCH):
        o_states[:, j] = head_sum[:, j] + o_rows[:, j * D : (j + 1) * D].astype(f32)
    wires.drain()
    swap_rows.leave()


def backward_call(depth, n_dev, mix, direct, streams, patch_sum, gains, saved, patch_proj, heads, grads):
    f32, low = jnp.float32, jnp.bfloat16
    vmem = pl.BlockSpec(memory_space=pltpu.VMEM)
    anywhere = pl.BlockSpec(memory_space=pl.ANY)
    shape = jax.ShapeDtypeStruct
    deep = grads[4].shape[0] // n_dev
    cut = [g.reshape(depth, 4, 2, g.shape[0] // n_dev, g.shape[1]) for g in grads]
    outs = [shape((TILE, width), f32) for _, width in PARTS] + [
        shape((deep, D), f32),
        shape((256, D), f32),
        shape((TILE, PATCH, D), f32),
        shape((HEAD_M, D), f32),
        shape((8, TILE, 512), f32),
        shape((TILE, COLS - 512), f32),
        shape((n_dev, 16, 512), low),
    ]
    scratch = [
        pltpu.VMEM((n_dev, TILE, D), low),
        pltpu.VMEM((depth, 8, TILE, COLS - 512), low),
        pltpu.VMEM((8, depth, TILE, COLS - 512), low),
        pltpu.VMEM((depth, TILE, COLS - 512), low),
        pltpu.VMEM((depth - 1, TILE, COLS - 512), low),
        pltpu.VMEM((TILE, PATCH * D), low),
        pltpu.VMEM((8, TILE, EXT), low),
        pltpu.VMEM((8 * TILE, COLS), low),
        pltpu.VMEM((TILE, PATCH, D), f32),
        pltpu.VMEM((depth, HEAD_M, D), low),
        pltpu.VMEM((depth - 1, HEAD_M, D), low),
        pltpu.VMEM((n_dev, TILE, 512), low),
        pltpu.VMEM((8, TILE, 512), low),
        pltpu.VMEM((depth - 1, 8, TILE, 512), low),
        pltpu.VMEM((8, TILE, 512), low),
        pltpu.VMEM((n_dev, TILE, 256), low),
        pltpu.VMEM((4, 2, TILE, D), low),
        pltpu.VMEM((4, TILE, D), low),
        pltpu.VMEM((3, TILE, D), low),
        pltpu.VMEM((depth, 4, TILE, WIDE), low),
        pltpu.VMEM((depth, 4, deep, D), low),
        pltpu.VMEM((2, TILE, WIDE), low),
        pltpu.VMEM((2, deep, D), low),
        pltpu.VMEM((depth, 2, TILE, WIDE - FAR_B), low),
        pltpu.VMEM((depth, 2, deep, D), low),
        pltpu.VMEM((depth, TILE, WIDE - FAR_B), low),
        pltpu.VMEM((depth, deep, D), low),
        pltpu.VMEM((depth - 1, TILE, WIDE - FAR_B), low),
        pltpu.VMEM((depth - 1, deep, D), low),
        pltpu.VMEM((depth - 1, 4, TILE, FAR_B), low),
        pltpu.VMEM((3, TILE, FAR_B), low),
        pltpu.SemaphoreType.DMA((N_WIRES,)),
        pltpu.SemaphoreType.DMA((N_WIRES,)),
        pltpu.SemaphoreType.DMA((n_dev,)),
        pltpu.SemaphoreType.DMA((n_dev,)),
        pltpu.SemaphoreType.DMA((5 * depth + 1,)),
    ]
    return pl.pallas_call(
        partial(backward_kernel, depth),
        out_shape=outs,
        in_specs=[vmem] * 2 + [anywhere] + [vmem] * 13 + [anywhere] * 5,
        out_specs=[vmem] * 11,
        scratch_shapes=scratch,
        compiler_params=pltpu.CompilerParams(
            collective_id=1, has_side_effects=True, vmem_limit_bytes=61 * 2**20
        ),
        name="global_backward",
    )(mix, direct, streams.reshape(TILE, PATCH, D), patch_sum, gains, *saved, patch_proj, heads, *cut)


BC = 2 * STATE


def fast_body(
    depth_fsdp,
    byte_states,
    doc_lengths,
    out_grad,
    patch_proj,
    global_gain,
    in_proj,
    conv_weight,
    conv_bias,
    dt_bias,
    a_log,
    skip_weight,
    mixer_gain,
    out_proj,
    attn_gain,
    qkv_proj,
    attn_out,
    ffn_gain,
    gate_proj,
    up_proj,
    down_proj,
):
    f32, low = jnp.float32, jnp.bfloat16
    depth, n_dev = depth_fsdp[0] // 2, depth_fsdp[0] * depth_fsdp[1]
    me = lax.axis_index("dp") * depth_fsdp[1] + lax.axis_index("fsdp")
    rows = byte_states.shape[0]
    patches = rows // PATCH

    shard_rows = in_proj.shape[0]
    maps_and_steps = jnp.pad(in_proj[:, 2 * DI :], ((0, 0), (0, SMALL_COLS - BC - MHEADS)))
    shorts = (conv_bias, global_gain, mixer_gain, attn_gain, ffn_gain, doc_lengths.reshape(-1).astype(low))
    flat, size = jnp.zeros((12 * SMALL_COLS,), low), 12 * SMALL_COLS
    for k, line in enumerate(shorts):
        begin = k * SMALL_COLS
        flat = flat + jnp.pad(line, (begin, size - begin - line.shape[0]))
    taps = jnp.pad(conv_weight.T, ((0, 0), (0, SMALL_COLS - conv_weight.shape[0])))
    vectors = jnp.concatenate([maps_and_steps, taps, flat.reshape(12, SMALL_COLS)])
    by_place = lambda cols: cols.reshape(shard_rows, 4, 8, HEAD_M).transpose(2, 0, 1, 3).reshape(8, shard_rows, 256)
    cols = jnp.concatenate([by_place(in_proj[:, :DI]), by_place(in_proj[:, DI : 2 * DI])], axis=2)
    heads_in = jnp.pad(jnp.stack([dt_bias, -jnp.exp(a_log), skip_weight]), ((0, 5), (0, 128 - MHEADS)))
    rows2 = byte_states.reshape(patches, PATCH * D)
    (block_out, grad_streams, mix, direct, gains), grads, patch_sum, saved = forward_call(
        depth,
        n_dev,
        rows2,
        patch_proj,
        cols,
        vectors,
        out_proj,
        heads_in,
        doc_lengths,
        byte_states,
        out_grad,
        qkv_proj,
        attn_out,
        gate_proj,
        up_proj,
        down_proj,
    )
    (g_qkv, g_attn, g_gate, g_up, g_down, g_patch, grad_states, g_out, g_cols, g_maps, everyone) = backward_call(
        depth,
        n_dev,
        mix,
        direct,
        grad_streams,
        patch_sum,
        gains,
        saved,
        patch_proj,
        heads_in,
        grads,
    )

    lines = everyone[:, : CONV + 9].astype(f32)
    by_plane = jnp.sum(lines.reshape(depth, 8, CONV + 9, 512), axis=0)
    sums = jnp.sum(by_plane, axis=0)
    own_part = lambda row: lax.dynamic_slice_in_dim(row, me * (D // n_dev), D // n_dev, 0)
    pair = lambda k: sums[CONV + 1 + 2 * k : CONV + 3 + 2 * k].reshape(-1)
    by_head = lambda rows_of: rows_of.reshape(8, -1, 4, HEAD_M).transpose(1, 2, 0, 3).reshape(-1, DI)
    heads_of = by_head(by_plane[:, : CONV + 2, :256])
    taps = jnp.concatenate([heads_of[: CONV + 1], sums[: CONV + 1, 256:512]], axis=1)
    share = CONV_CH // n_dev
    taps = lax.dynamic_slice_in_dim(taps, me * share, share, 1)
    gain_m_sum = lax.dynamic_slice_in_dim(heads_of[CONV + 1], me * HEAD_M, HEAD_M, 0)
    head_line = pair(0)
    back_cols = lambda cols: cols.reshape(8, shard_rows, 4, HEAD_M).transpose(1, 2, 0, 3).reshape(shard_rows, DI)
    grad_in_proj = jnp.concatenate(
        [back_cols(g_cols[..., :256]), back_cols(g_cols[..., 256:]), g_maps[:, : BC + MHEADS]], axis=1
    )
    return (
        block_out,
        grad_states.reshape(rows, D),
        g_patch,
        own_part(pair(3)),
        grad_in_proj,
        taps[:CONV].T,
        taps[CONV],
        head_line[256 : 256 + MHEADS],
        head_line[384 : 384 + MHEADS],
        head_line[512 : 512 + MHEADS],
        gain_m_sum,
        g_out,
        own_part(pair(1)),
        g_qkv,
        g_attn,
        own_part(pair(2)),
        g_gate,
        g_up,
        g_down,
    )


def solution(mesh):
    in_specs = (
        P(("dp", "fsdp"), None),
        P("dp", None),
        P(("dp", "fsdp"), None),
        P(("dp", "fsdp"), None),
        P(("dp", "fsdp")),
        P(("dp", "fsdp"), None),
        P(("dp", "fsdp"), None),
        P(("dp", "fsdp")),
        P(),
        P(),
        P(),
        P(("dp", "fsdp")),
        P(("dp", "fsdp"), None),
        P(("dp", "fsdp")),
        P(("dp", "fsdp"), None),
        P(("dp", "fsdp"), None),
        P(("dp", "fsdp")),
        P(("dp", "fsdp"), None),
        P(("dp", "fsdp"), None),
        P(("dp", "fsdp"), None),
    )
    out_specs = (
        P(("dp", "fsdp"), None),
        P(("dp", "fsdp"), None),
        P(("dp", "fsdp"), None),
        P(("dp", "fsdp")),
        P(("dp", "fsdp"), None),
        P(("dp", "fsdp"), None),
        P(("dp", "fsdp")),
        P(),
        P(),
        P(),
        P(("dp", "fsdp")),
        P(("dp", "fsdp"), None),
        P(("dp", "fsdp")),
        P(("dp", "fsdp"), None),
        P(("dp", "fsdp"), None),
        P(("dp", "fsdp")),
        P(("dp", "fsdp"), None),
        P(("dp", "fsdp"), None),
        P(("dp", "fsdp"), None),
    )
    dp, fsdp = mesh.shape["dp"], mesh.shape["fsdp"]
    fast = dp * fsdp == MHEADS and fsdp == 4
    chosen = partial(fast_body, (dp, fsdp)) if fast else body
    return jax.shard_map(chosen, mesh=mesh, in_specs=in_specs, out_specs=out_specs, check_vma=False)
```

```python
from functools import partial

import jax
import jax.numpy as jnp
from jax import lax
from jax.experimental import pallas as pl
from jax.experimental.pallas import tpu as pltpu
from jax.sharding import PartitionSpec as P

D = 1024
HEAD = 64
HEAD_M = 64
STATE = 128
CONV = 4
PATCH = 8
DI = 2048
MHEADS = 32
CONV_CH = 2304


EPSILON = 1e-05
HIGHEST = lax.Precision.HIGHEST


def shifted(block, axis, distance):
    devices = range(lax.axis_size(axis))
    route = [(i - distance, i) for i in devices if i - distance in devices]
    return lax.ppermute(block, axis, route)


def prefix(value, axis, combine, identity):
    devices, place = (lax.axis_size(axis), lax.axis_index(axis))
    everything = jax.tree.map(
        lambda part, kind: lax.all_gather(part.astype(kind), axis),
        value,
        (jnp.bfloat16, jnp.bfloat16),
    )
    start = jax.tree.map(
        lambda part, zero: jnp.broadcast_to(jnp.asarray(zero, part.dtype), part.shape),
        value,
        identity,
    )

    def prefix_step(k, before):
        reached = k < place
        new = combine(
            before, jax.tree.map(lambda part, own: part[k].astype(own.dtype), everything, value)
        )
        return jax.tree.map(lambda a, b: jnp.where(reached, a, b), new, before)

    return lax.fori_loop(0, devices, prefix_step, start)


def carried_in(value, axis, combine, identity):
    devices, place = (lax.axis_size(axis), lax.axis_index(axis))
    everything = jax.tree.map(
        lambda part, kind: lax.all_gather(part.astype(kind), axis),
        value,
        jax.tree.map(lambda a: jnp.bfloat16 if a.dtype == jnp.float32 else a.dtype, value),
    )
    start = jax.tree.map(
        lambda part, zero: jnp.broadcast_to(jnp.asarray(zero, part.dtype), part.shape),
        value,
        identity,
    )

    def carried_step(k, before):
        at = devices - 1 - k
        reached = at > place
        new = combine(
            before, jax.tree.map(lambda part, own: part[at].astype(own.dtype), everything, value)
        )
        return jax.tree.map(lambda a, b: jnp.where(reached, a, b), new, before)

    return lax.fori_loop(0, devices, carried_step, start)


def product(left, right):
    return jnp.dot(left, right, preferred_element_type=jnp.float32)


def weight_grad(left, right):
    return lax.dot_general(
        left, right, (((0,), (0,)), ((), ())), preferred_element_type=jnp.float32
    )


def input_grad(grad_rows, weight):
    return lax.dot_general(
        grad_rows, weight, (((1,), (1,)), ((), ())), preferred_element_type=jnp.float32
    )


def rms_scale(value, gain):
    return value * lax.rsqrt(jnp.mean(value * value, axis=-1, keepdims=True) + EPSILON) * gain


def gated_norm(core_out, gate_raw, gain):
    count = core_out.shape[0]
    return rms_scale(core_out.reshape(count, DI) * jax.nn.silu(gate_raw), gain)


def patch_docs(doc_lengths, start, count):
    places = start + jnp.arange(count, dtype=jnp.int32)
    first_end = doc_lengths[0, 0]
    second_end = first_end + doc_lengths[0, 1]
    numbers = (places >= first_end).astype(jnp.int32) + (places >= second_end).astype(jnp.int32)
    return jnp.where(places >= 0, numbers, -1)


def chain(earlier, later):
    return (earlier[0] * later[0], later[1] + later[0][:, None, None] * earlier[1])


def mixer_core(
    channels,
    rim,
    step_raw,
    state_in,
    conv_weight,
    conv_bias,
    dt_bias,
    a_log,
    skip_weight,
    docs,
    rim_docs,
    prev_doc,
):
    count = channels.shape[0]
    padded = jnp.concatenate([rim, channels], axis=0)
    padded_docs = jnp.concatenate([rim_docs, docs])
    total = conv_bias[None, :]
    for shift_k in range(CONV):
        same_doc = (padded_docs[shift_k : shift_k + count] == docs).astype(jnp.float32)
        total = (
            total
            + padded[shift_k : shift_k + count]
            * conv_weight[:, shift_k][None, :]
            * same_doc[:, None]
        )
    activated = jax.nn.silu(total)
    inputs = activated[:, :DI].reshape(count, MHEADS, HEAD_M)
    in_map = activated[:, DI : DI + STATE]
    out_map = activated[:, DI + STATE :]
    step_size = jax.nn.softplus(step_raw + dt_bias[None, :])
    rate = -jnp.exp(a_log)
    lower = jnp.tril(jnp.ones((count, count), jnp.float32))
    cumulative = jnp.dot(lower, step_size * rate[None, :], precision=HIGHEST)
    places = jnp.arange(count, dtype=jnp.int32)
    keep = ((places[:, None] >= places[None, :]) & (docs[:, None] == docs[None, :]))[:, :, None]
    spread = cumulative[:, None, :] - cumulative[None, :, :]
    decay_table = jnp.where(keep, jnp.exp(jnp.where(keep, spread, 0.0)), 0.0)
    inner = jnp.dot(out_map, in_map.T, precision=HIGHEST, preferred_element_type=jnp.float32)
    mixing = decay_table * inner[:, :, None] * step_size[None, :, :]
    outputs = jnp.einsum("tsh,shp->thp", mixing, inputs, precision=HIGHEST)
    carry_in = jnp.where((docs == prev_doc)[:, None], jnp.exp(cumulative), 0.0)
    outputs = outputs + carry_in[:, :, None] * jnp.einsum(
        "tn,hpn->thp", out_map, state_in, precision=HIGHEST
    )
    outputs = outputs + skip_weight[None, :, None] * inputs
    last_doc = docs[count - 1]
    tail_keep = (docs == last_doc)[:, None]
    tail_gap = cumulative[count - 1][None, :] - cumulative
    tail_weight = (
        jnp.where(tail_keep, jnp.exp(jnp.where(tail_keep, tail_gap, 0.0)), 0.0) * step_size
    )
    decay_total = jnp.where(prev_doc == last_doc, jnp.exp(cumulative[count - 1]), 0.0)
    state_out = jnp.einsum("sh,shp,sn->hpn", tail_weight, inputs, in_map, precision=HIGHEST)
    state_out = state_out + decay_total[:, None, None] * state_in
    return ((outputs, state_out), (decay_total, carry_in, out_map))


def attend(qkv_low, patches):
    heads = qkv_low.reshape(patches, PATCH, 3, -1, HEAD)
    queries = heads[:, :, 0]
    key_rows = heads[:, :, 1]
    value_rows = heads[:, :, 2]
    scores = jnp.einsum(
        "pihd,pjhd->phij", queries, key_rows, preferred_element_type=jnp.float32
    ) * HEAD ** (-0.5)
    places = jnp.arange(PATCH)
    causal = places[:, None] >= places[None, :]
    scores = jnp.where(causal, scores, -1e30)
    attn_weights = jax.nn.softmax(scores, axis=-1)
    attn_low = attn_weights.astype(jnp.bfloat16)
    mixed = jnp.einsum("phij,pjhd->pihd", attn_low, value_rows, preferred_element_type=jnp.float32)
    mixed = mixed.astype(jnp.bfloat16).reshape(patches * PATCH, -1)
    return ((queries, key_rows, value_rows, attn_weights, attn_low), mixed)


def attend_back(grad_mixed_low, pieces):
    queries, key_rows, value_rows, attn_weights, attn_low = pieces
    patches = queries.shape[0]
    grad_mixed = grad_mixed_low.reshape(patches, PATCH, -1, HEAD)
    grad_values = jnp.einsum(
        "phij,pihd->pjhd", attn_low, grad_mixed, preferred_element_type=jnp.float32
    )
    grad_weights = jnp.einsum(
        "pihd,pjhd->phij", grad_mixed, value_rows, preferred_element_type=jnp.float32
    )
    grad_scores = attn_weights * (
        grad_weights - jnp.sum(attn_weights * grad_weights, axis=-1, keepdims=True)
    )
    scores_low = grad_scores.astype(jnp.bfloat16)
    scale = HEAD ** (-0.5)
    grad_queries = (
        jnp.einsum("phij,pjhd->pihd", scores_low, key_rows, preferred_element_type=jnp.float32)
        * scale
    )
    grad_keys = (
        jnp.einsum("phij,pihd->pjhd", scores_low, queries, preferred_element_type=jnp.float32)
        * scale
    )
    stacked = jnp.stack([grad_queries, grad_keys, grad_values], axis=2).reshape(patches * PATCH, -1)
    return stacked.astype(jnp.bfloat16)


def local_forward(byte_states, mixed_patch, local_set, live):
    attn_gain, qkv_proj, attn_out, ffn_gain, gate_proj, up_proj, down_proj = local_set
    rows = byte_states.shape[0]
    streams = byte_states.astype(jnp.float32) + jnp.repeat(mixed_patch, PATCH, axis=0)
    normed_low = rms_scale(streams, attn_gain.astype(jnp.float32)).astype(jnp.bfloat16)
    qkv_low = product(normed_low, qkv_proj).astype(jnp.bfloat16)
    pieces, mixed_heads = attend(qkv_low, rows // PATCH)
    attended = streams + product(mixed_heads, attn_out)
    ffn_low = rms_scale(attended, ffn_gain.astype(jnp.float32)).astype(jnp.bfloat16)
    gate = product(ffn_low, gate_proj)
    upward = product(ffn_low, up_proj)
    hidden_low = (jax.nn.silu(gate) * upward).astype(jnp.bfloat16)
    block = live * (attended + product(hidden_low, down_proj))
    cache = (streams, normed_low, pieces, mixed_heads, attended, ffn_low, gate, upward, hidden_low)
    return (block, cache)


def local_backward(grad_block, cache, local_set):
    attn_gain, qkv_proj, attn_out, ffn_gain, gate_proj, up_proj, down_proj = local_set
    streams, normed_low, pieces, mixed_heads, attended, ffn_low, gate, upward, hidden_low = cache
    down_low = grad_block.astype(jnp.bfloat16)
    grad_down = weight_grad(hidden_low, down_low)
    grad_hidden = input_grad(down_low, down_proj)
    sigma = jax.nn.sigmoid(gate)
    grad_gate_low = (grad_hidden * upward * sigma * (1.0 + gate * (1.0 - sigma))).astype(
        jnp.bfloat16
    )
    grad_up_low = (grad_hidden * gate * sigma).astype(jnp.bfloat16)
    grad_gate = weight_grad(ffn_low, grad_gate_low)
    grad_up = weight_grad(ffn_low, grad_up_low)
    grad_ffn_in = input_grad(grad_gate_low, gate_proj) + input_grad(grad_up_low, up_proj)
    _, norm_back = jax.vjp(rms_scale, attended, ffn_gain.astype(jnp.float32))
    grad_attended_norm, grad_ffn_gain = norm_back(grad_ffn_in)
    grad_attended = grad_block + grad_attended_norm
    attn_grad_low = grad_attended.astype(jnp.bfloat16)
    grad_attn_out = weight_grad(mixed_heads, attn_grad_low)
    grad_mixed_low = input_grad(attn_grad_low, attn_out).astype(jnp.bfloat16)
    grad_qkv_low = attend_back(grad_mixed_low, pieces)
    grad_qkv = weight_grad(normed_low, grad_qkv_low)
    grad_normed = input_grad(grad_qkv_low, qkv_proj)
    _, norm_back = jax.vjp(rms_scale, streams, attn_gain.astype(jnp.float32))
    grad_streams_norm, grad_attn_gain = norm_back(grad_normed)
    grad_streams = grad_attended + grad_streams_norm
    return (
        grad_streams,
        (grad_qkv, grad_attn_out, grad_gate, grad_up, grad_down, grad_attn_gain, grad_ffn_gain),
    )


def body(
    byte_states,
    doc_lengths,
    out_grad,
    patch_proj,
    global_gain,
    in_proj,
    conv_weight,
    conv_bias,
    dt_bias,
    a_log,
    skip_weight,
    mixer_gain,
    out_proj,
    attn_gain,
    qkv_proj,
    attn_out,
    ffn_gain,
    gate_proj,
    up_proj,
    down_proj,
):
    rows = byte_states.shape[0]
    patches = rows // PATCH
    share = lax.axis_index("fsdp")
    start = share * patches
    docs = patch_docs(doc_lengths, start, patches)
    rim_docs = patch_docs(doc_lengths, start - (CONV - 1), CONV - 1)
    prev_doc = patch_docs(doc_lengths, start - 1, 1)[0]
    live = jnp.repeat((docs < 2).astype(jnp.float32), PATCH)[:, None]
    all_set = (
        lax.all_gather(patch_proj, ("dp", "fsdp"), axis=0, tiled=True),
        lax.all_gather(global_gain, ("dp", "fsdp"), axis=0, tiled=True),
        lax.all_gather(in_proj, ("dp", "fsdp"), axis=0, tiled=True),
        lax.all_gather(conv_weight, ("dp", "fsdp"), axis=0, tiled=True),
        lax.all_gather(conv_bias, ("dp", "fsdp"), axis=0, tiled=True),
        lax.all_gather(mixer_gain, ("dp", "fsdp"), axis=0, tiled=True),
        lax.all_gather(out_proj, ("dp", "fsdp"), axis=0, tiled=True),
        lax.all_gather(attn_gain, ("dp", "fsdp"), axis=0, tiled=True),
        lax.all_gather(qkv_proj, ("dp", "fsdp"), axis=0, tiled=True),
        lax.all_gather(attn_out, ("dp", "fsdp"), axis=0, tiled=True),
        lax.all_gather(ffn_gain, ("dp", "fsdp"), axis=0, tiled=True),
        lax.all_gather(gate_proj, ("dp", "fsdp"), axis=0, tiled=True),
        lax.all_gather(up_proj, ("dp", "fsdp"), axis=0, tiled=True),
        lax.all_gather(down_proj, ("dp", "fsdp"), axis=0, tiled=True),
    )
    global_set = all_set[:7]
    local_set = all_set[7:]
    patch_full, gain_g_full, in_full, conv_w_full, conv_b_full, gain_m_full, out_full = global_set
    patch_rows = byte_states.reshape(patches, PATCH * D)
    patch_sum = product(patch_rows, patch_full)
    gain_g = gain_g_full.astype(jnp.float32)
    global_low = rms_scale(patch_sum, gain_g).astype(jnp.bfloat16)
    projected = product(global_low, in_full)
    gate_raw = projected[:, :DI]
    channels = projected[:, DI : DI + CONV_CH]
    step_raw = projected[:, DI + CONV_CH :]
    rim = shifted(channels[patches - (CONV - 1) :], "fsdp", 1)
    core = partial(mixer_core, docs=docs, rim_docs=rim_docs, prev_doc=prev_doc)
    conv_w = conv_w_full.astype(jnp.float32)
    conv_b = conv_b_full.astype(jnp.float32)
    empty_state = jnp.zeros((MHEADS, HEAD_M, STATE), jnp.float32)
    (partial_out, local_state), aux = core(
        channels, rim, step_raw, empty_state, conv_w, conv_b, dt_bias, a_log, skip_weight
    )
    decay_total, carry_in, out_map = aux
    identity = (jnp.ones((MHEADS,), jnp.float32), jnp.zeros((MHEADS, HEAD_M, STATE), jnp.float32))
    arrived = prefix((decay_total, local_state), "fsdp", chain, identity)
    state_in = arrived[1]
    mixer_out = partial_out + carry_in[:, :, None] * jnp.einsum(
        "tn,hpn->thp", out_map, state_in, precision=HIGHEST
    )
    gain_m = gain_m_full.astype(jnp.float32)
    mixer_low = gated_norm(mixer_out, gate_raw, gain_m).astype(jnp.bfloat16)
    mixed_patch = patch_sum + product(mixer_low, out_full)
    block, cache = local_forward(byte_states, mixed_patch, local_set, live)
    block_out = block.astype(jnp.bfloat16)
    back_set = (
        lax.all_gather(patch_proj, ("dp", "fsdp"), axis=0, tiled=True),
        lax.all_gather(global_gain, ("dp", "fsdp"), axis=0, tiled=True),
        lax.all_gather(in_proj, ("dp", "fsdp"), axis=0, tiled=True),
        lax.all_gather(conv_weight, ("dp", "fsdp"), axis=0, tiled=True),
        lax.all_gather(conv_bias, ("dp", "fsdp"), axis=0, tiled=True),
        lax.all_gather(mixer_gain, ("dp", "fsdp"), axis=0, tiled=True),
        lax.all_gather(out_proj, ("dp", "fsdp"), axis=0, tiled=True),
        lax.all_gather(attn_gain, ("dp", "fsdp"), axis=0, tiled=True),
        lax.all_gather(qkv_proj, ("dp", "fsdp"), axis=0, tiled=True),
        lax.all_gather(attn_out, ("dp", "fsdp"), axis=0, tiled=True),
        lax.all_gather(ffn_gain, ("dp", "fsdp"), axis=0, tiled=True),
        lax.all_gather(gate_proj, ("dp", "fsdp"), axis=0, tiled=True),
        lax.all_gather(up_proj, ("dp", "fsdp"), axis=0, tiled=True),
        lax.all_gather(down_proj, ("dp", "fsdp"), axis=0, tiled=True),
    )
    global_back = back_set[:7]
    local_back = back_set[7:]
    _, cache = local_forward(byte_states, mixed_patch, local_back, live)
    patch_back, _, in_back, conv_w_back, conv_b_back, _, out_back = global_back
    grad_block = live * out_grad.astype(jnp.float32)
    grad_streams, local_grads = local_backward(grad_block, cache, local_back)
    reduced_local = (
        lax.psum_scatter(local_grads[0], ("dp", "fsdp"), scatter_dimension=0, tiled=True),
        lax.psum_scatter(local_grads[1], ("dp", "fsdp"), scatter_dimension=0, tiled=True),
        lax.psum_scatter(local_grads[2], ("dp", "fsdp"), scatter_dimension=0, tiled=True),
        lax.psum_scatter(local_grads[3], ("dp", "fsdp"), scatter_dimension=0, tiled=True),
        lax.psum_scatter(local_grads[4], ("dp", "fsdp"), scatter_dimension=0, tiled=True),
        lax.psum_scatter(local_grads[5], ("dp", "fsdp"), scatter_dimension=0, tiled=True),
        lax.psum_scatter(local_grads[6], ("dp", "fsdp"), scatter_dimension=0, tiled=True),
    )
    grad_patch_mix = grad_streams.reshape(patches, PATCH, D).sum(axis=1)
    mix_low = grad_patch_mix.astype(jnp.bfloat16)
    grad_out_proj = weight_grad(mixer_low, mix_low)
    grad_mixer_low = input_grad(mix_low, out_back)
    _, norm_back = jax.vjp(gated_norm, mixer_out, gate_raw, gain_m)
    grad_core, grad_gate_raw, grad_mixer_gain = norm_back(grad_mixer_low)
    state_part = jnp.einsum("th,thp,tn->hpn", carry_in, grad_core, out_map, precision=HIGHEST)
    returned = carried_in((decay_total, state_part), "fsdp", chain, identity)
    _, core_back, _ = jax.vjp(
        core,
        channels,
        rim,
        step_raw,
        state_in,
        conv_w_back.astype(jnp.float32),
        conv_b_back.astype(jnp.float32),
        dt_bias,
        a_log,
        skip_weight,
        has_aux=True,
    )
    core_grads = core_back((grad_core, returned[1]))
    (
        grad_channels,
        grad_rim,
        grad_step,
        _,
        grad_conv_w,
        grad_conv_b,
        grad_dt_bias,
        grad_a_log,
        grad_skip,
    ) = core_grads
    rim_grad = shifted(grad_rim, "fsdp", -1)
    cut = patches - (CONV - 1)
    grad_channels = jnp.concatenate([grad_channels[:cut], grad_channels[cut:] + rim_grad], axis=0)
    proj_low = jnp.concatenate([grad_gate_raw, grad_channels, grad_step], axis=1).astype(
        jnp.bfloat16
    )
    grad_in_proj = weight_grad(global_low, proj_low)
    grad_global_norm = input_grad(proj_low, in_back)
    _, norm_back = jax.vjp(rms_scale, patch_sum, gain_g)
    grad_sum_norm, grad_global_gain = norm_back(grad_global_norm)
    sum_low = (grad_patch_mix + grad_sum_norm).astype(jnp.bfloat16)
    grad_patch_proj = weight_grad(patch_rows, sum_low)
    grad_states = grad_streams + input_grad(sum_low, patch_back).reshape(rows, D)
    reduced_global = (
        lax.psum_scatter(grad_patch_proj, ("dp", "fsdp"), scatter_dimension=0, tiled=True),
        lax.psum_scatter(grad_global_gain, ("dp", "fsdp"), scatter_dimension=0, tiled=True),
        lax.psum_scatter(grad_in_proj, ("dp", "fsdp"), scatter_dimension=0, tiled=True),
        lax.psum_scatter(grad_conv_w, ("dp", "fsdp"), scatter_dimension=0, tiled=True),
        lax.psum_scatter(grad_conv_b, ("dp", "fsdp"), scatter_dimension=0, tiled=True),
        lax.psum_scatter(grad_mixer_gain, ("dp", "fsdp"), scatter_dimension=0, tiled=True),
        lax.psum_scatter(grad_out_proj, ("dp", "fsdp"), scatter_dimension=0, tiled=True),
    )
    head_sums = lax.psum((grad_dt_bias, grad_a_log, grad_skip), ("dp", "fsdp"))
    return (
        block_out,
        grad_states,
        reduced_global[0],
        reduced_global[1],
        reduced_global[2],
        reduced_global[3],
        reduced_global[4],
        head_sums[0],
        head_sums[1],
        head_sums[2],
        reduced_global[5],
        reduced_global[6],
        reduced_local[5],
        reduced_local[0],
        reduced_local[1],
        reduced_local[6],
        reduced_local[2],
        reduced_local[3],
        reduced_local[4],
    )


MESH = pl.DeviceIdType.MESH
WIDE = 12288
PARTS = ((0, 3072), (3072, 1024), (4096, 4096), (8192, 4096))
STEP = 1024
FAR_F, FAR_B = 2048, 2048
CUTS = (2048, 2048, 1024)
CUTS_F = (1536, 1024, 512)
TILE = 32
SMALL_ROWS, SMALL_COLS = 48, 384
EXT = D + 128


def device(z, x, y, c):
    return (z * 2 + x, y * 2 + c)


class Spot:
    def __init__(self, depth):
        dp, fs = lax.axis_index("dp"), lax.axis_index("fsdp")
        self.depth, self.count = depth, depth * 8
        self.me = dp * 4 + fs
        self.z, self.x, self.y, self.c = dp // 2, dp % 2, fs // 2, fs % 2
        self.q = self.x * 4 + self.y * 2 + self.c
        self.plane = self.x * 2 + self.y
        swap = lambda place: place + (place // 2) * (1 - 2 * (place % 2))
        self.turn = swap(self.z)
        self.column = [swap((self.turn + depth - j) % depth) for j in range(depth)]

    def flip(self, way):
        x = 1 - self.x if way & 2 else self.x
        y = 1 - self.y if way & 1 else self.y
        return device(self.z, x, y, self.c), x * 2 + y

    def sibling(self):
        return device(self.z, self.x, self.y, 1 - self.c)

    def onward(self):
        place = (self.turn + 1) % self.depth
        return device(place + (place // 2) * (1 - 2 * (place % 2)), self.x, self.y, self.c)

    def above(self, k):
        return device((self.z + k) % self.depth, self.x, self.y, self.c)


def greet(spot):
    barrier = pltpu.get_barrier_semaphore()

    def one(i, carry):
        to = (spot.me + i) % spot.count
        pl.semaphore_signal(barrier, inc=1, device_id=(to // 4, to % 4), device_id_type=MESH)
        return carry

    lax.fori_loop(1, spot.count, one, 0)
    pl.semaphore_wait(barrier, spot.count - 1)


class Wires:
    def __init__(self, send, recv):
        self.send, self.recv, self.used, self.open = send, recv, 0, []

    def copy(self, src, dst, to):
        i = self.used
        self.used += 1
        copy = pltpu.make_async_remote_copy(
            src_ref=src,
            dst_ref=dst,
            send_sem=self.send.at[i],
            recv_sem=self.recv.at[i],
            device_id=to,
            device_id_type=MESH,
        )
        copy.start()
        self.open.append(copy)
        return copy

    def drain(self):
        for copy in self.open:
            copy.wait_send()


def got(copies):
    for copy in copies:
        copy.wait_recv()


class Swap:
    def __init__(self, spot, send, recv, src_at, dst_at):
        self.spot, self.send, self.recv, self.src_at, self.dst_at = spot, send, recv, src_at, dst_at

    def copy(self, i):
        to = (self.spot.me + i) % self.spot.count
        return pltpu.make_async_remote_copy(
            src_ref=self.src_at(to),
            dst_ref=self.dst_at(self.spot.me),
            send_sem=self.send.at[i],
            recv_sem=self.recv.at[i],
            device_id=(to // 4, to % 4),
            device_id_type=MESH,
        )

    def each(self, act):
        def one(i, carry):
            act(self.copy(i))
            return carry

        lax.fori_loop(1, self.spot.count, one, 0)

    def start(self):
        self.each(lambda copy: copy.start())

    def arrive(self):
        self.each(lambda copy: copy.wait_recv())

    def leave(self):
        self.each(lambda copy: copy.wait_send())


def plane_swap(wires, spot, src_at, dst_at):
    copies = []
    for way in range(4):
        for other in range(2):
            if way or other:
                x = spot.x ^ (way >> 1)
                y = spot.y ^ (way & 1)
                c = spot.c ^ other
                copies.append(
                    wires.copy(src_at(x * 4 + y * 2 + c), dst_at(spot.q), device(spot.z, x, y, c))
                )
    return copies


def block_row(t, plane, c):
    return (t * 4 + plane) * 2 + c


def spread_all(wires, spot, buf, own=None):
    at = lambda t, plane, c: buf.at[block_row(t, plane, c)]
    mine = at(spot.z, spot.plane, spot.c)
    src = mine if own is None else own
    ring, flat, core = [], [], []
    for k in range(1, spot.depth):
        ring.append(wires.copy(src, mine, spot.above(k)))
    flat.append([wires.copy(src, mine, spot.flip(way)[0]) for way in (1, 2, 3)])
    core.append(wires.copy(src, mine, spot.sibling()))
    yield
    for j in range(1, spot.depth):
        got([ring[j - 1]])
        block = at((spot.z + spot.depth - j) % spot.depth, spot.plane, spot.c)
        flat.append([wires.copy(block, block, spot.flip(way)[0]) for way in (1, 2, 3)])
        core.append(wires.copy(block, block, spot.sibling()))
    yield
    for j in range(spot.depth):
        for way in (1, 2, 3):
            got([flat[j][way - 1]])
            block = at((spot.z + spot.depth - j) % spot.depth, spot.flip(way)[1], spot.c)
            core.append(wires.copy(block, block, spot.sibling()))
    yield
    got(core)


def spread_plane(wires, spot, buf):
    at = lambda plane: buf.at[plane * 2 + spot.c]
    mine = at(spot.plane)
    flat = [wires.copy(mine, mine, spot.flip(way)[0]) for way in (1, 2, 3)]
    core = [wires.copy(mine, mine, spot.sibling())]
    yield
    for way in (1, 2, 3):
        got([flat[way - 1]])
        block = at(spot.flip(way)[1])
        core.append(wires.copy(block, block, spot.sibling()))
    yield
    got(core)


def sum_plane(wires, spot, parts, pair, near):
    first = wires.copy(parts.at[:, 1 - spot.c], pair, spot.sibling())
    yield None
    got([first])
    f32 = jnp.float32
    pair[...] = (parts[:, spot.c].astype(f32) + pair[...].astype(f32)).astype(jnp.bfloat16)
    flat = [
        wires.copy(pair.at[spot.flip(way)[1]], near.at[way - 1], spot.flip(way)[0]) for way in (1, 2, 3)
    ]
    yield None
    got(flat)
    total = pair[spot.plane].astype(f32)
    for way in range(3):
        total = total + near[way].astype(f32)
    yield total


def sum_all(wires, spot, parts, pair, near, column, far, out):
    f32, low = jnp.float32, jnp.bfloat16
    half = parts.shape[-1] // 2
    cut = [pl.ds(h * half, half) for h in range(2)]
    first = [
        wires.copy(parts.at[:, 1 - spot.c, :, cut[h]], pair.at[:, :, cut[h]], spot.sibling()) for h in range(2)
    ]
    yield
    flat, ring = [], []
    rows = pair.shape[1]
    for h in range(2):
        got([first[h]])
        for b in range(4 * spot.depth):
            pair[b, :, cut[h]] = (
                parts[b, spot.c, :, cut[h]].astype(f32) + pair[b, :, cut[h]].astype(f32)
            ).astype(low)
        step = []
        for way in (1, 2, 3):
            to, plane = spot.flip(way)
            for t in range(spot.depth):
                step.append(
                    wires.copy(pair.at[t * 4 + plane, :, cut[h]], near.at[way - 1, t, :, cut[h]], to)
                )
        flat.append(step)
    yield
    for h in range(2):
        got(flat[h])
        for t in range(spot.depth):
            total = pair[t * 4 + spot.plane, :, cut[h]].astype(f32)
            for way in range(3):
                total = total + near[way, t, :, cut[h]].astype(f32)
            column[t, :, cut[h]] = total.astype(low)
        ring.append(
            [
                wires.copy(
                    column.at[(spot.z + k) % spot.depth, :, cut[h]], far.at[k - 1, :, cut[h]], spot.above(k)
                )
                for k in range(1, spot.depth)
            ]
        )
    yield
    for h in range(2):
        got(ring[h])
        total = column[spot.z, :, cut[h]].astype(f32)
        for k in range(1, spot.depth):
            total = total + far[k - 1, :, cut[h]].astype(f32)
        out[:, cut[h]] = total
    yield


def big_gather(wires, spot, ow, od, shards):
    down = od.shape[0] // spot.count
    xn, yn, cn, zn = spot.flip(2)[0], spot.flip(1)[0], spot.sibling(), spot.onward()
    here, xp, yp, xy = spot.plane, spot.flip(2)[1], spot.flip(1)[1], spot.flip(3)[1]
    parts = {"C": (WIDE - FAR_F, FAR_F, None), ("A", 0): (0, 2 * D, None), ("B", 0): (2 * D, 2 * D, None)}
    begin, side, at = 4 * D, (WIDE - FAR_F - 4 * D) // 2, 0
    for i, width in enumerate(CUTS_F, 1):
        last = i == len(CUTS_F)
        parts["A", i] = (begin + at, width, (0, down // 2) if last else None)
        parts["B", i] = (begin + side + at, width, (down // 2, down // 2) if last else None)
        at += width
    assert at == side
    mine = pl.multiple_of(spot.me * TILE, TILE)
    row = pl.multiple_of(spot.me * down, down)

    def refs(t, plane, part):
        begin, width, deep = parts[part]
        r = block_row(t, plane, spot.c)
        found = [ow.at[pl.ds(pl.multiple_of(r * TILE, TILE), TILE), pl.ds(begin, width)]]
        if deep:
            found.append(od.at[pl.ds(pl.multiple_of(r * down + deep[0], deep[1]), deep[1])])
        return found

    def go(t, plane, part, to):
        return [wires.copy(r, r, to) for r in refs(t, plane, part)]

    def own(part, to):
        begin, width, deep = parts[part]
        pairs = []
        for ref, (base, size) in zip(shards[:4], PARTS):
            low, high = max(begin, base), min(begin + width, base + size)
            if low < high:
                pairs.append(
                    (ref.at[:, pl.ds(low - base, high - low)], ow.at[pl.ds(mine, TILE), pl.ds(low, high - low)])
                )
        if deep:
            pairs.append(
                (shards[4].at[pl.ds(*deep)], od.at[pl.ds(pl.multiple_of(row + deep[0], deep[1]), deep[1])])
            )
        return [wires.copy(a, b, to) for a, b in pairs]

    T = spot.column
    core, ring, fx, fy, sx, sy = {i: [] for i in range(len(CUTS_F) + 2)}, {}, {}, {}, {}, {}

    landed = set()

    def arrived(j, i):
        if j and (j, i) not in landed:
            got(ring[j - 1, i])
            landed.add((j, i))

    def climb_on(j, i):
        send = own if j == 0 else (lambda part, to: go(T[j], here, part, to))
        arrived(j, i)
        ring[j, i] = send(("A", i), zn) + send(("B", i), zn)

    def first(j, i):
        send = own if j == 0 else (lambda part, to: go(T[j], here, part, to))
        arrived(j, i)
        fx[j, i], fy[j, i] = send(("A", i), xn), send(("B", i), yn)
        core[i].append(send(("A", i), cn) + send(("B", i), cn))

    def second(j, i):
        send = own if j == 0 else (lambda part, to: go(T[j], here, part, to))
        got(fx[j, i])
        sy[j, i] = send(("A", i), yn) + go(T[j], xp, ("A", i), yn)
        got(fy[j, i])
        sx[j, i] = send(("B", i), xn) + go(T[j], yp, ("B", i), xn)
        core[i].append(go(T[j], xp, ("A", i), cn) + go(T[j], yp, ("B", i), cn))

    def third(j, i):
        got(sy[j, i])
        core[i].append(go(T[j], yp, ("A", i), cn) + go(T[j], xy, ("A", i), cn))
        got(sx[j, i])
        core[i].append(go(T[j], xp, ("B", i), cn) + go(T[j], xy, ("B", i), cn))

    flat, climb = [], {}

    def far(j):
        if j < 0:
            flat.extend(own("C", spot.flip(way)[0]) for way in (1, 2, 3))
            core[len(CUTS_F) + 1].append(own("C", cn))
            return
        if j == 0:
            assert flat
            for copies in flat:
                got(copies)
        else:
            got(climb[j - 1])
        if j < spot.depth - 1:
            climb[j] = own("C", zn) if j == 0 else go(T[j], here, "C", zn)
            for plane in (xp, yp, xy):
                climb[j] += go(T[j], plane, "C", zn)
        for plane in (xp, yp, xy) + ((here,) if j else ()):
            core[len(CUTS_F) + 1].append(go(T[j], plane, "C", cn))

    chunks, n = range(len(CUTS_F) + 1), spot.depth
    steps = {far_step(j): partial(far, j) for j in range(-1, n)}
    for i in chunks:
        for j in range(n):
            for kind, act in enumerate((climb_on, first, second, third), 1):
                if act is not climb_on or j < n - 1:
                    steps[100 * kind + 10 * j + i] = partial(act, j, i)

    def close(which):
        for part in which:
            for copies in core.pop(part):
                got(copies)

    return steps, close


def far_step(j):
    return 510 + 10 * j


class Ticker:
    def __init__(self, steps, plan):
        self.steps, self.plan = dict(steps), iter(plan)

    def __call__(self):
        for name in next(self.plan):
            self.steps.pop(name)()

    def rest(self, order):
        for name in order:
            if name in self.steps:
                self.steps.pop(name)()
        assert not self.steps


def run(steps):
    for _ in steps:
        pass


def sigmoid(v):
    return 1.0 / (1.0 + jnp.exp(-v))


def lanes(shape, axis):
    return lax.broadcasted_iota(jnp.int32, shape, axis)


def flat_dot(a, b, dims=((1,), (0,))):
    return lax.dot_general(a, b, (dims, ((), ())), preferred_element_type=jnp.float32)


def exact_dot(a, b):
    return jnp.dot(a, b, precision=HIGHEST, preferred_element_type=jnp.float32)


def gain_row(values):
    n_dev, width = values.shape[0], D // values.shape[0]
    spread = (lanes((128, D), 0) == lanes((128, D), 1) & (width - 1)).astype(jnp.bfloat16)
    rows = flat_dot(values, spread)
    return jnp.sum(jnp.where(lanes((n_dev, D), 0) == lanes((n_dev, D), 1) >> (width.bit_length() - 1), rows, 0.0), axis=0, keepdims=True)


def tap_rows(spot, small):
    n_dev = spot.count
    share = CONV_CH // n_dev
    col = lanes((1, 512), 1)
    channel = jnp.where(col < 256, (spot.q + 8 * (col >> 6)) * HEAD_M + (col & 63), DI + col - 256)
    dev = lanes((n_dev, 512), 0)
    picks = (channel >= dev * share) & (channel < dev * share + share)
    owner = jnp.sum(jnp.where(picks, dev, 0), axis=0, keepdims=True)
    within = lanes((128, 512), 0) == channel - owner * share
    rows = []
    for k in range(CONV + 1):
        values = small[:, TILE + k, 0:128]
        spread = flat_dot(values, picks.astype(jnp.bfloat16), ((0,), (0,)))
        rows.append(jnp.sum(jnp.where(within, spread, 0.0), axis=0, keepdims=True))
    return rows


def entry(block, row, lane):
    at = (lanes(block.shape, 0) == row) & (lanes(block.shape, 1) == lane)
    return jnp.sum(jnp.where(at, block.astype(jnp.float32), 0.0), keepdims=True).reshape(1, 1)


class Slot:
    def __init__(self, spot, small, x, count):
        block = small[(spot.z * 2 + x) * 4, TILE : TILE + 16, 0:128].astype(jnp.float32)
        first = entry(block, 9, 0)
        second = first + entry(block, 9, 1)
        number = lambda p: (p >= first).astype(jnp.float32) + (p >= second).astype(jnp.float32)
        col = lanes((count, 1), 0).astype(jnp.float32)
        row = lanes((1, count), 1).astype(jnp.float32)
        docs = number(col)
        self.keep = (col >= row) & (docs == number(row))
        self.same = [((col >= s) & (number(col - s) == docs)).astype(jnp.float32) for s in range(CONV)]


def shift(block, by):
    return block if by == 0 else pltpu.roll(block, by % block.shape[0], 0)


class Mixed:
    def __init__(self, spot, slot, own, maps, step_raw, taps, dt_row, rate_row):
        count = own.shape[0]
        self.spot, self.slot, self.count = spot, slot, count
        self.channels = jnp.concatenate([own[:, 256:], maps], axis=1)
        conv = taps[CONV] + sum(
            taps[CONV - 1 - s] * (shift(self.channels, s) * slot.same[s]) for s in range(CONV)
        )
        self.conv, self.sig = conv, sigmoid(conv)
        act = conv * self.sig
        self.inputs = act[:, :256]
        self.in_map, self.out_map = act[:, 256:384].astype(jnp.bfloat16), act[:, 384:].astype(jnp.bfloat16)
        self.raw = step_raw + dt_row
        self.step = jnp.where(self.raw > 20.0, self.raw, jnp.log(1.0 + jnp.exp(jnp.minimum(self.raw, 20.0))))
        lower = lanes((count, count), 0) >= lanes((count, count), 1)
        self.upper = (lanes((count, count), 0) <= lanes((count, count), 1)).astype(jnp.float32)
        self.cum = exact_dot(lower.astype(jnp.float32), self.step * rate_row)
        self.cum_t, self.step_t = self.cum.T, self.step.T
        self.inner = flat_dot(self.out_map, self.in_map, ((1,), (1,)))

    def head(self, i):
        return self.spot.q + 8 * i

    def col(self, by_head, i):
        return jnp.sum(jnp.where(lanes((1, 128), 1) == self.head(i), by_head, 0.0), axis=1, keepdims=True)

    def row(self, by_head_t, i):
        return jnp.sum(jnp.where(lanes((128, 1), 0) == self.head(i), by_head_t, 0.0), axis=0, keepdims=True)

    def decay(self, i):
        gap = jnp.where(self.slot.keep, self.col(self.cum, i) - self.row(self.cum_t, i), 0.0)
        return jnp.where(self.slot.keep, jnp.exp(gap), 0.0)


def pick_lane(row, lane):
    return jnp.sum(jnp.where(lanes(row.shape, 1) == lane, row, 0.0), axis=1, keepdims=True)


def patch_pairs(count):
    i, j = lanes((count, count), 0), lanes((count, count), 1)
    return (i >= j) & ((i >> 3) == (j >> 3))


def rms_back(value, gain, grad):
    scale = lax.rsqrt(jnp.mean(value * value, axis=1, keepdims=True) + EPSILON)
    along = jnp.mean(grad * gain * value, axis=1, keepdims=True)
    d_value = scale * gain * grad - value * (scale * scale * scale * along)
    return d_value, jnp.sum(grad * value * scale, axis=0, keepdims=True)


def halves_of(block):
    left = lanes(block.shape, 1) < HEAD
    return left, [jnp.where(left, block, 0), jnp.where(left, 0, block)]


def local_block(
    tick,
    ready,
    whole,
    lengths,
    bytes_ref,
    grad_ref,
    sum_ref,
    mixed_ref,
    small_ref,
    wide,
    deep,
    o_block,
    o_streams,
    o_mix,
    o_direct,
    o_gains,
    g_qkv,
    g_attn,
    g_gate,
    g_up,
    g_down,
    attn_w,
    ffn_w,
    g_buf,
    streams,
    normed,
    qkv,
    weights,
    heads,
    attended,
    ffn_low,
    ffn_t,
    total,
    d_ffn,
    d_down,
    load_sem,
    ffn_sem,
    g_sem,
):
    f32, low = jnp.float32, jnp.bfloat16
    rows = bytes_ref.shape[0]
    scale = HEAD ** (-0.5)
    ready()
    load = pltpu.make_async_copy(wide.at[:, pl.ds(0, 4 * D)], attn_w, load_sem.at[0])
    load.start()

    def ffn_loads(j, slot):
        at = lambda base: pl.ds(pl.multiple_of(base + j * D, D), D)
        return [
            pltpu.make_async_copy(wide.at[:, at(4 * D)], ffn_w.at[slot, 0], ffn_sem.at[slot, 0]),
            pltpu.make_async_copy(wide.at[:, at(8 * D)], ffn_w.at[slot, 1], ffn_sem.at[slot, 1]),
            pltpu.make_async_copy(deep.at[at(0)], ffn_w.at[slot, 2], ffn_sem.at[slot, 2]),
        ]

    gain_a = gain_row(small_ref[:, TILE + 7, 0:128])
    gain_f = gain_row(small_ref[:, TILE + 8, 0:128])
    place = lax.axis_index("fsdp") * (rows // PATCH) + (lanes((rows, 1), 0) >> 3)
    live = (place < lengths[0, 0] + lengths[0, 1]).astype(f32)
    raw = mixed_ref[:, pl.ds(0, D)]
    mixer_r = lax.rsqrt(mixed_ref[:, pl.ds(D, 128)] * (1.0 / DI) + EPSILON)[:, 0:1]
    patch = sum_ref[...] + raw * mixer_r
    patch = jnp.broadcast_to(patch[:, None, :], (rows // PATCH, PATCH, D)).reshape(rows, D)
    streams[...] = bytes_ref[...].astype(f32) + patch
    normed[...] = rms_scale(streams[...], gain_a).astype(low)
    d_down[...] = (live * grad_ref[...].astype(f32)).astype(low)
    load.wait()
    for i in range(3):
        at = pl.ds(i * D, D)
        qkv[:, at] = flat_dot(normed[...], attn_w[:, at]).astype(low)
        tick()
    pairs = patch_pairs(128)

    def blocks(p, b):
        row = pl.ds(b * 128, 128)
        return row, [pl.ds(pl.multiple_of(base + p * 128, 128), 128) for base in (0, D, 2 * D)]

    def attend(p, carry):
        for b in range(rows // 128):
            row, (qa, ka, va) = blocks(p, b)
            k, v = qkv[row, ka], qkv[row, va]
            left, queries = halves_of(qkv[row, qa])
            outs = []
            for h in range(2):
                scores = flat_dot(queries[h], k, ((1,), (1,))) * scale
                scores = jnp.where(pairs, scores, -1e30)
                e = jnp.exp(scores - jnp.max(scores, axis=1, keepdims=True))
                w = e / jnp.sum(e, axis=1, keepdims=True)
                weights[p, b, h] = w
                outs.append(flat_dot(w.astype(low), v))
            heads[row, qa] = jnp.where(left, outs[0], outs[1]).astype(low)
        return carry

    for begin in range(0, D // 128, 2):
        lax.fori_loop(begin, begin + 2, attend, 0)
        tick()
    attended[...] = streams[...] + flat_dot(heads[...], attn_w[:, pl.ds(3 * D, D)])
    ffn_low[...] = rms_scale(attended[...], gain_f).astype(low)
    whole()
    for copy in ffn_loads(0, 0):
        copy.start()
    ffn_t[...] = ffn_low[...].astype(f32).T.astype(low)
    total[...] = attended[...]
    d_ffn[...] = jnp.zeros_like(d_ffn)
    n_ffn = deep.shape[0] // D

    def stores(j):
        at = pl.ds(pl.multiple_of(j * D, D), D)
        return [
            pltpu.make_async_copy(g_buf.at[0], g_gate.at[:, at], g_sem.at[0]),
            pltpu.make_async_copy(g_buf.at[1], g_up.at[:, at], g_sem.at[1]),
            pltpu.make_async_copy(g_buf.at[2], g_down.at[at], g_sem.at[2]),
        ]

    def feed(j, carry):
        slot = lax.rem(j, 2)
        for copy in ffn_loads(j, slot):
            copy.wait()

        @pl.when(j + 1 < n_ffn)
        def _():
            for copy in ffn_loads(j + 1, 1 - slot):
                copy.start()

        gate = flat_dot(ffn_low[...], ffn_w[slot, 0])
        upward = flat_dot(ffn_low[...], ffn_w[slot, 1])
        sig = sigmoid(gate)
        act = gate * sig
        hidden = (act * upward).astype(low)
        total[...] += flat_dot(hidden, ffn_w[slot, 2])
        d_hidden = flat_dot(d_down[...], ffn_w[slot, 2], ((1,), (1,)))
        d_gate = (d_hidden * upward * (sig + act * (1.0 - sig))).astype(low)
        d_up = (d_hidden * act).astype(low)
        d_ffn[...] += flat_dot(d_gate, ffn_w[slot, 0], ((1,), (1,)))
        d_ffn[...] += flat_dot(d_up, ffn_w[slot, 1], ((1,), (1,)))

        @pl.when(j > 0)
        def _():
            for copy in stores(j - 1):
                copy.wait()

        g_buf[0] = flat_dot(ffn_t[...], d_gate).astype(low)
        g_buf[1] = flat_dot(ffn_t[...], d_up).astype(low)
        g_buf[2] = flat_dot(hidden.astype(f32).T.astype(low), d_down[...]).astype(low)
        for copy in stores(j):
            copy.start()
        return carry

    lax.fori_loop(0, n_ffn, feed, 0)
    o_block[...] = (live * total[...]).astype(low)
    d_norm, gain_f_sum = rms_back(attended[...], gain_f, d_ffn[...])
    d_attended = live * grad_ref[...].astype(f32) + d_norm
    total[...] = d_attended
    d_low = d_attended.astype(low)
    for copy in stores(n_ffn - 1):
        copy.wait()
    d_down[...] = flat_dot(d_low, attn_w[:, pl.ds(3 * D, D)], ((1,), (1,))).astype(low)
    g_buf[0] = flat_dot(heads[...].astype(f32).T.astype(low), d_low).astype(low)
    last = [pltpu.make_async_copy(g_buf.at[0], g_attn, g_sem.at[0])]
    last[0].start()

    def attend_back(p, carry):
        for b in range(rows // 128):
            row, (qa, ka, va) = blocks(p, b)
            q, k, v = qkv[row, qa], qkv[row, ka], qkv[row, va]
            grad = d_down[row, qa]
            left, grads = halves_of(grad)
            dq, dk, dv = [], [], []
            for h in range(2):
                w = weights[p, b, h]
                dv.append(flat_dot(w.T.astype(low), grad))
                d_w = flat_dot(grads[h], v, ((1,), (1,)))
                d_s = w * (d_w - jnp.sum(w * d_w, axis=1, keepdims=True))
                dq.append(flat_dot(d_s.astype(low), k) * scale)
                dk.append(flat_dot(d_s.T.astype(low), q) * scale)
            qkv[row, qa] = jnp.where(left, dq[0], dq[1]).astype(low)
            qkv[row, ka] = jnp.where(left, dk[0], dk[1]).astype(low)
            qkv[row, va] = jnp.where(left, dv[0], dv[1]).astype(low)
        return carry

    lax.fori_loop(0, D // 128, attend_back, 0)
    ffn_t[...] = normed[...].astype(f32).T.astype(low)
    for i in range(3):
        at = pl.ds(i * D, D)
        if i == 2:
            last[0].wait()
        buf = (i + 1) % 3
        g_buf[buf] = flat_dot(ffn_t[...], qkv[:, at]).astype(low)
        copy = pltpu.make_async_copy(g_buf.at[buf], g_qkv.at[:, at], g_sem.at[buf])
        copy.start()
        last.append(copy)
    d_ffn[...] = flat_dot(qkv[...], attn_w[:, pl.ds(0, 3 * D)], ((1,), (1,)))
    d_norm, gain_a_sum = rms_back(streams[...], gain_a, d_ffn[...])
    d_streams = total[...] + d_norm
    o_streams[...] = d_streams
    direct = jnp.sum(d_streams.reshape(rows // PATCH, PATCH, D), axis=1)
    o_direct[...] = direct
    mix = direct.astype(low)
    along = jnp.sum(mix.astype(f32) * raw, axis=1, keepdims=True)
    high_r, high_a = (v.astype(low).astype(f32) for v in (mixer_r, along))
    lane = lanes((rows // PATCH, 128), 1)
    ext = jnp.zeros((rows // PATCH, 128), f32)
    for i, v in enumerate((high_r, high_a, mixer_r - high_r, along - high_a)):
        ext = jnp.where(lane == i, v, ext)
    o_mix[:, pl.ds(0, D)] = mix
    o_mix[:, pl.ds(D, 128)] = ext.astype(low)
    o_gains[...] = jnp.concatenate([gain_a_sum, gain_f_sum, jnp.zeros((6, D), f32)], axis=0)
    for copy in last[1:]:
        copy.wait()


N_WIRES = 512
PLAN_F = (
    (500, 100, 200),
    (),
    (),
    (300, 201),
    (),
    (110, 210, 101),
    (),
    (310, 202, 120, 203),
    (400, 410),
    (220, 301, 302),
    (320, 102, 103, 230),
    (111, 211),
    (),
    (),
    (),
    (510,),
    (330,),
    (420,),
    (112, 212),
    (303,),
    (113, 213),
    (),
    (430, 311, 312, 520),
    (121, 221),
    (313, 122, 222),
    (401, 402),
    (123, 223, 321),
    (322, 403, 411),
    (231, 323, 412),
    (530, 232, 413),
)
REST_F = (
    331,
    233,
    332,
    333,
    540,
    421,
    422,
    423,
    431,
    432,
    433,
)
PLAN_B = (
    (),
    (),
    (200, 210),
    (201, 202),
    (510, 520),
    (211,),
    (300,),
    (220,),
    (530,),
    (),
    (),
    (),
    (400,),
    (),
    (),
    (),
    (301, 212),
    (),
    (),
    (302,),
    (310, 221),
    (),
    (),
    (222, 401, 311, 410),
    (230, 312, 402),
    (231, 320),
    (411, 232, 321, 540),
)
REST_B = (
    412,
    322,
    420,
    330,
    421,
    331,
    422,
    332,
    430,
    550,
    431,
    432,
)


def forward_kernel(
    depth,
    rows_ref,
    patch_ref,
    cols_ref,
    vec_ref,
    out_ref,
    heads_ref,
    lengths,
    states_ref,
    grad_ref,
    qkv,
    attn,
    gate,
    up,
    down,
    ow,
    od,
    o_block,
    o_streams,
    o_mix,
    o_direct,
    o_gains,
    g_qkv,
    g_attn,
    g_gate,
    g_up,
    g_down,
    sum_ref,
    small_ref,
    bytes_ref,
    norm_ref,
    proj_ref,
    head_w_ref,
    own_ref,
    maps_ref,
    step_ref,
    core_ref,
    mixed_ref,
    attn_w,
    ffn_w,
    g_buf,
    streams,
    normed,
    qkv_low,
    weights,
    mixed_heads,
    attended,
    ffn_low,
    ffn_t,
    total_ref,
    d_ffn,
    d_down,
    load_sem,
    ffn_sem,
    g_sem,
    parts,
    pair,
    near,
    column,
    far,
    parts8,
    pair8,
    near8,
    send,
    recv,
    swap_send,
    swap_recv,
    local,
):
    f32, low = jnp.float32, jnp.bfloat16
    spot = Spot(depth)
    count = 128
    wires = Wires(send, recv)
    mine = pl.multiple_of(spot.me * TILE, TILE)
    bytes_ref[pl.ds(mine, TILE)] = rows_ref[:, pl.ds(pl.multiple_of(spot.me * 256, 256), 256)]
    small_ref[spot.me] = vec_ref[...]
    proj_ref[pl.ds(mine, TILE)] = cols_ref[spot.q]
    head_w_ref[spot.z] = out_ref[...]
    greet(spot)

    def lanes_of(to):
        return rows_ref.at[:, pl.ds(pl.multiple_of(to * 256, 256), 256)]

    swap_bytes = Swap(
        spot,
        swap_send,
        swap_recv,
        lanes_of,
        lambda me: bytes_ref.at[pl.ds(pl.multiple_of(me * TILE, TILE), TILE)],
    )
    swap_bytes.start()
    steps, close = big_gather(wires, spot, ow, od, (qkv, attn, gate, up, down))
    near_proj = plane_swap(
        wires,
        spot,
        lambda q: cols_ref.at[q],
        lambda q: proj_ref.at[pl.ds(pl.multiple_of((spot.z * 8 + q) * TILE, TILE), TILE)],
    )
    small = spread_all(wires, spot, small_ref)
    next(small)
    tick = Ticker(steps, PLAN_F)
    tick()
    own_rows = []
    at = 0
    for i, ref in enumerate((qkv, attn, gate, up)):
        width = ref.shape[1]
        own_rows.append(pltpu.make_async_copy(ref, ow.at[pl.ds(mine, TILE), pl.ds(at, width)], local.at[i]))
        at += width
    deep = down.shape[0]
    own_rows.append(
        pltpu.make_async_copy(down, od.at[pl.ds(pl.multiple_of(spot.me * deep, deep), deep)], local.at[4])
    )
    for copy in own_rows:
        copy.start()
    tick()
    swap_bytes.arrive()
    got(near_proj)
    layer = proj_ref.at[pl.ds(pl.multiple_of(spot.z * 8 * TILE, 8 * TILE), 8 * TILE)]
    far_proj = [wires.copy(layer, layer, spot.above(k)) for k in range(1, depth)]

    for b in range(4):
        block = flat_dot(bytes_ref[pl.ds(b * 256, 256)], patch_ref[...]).astype(low)
        parts[pl.ds(b * 4, 4)] = block.reshape(4, 2, TILE, D)
    tick()
    total = sum_all(wires, spot, parts, pair, near, column, far, sum_ref)
    next(total)
    next(small)
    tick()
    next(total)
    tick()
    next(total)
    next(small)
    tick()
    head_w = [wires.copy(out_ref, head_w_ref.at[spot.z], spot.above(k)) for k in range(1, depth)]
    next(total)
    tick()
    run(small)
    patch_sum = sum_ref[...]
    scale = lax.rsqrt(jnp.mean(patch_sum * patch_sum, axis=1, keepdims=True) + EPSILON)
    gain = gain_row(small_ref[:, TILE + 5, 0:128])
    norm_ref[spot.q] = (patch_sum * scale * gain).astype(low)
    plane = spread_plane(wires, spot, norm_ref)
    next(plane)
    tick()
    next(plane)
    tick()
    got(far_proj)
    taps = tap_rows(spot, small_ref)
    run(plane)
    tick()

    norm = norm_ref[...].reshape(2 * count, D)
    own_ref[...] = flat_dot(norm, proj_ref[...])
    maps_ref[...] = flat_dot(norm, small_ref[:, :TILE, 0:256].reshape(D, 256))
    step_ref[...] = flat_dot(norm, small_ref[:, :TILE, 256:384].reshape(D, 128))
    dt_row, rate_row, skip_row = heads_ref[0:1], heads_ref[1:2], heads_ref[2:3]
    tick()
    got(head_w)
    gains = jnp.concatenate(
        [small_ref[spot.q + 8 * i, TILE : TILE + 16, 0:HEAD_M][6:7].astype(f32) for i in range(4)], axis=1
    )
    for x in range(2):
        at = pl.ds(x * count, count)
        slot = Slot(spot, small_ref, x, count)
        own, maps = own_ref[at], maps_ref[at]
        mix = Mixed(spot, slot, own, maps, step_ref[at], taps, dt_row, rate_row)
        outs = []
        for i in range(4):
            tick()
            inputs = mix.inputs[:, i * HEAD_M : (i + 1) * HEAD_M]
            mixing = (mix.decay(i) * mix.inner * mix.row(mix.step_t, i)).astype(low)
            skip = pick_lane(skip_row, mix.head(i))
            outs.append(flat_dot(mixing, inputs.astype(low)) + skip * inputs)
        core = jnp.concatenate(outs, axis=1)
        core_ref[at] = core
        raw = own[:, :256]
        gated = core * raw * sigmoid(raw)
        part = flat_dot((gated * gains).astype(low), head_w_ref[...].reshape(256, D))
        squares = jnp.sum(gated * gated, axis=1, keepdims=True)
        parts8[pl.ds(x * 2, 2), :, :, pl.ds(0, D)] = part.astype(low).reshape(2, 2, TILE, D)
        parts8[pl.ds(x * 2, 2), :, :, pl.ds(D, 128)] = (
            jnp.broadcast_to(squares, (count, 128)).astype(low).reshape(2, 2, TILE, 128)
        )
        tick()
    for total in sum_plane(wires, spot, parts8, pair8, near8):
        if total is None:
            tick()
    mixed_ref[...] = total

    def ready():
        for copy in own_rows:
            copy.wait()
        close([0])

    def whole():
        tick.rest(REST_F)
        close(range(1, len(CUTS_F) + 2))

    local_block(
        tick,
        ready,
        whole,
        lengths,
        states_ref,
        grad_ref,
        sum_ref,
        mixed_ref,
        small_ref,
        ow,
        od,
        o_block,
        o_streams,
        o_mix,
        o_direct,
        o_gains,
        g_qkv,
        g_attn,
        g_gate,
        g_up,
        g_down,
        attn_w,
        ffn_w,
        g_buf,
        streams,
        normed,
        qkv_low,
        weights,
        mixed_heads,
        attended,
        ffn_low,
        ffn_t,
        total_ref,
        d_ffn,
        d_down,
        load_sem,
        ffn_sem,
        g_sem,
    )
    wires.drain()
    swap_bytes.leave()


def forward_call(
    depth,
    n_dev,
    rows2,
    patch_proj,
    cols,
    vectors,
    out_proj,
    heads,
    lengths,
    byte_states,
    out_grad,
    qkv,
    attn,
    gate,
    up,
    down,
):
    f32, low = jnp.float32, jnp.bfloat16
    vmem = pl.BlockSpec(memory_space=pltpu.VMEM)
    anywhere = pl.BlockSpec(memory_space=pl.ANY)
    smem = pl.BlockSpec(memory_space=pltpu.SMEM)
    shape = jax.ShapeDtypeStruct
    plane_patches = 8 * TILE
    rows, hidden = byte_states.shape[0], down.shape[0] * n_dev
    outs = [
        shape((D, WIDE), low),
        shape((hidden, D), low),
        shape((rows, D), low),
        shape((rows, D), f32),
        shape((rows // PATCH, EXT), low),
        shape((rows // PATCH, D), f32),
        shape((8, D), f32),
        shape((D, 3 * D), low),
        shape((D, D), low),
        shape((D, hidden), low),
        shape((D, hidden), low),
        shape((hidden, D), low),
        shape((TILE, D), f32),
        shape((n_dev, SMALL_ROWS, SMALL_COLS), low),
        shape((n_dev * TILE, 256), low),
        shape((8, TILE, D), low),
        shape((n_dev * TILE, 512), low),
        shape((depth, HEAD_M, D), low),
        shape((plane_patches, 512), f32),
        shape((plane_patches, 256), f32),
        shape((plane_patches, 128), f32),
        shape((plane_patches, 256), f32),
    ]
    scratch = [
        pltpu.VMEM((TILE, EXT), f32),
        pltpu.VMEM((D, 4 * D), low),
        pltpu.VMEM((2, 3, D, D), low),
        pltpu.VMEM((3, D, D), low),
        pltpu.VMEM((rows, D), f32),
        pltpu.VMEM((rows, D), low),
        pltpu.VMEM((rows, 3 * D), low),
        pltpu.VMEM((D // 128, rows // 128, 2, 128, 128), f32),
        pltpu.VMEM((rows, D), low),
        pltpu.VMEM((rows, D), f32),
        pltpu.VMEM((rows, D), low),
        pltpu.VMEM((D, rows), low),
        pltpu.VMEM((rows, D), f32),
        pltpu.VMEM((rows, D), f32),
        pltpu.VMEM((rows, D), low),
        pltpu.SemaphoreType.DMA((1,)),
        pltpu.SemaphoreType.DMA((2, 3)),
        pltpu.SemaphoreType.DMA((3,)),
        pltpu.VMEM((16, 2, TILE, D), low),
        pltpu.VMEM((16, TILE, D), low),
        pltpu.VMEM((3, depth, TILE, D), low),
        pltpu.VMEM((depth, TILE, D), low),
        pltpu.VMEM((depth - 1, TILE, D), low),
        pltpu.VMEM((4, 2, TILE, EXT), low),
        pltpu.VMEM((4, TILE, EXT), low),
        pltpu.VMEM((3, TILE, EXT), low),
        pltpu.SemaphoreType.DMA((N_WIRES,)),
        pltpu.SemaphoreType.DMA((N_WIRES,)),
        pltpu.SemaphoreType.DMA((n_dev,)),
        pltpu.SemaphoreType.DMA((n_dev,)),
        pltpu.SemaphoreType.DMA((5,)),
    ]
    found = pl.pallas_call(
        partial(forward_kernel, depth),
        out_shape=outs,
        in_specs=[vmem] * 6 + [smem] + [vmem] * 2 + [anywhere] * 5,
        out_specs=[anywhere] * 2 + [vmem] * 5 + [anywhere] * 5 + [vmem] * 10,
        scratch_shapes=scratch,
        compiler_params=pltpu.CompilerParams(
            collective_id=0, has_side_effects=True, vmem_limit_bytes=58 * 2**20
        ),
        name="global_forward",
    )(rows2, patch_proj, cols, vectors, out_proj, heads, lengths, byte_states, out_grad, qkv, attn, gate, up, down)
    block, streams, mix, direct, gains, *rest = found[2:]
    return (block, streams, mix, direct, gains), rest[:5], rest[5], rest[6:]


def add_to(dst, sources, width):
    def one(i, carry):
        at = pl.ds(pl.multiple_of(i * STEP, STEP), STEP)
        total = sources[0](at).astype(jnp.float32)
        for source in sources[1:]:
            total = total + source(at).astype(jnp.float32)
        dst(at, total)
        return carry

    lax.fori_loop(0, width // STEP, one, 0)


def big_scatter(wires, spot, grads, bufs, outs, local):
    f32, low = jnp.float32, jnp.bfloat16
    held_w, held_d, stage_w, stage_d, near_w, near_d, last_w, last_d, ring_w, ring_d, climb_c, flat_c = bufs
    half, deep = (WIDE - FAR_B) // 2, held_d.shape[2]
    xn, yn, cn, zn = spot.flip(2)[0], spot.flip(1)[0], spot.sibling(), spot.onward()
    here, xp, yp, xy = spot.plane, spot.flip(2)[1], spot.flip(1)[1], spot.flip(3)[1]
    T = [spot.column[k % spot.depth] for k in range(1, spot.depth + 1)]
    core, fetch, near, last, ring = {}, {}, {}, {}, {}
    A, B, C = pl.ds(0, half), pl.ds(half, half), pl.ds(2 * half, FAR_B)
    AB = pl.ds(0, 2 * half)
    climb, flat = {}, []
    DA, DB = pl.ds(0, deep // 2), pl.ds(deep // 2, deep // 2)

    def load(k, side):
        fetch[k, side] = []
        for i, ref in enumerate(grads):
            dst = stage_w.at[:, :, pl.ds(*PARTS[i])] if i < 4 else stage_d
            copy = pltpu.make_async_copy(ref.at[T[k], pl.ds(2 * side, 2), spot.c], dst, local.at[k * 5 + i])
            copy.start()
            fetch[k, side].append(copy)

    def open_core(k):
        core[k] = []
        for i, ref in enumerate(grads):
            dst = held_w.at[T[k], :, :, pl.ds(*PARTS[i])] if i < 4 else held_d.at[T[k]]
            core[k].append(wires.copy(ref.at[T[k], :, 1 - spot.c], dst, cn))

    def join(k):
        if k not in core:
            return
        t = T[k]
        got(core.pop(k))
        for side in range(2):
            for copy in fetch[k, side]:
                copy.wait()
            for half_at in range(2):
                plane = 2 * side + half_at

                def put_w(at, total, plane=plane):
                    held_w[t, plane, :, at] = total.astype(low)

                add_to(
                    put_w,
                    [lambda at, p=plane: held_w[t, p, :, at], lambda at, h=half_at: stage_w[h, :, at]],
                    WIDE,
                )
                held_d[t, plane] = (held_d[t, plane].astype(f32) + stage_d[half_at].astype(f32)).astype(low)
            if side == 0:
                load(k, 1)
            elif k + 1 < spot.depth:
                load(k + 1, 0)

    parts, at = [], 0
    for i, width in enumerate(CUTS):
        end = i == len(CUTS) - 1
        width = half - at if end else width
        parts.append((at, width, end))
        at += width

    def spans(i):
        at, width, end = parts[i]
        found = [(pl.ds(at, width), pl.ds(half + at, width))]
        return found, end

    def near_sends(k, i):
        t = T[k]
        [(a, b)], end = spans(i)
        sends = []
        for x in range(2):
            src = x * 2 + (1 - spot.y)
            sends.append(wires.copy(held_w.at[t, src, :, a], near_w.at[k, x, :, a], yn))
            if end:
                sends.append(wires.copy(held_d.at[t, src, DA], near_d.at[k, x, DA], yn))
        for y in range(2):
            src = (1 - spot.x) * 2 + y
            sends.append(wires.copy(held_w.at[t, src, :, b], near_w.at[k, y, :, b], xn))
            if end:
                sends.append(wires.copy(held_d.at[t, src, DB], near_d.at[k, y, DB], xn))
        near[k, i] = sends

    def first(k, i):
        join(k)
        near_sends(k, i)

    def second(k, i):
        t = T[k]
        got(near[k, i])
        at, width, end = parts[i]
        for other in range(2):
            for plane, base in ((other * 2 + spot.y, at), (spot.x * 2 + other, half + at)):
                moved = lambda c, base=base: pl.ds(pl.multiple_of(c.start + base, STEP), STEP)

                def put(c, total, plane=plane, moved=moved):
                    held_w[t, plane, :, moved(c)] = total.astype(low)

                add_to(
                    put,
                    [
                        lambda c, p=plane, m=moved: held_w[t, p, :, m(c)],
                        lambda c, o=other, m=moved: near_w[k, o, :, m(c)],
                    ],
                    width,
                )
            if end:
                pa, pb = other * 2 + spot.y, spot.x * 2 + other
                held_d[t, pa, DA] = (held_d[t, pa, DA].astype(f32) + near_d[k, other, DA].astype(f32)).astype(low)
                held_d[t, pb, DB] = (held_d[t, pb, DB].astype(f32) + near_d[k, other, DB].astype(f32)).astype(low)
        [(a, b)], _ = spans(i)
        sends = [
            wires.copy(held_w.at[t, xp, :, a], last_w.at[k, :, a], xn),
            wires.copy(held_w.at[t, yp, :, b], last_w.at[k, :, b], yn),
        ]
        if end:
            sends.append(wires.copy(held_d.at[t, xp, DA], last_d.at[k, DA], xn))
            sends.append(wires.copy(held_d.at[t, yp, DB], last_d.at[k, DB], yn))
        last[k, i] = sends

    def finish(terms, begin, end):
        for out, (base, size) in zip(outs, PARTS):
            a, b = max(begin, base), min(end, base + size)

            def put_out(at, total, out=out, shift_by=a - base):
                out[:, pl.ds(pl.multiple_of(at.start + shift_by, STEP), STEP)] = total

            if a < b:
                moved = [
                    lambda at, f=f, a=a: f(pl.ds(pl.multiple_of(at.start + a, STEP), STEP)) for f in terms
                ]
                add_to(put_out, moved, b - a)

    def far(k):
        join(k)
        t = T[k]
        if k:
            got(climb[k - 1])
            for plane in range(4):
                base = lambda at: pl.ds(pl.multiple_of(at.start + 2 * half, STEP), STEP)

                def put_far(at, total, plane=plane):
                    held_w[t, plane, :, base(at)] = total.astype(low)

                terms = [
                    lambda at, p=plane: held_w[t, p, :, base(at)],
                    lambda at, p=plane: climb_c[k - 1, p, :, at],
                ]
                add_to(put_far, terms, FAR_B)
        if k < spot.depth - 1:
            climb[k] = [wires.copy(held_w.at[t, :, :, C], climb_c.at[k], zn)]
        else:
            for way in (1, 2, 3):
                to, plane = spot.flip(way)
                flat.append(wires.copy(held_w.at[t, plane, :, C], flat_c.at[way - 1], to))

    def far_end():
        assert flat
        got(flat)
        terms = [lambda at: held_w[T[-1], here, :, at]]
        for way in range(3):
            terms.append(
                lambda at, w=way: flat_c[w, :, pl.ds(pl.multiple_of(at.start - 2 * half, STEP), STEP)]
            )
        finish(terms, 2 * half, WIDE)

    def third(k, i):
        t = T[k]
        got(last[k, i])
        if k:
            got(ring[k - 1, i])
        at, width, end = parts[i]
        [(a, b)], _ = spans(i)
        terms = [lambda c: held_w[t, here, :, c], lambda c: last_w[k, :, c]]
        if k:
            terms.append(lambda c: ring_w[k - 1, :, c])
        if end:
            down = held_d[t, here].astype(f32) + last_d[k].astype(f32)
            if k:
                down = down + ring_d[k - 1].astype(f32)
        if k == spot.depth - 1:
            finish(terms, at, at + width)
            finish(terms, half + at, half + at + width)
            if end:
                outs[4][...] = down
            return
        for base in (at, half + at):
            moved = lambda c, base=base: pl.ds(pl.multiple_of(c.start + base, STEP), STEP)

            def put_on(c, total, moved=moved):
                held_w[t, here, :, moved(c)] = total.astype(low)

            add_to(put_on, [lambda c, f=f, m=moved: f(m(c)) for f in terms], width)
        ring[k, i] = [wires.copy(held_w.at[t, here, :, c], ring_w.at[k, :, c], zn) for c in (a, b)]
        if end:
            held_d[t, here] = down.astype(low)
            ring[k, i].append(wires.copy(held_d.at[t, here], ring_d.at[k], zn))

    load(0, 0)
    for k in range(spot.depth):
        open_core(k)
    steps = {far_step(k): partial(far, k) for k in range(spot.depth)}
    steps[far_step(spot.depth)] = far_end
    for i in range(len(CUTS)):
        for k in range(spot.depth):
            for kind, act in enumerate((first, second, third), 2):
                steps[100 * kind + 10 * k + i] = partial(act, k, i)
    return steps


class Back:
    def __init__(self, mix, own, core, ext, d_patch, gains, head_w, heads, taps, tick):
        f32, low = jnp.float32, jnp.bfloat16
        count = mix.count
        dt_row, rate_row, skip_row = heads[0:1], heads[1:2], heads[2:3]
        r = ext[:, 0:1] + ext[:, 2:3]
        along = ext[:, 1:2] + ext[:, 3:4]
        raw = own[:, :256]
        sig = sigmoid(raw)
        gated = core * raw * sig
        back = flat_dot(d_patch, head_w, ((1,), (1,)))
        self.norm = (gated * r * gains).astype(low)
        self.gain = jnp.sum(back * gated * r, axis=0, keepdims=True)
        d_gated = r * gains * back - gated * (r * r * r * along * (1.0 / DI))
        d_core = d_gated * raw * sig
        d_gate = d_gated * core * sig * (1.0 + raw * (1.0 - sig))
        lane = lanes((1, 128), 1)
        graph = jnp.zeros((count, count), f32)
        d_inputs = []
        direct = jnp.zeros((count, 128), f32)
        flow = jnp.zeros((count, 128), f32)
        d_skip = jnp.zeros((1, 128), f32)
        for i in range(4):
            tick()
            cut = slice(i * HEAD_M, (i + 1) * HEAD_M)
            inputs, grad = mix.inputs[:, cut], d_core[:, cut]
            decay, step = mix.decay(i), mix.row(mix.step_t, i)
            kept = decay * mix.inner
            skip = pick_lane(skip_row, mix.head(i))
            d_mixing = flat_dot(grad.astype(low), inputs.astype(low), ((1,), (1,)))
            d_inputs.append(
                flat_dot((kept * step).astype(low), grad.astype(low), ((0,), (0,))) + skip * grad
            )
            graph = graph + decay * step * d_mixing
            turn = kept * d_mixing
            arrive = jnp.sum(turn.T, axis=1, keepdims=True)
            leave = jnp.sum(turn * step, axis=1, keepdims=True)
            here = lane == mix.head(i)
            direct = direct + jnp.where(here, arrive, 0.0)
            flow = flow + jnp.where(here, leave - mix.col(mix.step, i) * arrive, 0.0)
            d_skip = d_skip + jnp.where(here, jnp.sum(grad * inputs, keepdims=True).reshape(1, 1), 0.0)
        tail = exact_dot(mix.upper, flow)
        mine = own_lanes(lane, mix)
        d_step = jnp.where(mine, direct + rate_row * tail, 0.0)
        d_raw = d_step * sigmoid(mix.raw)
        self.skip = d_skip
        self.rate = jnp.sum(rate_row * mix.step * jnp.where(mine, tail, 0.0), axis=0, keepdims=True)
        self.bias = jnp.sum(d_raw, axis=0, keepdims=True)
        low_graph = graph.astype(low)
        d_out_map = flat_dot(low_graph, mix.in_map)
        d_in_map = flat_dot(low_graph, mix.out_map, ((0,), (0,)))
        d_act = jnp.concatenate(d_inputs + [d_in_map, d_out_map], axis=1)
        d_conv = d_act * (mix.sig * (1.0 + mix.conv * (1.0 - mix.sig)))
        d_channels = jnp.zeros_like(d_conv)
        self.taps = [None] * CONV + [jnp.sum(d_conv, axis=0, keepdims=True)]
        for s in range(CONV):
            kept = d_conv * mix.slot.same[s]
            d_channels = d_channels + taps[CONV - 1 - s] * shift(kept, -s)
            self.taps[CONV - 1 - s] = jnp.sum(kept * shift(mix.channels, s), axis=0, keepdims=True)
        self.rows = jnp.concatenate([d_gate, d_channels, d_raw], axis=1).astype(low)


def own_lanes(lane, mix):
    mine = lane == mix.head(0)
    for i in range(1, 4):
        mine = mine | (lane == mix.head(i))
    return mine


COLS = 512 + 256 + 128


def backward_kernel(
    depth,
    mix_ref,
    direct_ref,
    streams_ref,
    sum_ref,
    gains_ref,
    small_ref,
    bytes_ref,
    norm_ref,
    proj_ref,
    head_w_ref,
    own_ref,
    maps_ref,
    step_ref,
    core_ref,
    patch_ref,
    heads_ref,
    g_qkv,
    g_attn,
    g_gate,
    g_up,
    g_down,
    o_qkv,
    o_attn,
    o_gate,
    o_up,
    o_down,
    o_patch,
    o_states,
    o_head,
    o_cols,
    o_maps,
    extra_ref,
    all_ref,
    map_send,
    map_near,
    map_sum,
    map_far,
    o_rows,
    mix_all,
    rows_all,
    head_sum,
    head_low,
    head_far,
    col_send,
    col_recv,
    col_far,
    col_sum,
    back_send,
    parts8,
    pair8,
    near8,
    held_w,
    held_d,
    stage_w,
    stage_d,
    near_w,
    near_d,
    last_w,
    last_d,
    ring_w,
    ring_d,
    climb_c,
    flat_c,
    send,
    recv,
    swap_send,
    swap_recv,
    local,
):
    f32, low = jnp.float32, jnp.bfloat16
    spot = Spot(depth)
    count = 128
    wires = Wires(send, recv)
    mix_all[spot.q] = mix_ref[...]
    greet(spot)
    plane = spread_plane(wires, spot, mix_all)
    next(plane)
    steps = big_scatter(
        wires,
        spot,
        (g_qkv, g_attn, g_gate, g_up, g_down),
        (held_w, held_d, stage_w, stage_d, near_w, near_d, last_w, last_d, ring_w, ring_d, climb_c, flat_c),
        (o_qkv, o_attn, o_gate, o_up, o_down),
        local,
    )
    tick = Ticker(steps, PLAN_B)
    tick()
    next(plane)
    tick()
    taps = tap_rows(spot, small_ref)
    heads = heads_ref[...]
    dt_row, rate_row = heads[0:1], heads[1:2]
    gains = jnp.concatenate(
        [small_ref[spot.q + 8 * i, TILE : TILE + 16, 0:HEAD_M][6:7].astype(f32) for i in range(4)], axis=1
    )
    gain = gain_row(small_ref[:, TILE + 5, 0:128])
    run(plane)
    tick()
    sums = None
    for x in range(2):
        at = pl.ds(x * count, count)
        slot = Slot(spot, small_ref, x, count)
        mix = Mixed(spot, slot, own_ref[at], maps_ref[at], step_ref[at], taps, dt_row, rate_row)
        d_patch = mix_all[pl.ds(x * 4, 4), :, pl.ds(0, D)].reshape(count, D)
        ext = mix_all[pl.ds(x * 4, 4), :, pl.ds(D, 128)].reshape(count, 128).astype(f32)
        back = Back(
            mix, own_ref[at], core_ref[at], ext, d_patch, gains, head_w_ref[...].reshape(256, D), heads, taps, tick
        )
        rows_all[at] = back.rows
        tick()
        head = flat_dot(back.norm, d_patch, ((0,), (0,)))
        head = head.reshape(TILE, PATCH, D)
        head_sum[...] = head if x == 0 else head_sum[...] + head
        new = [*back.taps, back.gain, back.bias, back.rate, back.skip]
        sums = new if sums is None else [a + b for a, b in zip(sums, new)]
        grad = flat_dot(back.rows[:, :512], proj_ref[...], ((1,), (1,)))
        grad = grad + flat_dot(
            back.rows[:, 512:], small_ref[:, :TILE, :].reshape(D, SMALL_COLS), ((1,), (1,))
        )
        parts8[pl.ds(x * 2, 2)] = grad.astype(low).reshape(2, 2, TILE, D)
        tick()
    total8 = sum_plane(wires, spot, parts8, pair8, near8)
    next(total8)
    tick()
    head_low[...] = head_sum[...].reshape(256, D).astype(low).reshape(depth, HEAD_M, D)
    fetch = pltpu.make_async_copy(streams_ref, head_sum, local.at[5 * depth])
    fetch.start()
    next(total8)
    tick()
    norm = norm_ref[...].reshape(2 * count, D)
    rows = rows_all[...]
    for b in range(4):
        block = flat_dot(norm[:, b * 256 : (b + 1) * 256], rows, ((0,), (0,)))
        block = block.astype(low).reshape(8, TILE, COLS)
        col_send[pl.ds(b * 8, 8)] = block[:, :, :512]
        map_send[b] = block[:, :, 512:]
    tick()
    grad_norm = next(total8)
    tick()
    patch_sum = sum_ref[...]
    scale = lax.rsqrt(jnp.mean(patch_sum * patch_sum, axis=1, keepdims=True) + EPSILON)
    along = jnp.mean(grad_norm * gain * patch_sum, axis=1, keepdims=True)
    d_sum = direct_ref[...] + scale * gain * grad_norm - patch_sum * (scale * scale * scale * along)
    gain_sum = jnp.sum(grad_norm * patch_sum * scale, axis=0, keepdims=True)
    lines = sums[: CONV + 1]
    for row in (jnp.concatenate([*sums[CONV + 1 :], jnp.zeros((1, 384), f32)], axis=1), gains_ref[0:1], gains_ref[1:2], gain_sum):
        lines += [row[:, :512], row[:, 512:]]
    lines += [jnp.zeros((16 - len(lines), 512), f32)]
    all_ref[spot.me] = d_sum.astype(low)
    extra_ref[spot.me] = jnp.concatenate(lines, axis=0).astype(low)
    spread = spread_all(wires, spot, all_ref)
    next(spread)
    col_ring = [
        wires.copy(col_send.at[pl.ds(((spot.z + k) % depth) * 8, 8)], col_far.at[k - 1], spot.above(k))
        for k in range(1, depth)
    ]
    tick()
    next(spread)
    map_plane = plane_swap(wires, spot, lambda q: map_send.at[:, q], lambda q: map_near.at[q])
    tick()
    next(spread)
    tick()
    run(spread)
    tick()
    d_all = all_ref[...].reshape(-1, D)
    for b in range(4):
        back_send[pl.ds(b * 8, 8)] = (
            flat_dot(d_all[b * 256 : (b + 1) * 256], patch_ref[...], ((1,), (1,))).astype(low).reshape(8, TILE, 256)
        )
    swap_rows = Swap(
        spot,
        swap_send,
        swap_recv,
        lambda to: back_send.at[to],
        lambda me: o_rows.at[:, pl.ds(pl.multiple_of(me * 256, 256), 256)],
    )
    swap_rows.start()
    extra = spread_all(wires, spot, extra_ref)
    next(extra)
    tick()
    o_rows[:, pl.ds(pl.multiple_of(spot.me * 256, 256), 256)] = back_send[spot.me]
    o_patch[...] = flat_dot(bytes_ref[...], d_all, ((0,), (0,)))
    got(col_ring)
    for q in range(8):
        total = col_send[spot.z * 8 + q].astype(f32)
        for k in range(depth - 1):
            total = total + col_far[k, q].astype(f32)
        col_sum[q] = total.astype(low)
    col_plane = plane_swap(wires, spot, lambda q: col_sum.at[q], lambda q: col_recv.at[q])
    col_recv[spot.q] = col_sum[spot.q]
    got(map_plane)
    map_near[spot.q] = map_send[:, spot.q]
    for t in range(depth):
        total = map_near[0, t].astype(f32)
        for q in range(1, 8):
            total = total + map_near[q, t].astype(f32)
        map_sum[t] = total.astype(low)
    map_ring = [
        wires.copy(map_sum.at[(spot.z + k) % depth], map_far.at[k - 1], spot.above(k)) for k in range(1, depth)
    ]
    head_ring = [
        wires.copy(head_low.at[(spot.z + k) % depth], head_far.at[k - 1], spot.above(k)) for k in range(1, depth)
    ]
    next(extra)
    tick()
    next(extra)
    tick()
    tick()
    tick.rest(REST_B)
    got(head_ring)
    total = head_low[spot.z].astype(f32)
    for k in range(depth - 1):
        total = total + head_far[k].astype(f32)
    o_head[...] = total
    got(col_plane)
    for q in range(8):
        o_cols[q] = col_recv[q].astype(f32)
    got(map_ring)
    total = map_sum[spot.z].astype(f32)
    for k in range(depth - 1):
        total = total + map_far[k].astype(f32)
    o_maps[...] = total
    run(extra)
    swap_rows.arrive()
    fetch.wait()
    for j in range(PATCH):
        o_states[:, j] = head_sum[:, j] + o_rows[:, j * D : (j + 1) * D].astype(f32)
    wires.drain()
    swap_rows.leave()


def backward_call(depth, n_dev, mix, direct, streams, patch_sum, gains, saved, patch_proj, heads, grads):
    f32, low = jnp.float32, jnp.bfloat16
    vmem = pl.BlockSpec(memory_space=pltpu.VMEM)
    anywhere = pl.BlockSpec(memory_space=pl.ANY)
    shape = jax.ShapeDtypeStruct
    deep = grads[4].shape[0] // n_dev
    cut = [g.reshape(depth, 4, 2, g.shape[0] // n_dev, g.shape[1]) for g in grads]
    outs = [shape((TILE, width), f32) for _, width in PARTS] + [
        shape((deep, D), f32),
        shape((256, D), f32),
        shape((TILE, PATCH, D), f32),
        shape((HEAD_M, D), f32),
        shape((8, TILE, 512), f32),
        shape((TILE, COLS - 512), f32),
        shape((n_dev, 16, 512), low),
    ]
    scratch = [
        pltpu.VMEM((n_dev, TILE, D), low),
        pltpu.VMEM((depth, 8, TILE, COLS - 512), low),
        pltpu.VMEM((8, depth, TILE, COLS - 512), low),
        pltpu.VMEM((depth, TILE, COLS - 512), low),
        pltpu.VMEM((depth - 1, TILE, COLS - 512), low),
        pltpu.VMEM((TILE, PATCH * D), low),
        pltpu.VMEM((8, TILE, EXT), low),
        pltpu.VMEM((8 * TILE, COLS), low),
        pltpu.VMEM((TILE, PATCH, D), f32),
        pltpu.VMEM((depth, HEAD_M, D), low),
        pltpu.VMEM((depth - 1, HEAD_M, D), low),
        pltpu.VMEM((n_dev, TILE, 512), low),
        pltpu.VMEM((8, TILE, 512), low),
        pltpu.VMEM((depth - 1, 8, TILE, 512), low),
        pltpu.VMEM((8, TILE, 512), low),
        pltpu.VMEM((n_dev, TILE, 256), low),
        pltpu.VMEM((4, 2, TILE, D), low),
        pltpu.VMEM((4, TILE, D), low),
        pltpu.VMEM((3, TILE, D), low),
        pltpu.VMEM((depth, 4, TILE, WIDE), low),
        pltpu.VMEM((depth, 4, deep, D), low),
        pltpu.VMEM((2, TILE, WIDE), low),
        pltpu.VMEM((2, deep, D), low),
        pltpu.VMEM((depth, 2, TILE, WIDE - FAR_B), low),
        pltpu.VMEM((depth, 2, deep, D), low),
        pltpu.VMEM((depth, TILE, WIDE - FAR_B), low),
        pltpu.VMEM((depth, deep, D), low),
        pltpu.VMEM((depth - 1, TILE, WIDE - FAR_B), low),
        pltpu.VMEM((depth - 1, deep, D), low),
        pltpu.VMEM((depth - 1, 4, TILE, FAR_B), low),
        pltpu.VMEM((3, TILE, FAR_B), low),
        pltpu.SemaphoreType.DMA((N_WIRES,)),
        pltpu.SemaphoreType.DMA((N_WIRES,)),
        pltpu.SemaphoreType.DMA((n_dev,)),
        pltpu.SemaphoreType.DMA((n_dev,)),
        pltpu.SemaphoreType.DMA((5 * depth + 1,)),
    ]
    return pl.pallas_call(
        partial(backward_kernel, depth),
        out_shape=outs,
        in_specs=[vmem] * 2 + [anywhere] + [vmem] * 13 + [anywhere] * 5,
        out_specs=[vmem] * 11,
        scratch_shapes=scratch,
        compiler_params=pltpu.CompilerParams(
            collective_id=1, has_side_effects=True, vmem_limit_bytes=61 * 2**20
        ),
        name="global_backward",
    )(mix, direct, streams.reshape(TILE, PATCH, D), patch_sum, gains, *saved, patch_proj, heads, *cut)


BC = 2 * STATE


def fast_body(
    depth_fsdp,
    byte_states,
    doc_lengths,
    out_grad,
    patch_proj,
    global_gain,
    in_proj,
    conv_weight,
    conv_bias,
    dt_bias,
    a_log,
    skip_weight,
    mixer_gain,
    out_proj,
    attn_gain,
    qkv_proj,
    attn_out,
    ffn_gain,
    gate_proj,
    up_proj,
    down_proj,
):
    f32, low = jnp.float32, jnp.bfloat16
    depth, n_dev = depth_fsdp[0] // 2, depth_fsdp[0] * depth_fsdp[1]
    me = lax.axis_index("dp") * depth_fsdp[1] + lax.axis_index("fsdp")
    rows = byte_states.shape[0]
    patches = rows // PATCH

    shard_rows = in_proj.shape[0]
    maps_and_steps = jnp.pad(in_proj[:, 2 * DI :], ((0, 0), (0, SMALL_COLS - BC - MHEADS)))
    shorts = (conv_bias, global_gain, mixer_gain, attn_gain, ffn_gain, doc_lengths.reshape(-1).astype(low))
    flat, size = jnp.zeros((12 * SMALL_COLS,), low), 12 * SMALL_COLS
    for k, line in enumerate(shorts):
        begin = k * SMALL_COLS
        flat = flat + jnp.pad(line, (begin, size - begin - line.shape[0]))
    taps = jnp.pad(conv_weight.T, ((0, 0), (0, SMALL_COLS - conv_weight.shape[0])))
    vectors = jnp.concatenate([maps_and_steps, taps, flat.reshape(12, SMALL_COLS)])
    by_place = lambda cols: cols.reshape(shard_rows, 4, 8, HEAD_M).transpose(2, 0, 1, 3).reshape(8, shard_rows, 256)
    cols = jnp.concatenate([by_place(in_proj[:, :DI]), by_place(in_proj[:, DI : 2 * DI])], axis=2)
    heads_in = jnp.pad(jnp.stack([dt_bias, -jnp.exp(a_log), skip_weight]), ((0, 5), (0, 128 - MHEADS)))
    rows2 = byte_states.reshape(patches, PATCH * D)
    (block_out, grad_streams, mix, direct, gains), grads, patch_sum, saved = forward_call(
        depth,
        n_dev,
        rows2,
        patch_proj,
        cols,
        vectors,
        out_proj,
        heads_in,
        doc_lengths,
        byte_states,
        out_grad,
        qkv_proj,
        attn_out,
        gate_proj,
        up_proj,
        down_proj,
    )
    (g_qkv, g_attn, g_gate, g_up, g_down, g_patch, grad_states, g_out, g_cols, g_maps, everyone) = backward_call(
        depth,
        n_dev,
        mix,
        direct,
        grad_streams,
        patch_sum,
        gains,
        saved,
        patch_proj,
        heads_in,
        grads,
    )

    lines = everyone[:, : CONV + 9].astype(f32)
    by_plane = jnp.sum(lines.reshape(depth, 8, CONV + 9, 512), axis=0)
    sums = jnp.sum(by_plane, axis=0)
    own_part = lambda row: lax.dynamic_slice_in_dim(row, me * (D // n_dev), D // n_dev, 0)
    pair = lambda k: sums[CONV + 1 + 2 * k : CONV + 3 + 2 * k].reshape(-1)
    by_head = lambda rows_of: rows_of.reshape(8, -1, 4, HEAD_M).transpose(1, 2, 0, 3).reshape(-1, DI)
    heads_of = by_head(by_plane[:, : CONV + 2, :256])
    taps = jnp.concatenate([heads_of[: CONV + 1], sums[: CONV + 1, 256:512]], axis=1)
    share = CONV_CH // n_dev
    taps = lax.dynamic_slice_in_dim(taps, me * share, share, 1)
    gain_m_sum = lax.dynamic_slice_in_dim(heads_of[CONV + 1], me * HEAD_M, HEAD_M, 0)
    head_line = pair(0)
    back_cols = lambda cols: cols.reshape(8, shard_rows, 4, HEAD_M).transpose(1, 2, 0, 3).reshape(shard_rows, DI)
    grad_in_proj = jnp.concatenate(
        [back_cols(g_cols[..., :256]), back_cols(g_cols[..., 256:]), g_maps[:, : BC + MHEADS]], axis=1
    )
    return (
        block_out,
        grad_states.reshape(rows, D),
        g_patch,
        own_part(pair(3)),
        grad_in_proj,
        taps[:CONV].T,
        taps[CONV],
        head_line[256 : 256 + MHEADS],
        head_line[384 : 384 + MHEADS],
        head_line[512 : 512 + MHEADS],
        gain_m_sum,
        g_out,
        own_part(pair(1)),
        g_qkv,
        g_attn,
        own_part(pair(2)),
        g_gate,
        g_up,
        g_down,
    )


def solution(mesh):
    in_specs = (
        P(("dp", "fsdp"), None),
        P("dp", None),
        P(("dp", "fsdp"), None),
        P(("dp", "fsdp"), None),
        P(("dp", "fsdp")),
        P(("dp", "fsdp"), None),
        P(("dp", "fsdp"), None),
        P(("dp", "fsdp")),
        P(),
        P(),
        P(),
        P(("dp", "fsdp")),
        P(("dp", "fsdp"), None),
        P(("dp", "fsdp")),
        P(("dp", "fsdp"), None),
        P(("dp", "fsdp"), None),
        P(("dp", "fsdp")),
        P(("dp", "fsdp"), None),
        P(("dp", "fsdp"), None),
        P(("dp", "fsdp"), None),
    )
    out_specs = (
        P(("dp", "fsdp"), None),
        P(("dp", "fsdp"), None),
        P(("dp", "fsdp"), None),
        P(("dp", "fsdp")),
        P(("dp", "fsdp"), None),
        P(("dp", "fsdp"), None),
        P(("dp", "fsdp")),
        P(),
        P(),
        P(),
        P(("dp", "fsdp")),
        P(("dp", "fsdp"), None),
        P(("dp", "fsdp")),
        P(("dp", "fsdp"), None),
        P(("dp", "fsdp"), None),
        P(("dp", "fsdp")),
        P(("dp", "fsdp"), None),
        P(("dp", "fsdp"), None),
        P(("dp", "fsdp"), None),
    )
    dp, fsdp = mesh.shape["dp"], mesh.shape["fsdp"]
    fast = dp * fsdp == MHEADS and fsdp == 4
    chosen = partial(fast_body, (dp, fsdp)) if fast else body
    return jax.shard_map(chosen, mesh=mesh, in_specs=in_specs, out_specs=out_specs, check_vma=False)
```
